32 devices in a mesh: dp: 4 (over z), ctx: 2 (over y), tp: 4 (over x, core).
Axes of the slice: x: 2, y: 2, z: 4, core: 2. Of those that a mesh axis runs over, the one named last changes fastest.
Arguments:
- q_feat: bfloat16 [2048, 4096], P(('dp', 'ctx'), 'tp'), parts along dimension 0, may hold values from -6 to 6
- k_feat: bfloat16 [2048, 4096], P(('dp', 'ctx'), 'tp'), parts along dimension 0, may hold values from -6 to 6
- v_feat: bfloat16 [2048, 4096], P(('dp', 'ctx'), 'tp'), parts along dimension 0, may hold values from -6 to 6
- short_taps: float32 [3, 3, 4096], P(None, None, 'tp'), may hold values from -3 to 3
- decay_rate: float32 [4096, 16], P('tp'), may hold values from 0.000390625 to 0.04
- residue: float32 [4096, 16], P('tp'), may hold values from -4 to 4
- out_weight: bfloat16 [4096, 4096], P('tp', 'ctx'), may hold values from -0.8125 to 0.8125
- direction: float32 [4096], replicated, may hold values from -120 to 120
Outputs:
- ablated: bfloat16 [2048, 4096], P(('dp', 'ctx'), 'tp'), parts along dimension 0
- feature_level: float32 [2048], P(('dp', 'ctx')), parts along dimension 0
The draws below stay inside these ranges and needn't reach their ends.
There are 4 independent parts, one for each index of `dp`. The reference program is written for one: setup_inputs(seed, part) draws one part's arguments, and reference() takes and returns one part's arrays. A program takes and returns all parts, laid end to end along the dimension named above; an argument that names none is the same for every part. Nothing has to cross between parts.
All inputs are finite; a program needn't handle non-finite values.
Results may differ from the reference program's by a relative error of at most 0.019.
Values may be sent and summed in bfloat16 or wider, within the bound.
No kernel may reach another device: no remote copies, remote signals or barrier semaphores. Data moves between devices by JAX's collectives and lax.ppermute only.
A program may use at most 128 MiB of HBM per device.

```python
import math
import jax
import jax.numpy as jnp
from jax import lax

C = 4096
DOUT = 4096
M = 16
K = 3
SEQ = 512
N_TP = 4


def draw_decay_rate(key, part):
    lowest = 0.2 / SEQ
    highest = 0.04
    spread = jax.random.uniform(key, (C, M), jnp.float32)
    return lowest * (highest / lowest) ** spread


def shared_direction(key):
    value_key = jax.random.fold_in(key, 101)
    scale_key = jax.random.fold_in(key, 202)
    column = jnp.arange(DOUT, dtype=jnp.float32) / DOUT
    values = jax.random.truncated_normal(value_key, -4.0, 4.0, (DOUT,), jnp.float32)
    scales = jnp.exp(jax.random.uniform(scale_key, (DOUT,), jnp.float32) * math.log(10.0) + column * math.log(3.0))
    return values * scales


def draw_direction(key, part):
    return shared_direction(key)


def draw_out_weight(key, part):
    direction = shared_direction(key)
    base_key = jax.random.fold_in(key, 303)
    mix_key = jax.random.fold_in(key, 404)
    base_part = jax.random.truncated_normal(base_key, -4.0, 4.0, (C, DOUT), jnp.float32)
    mixing = jax.random.truncated_normal(mix_key, -4.0, 4.0, (C,), jnp.float32)
    return ((base_part + 0.1 * mixing[:, None] * direction[None, :]) / math.sqrt(C)).astype(jnp.bfloat16)


def block_scale(own_key, shape, cuts, smallest, largest):
    def one(dim, shards_of):
        heights = jax.random.uniform(jax.random.fold_in(jax.random.fold_in(own_key, 6), dim), (shards_of,), jnp.float32, smallest / len(cuts), largest / len(cuts))
        return jnp.repeat(jnp.exp(heights), shape[dim] // shards_of).reshape((-1,) + (1,) * (len(shape) - dim - 1))

    factor_of = one(*cuts[0])
    for cut in cuts[1:]:
        factor_of = factor_of * one(*cut)
    return factor_of


def normal_values(own_key, extent, scale, most, cuts=(), held_as=jnp.bfloat16):
    drawn = scale * jax.random.normal(own_key, extent, jnp.float32)
    if cuts:
        drawn = drawn * block_scale(own_key, extent, cuts, -0.22, 0.18)
    return jnp.clip(drawn, -most, most).astype(held_as)


def setup_inputs(seed: int = 0, part: int = 0) -> dict:
    splits = jax.random.split(jax.random.key(seed), 9)
    part_splits = jax.random.split(jax.random.fold_in(splits[8], part), 9)
    return {
        "q_feat": normal_values(part_splits[0], (SEQ, C), 1.0, 6.0, ((0, 2), (1, 4))),
        "k_feat": normal_values(part_splits[1], (SEQ, C), 1.0, 6.0, ((0, 2), (1, 4))),
        "v_feat": normal_values(part_splits[2], (SEQ, C), 1.0, 6.0, ((0, 2), (1, 4))),
        "short_taps": normal_values(splits[3], (3, K, C), 0.6, 3.0, ((2, 4),), jnp.float32),
        "decay_rate": draw_decay_rate(jax.random.fold_in(splits[8], 71), part),
        "residue": normal_values(splits[5], (C, M), 1.0, 4.0, ((0, 4),), jnp.float32),
        "out_weight": draw_out_weight(jax.random.fold_in(splits[8], 71), part),
        "direction": draw_direction(jax.random.fold_in(splits[8], 71), part),
    }


EPSILON = 1e-06

def short_filter(values, filter_taps):
    length = values.shape[0]
    padded = jnp.concatenate([jnp.zeros((K - 1, values.shape[1]), jnp.float32), values.astype(jnp.float32)], axis=0)
    summed = jnp.zeros((length, values.shape[1]), jnp.float32)
    for offset in range(K):
        summed = summed + filter_taps[offset][None, :] * padded[K - 1 - offset:K - 1 - offset + length]
    return summed

def long_filter(signal, decay_rate, gains):
    block_width = 128 if C % 128 == 0 else C
    block_count = C // block_width
    positions = jnp.arange(SEQ, dtype=jnp.float32)
    signal_blocks = signal.T.reshape(block_count, block_width, SEQ)
    rate_blocks = decay_rate.reshape(block_count, block_width, M)
    gain_blocks = gains.reshape(block_count, block_width, M)
    fft_length = 2 * SEQ

    def one_block(block_items):
        signal_block, rate_block, gain_block = block_items
        response = lax.optimization_barrier(jnp.sum(gain_block[:, :, None] * jnp.exp(-rate_block[:, :, None] * positions[None, None, :]), axis=1))
        product = jnp.fft.rfft(response, n=fft_length) * jnp.fft.rfft(signal_block, n=fft_length)
        return jnp.fft.irfft(product, n=fft_length)[:, :SEQ]
    result = lax.map(one_block, (signal_blocks, rate_blocks, gain_blocks))
    return result.reshape(C, SEQ).T

def reference(q_feat, k_feat, v_feat, short_taps, decay_rate, residue, out_weight, direction):
    query_short = short_filter(q_feat, short_taps[0])
    key_short = short_filter(k_feat, short_taps[1])
    value_short = short_filter(v_feat, short_taps[2])
    gains = residue * jnp.sqrt(-jnp.expm1(-2.0 * decay_rate)) * M ** (-0.5)
    mixed = long_filter(key_short * value_short, decay_rate, gains)
    gated = (query_short * mixed).astype(jnp.bfloat16)
    group_width = C // N_TP
    summed = jnp.zeros((SEQ, DOUT), jnp.float32)
    for group_index in range(N_TP):
        lower = group_index * group_width
        term_block = jnp.dot(gated[:, lower:lower + group_width], out_weight[lower:lower + group_width], preferred_element_type=jnp.float32)
        summed = summed + lax.optimization_barrier(term_block.astype(jnp.bfloat16)).astype(jnp.float32)
    norm_total = jnp.sum(direction * direction) + EPSILON
    feature_level = jnp.dot(summed, direction, precision=lax.Precision.HIGHEST) / norm_total
    ablated = (summed - feature_level[:, None] * direction[None, :]).astype(jnp.bfloat16)
    return (ablated, feature_level)
```

```python
import functools

import jax
import jax.numpy as jnp
from jax import lax
from jax.experimental import pallas as pl
from jax.experimental.pallas import tpu as pltpu
from jax.sharding import PartitionSpec as P

EPSILON = 1e-06
HIGHEST = lax.Precision.HIGHEST
LANES = 128
GROUP = 8
VMEM_LIMIT = 48 * 1024 * 1024
WHOLE = pl.BlockSpec(memory_space=pltpu.VMEM)


def params(limit=VMEM_LIMIT):
    return pltpu.CompilerParams(vmem_limit_bytes=limit)


def spread(source, scratch, rows):
    blocks = source.shape[1] // LANES
    for row in range(0, rows, 16):
        for block in range(blocks):
            piece = source[row : row + 16, block * LANES : (block + 1) * LANES].astype(jnp.float32)
            for half in range(2):
                start = ((row // GROUP + half) * blocks + block) * GROUP
                scratch[start : start + GROUP, :] = piece[half * GROUP : (half + 1) * GROUP]


def token(scratch, group, place, blocks):
    return scratch[pl.ds(group * (blocks * GROUP) + place, blocks, stride=GROUP), :]


def state_kernel(carry_ref, q_ref, k_ref, v_ref, taps_ref, decay_ref, out_ref, k_wide, v_wide):
    rows, width = k_ref.shape
    blocks = width // LANES
    modes = decay_ref.shape[0]
    spread(k_ref, k_wide, rows)
    spread(v_ref, v_wide, rows)
    start = tuple(carry_ref[m] for m in range(modes + 4))

    def step(group, held):
        state, (k2, k1, v2, v1) = list(held[:modes]), held[modes:]
        for place in range(GROUP):
            k0 = token(k_wide, group, place, blocks)
            v0 = token(v_wide, group, place, blocks)
            key = taps_ref[3] * k0 + taps_ref[4] * k1 + taps_ref[5] * k2
            value = taps_ref[6] * v0 + taps_ref[7] * v1 + taps_ref[8] * v2
            signal = key * value
            state = [decay_ref[m] * state[m] + signal for m in range(modes)]
            k2, k1, v2, v1 = k1, k0, v1, v0
        return tuple(state) + (k2, k1, v2, v1)

    held = lax.fori_loop(0, rows // GROUP, step, start)
    for m in range(modes + 4):
        out_ref[m] = held[m]
    tail = q_ref[...].astype(jnp.float32)
    for row in range(2):
        for block in range(blocks):
            out_ref[modes + 4 + row, block : block + 1, :] = tail[
                14 + row : 15 + row, block * LANES : (block + 1) * LANES
            ]


def filter_kernel(
    carry_ref, q_ref, k_ref, v_ref, taps_ref, decay_ref, gain_ref, gated_ref, out_ref, q_wide, k_wide, v_wide, g_wide
):
    rows, width = k_ref.shape
    blocks = width // LANES
    modes = decay_ref.shape[0]
    spread(q_ref, q_wide, rows)
    spread(k_ref, k_wide, rows)
    spread(v_ref, v_wide, rows)
    start = tuple(carry_ref[m] for m in range(modes + 6))

    def step(group, held):
        state, (k2, k1, v2, v1, q2, q1) = list(held[:modes]), held[modes:]
        for place in range(GROUP):
            q0 = token(q_wide, group, place, blocks)
            k0 = token(k_wide, group, place, blocks)
            v0 = token(v_wide, group, place, blocks)
            query = taps_ref[0] * q0 + taps_ref[1] * q1 + taps_ref[2] * q2
            key = taps_ref[3] * k0 + taps_ref[4] * k1 + taps_ref[5] * k2
            value = taps_ref[6] * v0 + taps_ref[7] * v1 + taps_ref[8] * v2
            signal = key * value
            state = [decay_ref[m] * state[m] + signal for m in range(modes)]
            sums = [gain_ref[m] * state[m] for m in range(modes)]
            while len(sums) > 1:
                sums = [sums[i] + sums[i + 1] for i in range(0, len(sums), 2)]
            g_wide[pl.ds(group * (blocks * GROUP) + place, blocks, stride=GROUP), :] = query * sums[0]
            k2, k1, v2, v1, q2, q1 = k1, k0, v1, v0, q1, q0
        return tuple(state) + (k2, k1, v2, v1, q2, q1)

    held = lax.fori_loop(0, rows // GROUP, step, start)
    for m in range(modes + 6):
        out_ref[m] = held[m]
    for row in range(0, rows, 16):
        for block in range(blocks):
            halves = []
            for half in range(2):
                begin = ((row // GROUP + half) * blocks + block) * GROUP
                halves.append(g_wide[begin : begin + GROUP, :])
            gated_ref[row : row + 16, block * LANES : (block + 1) * LANES] = jnp.concatenate(halves, axis=0).astype(
                jnp.bfloat16
            )


def rows_block(rows, width, index):
    return pl.BlockSpec((rows, width), lambda i: (index, 0))


def whole_block(shape):
    return pl.BlockSpec(shape, lambda i: (0,) * len(shape))


def run_state(carry, q, k, v, taps, decay):
    rows, width = k.shape
    wide = pltpu.VMEM((rows * width // LANES, LANES), jnp.float32)
    return pl.pallas_call(
        state_kernel,
        grid=(1,),
        out_shape=jax.ShapeDtypeStruct(carry.shape, jnp.float32),
        in_specs=[whole_block(carry.shape)]
        + [pl.BlockSpec((16, width), lambda i: (rows // 16 - 1, 0))]
        + [rows_block(rows, width, 0)] * 2
        + [whole_block(taps.shape), whole_block(decay.shape)],
        out_specs=whole_block(carry.shape),
        scratch_shapes=[wide, wide],
        compiler_params=params(),
        cost_estimate=pl.CostEstimate(flops=rows * width * 44, bytes_accessed=rows * width * 4, transcendentals=0),
        name="end_state",
    )(carry, q, k, v, taps, decay)


def run_filter(carry, q, k, v, taps, decay, gain, index, count):
    rows, width = k.shape
    rows //= count
    wide = pltpu.VMEM((rows * width // LANES, LANES), jnp.float32)
    return pl.pallas_call(
        filter_kernel,
        grid=(1,),
        out_shape=(
            jax.ShapeDtypeStruct((rows, width), jnp.bfloat16),
            jax.ShapeDtypeStruct(carry.shape, jnp.float32),
        ),
        in_specs=[whole_block(carry.shape)]
        + [rows_block(rows, width, index)] * 3
        + [whole_block(taps.shape), whole_block(decay.shape), whole_block(gain.shape)],
        out_specs=(rows_block(rows, width, 0), whole_block(carry.shape)),
        scratch_shapes=[wide] * 4,
        compiler_params=params(),
        cost_estimate=pl.CostEstimate(flops=rows * width * 80, bytes_accessed=rows * width * 8, transcendentals=0),
        name="long_filter",
    )(carry, q, k, v, taps, decay, gain)


def modal_arrays(short_taps, decay_rate, residue):
    width, modes = decay_rate.shape
    blocks = width // LANES
    decay = jnp.exp(-decay_rate).T.reshape(modes, blocks, LANES)
    gain = (residue * jnp.sqrt(-jnp.expm1(-2.0 * decay_rate)) * modes ** (-0.5)).T.reshape(modes, blocks, LANES)
    taps = short_taps.reshape(9, blocks, LANES)
    return taps, decay, gain


def last_rows(k, v, q, blocks):
    pieces = jnp.concatenate([k[-2:], v[-2:], q[-2:]], axis=0).astype(jnp.float32)
    return pieces.reshape(6, blocks, LANES)


def split_three(x):
    high = x.astype(jnp.bfloat16)
    rest = x - high.astype(jnp.float32)
    middle = rest.astype(jnp.bfloat16)
    low = (rest - middle.astype(jnp.float32)).astype(jnp.bfloat16)
    return high, middle, low


def dot_rows(row, matrix):
    parts = jnp.concatenate(list(split_three(row)) + [jnp.zeros((13, row.shape[1]), jnp.bfloat16)], axis=0)
    out = lax.dot_general(parts, matrix, (((1,), (1,)), ((), ())), preferred_element_type=jnp.float32)
    return out[0:1] + out[1:2] + out[2:3]


def weight_direction_kernel(weight_ref, direction_ref, out_ref):
    out_ref[...] = dot_rows(direction_ref[...], weight_ref[...])


def project_kernel(side, with_level, *refs):
    if with_level:
        side_ref, gated_ref, weight_ref, inner_ref, keep_ref, send_ref, level_ref = refs
        level_ref[...] = dot_rows(inner_ref[...], gated_ref[...])
    else:
        side_ref, gated_ref, weight_ref, keep_ref, send_ref = refs
    width = keep_ref.shape[1]
    mine = side_ref[0]
    for which, ref in ((1 - mine, send_ref), (mine, keep_ref)):
        for part in range(0, width, 256):
            columns = pl.ds(pl.multiple_of(which * width + part, 256), 256)
            out = jnp.dot(gated_ref[...], weight_ref[:, columns], preferred_element_type=jnp.float32)
            ref[:, part : part + 256] = out.astype(ref.dtype)


def run_project(side, gated, weight, inner):
    rows = gated.shape[0]
    width = weight.shape[1] // 2
    out_shape = [
        jax.ShapeDtypeStruct((rows, width), jnp.float32),
        jax.ShapeDtypeStruct((rows, width), jnp.bfloat16),
    ]
    operands = [side, gated, weight]
    in_specs = [pl.BlockSpec(memory_space=pltpu.SMEM), WHOLE, WHOLE]
    if inner is not None:
        operands.append(inner)
        in_specs.append(WHOLE)
        out_shape.append(jax.ShapeDtypeStruct((1, rows), jnp.float32))
    return pl.pallas_call(
        functools.partial(project_kernel, None, inner is not None),
        out_shape=out_shape,
        in_specs=in_specs,
        out_specs=[WHOLE] * len(out_shape),
        compiler_params=params(),
        cost_estimate=pl.CostEstimate(
            flops=4 * rows * weight.shape[0] * width, bytes_accessed=weight.size * 2, transcendentals=0
        ),
        name="project",
    )(*operands)


def finish_kernel(own_sides, *refs):
    flag_ref, level_ref, direction_ref = refs[:3]
    keeps = refs[3 : 3 + own_sides]
    cores = refs[3 + own_sides : 3 + 2 * own_sides]
    hops = refs[3 + 2 * own_sides : 3 + 3 * own_sides]
    arrived = refs[3 + 3 * own_sides : 3 + 4 * own_sides]
    out_ref = refs[-1]
    direction = direction_ref[...]
    rows = keeps[0].shape[0]
    for i in range(own_sides):
        level = jnp.transpose(jnp.broadcast_to(level_ref[0:1, i * rows : (i + 1) * rows], (LANES, rows)))[:, 0:1]
        here = slice(i * rows, (i + 1) * rows)

        @pl.when(flag_ref[0] == 1)
        def _():
            total = keeps[i][...] + cores[i][...].astype(jnp.float32) + hops[i][...].astype(jnp.float32)
            out_ref[here, :] = (total - level * direction).astype(jnp.bfloat16)

        @pl.when(flag_ref[0] == 0)
        def _():
            out_ref[here, :] = (arrived[i][...].astype(jnp.float32) - level * direction).astype(jnp.bfloat16)


def plane_plan(q, k, v, short_taps, decay_rate, residue, out_weight, direction):
    rows, width = q.shape
    blocks = width // LANES
    modes = decay_rate.shape[1]
    count = 2
    ctx, tp = lax.axis_index("ctx"), lax.axis_index("tp")
    axes = ("ctx", "tp")
    side = (tp % 2).astype(jnp.int32).reshape(1)
    keeper = (tp // 2 == ctx).astype(jnp.int32).reshape(1)

    forward = [(p, 4 + p) for p in range(4)]
    across = [(4 * c + p, 4 * (1 - c) + p) for c in range(2) for p in range(4)]
    sibling = [(4 * c + p, 4 * c + (p ^ 1)) for c in range(2) for p in range(4)]
    pair = [(4 * c + p, 4 * c + (p ^ 2)) for c in range(2) for p in range(4)]
    inward = [(4 * c + 2 * (1 - c) + a, 4 * c + 2 * c + a) for c in range(2) for a in range(2)]
    outward = [(4 * c + 2 * c + a, 4 * (1 - c) + 2 * c + a) for c in range(2) for a in range(2)]

    taps, decay, gain = modal_arrays(short_taps, decay_rate, residue)
    zero = jnp.zeros((modes + 6, blocks, LANES), jnp.float32)
    carry = lax.ppermute(run_state(zero, q, k, v, taps, decay), axes, forward)

    half = out_weight.shape[1]
    direction_half = lax.dynamic_slice_in_dim(direction, ctx * half, half, 0).reshape(1, half)
    inner = pl.pallas_call(
        weight_direction_kernel,
        out_shape=jax.ShapeDtypeStruct((1, width), jnp.float32),
        in_specs=[WHOLE, WHOLE],
        out_specs=WHOLE,
        compiler_params=params(),
        name="weight_direction",
    )(out_weight, direction_half)
    inner = inner + lax.ppermute(inner, axes, across)

    gated, theirs = [], []
    for index in range(count):
        piece, carry = run_filter(carry, q, k, v, taps, decay, gain, index, count)
        gated.append(piece)
        theirs.append(lax.ppermute(piece, axes, across))

    keeps, cores, hops, levels = [], [], [], []
    for index in range(count):
        keep, send, level = run_project(side, gated[index], out_weight, inner)
        core = lax.ppermute(send, axes, sibling)
        hop = lax.ppermute((keep + core.astype(jnp.float32)).astype(jnp.bfloat16), axes, inward)
        keeps.append(keep)
        cores.append(core)
        hops.append(hop)
        levels.append(level)
    arrived = []
    for index in range(count):
        keep, send = run_project(side, theirs[index], out_weight, None)
        core = lax.ppermute(send, axes, sibling)
        merged = keep + core.astype(jnp.float32)
        hop = lax.ppermute(merged.astype(jnp.bfloat16), axes, inward)
        arrived.append(lax.ppermute((merged + hop.astype(jnp.float32)).astype(jnp.bfloat16), axes, outward))

    level = jnp.concatenate(levels, axis=1)
    level = level + lax.ppermute(level, axes, sibling)
    level = level + lax.ppermute(level, axes, pair)
    level = level / (jnp.sum(direction * direction) + EPSILON)
    out_width = half // 2
    direction_here = lax.dynamic_slice_in_dim(direction, tp * out_width, out_width, 0).reshape(1, out_width)
    ablated = pl.pallas_call(
        functools.partial(finish_kernel, count),
        out_shape=jax.ShapeDtypeStruct((rows, out_width), jnp.bfloat16),
        in_specs=[pl.BlockSpec(memory_space=pltpu.SMEM)] + [WHOLE] * (2 + 4 * count),
        out_specs=WHOLE,
        compiler_params=params(),
        name="finish",
    )(keeper, level, direction_here, *keeps, *cores, *hops, *arrived)
    return ablated, level.reshape(rows)


def gather_plan(q, k, v, short_taps, decay_rate, residue, out_weight, direction):
    rows, width = q.shape
    blocks = width // LANES
    modes = decay_rate.shape[1]
    ctx, tp = lax.axis_index("ctx"), lax.axis_index("tp")
    ctx_size = lax.axis_size("ctx")
    taps, decay, gain = modal_arrays(short_taps, decay_rate, residue)
    next_one = [(i, i + 1) for i in range(ctx_size - 1)]
    halo = lax.ppermute(last_rows(k, v, q, blocks), "ctx", next_one)
    zero = jnp.zeros((modes, blocks, LANES), jnp.float32)
    ended = run_state(jnp.concatenate([zero, halo], axis=0), q, k, v, taps, decay)[:modes]
    total = jnp.exp(-decay_rate * rows).T.reshape(modes, blocks, LANES)
    reach = 1
    while reach < ctx_size:
        earlier = lax.ppermute(ended, "ctx", [(i, i + reach) for i in range(ctx_size - reach)])
        ended = ended + total * earlier
        total = total * total
        reach *= 2
    start = lax.ppermute(ended, "ctx", next_one)
    gated, _ = run_filter(jnp.concatenate([start, halo], axis=0), q, k, v, taps, decay, gain, 0, 1)
    partial_terms = lax.dot_general(
        gated,
        lax.all_gather(out_weight, "ctx", axis=1, tiled=True),
        (((1,), (0,)), ((), ())),
        preferred_element_type=jnp.float32,
    )
    summed = lax.psum_scatter(
        partial_terms.astype(jnp.bfloat16), "tp", scatter_dimension=1, tiled=True
    ).astype(jnp.float32)
    width_here = summed.shape[1]
    direction_here = lax.dynamic_slice_in_dim(direction, tp * width_here, width_here, 0)
    norm_total = jnp.sum(direction * direction) + EPSILON
    local_inner = jnp.dot(summed, direction_here, precision=HIGHEST)
    feature_level = lax.psum(local_inner, "tp") / norm_total
    ablated = (summed - feature_level[:, None] * direction_here[None, :]).astype(jnp.bfloat16)
    return ablated, feature_level


def solution(mesh):
    placed = (
        P(("dp", "ctx"), "tp"),
        P(("dp", "ctx"), "tp"),
        P(("dp", "ctx"), "tp"),
        P(None, None, "tp"),
        P("tp", None),
        P("tp", None),
        P("tp", "ctx"),
        P(),
    )
    plane = mesh.shape["ctx"] == 2 and mesh.shape["tp"] == 4
    return jax.shard_map(
        plane_plan if plane else gather_plan,
        mesh=mesh,
        in_specs=placed,
        out_specs=(P(("dp", "ctx"), "tp"), P(("dp", "ctx"))),
        check_vma=False,
    )
```

```python
import functools

import jax
import jax.numpy as jnp
from jax import lax
from jax.experimental import pallas as pl
from jax.experimental.pallas import tpu as pltpu
from jax.sharding import PartitionSpec as P

EPSILON = 1e-06
HIGHEST = lax.Precision.HIGHEST
LANES = 128
GROUP = 8
STEP = 16
WHOLE = pl.BlockSpec(memory_space=pltpu.VMEM)
SCALARS = pl.BlockSpec(memory_space=pltpu.SMEM)
AWAY = pl.BlockSpec(memory_space=pltpu.HBM)


def params(mebibytes=20):
    return pltpu.CompilerParams(vmem_limit_bytes=mebibytes * 1024 * 1024)


def cost(flops):
    return pl.CostEstimate(flops=flops, bytes_accessed=1024, transcendentals=0)


def spread(source, scratch, row, to):
    blocks = source.shape[1] // LANES
    for block in range(blocks):
        piece = source[pl.ds(row, STEP), block * LANES : (block + 1) * LANES].astype(jnp.float32)
        for half in range(STEP // GROUP):
            start = (half * blocks + block) * GROUP
            scratch[pl.ds(to + start, GROUP), :] = piece[half * GROUP : (half + 1) * GROUP]


def spread_rows(source, target):
    count, width = source.shape
    blocks = width // LANES
    for block in range(blocks):
        target[pl.ds(block, count, stride=blocks), :] = source[:, block * LANES : (block + 1) * LANES]


def place_of(index, blocks):
    return pl.ds((index // GROUP) * (blocks * GROUP) + index % GROUP, blocks, stride=GROUP)


def tile(ref, index, blocks):
    return ref[index * blocks : (index + 1) * blocks, :]


def moving_tile(index, blocks):
    return pl.ds(pl.multiple_of(index * blocks, blocks), blocks)


def front_kernel(
    k_hbm, v_hbm, q_hbm, taps_hbm, rate_hbm,
    carry_ref, signal_ref, decay_ref, taps_ref, edge_ref, rate_ref,
    k_near, v_near, q_near, taps_near, k_wide, v_wide, sems,
):
    rows, width = k_near.shape
    blocks = width // LANES
    modes = rate_ref.shape[0]
    pieces = sems.shape[0] // 2 - 2
    height = rows // pieces

    def part(i):
        here = pl.ds(i * height, height)
        return (
            pltpu.make_async_copy(k_hbm.at[here], k_near.at[here], sems.at[2 * i]),
            pltpu.make_async_copy(v_hbm.at[here], v_near.at[here], sems.at[2 * i + 1]),
        )

    rate_copy = pltpu.make_async_copy(rate_hbm, rate_ref, sems.at[2 * pieces])
    taps_copy = pltpu.make_async_copy(taps_hbm, taps_near, sems.at[2 * pieces + 1])
    tail_copy = pltpu.make_async_copy(q_hbm.at[pl.ds(rows - STEP, STEP)], q_near, sems.at[2 * pieces + 2])
    rate_copy.start()
    taps_copy.start()
    for i in range(pieces):
        for copy in part(i):
            copy.start()
    tail_copy.start()
    rate_copy.wait()
    taps_copy.wait()
    spread_rows(jnp.exp(-rate_ref[...]), decay_ref)
    for i in range(3):
        for block in range(blocks):
            taps_ref[pl.ds(3 * i * blocks + block, 3, stride=blocks), :] = taps_near[
                i, :, block * LANES : (block + 1) * LANES
            ]
    zero = jnp.zeros((blocks, LANES), jnp.float32)
    key_taps = [tile(taps_ref, 3 + j, blocks) for j in range(3)]
    value_taps = [tile(taps_ref, 6 + j, blocks) for j in range(3)]

    def step(row, held, first):
        spread(k_near, k_wide, row, 0)
        spread(v_near, v_wide, row, 0)
        state, (k2, k1, v2, v1) = list(held[:modes]), held[modes:]
        for index in range(STEP):
            k0 = k_wide[place_of(index, blocks), :]
            v0 = v_wide[place_of(index, blocks), :]
            key = key_taps[0] * k0 + key_taps[1] * k1 + key_taps[2] * k2
            value = value_taps[0] * v0 + value_taps[1] * v1 + value_taps[2] * v2
            if first and index < 2:
                edge_ref[index * blocks : (index + 1) * blocks, :] = key
                edge_ref[(2 + index) * blocks : (3 + index) * blocks, :] = value
            signal = key * value
            signal_ref[moving_tile(row + index, blocks), :] = signal
            state = [tile(decay_ref, m, blocks) * state[m] + signal for m in range(modes)]
            k2, k1, v2, v1 = k1, k0, v1, v0
        return tuple(state) + (k2, k1, v2, v1)

    held = (zero,) * (modes + 4)
    for i in range(pieces):
        for copy in part(i):
            copy.wait()
        begin = 0
        if i == 0:
            held = step(0, held, True)
            begin = 1
        held = lax.fori_loop(
            begin,
            height // STEP,
            lambda j, held, i=i: step(pl.multiple_of(i * height + j * STEP, STEP), held, False),
            held,
        )
    for m in range(modes + 4):
        carry_ref[m * blocks : (m + 1) * blocks, :] = held[m]
    tail_copy.wait()
    spread(q_near, k_wide, 0, 0)
    for i in range(2):
        start = (modes + 4 + i) * blocks
        carry_ref[start : start + blocks, :] = k_wide[place_of(STEP - 2 + i, blocks), :]


def run_front(q, k, v, short_taps, rate):
    rows, width = k.shape
    modes = rate.shape[0]
    blocks = width // LANES
    pieces = 4

    def wide(n):
        return jax.ShapeDtypeStruct((n * blocks, LANES), jnp.float32)

    return pl.pallas_call(
        front_kernel,
        out_shape=(
            wide(modes + 6),
            wide(rows),
            wide(modes),
            wide(9),
            wide(4),
            jax.ShapeDtypeStruct(rate.shape, jnp.float32),
        ),
        in_specs=[AWAY] * 5,
        out_specs=[WHOLE] * 6,
        scratch_shapes=[
            pltpu.VMEM((rows, width), jnp.bfloat16),
            pltpu.VMEM((rows, width), jnp.bfloat16),
            pltpu.VMEM((STEP, width), jnp.bfloat16),
            pltpu.VMEM(short_taps.shape, jnp.float32),
            pltpu.VMEM((STEP * blocks, LANES), jnp.float32),
            pltpu.VMEM((STEP * blocks, LANES), jnp.float32),
            pltpu.SemaphoreType.DMA((2 * pieces + 4,)),
        ],
        compiler_params=params(),
        cost_estimate=cost(10**8),
        name="front",
    )(k, v, q, short_taps, rate)


def local_kernel(
    q_hbm, signal_ref, decay_ref, taps_ref, gain_near, out_ref, query_ref, gain_ref, q_near, q_wide, sems
):
    rows, width = q_near.shape
    blocks = width // LANES
    modes = gain_near.shape[0]
    pieces = sems.shape[0]
    height = rows // pieces

    def part(i):
        here = pl.ds(i * height, height)
        return pltpu.make_async_copy(q_hbm.at[here], q_near.at[here], sems.at[i])

    for i in range(pieces):
        part(i).start()
    spread_rows(gain_near[...], gain_ref)
    zero = jnp.zeros((blocks, LANES), jnp.float32)
    taps = [tile(taps_ref, j, blocks) for j in range(3)]

    def step(row, held):
        spread(q_near, q_wide, row, 0)
        state, (q2, q1) = list(held[:modes]), held[modes:]
        for index in range(STEP):
            q0 = q_wide[place_of(index, blocks), :]
            here = moving_tile(row + index, blocks)
            signal = signal_ref[here, :]
            query_ref[here, :] = taps[0] * q0 + taps[1] * q1 + taps[2] * q2
            state = [tile(decay_ref, m, blocks) * state[m] + signal for m in range(modes)]
            sums = [tile(gain_ref, m, blocks) * state[m] for m in range(modes)]
            while len(sums) > 1:
                sums = [sums[i] + sums[i + 1] for i in range(0, len(sums), 2)]
            out_ref[here, :] = sums[0]
            q2, q1 = q1, q0
        return tuple(state) + (q2, q1)

    held = (zero,) * (modes + 2)
    for i in range(pieces):
        part(i).wait()
        held = lax.fori_loop(
            0,
            height // STEP,
            lambda j, held, i=i: step(pl.multiple_of(i * height + j * STEP, STEP), held),
            held,
        )


def run_local(q, signal, decay, taps, gain):
    rows, width = q.shape
    blocks = width // LANES
    pieces = 2
    wide = jax.ShapeDtypeStruct((rows * blocks, LANES), jnp.float32)
    return pl.pallas_call(
        local_kernel,
        out_shape=(wide, wide, jax.ShapeDtypeStruct(decay.shape, jnp.float32)),
        in_specs=[AWAY] + [WHOLE] * 4,
        out_specs=[WHOLE] * 3,
        scratch_shapes=[
            pltpu.VMEM((rows, width), jnp.bfloat16),
            pltpu.VMEM((STEP * blocks, LANES), jnp.float32),
            pltpu.SemaphoreType.DMA((pieces,)),
        ],
        compiler_params=params(),
        cost_estimate=cost(10**6),
        name="local_filter",
    )(q, signal, decay, taps, gain)


def correct_kernel(count, blocks, *refs):
    carry_ref, decay_ref, gain_ref, taps_ref, edge_ref, local_ref, query_ref = refs[:7]
    outs, wide = refs[7:-1], refs[-1]
    modes = decay_ref.shape[0] // blocks
    height = outs[0].shape[0]
    width = outs[0].shape[1]
    k2, k1, v2, v1, q2, q1 = [tile(carry_ref, modes + i, blocks) for i in range(6)]
    tap = [tile(taps_ref, i, blocks) for i in range(9)]
    key0, key1, value0, value1 = [tile(edge_ref, i, blocks) for i in range(4)]
    extra = [
        (key0 + tap[4] * k1 + tap[5] * k2) * (value0 + tap[7] * v1 + tap[8] * v2) - key0 * value0,
        (key1 + tap[5] * k1) * (value1 + tap[8] * v1) - key1 * value1,
    ]
    query_extra = [tap[1] * q1 + tap[2] * q2, tap[2] * q1]
    state = [tile(gain_ref, m, blocks) * tile(carry_ref, m, blocks) for m in range(modes)]

    def step(out_ref, row, base, state, first):
        state = list(state)
        for index in range(STEP):
            here = moving_tile(base + row + index, blocks)
            state = [tile(decay_ref, m, blocks) * state[m] for m in range(modes)]
            query = query_ref[here, :]
            if first and index < 2:
                state = [state[m] + tile(gain_ref, m, blocks) * extra[index] for m in range(modes)]
                query = query + query_extra[index]
            sums = state
            while len(sums) > 1:
                sums = [sums[i] + sums[i + 1] for i in range(0, len(sums), 2)]
            wide[place_of(index, blocks), :] = query * (local_ref[here, :] + sums[0])
        for block in range(blocks):
            halves = [
                wide[(half * blocks + block) * GROUP : (half * blocks + block + 1) * GROUP, :]
                for half in range(STEP // GROUP)
            ]
            out_ref[pl.ds(row, STEP), block * LANES : (block + 1) * LANES] = jnp.concatenate(
                halves, axis=0
            ).astype(jnp.bfloat16)
        return tuple(state)

    state = tuple(state)
    for i in range(count):
        begin = 0
        if i == 0:
            state = step(outs[0], 0, 0, state, True)
            begin = 1
        state = lax.fori_loop(
            begin,
            height // STEP,
            lambda j, state, i=i: step(
                outs[i], pl.multiple_of(j * STEP, STEP), i * height, state, False
            ),
            state,
        )


def run_correct(carry, decay, gain, taps, edge, local, query, blocks, count):
    rows = local.shape[0] // blocks
    width = blocks * LANES
    return pl.pallas_call(
        functools.partial(correct_kernel, count, blocks),
        out_shape=[jax.ShapeDtypeStruct((rows // count, width), jnp.bfloat16)] * count,
        in_specs=[WHOLE] * 7,
        out_specs=[WHOLE] * count,
        scratch_shapes=[pltpu.VMEM((STEP * blocks, LANES), jnp.float32)],
        compiler_params=params(),
        cost_estimate=cost(10**8),
        name="carried_filter",
    )(carry, decay, gain, taps, edge, local, query)


def gains_of(rate, residue):
    return residue * jnp.sqrt(-jnp.expm1(-2.0 * rate)) * rate.shape[0] ** (-0.5)


def split_three(x):
    high = x.astype(jnp.bfloat16)
    rest = x - high.astype(jnp.float32)
    middle = rest.astype(jnp.bfloat16)
    low = (rest - middle.astype(jnp.float32)).astype(jnp.bfloat16)
    return high, middle, low


def dot_rows(row, matrix):
    parts = jnp.concatenate(list(split_three(row)) + [jnp.zeros((13, row.shape[1]), jnp.bfloat16)], axis=0)
    out = lax.dot_general(parts, matrix, (((1,), (1,)), ((), ())), preferred_element_type=jnp.float32)
    return out[0:1] + out[1:2] + out[2:3]


def weight_kernel(place_ref, weight_hbm, direction_ref, weight_ref, inner_ref, norm_ref, sems):
    depth, width = weight_ref.shape
    pieces = sems.shape[0]
    height = depth // pieces

    def part(i):
        here = pl.ds(i * height, height)
        return pltpu.make_async_copy(weight_hbm.at[here], weight_ref.at[here], sems.at[i])

    for i in range(pieces):
        part(i).start()
    everything = direction_ref[...]
    norm_ref[...] = jnp.broadcast_to(
        jnp.sum(everything * everything, axis=1, keepdims=True) + EPSILON, norm_ref.shape
    )
    here = direction_ref[:, pl.ds(pl.multiple_of(place_ref[0] * width, LANES), width)]
    for i in range(pieces):
        part(i).wait()
        inner_ref[:, i * height : (i + 1) * height] = dot_rows(here, weight_ref[i * height : (i + 1) * height, :])


def run_weight(place, weight, direction):
    pieces = 4
    return pl.pallas_call(
        weight_kernel,
        out_shape=(
            jax.ShapeDtypeStruct(weight.shape, weight.dtype),
            jax.ShapeDtypeStruct((1, weight.shape[0]), jnp.float32),
            jax.ShapeDtypeStruct((1, LANES), jnp.float32),
        ),
        in_specs=[SCALARS, AWAY, WHOLE],
        out_specs=[WHOLE] * 3,
        scratch_shapes=[pltpu.SemaphoreType.DMA((pieces,))],
        compiler_params=params(),
        cost_estimate=cost(10**6),
        name="weights",
    )(place, weight, direction)


def project_kernel(count, place_ref, weight_ref, *refs):
    pieces, (keep_ref, send_ref) = refs[:count], refs[count:]
    width = keep_ref.shape[1]
    height = pieces[0].shape[0]
    mine = place_ref[1] % 2
    for which, ref in ((1 - mine, send_ref), (mine, keep_ref)):
        for part in range(0, width, 256):
            columns = weight_ref[:, pl.ds(pl.multiple_of(which * width + part, 256), 256)]
            for i, piece in enumerate(pieces):
                out = jnp.dot(piece[...], columns, preferred_element_type=jnp.float32)
                ref[i * height : (i + 1) * height, part : part + 256] = out.astype(ref.dtype)


def run_project(place, weight, pieces):
    rows = sum(piece.shape[0] for piece in pieces)
    width = weight.shape[1] // 2
    return pl.pallas_call(
        functools.partial(project_kernel, len(pieces)),
        out_shape=[
            jax.ShapeDtypeStruct((rows, width), jnp.float32),
            jax.ShapeDtypeStruct((rows, width), jnp.bfloat16),
        ],
        in_specs=[SCALARS] + [WHOLE] * (1 + len(pieces)),
        out_specs=[WHOLE] * 2,
        compiler_params=params(),
        cost_estimate=cost(10**6),
        name="project",
    )(place, weight, *pieces)


def level_kernel(count, inner_ref, other_ref, *refs):
    pieces, out_ref = refs[:count], refs[-1]
    inner = inner_ref[...] + other_ref[...]
    height = pieces[0].shape[0]
    for i, piece in enumerate(pieces):
        out_ref[:, i * height : (i + 1) * height] = dot_rows(inner, piece[...])


def run_level(inner, other, pieces):
    rows = sum(piece.shape[0] for piece in pieces)
    return pl.pallas_call(
        functools.partial(level_kernel, len(pieces)),
        out_shape=jax.ShapeDtypeStruct((1, rows), jnp.float32),
        in_specs=[WHOLE] * (2 + len(pieces)),
        out_specs=WHOLE,
        compiler_params=params(),
        cost_estimate=cost(10**6),
        name="level",
    )(inner, other, *pieces)


def finish_kernel(count, place_ref, level_ref, direction_ref, keep_ref, core_ref, hop_ref, *refs):
    straight, diagonal, out_ref = refs[:count], refs[count : 2 * count], refs[-1]
    width = out_ref.shape[1]
    height = straight[0].shape[0]
    direction = direction_ref[:, pl.ds(pl.multiple_of(place_ref[1] * width, LANES), width)]
    keeper = place_ref[1] // 2 == place_ref[0]
    for i in range(count):
        here = slice(i * height, (i + 1) * height)
        level = jnp.transpose(jnp.broadcast_to(level_ref[0:1, here], (LANES, height)))[:, 0:1]

        @pl.when(keeper)
        def _():
            total = keep_ref[here, :] + core_ref[here, :].astype(jnp.float32) + hop_ref[here, :].astype(jnp.float32)
            out_ref[here, :] = (total - level * direction).astype(jnp.bfloat16)

        @pl.when(jnp.logical_not(keeper))
        def _():
            total = straight[i][...].astype(jnp.float32) + diagonal[i][...].astype(jnp.float32)
            out_ref[here, :] = (total - level * direction).astype(jnp.bfloat16)


def plane_plan(q, k, v, short_taps, decay_rate, residue, out_weight, direction):
    rows, width = q.shape
    blocks = width // LANES
    count = 2
    ctx, tp = lax.axis_index("ctx"), lax.axis_index("tp")
    axes = ("ctx", "tp")
    place = jnp.stack([ctx, tp]).astype(jnp.int32)
    direction = direction.reshape(1, -1)

    forward = [(p, 4 + p) for p in range(4)]
    across = [(4 * c + p, 4 * (1 - c) + p) for c in range(2) for p in range(4)]
    sibling = [(4 * c + p, 4 * c + (p ^ 1)) for c in range(2) for p in range(4)]
    pair = [(4 * c + p, 4 * c + (p ^ 2)) for c in range(2) for p in range(4)]
    inward = [(4 * c + 2 * (1 - c) + a, 4 * c + 2 * c + a) for c in range(2) for a in range(2)]
    outward = [(4 * c + 2 * c + a, 4 * (1 - c) + 2 * c + a) for c in range(2) for a in range(2)]
    slanted = [(4 * c + 2 * (1 - c) + a, 4 * (1 - c) + 2 * c + a) for c in range(2) for a in range(2)]

    ended, signal, decay, taps, edge, rate = run_front(q, k, v, short_taps, decay_rate.T)
    carry = lax.ppermute(ended, axes, forward)
    local, query, gain = run_local(q, signal, decay, taps, gains_of(rate, residue.T))
    gated = run_correct(carry, decay, gain, taps, edge, local, query, blocks, count)
    theirs = [lax.ppermute(piece, axes, across) for piece in gated]

    weight, inner, norm = run_weight(place, out_weight, direction)
    keep, send = run_project(place, weight, gated)
    core = lax.ppermute(send, axes, sibling)
    hop = lax.ppermute((keep + core.astype(jnp.float32)).astype(jnp.bfloat16), axes, inward)

    straight, diagonal = [], []
    for piece in theirs:
        far_keep, far_send = run_project(place, weight, [piece])
        far_core = lax.ppermute(far_send, axes, sibling)
        merged = (far_keep + far_core.astype(jnp.float32)).astype(jnp.bfloat16)
        straight.append(lax.ppermute(merged, axes, outward))
        diagonal.append(lax.ppermute(merged, axes, slanted))

    level = run_level(inner, lax.ppermute(inner, axes, across), gated)
    level = level + lax.ppermute(level, axes, sibling)
    level = level + lax.ppermute(level, axes, pair)
    level = level / norm[:, 0:1]
    ablated = pl.pallas_call(
        functools.partial(finish_kernel, count),
        out_shape=jax.ShapeDtypeStruct((rows, keep.shape[1]), jnp.bfloat16),
        in_specs=[SCALARS] + [WHOLE] * (5 + 2 * count),
        out_specs=WHOLE,
        compiler_params=params(),
        cost_estimate=cost(10**6),
        name="finish",
    )(place, level, direction, keep, core, hop, *straight, *diagonal)
    return ablated, level.reshape(rows)


def gather_plan(q, k, v, short_taps, decay_rate, residue, out_weight, direction):
    rows, width = q.shape
    blocks = width // LANES
    modes = decay_rate.shape[1]
    tp = lax.axis_index("tp")
    ctx_size = lax.axis_size("ctx")
    next_one = [(i, i + 1) for i in range(ctx_size - 1)]
    ended, signal, decay, taps, edge, rate = run_front(q, k, v, short_taps, decay_rate.T)
    halo = lax.ppermute(ended[modes * blocks :], "ctx", next_one)
    local, query, gain = run_local(q, signal, decay, taps, gains_of(rate, residue.T))
    k2, k1, v2, v1 = [halo[i * blocks : (i + 1) * blocks] for i in range(4)]
    tap = taps.reshape(9, blocks, LANES)
    key0, key1, value0, value1 = edge.reshape(4, blocks, LANES)
    extra0 = (key0 + tap[4] * k1 + tap[5] * k2) * (value0 + tap[7] * v1 + tap[8] * v2) - key0 * value0
    extra1 = (key1 + tap[5] * k1) * (value1 + tap[8] * v1) - key1 * value1
    wide_rate = decay_rate.T.reshape(modes, blocks, LANES)
    state = (
        ended[: modes * blocks].reshape(modes, blocks, LANES)
        + jnp.exp(-wide_rate * (rows - 1)) * extra0
        + jnp.exp(-wide_rate * (rows - 2)) * extra1
    )
    reach = 1
    while reach < ctx_size:
        earlier = lax.ppermute(state, "ctx", [(i, i + reach) for i in range(ctx_size - reach)])
        state = state + jnp.exp(-wide_rate * (rows * reach)) * earlier
        reach *= 2
    start = lax.ppermute(state, "ctx", next_one).reshape(modes * blocks, LANES)
    carry = jnp.concatenate([start, halo], axis=0)
    (gated,) = run_correct(carry, decay, gain, taps, edge, local, query, blocks, 1)
    partial_terms = lax.dot_general(
        gated,
        lax.all_gather(out_weight, "ctx", axis=1, tiled=True),
        (((1,), (0,)), ((), ())),
        preferred_element_type=jnp.float32,
    )
    summed = lax.psum_scatter(
        partial_terms.astype(jnp.bfloat16), "tp", scatter_dimension=1, tiled=True
    ).astype(jnp.float32)
    width_here = summed.shape[1]
    direction_here = lax.dynamic_slice_in_dim(direction, tp * width_here, width_here, 0)
    norm_total = jnp.sum(direction * direction) + EPSILON
    local_inner = jnp.dot(summed, direction_here, precision=HIGHEST)
    feature_level = lax.psum(local_inner, "tp") / norm_total
    ablated = (summed - feature_level[:, None] * direction_here[None, :]).astype(jnp.bfloat16)
    return ablated, feature_level


def solution(mesh):
    placed = (
        P(("dp", "ctx"), "tp"),
        P(("dp", "ctx"), "tp"),
        P(("dp", "ctx"), "tp"),
        P(None, None, "tp"),
        P("tp", None),
        P("tp", None),
        P("tp", "ctx"),
        P(),
    )
    plane = mesh.shape["ctx"] == 2 and mesh.shape["tp"] == 4
    return jax.shard_map(
        plane_plan if plane else gather_plan,
        mesh=mesh,
        in_specs=placed,
        out_specs=(P(("dp", "ctx"), "tp"), P(("dp", "ctx"))),
        check_vma=False,
    )
```

```python
import functools

import jax
import jax.numpy as jnp
from jax import lax
from jax.experimental import pallas as pl
from jax.experimental.pallas import tpu as pltpu
from jax.sharding import PartitionSpec as P

EPSILON = 1e-06
HIGHEST = lax.Precision.HIGHEST
LANES = 128
GROUP = 8
STEP = 16
WHOLE = pl.BlockSpec(memory_space=pltpu.VMEM)
SCALARS = pl.BlockSpec(memory_space=pltpu.SMEM)
AWAY = pl.BlockSpec(memory_space=pltpu.HBM)


def params(mebibytes=20):
    return pltpu.CompilerParams(vmem_limit_bytes=mebibytes * 1024 * 1024)


def cost(flops):
    return pl.CostEstimate(flops=flops, bytes_accessed=1024, transcendentals=0)


def spread(source, scratch, row, to):
    blocks = source.shape[1] // LANES
    for block in range(blocks):
        piece = source[pl.ds(row, STEP), block * LANES : (block + 1) * LANES].astype(jnp.float32)
        for half in range(STEP // GROUP):
            start = (half * blocks + block) * GROUP
            scratch[pl.ds(to + start, GROUP), :] = piece[half * GROUP : (half + 1) * GROUP]


def spread_rows(source, target):
    count, width = source.shape
    blocks = width // LANES
    for block in range(blocks):
        target[pl.ds(block, count, stride=blocks), :] = source[:, block * LANES : (block + 1) * LANES]


def place_of(index, blocks):
    return pl.ds((index // GROUP) * (blocks * GROUP) + index % GROUP, blocks, stride=GROUP)


def tile(ref, index, blocks):
    return ref[index * blocks : (index + 1) * blocks, :]


def moving_tile(index, blocks):
    return pl.ds(pl.multiple_of(index * blocks, blocks), blocks)


def front_kernel(with_weight, *refs):
    if with_weight:
        place_ref, weight_hbm, direction_hbm = refs[:3]
        refs = refs[3:]
    k_hbm, v_hbm, q_hbm, taps_hbm, rate_hbm, residue_hbm = refs[:6]
    carry_ref, signal_ref, decay_ref, taps_ref, edge_ref, rate_ref, residue_ref, q_near = refs[6:14]
    if with_weight:
        mine_ref, other_ref, direction_ref = refs[14:17]
    k_near, v_near, taps_near, k_wide, v_wide, sems, late_sems = refs[-7:]
    rows, width = k_near.shape
    blocks = width // LANES
    modes = rate_ref.shape[0]
    pieces = sems.shape[0] // 2 - 1
    height = rows // pieces

    def part(i):
        here = pl.ds(i * height, height)
        return (
            pltpu.make_async_copy(k_hbm.at[here], k_near.at[here], sems.at[2 * i]),
            pltpu.make_async_copy(v_hbm.at[here], v_near.at[here], sems.at[2 * i + 1]),
        )

    rate_copy = pltpu.make_async_copy(rate_hbm, rate_ref, sems.at[2 * pieces])
    taps_copy = pltpu.make_async_copy(taps_hbm, taps_near, sems.at[2 * pieces + 1])
    late = [(residue_hbm, residue_ref), (q_hbm, q_near)]
    if with_weight:
        half = mine_ref.shape[1]
        side = place_ref[1] % 2
        for which, ref in ((1 - side, other_ref), (side, mine_ref)):
            late.append((weight_hbm.at[:, pl.ds(pl.multiple_of(which * half, half), half)], ref))
        late.append((direction_hbm, direction_ref))
    late = [pltpu.make_async_copy(source, target, late_sems.at[i]) for i, (source, target) in enumerate(late)]
    rate_copy.start()
    taps_copy.start()
    for i in range(pieces):
        for copy in part(i):
            copy.start()
    for copy in late:
        copy.start()
    rate_copy.wait()
    taps_copy.wait()
    spread_rows(jnp.exp(-rate_ref[...]), decay_ref)
    for i in range(3):
        for block in range(blocks):
            taps_ref[pl.ds(3 * i * blocks + block, 3, stride=blocks), :] = taps_near[
                i, :, block * LANES : (block + 1) * LANES
            ]
    zero = jnp.zeros((blocks, LANES), jnp.float32)
    key_taps = [tile(taps_ref, 3 + j, blocks) for j in range(3)]
    value_taps = [tile(taps_ref, 6 + j, blocks) for j in range(3)]
    decay = [tile(decay_ref, m, blocks) for m in range(modes)]

    def step(row, held, first):
        spread(k_near, k_wide, row, 0)
        spread(v_near, v_wide, row, 0)
        state, (k2, k1, v2, v1) = list(held[:modes]), held[modes:]
        for index in range(STEP):
            k0 = k_wide[place_of(index, blocks), :]
            v0 = v_wide[place_of(index, blocks), :]
            key = key_taps[0] * k0 + key_taps[1] * k1 + key_taps[2] * k2
            value = value_taps[0] * v0 + value_taps[1] * v1 + value_taps[2] * v2
            if first and index < 2:
                edge_ref[index * blocks : (index + 1) * blocks, :] = key
                edge_ref[(2 + index) * blocks : (3 + index) * blocks, :] = value
            signal = key * value
            signal_ref[moving_tile(row + index, blocks), :] = signal
            state = [decay[m] * state[m] + signal for m in range(modes)]
            k2, k1, v2, v1 = k1, k0, v1, v0
        return tuple(state) + (k2, k1, v2, v1)

    held = (zero,) * (modes + 4)
    for i in range(pieces):
        for copy in part(i):
            copy.wait()
        begin = 0
        if i == 0:
            held = step(0, held, True)
            begin = 1
        held = lax.fori_loop(
            begin,
            height // STEP,
            lambda j, held, i=i: step(pl.multiple_of(i * height + j * STEP, STEP), held, False),
            held,
        )
    for m in range(modes + 4):
        carry_ref[m * blocks : (m + 1) * blocks, :] = held[m]
    for copy in late:
        copy.wait()
    spread(q_near, k_wide, rows - STEP, 0)
    for i in range(2):
        start = (modes + 4 + i) * blocks
        carry_ref[start : start + blocks, :] = k_wide[place_of(STEP - 2 + i, blocks), :]


def far(x):
    return pltpu.with_memory_space_constraint(x, pltpu.HBM)


def run_front(q, k, v, short_taps, rate, residue, extra=()):
    rows, width = k.shape
    modes = rate.shape[0]
    blocks = width // LANES
    pieces = 4

    def wide(n):
        return jax.ShapeDtypeStruct((n * blocks, LANES), jnp.float32)

    def like(x):
        return jax.ShapeDtypeStruct(x.shape, x.dtype)

    out_shape = [wide(modes + 6), wide(rows), wide(modes), wide(9), wide(4), like(rate), like(residue), like(q)]
    in_specs = [AWAY] * 6
    operands = [k, v, q, short_taps, rate, residue]
    if extra:
        place, weight, direction = extra
        half = jax.ShapeDtypeStruct((weight.shape[0], weight.shape[1] // 2), weight.dtype)
        out_shape += [half, half, like(direction)]
        in_specs = [SCALARS, AWAY, AWAY] + in_specs
        operands = [weight, direction] + operands
    operands = [far(x) for x in operands]
    if extra:
        operands = [place] + operands
    return pl.pallas_call(
        functools.partial(front_kernel, bool(extra)),
        out_shape=out_shape,
        in_specs=in_specs,
        out_specs=[WHOLE] * len(out_shape),
        scratch_shapes=[
            pltpu.VMEM((rows, width), jnp.bfloat16),
            pltpu.VMEM((rows, width), jnp.bfloat16),
            pltpu.VMEM(short_taps.shape, jnp.float32),
            pltpu.VMEM((STEP * blocks, LANES), jnp.float32),
            pltpu.VMEM((STEP * blocks, LANES), jnp.float32),
            pltpu.SemaphoreType.DMA((2 * pieces + 2,)),
            pltpu.SemaphoreType.DMA((5,)),
        ],
        compiler_params=params(),
        cost_estimate=cost(10**8),
        name="front",
    )(*operands)


def local_kernel(q_near, signal_ref, decay_ref, taps_ref, gain_near, out_ref, query_ref, gain_ref, q_wide):
    rows, width = q_near.shape
    blocks = width // LANES
    modes = gain_near.shape[0]
    spread_rows(gain_near[...], gain_ref)
    zero = jnp.zeros((blocks, LANES), jnp.float32)
    taps = [tile(taps_ref, j, blocks) for j in range(3)]
    decay = [tile(decay_ref, m, blocks) for m in range(modes)]
    gain = [tile(gain_ref, m, blocks) for m in range(modes)]

    def step(j, held):
        row = pl.multiple_of(j * STEP, STEP)
        spread(q_near, q_wide, row, 0)
        state, (q2, q1) = list(held[:modes]), held[modes:]
        for index in range(STEP):
            q0 = q_wide[place_of(index, blocks), :]
            here = moving_tile(row + index, blocks)
            signal = signal_ref[here, :]
            query_ref[here, :] = taps[0] * q0 + taps[1] * q1 + taps[2] * q2
            state = [decay[m] * state[m] + signal for m in range(modes)]
            sums = [gain[m] * state[m] for m in range(modes)]
            while len(sums) > 1:
                sums = [sums[i] + sums[i + 1] for i in range(0, len(sums), 2)]
            out_ref[here, :] = sums[0]
            q2, q1 = q1, q0
        return tuple(state) + (q2, q1)

    lax.fori_loop(0, rows // STEP, step, (zero,) * (modes + 2))


def run_local(q, signal, decay, taps, gain):
    rows, width = q.shape
    blocks = width // LANES
    wide = jax.ShapeDtypeStruct((rows * blocks, LANES), jnp.float32)
    return pl.pallas_call(
        local_kernel,
        out_shape=(wide, wide, jax.ShapeDtypeStruct(decay.shape, jnp.float32)),
        in_specs=[WHOLE] * 5,
        out_specs=[WHOLE] * 3,
        scratch_shapes=[pltpu.VMEM((STEP * blocks, LANES), jnp.float32)],
        compiler_params=params(),
        cost_estimate=cost(10**6),
        name="local_filter",
    )(q, signal, decay, taps, gain)


def correct_kernel(count, blocks, *refs):
    carry_ref, decay_ref, gain_ref, taps_ref, edge_ref, local_ref, query_ref = refs[:7]
    outs, whole_ref, wide = refs[7 : 7 + count], refs[-2], refs[-1]
    modes = decay_ref.shape[0] // blocks
    height = outs[0].shape[0]
    width = outs[0].shape[1]
    k2, k1, v2, v1, q2, q1 = [tile(carry_ref, modes + i, blocks) for i in range(6)]
    tap = [tile(taps_ref, i, blocks) for i in range(9)]
    key0, key1, value0, value1 = [tile(edge_ref, i, blocks) for i in range(4)]
    extra = [
        (key0 + tap[4] * k1 + tap[5] * k2) * (value0 + tap[7] * v1 + tap[8] * v2) - key0 * value0,
        (key1 + tap[5] * k1) * (value1 + tap[8] * v1) - key1 * value1,
    ]
    query_extra = [tap[1] * q1 + tap[2] * q2, tap[2] * q1]
    state = [tile(gain_ref, m, blocks) * tile(carry_ref, m, blocks) for m in range(modes)]
    decay = [tile(decay_ref, m, blocks) for m in range(modes)]

    def step(out_ref, row, base, state, first):
        state = list(state)
        for index in range(STEP):
            here = moving_tile(base + row + index, blocks)
            state = [decay[m] * state[m] for m in range(modes)]
            query = query_ref[here, :]
            if first and index < 2:
                state = [state[m] + tile(gain_ref, m, blocks) * extra[index] for m in range(modes)]
                query = query + query_extra[index]
            sums = state
            while len(sums) > 1:
                sums = [sums[i] + sums[i + 1] for i in range(0, len(sums), 2)]
            wide[place_of(index, blocks), :] = query * (local_ref[here, :] + sums[0])
        for block in range(blocks):
            halves = [
                wide[(half * blocks + block) * GROUP : (half * blocks + block + 1) * GROUP, :]
                for half in range(STEP // GROUP)
            ]
            rounded = jnp.concatenate(halves, axis=0).astype(jnp.bfloat16)
            columns = slice(block * LANES, (block + 1) * LANES)
            out_ref[pl.ds(row, STEP), columns] = rounded
            if whole_ref is not out_ref:
                whole_ref[pl.ds(pl.multiple_of(base + row, STEP), STEP), columns] = rounded
        return tuple(state)

    state = tuple(state)
    for i in range(count):
        begin = 0
        if i == 0:
            state = step(outs[0], 0, 0, state, True)
            begin = 1
        state = lax.fori_loop(
            begin,
            height // STEP,
            lambda j, state, i=i: step(
                outs[i], pl.multiple_of(j * STEP, STEP), i * height, state, False
            ),
            state,
        )


def run_correct(carry, decay, gain, taps, edge, local, query, blocks, count):
    rows = local.shape[0] // blocks
    width = blocks * LANES
    return pl.pallas_call(
        functools.partial(correct_kernel, count, blocks),
        out_shape=[jax.ShapeDtypeStruct((rows // count, width), jnp.bfloat16)] * count
        + [jax.ShapeDtypeStruct((rows, width), jnp.bfloat16)] * (count > 1),
        in_specs=[WHOLE] * 7,
        out_specs=[WHOLE] * (count + (count > 1)),
        scratch_shapes=[pltpu.VMEM((STEP * blocks, LANES), jnp.float32)],
        compiler_params=params(),
        cost_estimate=cost(10**8),
        name="carried_filter",
    )(carry, decay, gain, taps, edge, local, query)


def gains_of(rate, residue):
    return residue * jnp.sqrt(-jnp.expm1(-2.0 * rate)) * rate.shape[0] ** (-0.5)


def split_three(x):
    high = x.astype(jnp.bfloat16)
    rest = x - high.astype(jnp.float32)
    middle = rest.astype(jnp.bfloat16)
    low = (rest - middle.astype(jnp.float32)).astype(jnp.bfloat16)
    return high, middle, low


def dot_rows(row, matrix):
    parts = jnp.concatenate(list(split_three(row)) + [jnp.zeros((13, row.shape[1]), jnp.bfloat16)], axis=0)
    out = lax.dot_general(parts, matrix, (((1,), (1,)), ((), ())), preferred_element_type=jnp.float32)
    return out[0:1] + out[1:2] + out[2:3]


def inner_kernel(place_ref, direction_ref, mine_ref, other_ref, inner_ref, norm_ref):
    width = mine_ref.shape[1]
    everything = direction_ref[...]
    norm_ref[...] = jnp.broadcast_to(
        jnp.sum(everything * everything, axis=1, keepdims=True) + EPSILON, norm_ref.shape
    )
    start = (2 * place_ref[0] + place_ref[1] % 2) * width
    here = direction_ref[:, pl.ds(pl.multiple_of(start, LANES), width)]
    for i, ref in enumerate((mine_ref, other_ref)):
        inner_ref[i : i + 1, :] = dot_rows(here, ref[...])


def run_inner(place, direction, mine, other):
    return pl.pallas_call(
        inner_kernel,
        out_shape=(
            jax.ShapeDtypeStruct((2, mine.shape[0]), jnp.float32),
            jax.ShapeDtypeStruct((1, LANES), jnp.float32),
        ),
        in_specs=[SCALARS] + [WHOLE] * 3,
        out_specs=[WHOLE] * 2,
        compiler_params=params(),
        cost_estimate=cost(10**6),
        name="inner",
    )(place, direction, mine, other)


def project_kernel(count, with_keep, mine_ref, other_ref, inner_ref, *refs):
    here, there = refs[:count], refs[count : 2 * count]
    outs = refs[2 * count :]
    width = mine_ref.shape[1]
    height = here[0].shape[0]
    for part in range(0, width, 256):
        columns = slice(part, part + 256)
        for i in range(count):
            rows = slice(i * height, (i + 1) * height)
            out = jnp.dot(here[i][...], mine_ref[:, columns], preferred_element_type=jnp.float32)
            out = out + jnp.dot(there[i][...], other_ref[:, columns], preferred_element_type=jnp.float32)
            outs[0][rows, columns] = out.astype(jnp.bfloat16)
            if with_keep:
                outs[1][rows, columns] = out
    for i in range(count):
        rows = slice(i * height, (i + 1) * height)
        outs[-1][:, rows] = dot_rows(inner_ref[0:1, :], here[i][...]) + dot_rows(inner_ref[1:2, :], there[i][...])


def run_project(mine, other, inner, here, there, with_keep):
    rows = sum(piece.shape[0] for piece in here)
    width = mine.shape[1]
    out_shape = [jax.ShapeDtypeStruct((rows, width), jnp.bfloat16)]
    if with_keep:
        out_shape.append(jax.ShapeDtypeStruct((rows, width), jnp.float32))
    out_shape.append(jax.ShapeDtypeStruct((1, rows), jnp.float32))
    return pl.pallas_call(
        functools.partial(project_kernel, len(here), with_keep),
        out_shape=out_shape,
        in_specs=[WHOLE] * (3 + 2 * len(here)),
        out_specs=[WHOLE] * len(out_shape),
        compiler_params=params(),
        cost_estimate=cost(10**6),
        name="project",
    )(mine, other, inner, *here, *there)


def finish_kernel(
    place_ref, levels_ref, norm_ref, direction_ref, keep_ref, hop_ref, straight_ref, turned_ref, merged_ref,
    out_ref, level_ref,
):
    rows, width = out_ref.shape
    half = rows // 2
    devices = levels_ref.shape[0]
    row = lax.broadcasted_iota(jnp.int32, (devices, rows), 0) // (devices // 2)
    level = jnp.where(row == place_ref[0], levels_ref[:, :rows], levels_ref[:, rows:])
    level = jnp.sum(level, axis=0, keepdims=True) / norm_ref[0:1, 0:1]
    level_ref[...] = level
    direction = direction_ref[:, pl.ds(pl.multiple_of(place_ref[1] * width, LANES), width)]
    keeper = place_ref[1] // 2 == place_ref[0]
    for i in range(2):
        here = slice(i * half, (i + 1) * half)
        column = jnp.transpose(jnp.broadcast_to(level[:, here], (LANES, half)))[:, 0:1]

        @pl.when(keeper)
        def _():
            total = keep_ref[here, :] + hop_ref[here, :].astype(jnp.float32)
            out_ref[here, :] = (total - column * direction).astype(jnp.bfloat16)

        @pl.when(jnp.logical_not(keeper))
        def _():
            if i == 0:
                total = straight_ref[...].astype(jnp.float32) + turned_ref[...].astype(jnp.float32)
            else:
                total = merged_ref[...].astype(jnp.float32)
            out_ref[here, :] = (total - column * direction).astype(jnp.bfloat16)


def plane_plan(q, k, v, short_taps, decay_rate, residue, out_weight, direction):
    rows, width = q.shape
    blocks = width // LANES
    ctx, tp = lax.axis_index("ctx"), lax.axis_index("tp")
    axes = ("ctx", "tp")
    place = jnp.stack([ctx, tp]).astype(jnp.int32)

    forward = [(p, 4 + p) for p in range(4)]
    across = [(4 * c + p, 4 * (1 - c) + p) for c in range(2) for p in range(4)]
    sibling = [(4 * c + p, 4 * c + (p ^ 1)) for c in range(2) for p in range(4)]
    inward = [(4 * c + 2 * (1 - c) + a, 4 * c + 2 * c + a) for c in range(2) for a in range(2)]
    outward = [(4 * c + 2 * c + a, 4 * c + 2 * (1 - c) + a) for c in range(2) for a in range(2)]
    onward = [(4 * c + 2 * c + a, 4 * (1 - c) + 2 * c + a) for c in range(2) for a in range(2)]

    ended, signal, decay, taps, edge, rate, residue, q, mine, lent, direction = run_front(
        q, k, v, short_taps, decay_rate.T, residue.T, (place, out_weight, direction.reshape(1, -1))
    )
    carry = lax.ppermute(ended, axes, forward)
    other = lax.ppermute(lent, axes, sibling)
    local, query, gain = run_local(q, signal, decay, taps, gains_of(rate, residue))
    first, second, whole = run_correct(carry, decay, gain, taps, edge, local, query, blocks, 2)
    far_first = lax.ppermute(first, axes, across)
    far_second = lax.ppermute(second, axes, across)
    beside = lax.ppermute(whole, axes, sibling)

    inner, norm = run_inner(place, direction, mine, other)
    sent, keep, level = run_project(mine, other, inner, [whole], [beside], True)
    hop = lax.ppermute(sent, axes, inward)

    far_beside = lax.ppermute(far_first, axes, sibling)
    sums, level_first = run_project(mine, other, inner, [far_first], [far_beside], False)
    straight = lax.ppermute(sums, axes, across)
    turned = lax.ppermute(straight, axes, outward)

    far_beside = lax.ppermute(far_second, axes, sibling)
    sums, level_second = run_project(mine, other, inner, [far_second], [far_beside], False)
    merged = sums.astype(jnp.float32) + lax.ppermute(sums, axes, inward).astype(jnp.float32)
    merged = lax.ppermute(merged.astype(jnp.bfloat16), axes, onward)

    levels = lax.all_gather(jnp.concatenate([level, level_first, level_second], axis=1), axes, axis=0, tiled=True)
    ablated, level = pl.pallas_call(
        finish_kernel,
        out_shape=(
            jax.ShapeDtypeStruct((rows, mine.shape[1]), jnp.bfloat16),
            jax.ShapeDtypeStruct((1, rows), jnp.float32),
        ),
        in_specs=[SCALARS] + [WHOLE] * 8,
        out_specs=[WHOLE] * 2,
        compiler_params=params(),
        cost_estimate=cost(10**6),
        name="finish",
    )(place, levels, norm, direction, keep, hop, straight, turned, merged)
    return ablated, level.reshape(rows)


def gather_plan(q, k, v, short_taps, decay_rate, residue, out_weight, direction):
    rows, width = q.shape
    blocks = width // LANES
    modes = decay_rate.shape[1]
    tp = lax.axis_index("tp")
    ctx_size = lax.axis_size("ctx")
    next_one = [(i, i + 1) for i in range(ctx_size - 1)]
    ended, signal, decay, taps, edge, rate, residue, q = run_front(q, k, v, short_taps, decay_rate.T, residue.T)
    halo = lax.ppermute(ended[modes * blocks :], "ctx", next_one)
    local, query, gain = run_local(q, signal, decay, taps, gains_of(rate, residue))
    k2, k1, v2, v1 = [halo[i * blocks : (i + 1) * blocks] for i in range(4)]
    tap = taps.reshape(9, blocks, LANES)
    key0, key1, value0, value1 = edge.reshape(4, blocks, LANES)
    extra0 = (key0 + tap[4] * k1 + tap[5] * k2) * (value0 + tap[7] * v1 + tap[8] * v2) - key0 * value0
    extra1 = (key1 + tap[5] * k1) * (value1 + tap[8] * v1) - key1 * value1
    wide_rate = decay_rate.T.reshape(modes, blocks, LANES)
    state = (
        ended[: modes * blocks].reshape(modes, blocks, LANES)
        + jnp.exp(-wide_rate * (rows - 1)) * extra0
        + jnp.exp(-wide_rate * (rows - 2)) * extra1
    )
    reach = 1
    while reach < ctx_size:
        earlier = lax.ppermute(state, "ctx", [(i, i + reach) for i in range(ctx_size - reach)])
        state = state + jnp.exp(-wide_rate * (rows * reach)) * earlier
        reach *= 2
    start = lax.ppermute(state, "ctx", next_one).reshape(modes * blocks, LANES)
    carry = jnp.concatenate([start, halo], axis=0)
    (gated,) = run_correct(carry, decay, gain, taps, edge, local, query, blocks, 1)
    partial_terms = lax.dot_general(
        gated,
        lax.all_gather(out_weight, "ctx", axis=1, tiled=True),
        (((1,), (0,)), ((), ())),
        preferred_element_type=jnp.float32,
    )
    summed = lax.psum_scatter(
        partial_terms.astype(jnp.bfloat16), "tp", scatter_dimension=1, tiled=True
    ).astype(jnp.float32)
    width_here = summed.shape[1]
    direction_here = lax.dynamic_slice_in_dim(direction, tp * width_here, width_here, 0)
    norm_total = jnp.sum(direction * direction) + EPSILON
    local_inner = jnp.dot(summed, direction_here, precision=HIGHEST)
    feature_level = lax.psum(local_inner, "tp") / norm_total
    ablated = (summed - feature_level[:, None] * direction_here[None, :]).astype(jnp.bfloat16)
    return ablated, feature_level


def solution(mesh):
    placed = (
        P(("dp", "ctx"), "tp"),
        P(("dp", "ctx"), "tp"),
        P(("dp", "ctx"), "tp"),
        P(None, None, "tp"),
        P("tp", None),
        P("tp", None),
        P("tp", "ctx"),
        P(),
    )
    plane = mesh.shape["ctx"] == 2 and mesh.shape["tp"] == 4
    return jax.shard_map(
        plane_plan if plane else gather_plan,
        mesh=mesh,
        in_specs=placed,
        out_specs=(P(("dp", "ctx"), "tp"), P(("dp", "ctx"))),
        check_vma=False,
    )
```

```python
import functools

import jax
import jax.numpy as jnp
from jax import lax
from jax.experimental import pallas as pl
from jax.experimental.pallas import tpu as pltpu
from jax.sharding import PartitionSpec as P

EPSILON = 1e-06
HIGHEST = lax.Precision.HIGHEST
LANES = 128
GROUP = 8
STEP = 16
WHOLE = pl.BlockSpec(memory_space=pltpu.VMEM)
SCALARS = pl.BlockSpec(memory_space=pltpu.SMEM)
AWAY = pl.BlockSpec(memory_space=pltpu.HBM)


def params(mebibytes=20):
    return pltpu.CompilerParams(vmem_limit_bytes=mebibytes * 1024 * 1024)


def cost(flops):
    return pl.CostEstimate(flops=flops, bytes_accessed=1024, transcendentals=0)


def spread(source, scratch, row, to):
    blocks = source.shape[1] // LANES
    for block in range(blocks):
        piece = source[pl.ds(row, STEP), block * LANES : (block + 1) * LANES].astype(jnp.float32)
        for half in range(STEP // GROUP):
            start = (half * blocks + block) * GROUP
            scratch[pl.ds(to + start, GROUP), :] = piece[half * GROUP : (half + 1) * GROUP]


def spread_rows(source, target):
    count, width = source.shape
    blocks = width // LANES
    for block in range(blocks):
        target[pl.ds(block, count, stride=blocks), :] = source[:, block * LANES : (block + 1) * LANES]


def place_of(index, blocks):
    return pl.ds((index // GROUP) * (blocks * GROUP) + index % GROUP, blocks, stride=GROUP)


def tile(ref, index, blocks):
    return ref[index * blocks : (index + 1) * blocks, :]


def moving_tile(index, blocks):
    return pl.ds(pl.multiple_of(index * blocks, blocks), blocks)


def front_kernel(with_weight, *refs):
    if with_weight:
        weight_hbm, direction_hbm = refs[:2]
        refs = refs[2:]
    k_hbm, v_hbm, q_hbm, taps_hbm, rate_hbm, residue_hbm = refs[:6]
    carry_ref, signal_ref, decay_ref, taps_ref, edge_ref, rate_ref, residue_ref, q_near = refs[6:14]
    if with_weight:
        weight_ref, direction_ref = refs[14:16]
    k_near, v_near, taps_near, k_wide, v_wide, sems, late_sems = refs[-7:]
    rows, width = k_near.shape
    blocks = width // LANES
    modes = rate_ref.shape[0]
    pieces = sems.shape[0] // 2 - 1
    height = rows // pieces

    def part(i):
        here = pl.ds(i * height, height)
        return (
            pltpu.make_async_copy(k_hbm.at[here], k_near.at[here], sems.at[2 * i]),
            pltpu.make_async_copy(v_hbm.at[here], v_near.at[here], sems.at[2 * i + 1]),
        )

    rate_copy = pltpu.make_async_copy(rate_hbm, rate_ref, sems.at[2 * pieces])
    taps_copy = pltpu.make_async_copy(taps_hbm, taps_near, sems.at[2 * pieces + 1])
    late = [(residue_hbm, residue_ref), (q_hbm, q_near)]
    if with_weight:
        depth = weight_ref.shape[0] // 4
        for i in range(4):
            here = pl.ds(i * depth, depth)
            late.append((weight_hbm.at[here], weight_ref.at[here]))
        late.append((direction_hbm, direction_ref))
    late = [pltpu.make_async_copy(source, target, late_sems.at[i]) for i, (source, target) in enumerate(late)]
    rate_copy.start()
    taps_copy.start()
    for i in range(pieces):
        for copy in part(i):
            copy.start()
    for copy in late:
        copy.start()
    rate_copy.wait()
    taps_copy.wait()
    spread_rows(jnp.exp(-rate_ref[...]), decay_ref)
    for i in range(3):
        for block in range(blocks):
            taps_ref[pl.ds(3 * i * blocks + block, 3, stride=blocks), :] = taps_near[
                i, :, block * LANES : (block + 1) * LANES
            ]
    zero = jnp.zeros((blocks, LANES), jnp.float32)
    key_taps = [tile(taps_ref, 3 + j, blocks) for j in range(3)]
    value_taps = [tile(taps_ref, 6 + j, blocks) for j in range(3)]
    decay = [tile(decay_ref, m, blocks) for m in range(modes)]

    def step(row, held, first):
        spread(k_near, k_wide, row, 0)
        spread(v_near, v_wide, row, 0)
        state, (k2, k1, v2, v1) = list(held[:modes]), held[modes:]
        for index in range(STEP):
            k0 = k_wide[place_of(index, blocks), :]
            v0 = v_wide[place_of(index, blocks), :]
            key = key_taps[0] * k0 + key_taps[1] * k1 + key_taps[2] * k2
            value = value_taps[0] * v0 + value_taps[1] * v1 + value_taps[2] * v2
            if first and index < 2:
                edge_ref[index * blocks : (index + 1) * blocks, :] = key
                edge_ref[(2 + index) * blocks : (3 + index) * blocks, :] = value
            signal = key * value
            signal_ref[moving_tile(row + index, blocks), :] = signal
            state = [decay[m] * state[m] + signal for m in range(modes)]
            k2, k1, v2, v1 = k1, k0, v1, v0
        return tuple(state) + (k2, k1, v2, v1)

    held = (zero,) * (modes + 4)
    for i in range(pieces):
        for copy in part(i):
            copy.wait()
        begin = 0
        if i == 0:
            held = step(0, held, True)
            begin = 1
        held = lax.fori_loop(
            begin,
            height // STEP,
            lambda j, held, i=i: step(pl.multiple_of(i * height + j * STEP, STEP), held, False),
            held,
        )
    for m in range(modes + 4):
        carry_ref[m * blocks : (m + 1) * blocks, :] = held[m]
    for copy in late:
        copy.wait()
    spread(q_near, k_wide, rows - STEP, 0)
    for i in range(2):
        start = (modes + 4 + i) * blocks
        carry_ref[start : start + blocks, :] = k_wide[place_of(STEP - 2 + i, blocks), :]


def far(x):
    return pltpu.with_memory_space_constraint(x, pltpu.HBM)


def run_front(q, k, v, short_taps, rate, residue, extra=()):
    rows, width = k.shape
    modes = rate.shape[0]
    blocks = width // LANES
    pieces = 4

    def wide(n):
        return jax.ShapeDtypeStruct((n * blocks, LANES), jnp.float32)

    def like(x):
        return jax.ShapeDtypeStruct(x.shape, x.dtype)

    out_shape = [wide(modes + 6), wide(rows), wide(modes), wide(9), wide(4), like(rate), like(residue), like(q)]
    in_specs = [AWAY] * 6
    operands = [k, v, q, short_taps, rate, residue]
    if extra:
        out_shape += [like(x) for x in extra]
        in_specs = [AWAY] * len(extra) + in_specs
        operands = list(extra) + operands
    operands = [far(x) for x in operands]
    return pl.pallas_call(
        functools.partial(front_kernel, bool(extra)),
        out_shape=out_shape,
        in_specs=in_specs,
        out_specs=[WHOLE] * len(out_shape),
        scratch_shapes=[
            pltpu.VMEM((rows, width), jnp.bfloat16),
            pltpu.VMEM((rows, width), jnp.bfloat16),
            pltpu.VMEM(short_taps.shape, jnp.float32),
            pltpu.VMEM((STEP * blocks, LANES), jnp.float32),
            pltpu.VMEM((STEP * blocks, LANES), jnp.float32),
            pltpu.SemaphoreType.DMA((2 * pieces + 2,)),
            pltpu.SemaphoreType.DMA((8,)),
        ],
        compiler_params=params(),
        cost_estimate=cost(10**8),
        name="front",
    )(*operands)


def local_kernel(q_near, signal_ref, decay_ref, taps_ref, gain_near, *refs):
    if len(refs) > 4:
        place_ref, direction_ref, weight_ref, parts_ref, norm_ref = refs[:3] + refs[6:8]
        everything = direction_ref[...]
        norm_ref[...] = jnp.broadcast_to(
            jnp.sum(everything * everything, axis=1, keepdims=True) + EPSILON, norm_ref.shape
        )
        size = weight_ref.shape[1]
        here = direction_ref[:, pl.ds(pl.multiple_of(place_ref[0] * size, LANES), size)]
        parts_ref[...] = in_parts(dot_parts(in_parts(here), weight_ref[...]))
        refs = refs[3:6] + refs[8:]
    out_ref, query_ref, gain_ref, q_wide = refs
    rows, width = q_near.shape
    blocks = width // LANES
    modes = gain_near.shape[0]
    spread_rows(gain_near[...], gain_ref)
    zero = jnp.zeros((blocks, LANES), jnp.float32)
    taps = [tile(taps_ref, j, blocks) for j in range(3)]
    decay = [tile(decay_ref, m, blocks) for m in range(modes)]
    gain = [tile(gain_ref, m, blocks) for m in range(modes)]

    def step(j, held):
        row = pl.multiple_of(j * STEP, STEP)
        spread(q_near, q_wide, row, 0)
        state, (q2, q1) = list(held[:modes]), held[modes:]
        for index in range(STEP):
            q0 = q_wide[place_of(index, blocks), :]
            here = moving_tile(row + index, blocks)
            signal = signal_ref[here, :]
            query_ref[here, :] = taps[0] * q0 + taps[1] * q1 + taps[2] * q2
            state = [decay[m] * state[m] + signal for m in range(modes)]
            sums = [gain[m] * state[m] for m in range(modes)]
            while len(sums) > 1:
                sums = [sums[i] + sums[i + 1] for i in range(0, len(sums), 2)]
            out_ref[here, :] = sums[0]
            q2, q1 = q1, q0
        return tuple(state) + (q2, q1)

    lax.fori_loop(0, rows // STEP, step, (zero,) * (modes + 2))


def run_local(q, signal, decay, taps, gain, *inner):
    rows, width = q.shape
    blocks = width // LANES
    wide = jax.ShapeDtypeStruct((rows * blocks, LANES), jnp.float32)
    out_shape = [wide, wide, jax.ShapeDtypeStruct(decay.shape, jnp.float32)]
    if inner:
        out_shape += [jax.ShapeDtypeStruct((STEP, width), jnp.bfloat16), jax.ShapeDtypeStruct((1, LANES), jnp.float32)]
    return pl.pallas_call(
        local_kernel,
        out_shape=out_shape,
        in_specs=[WHOLE] * 5 + ([SCALARS] + [WHOLE] * 2 if inner else []),
        out_specs=[WHOLE] * len(out_shape),
        scratch_shapes=[pltpu.VMEM((STEP * blocks, LANES), jnp.float32)],
        compiler_params=params(),
        cost_estimate=cost(10**6),
        name="local_filter",
    )(q, signal, decay, taps, gain, *inner)


def correct_kernel(blocks, carry_ref, decay_ref, gain_ref, taps_ref, edge_ref, local_ref, query_ref, *refs):
    out_ref, wide = refs[-2:]
    rows = local_ref.shape[0] // blocks
    if len(refs) > 2:
        out_ref[rows:, :] = refs[0][...]
    modes = decay_ref.shape[0] // blocks
    k2, k1, v2, v1, q2, q1 = [tile(carry_ref, modes + i, blocks) for i in range(6)]
    tap = [tile(taps_ref, i, blocks) for i in range(9)]
    key0, key1, value0, value1 = [tile(edge_ref, i, blocks) for i in range(4)]
    extra = [
        (key0 + tap[4] * k1 + tap[5] * k2) * (value0 + tap[7] * v1 + tap[8] * v2) - key0 * value0,
        (key1 + tap[5] * k1) * (value1 + tap[8] * v1) - key1 * value1,
    ]
    query_extra = [tap[1] * q1 + tap[2] * q2, tap[2] * q1]
    state = [tile(gain_ref, m, blocks) * tile(carry_ref, m, blocks) for m in range(modes)]
    decay = [tile(decay_ref, m, blocks) for m in range(modes)]

    def step(row, state, first):
        state = list(state)
        for index in range(STEP):
            here = moving_tile(row + index, blocks)
            state = [decay[m] * state[m] for m in range(modes)]
            query = query_ref[here, :]
            if first and index < 2:
                state = [state[m] + tile(gain_ref, m, blocks) * extra[index] for m in range(modes)]
                query = query + query_extra[index]
            sums = state
            while len(sums) > 1:
                sums = [sums[i] + sums[i + 1] for i in range(0, len(sums), 2)]
            wide[place_of(index, blocks), :] = query * (local_ref[here, :] + sums[0])
        for block in range(blocks):
            halves = [
                wide[(half * blocks + block) * GROUP : (half * blocks + block + 1) * GROUP, :]
                for half in range(STEP // GROUP)
            ]
            out_ref[pl.ds(row, STEP), block * LANES : (block + 1) * LANES] = jnp.concatenate(
                halves, axis=0
            ).astype(jnp.bfloat16)
        return tuple(state)

    lax.fori_loop(
        1,
        rows // STEP,
        lambda j, state: step(pl.multiple_of(j * STEP, STEP), state, False),
        step(0, tuple(state), True),
    )


def run_correct(carry, decay, gain, taps, edge, local, query, blocks, *parts):
    rows = local.shape[0] // blocks + STEP * len(parts)
    return pl.pallas_call(
        functools.partial(correct_kernel, blocks),
        out_shape=jax.ShapeDtypeStruct((rows, blocks * LANES), jnp.bfloat16),
        in_specs=[WHOLE] * (7 + len(parts)),
        out_specs=WHOLE,
        scratch_shapes=[pltpu.VMEM((STEP * blocks, LANES), jnp.float32)],
        compiler_params=params(),
        cost_estimate=cost(10**8),
        name="carried_filter",
    )(carry, decay, gain, taps, edge, local, query, *parts)


def gains_of(rate, residue):
    return residue * jnp.sqrt(-jnp.expm1(-2.0 * rate)) * rate.shape[0] ** (-0.5)


def split_three(x):
    high = x.astype(jnp.bfloat16)
    rest = x - high.astype(jnp.float32)
    middle = rest.astype(jnp.bfloat16)
    low = (rest - middle.astype(jnp.float32)).astype(jnp.bfloat16)
    return high, middle, low


def in_parts(row):
    return jnp.concatenate(list(split_three(row)) + [jnp.zeros((13, row.shape[1]), jnp.bfloat16)], axis=0)


def dot_parts(parts, matrix):
    out = lax.dot_general(parts, matrix, (((1,), (1,)), ((), ())), preferred_element_type=jnp.float32)
    return out[0:1] + out[1:2] + out[2:3]


def idle_kernel(*refs):
    pass


def after(array, *others):
    return pl.pallas_call(
        idle_kernel,
        out_shape=jax.ShapeDtypeStruct(array.shape, array.dtype),
        in_specs=[pl.BlockSpec(memory_space=pl.ANY)] * (1 + len(others)),
        out_specs=pl.BlockSpec(memory_space=pl.ANY),
        input_output_aliases={0: 0},
        compiler_params=params(),
        cost_estimate=cost(1),
        name="after",
    )(array, *others)


def call(kernel, name, out_shape, in_specs, *operands):
    return pl.pallas_call(
        kernel,
        out_shape=out_shape,
        in_specs=in_specs,
        out_specs=[WHOLE] * len(out_shape),
        compiler_params=params(),
        cost_estimate=cost(10**6),
        name=name,
    )(*operands)


def rows_of(count, like, dtype=jnp.bfloat16):
    return jax.ShapeDtypeStruct((count, like.shape[1]), dtype)


def rows_of(count, like, dtype=jnp.bfloat16):
    return jax.ShapeDtypeStruct((count, like.shape[1]), dtype)


def project_kernel(with_level, place_ref, weight_ref, piece_ref, *refs):
    if with_level:
        whole_ref, send_ref, keep_ref, level_ref = refs
    else:
        send_ref, keep_ref = refs
    rows, width = keep_ref.shape
    side = place_ref[1] % 2
    for which, ref in ((1 - side, send_ref), (side, keep_ref)):
        for part in range(0, width, 256):
            columns = pl.ds(pl.multiple_of(which * width + part, 256), 256)
            out = jnp.dot(piece_ref[:rows, :], weight_ref[:, columns], preferred_element_type=jnp.float32)
            ref[:rows, part : part + 256] = out.astype(ref.dtype)
    if with_level:
        level = dot_parts(piece_ref[rows:, :], whole_ref[:rows, :]) + dot_parts(whole_ref[rows:, :], whole_ref[:rows, :])
        level_ref[...] = level
        send_ref[rows:, :] = jnp.zeros((STEP, width), jnp.bfloat16)
        send_ref[rows:, :rows] = in_parts(level)


def run_project(place, weight, piece, *whole):
    width = weight.shape[1] // 2
    rows = piece.shape[0] - STEP
    out_shape = [
        jax.ShapeDtypeStruct((rows + STEP * len(whole), width), jnp.bfloat16),
        jax.ShapeDtypeStruct((rows, width), jnp.float32),
    ]
    if whole:
        out_shape.append(jax.ShapeDtypeStruct((1, rows), jnp.float32))
    return pl.pallas_call(
        functools.partial(project_kernel, bool(whole)),
        out_shape=out_shape,
        in_specs=[SCALARS] + [WHOLE] * (2 + len(whole)),
        out_specs=[WHOLE] * len(out_shape),
        compiler_params=params(),
        cost_estimate=cost(10**6),
        name="project",
    )(place, weight, piece, *whole)


def merge_kernel(keep_ref, core_ref, *refs):
    outs = refs
    if len(refs) > 2:
        level_ref, outs, total_ref = refs[0], refs[1:-1], refs[-1]
    start = 0
    rows, width = keep_ref.shape
    for ref in outs:
        height = ref.shape[0] - ref.shape[0] % (2 * STEP)
        here = slice(start, start + height)
        ref[:height, :] = (keep_ref[here, :] + core_ref[here, :].astype(jnp.float32)).astype(jnp.bfloat16)
        start += height
    if len(refs) > 2:
        level = level_ref[...] + jnp.sum(core_ref[rows:, :rows].astype(jnp.float32), axis=0, keepdims=True)
        total_ref[...] = level
        outs[-1][height:, :] = jnp.zeros((STEP, width), jnp.bfloat16)
        outs[-1][height:, :rows] = in_parts(level)


def run_merge(keep, core, *level):
    half = keep.shape[0] // 2
    out_shape = [rows_of(half, keep), rows_of(half + STEP * len(level), keep)]
    out_shape += [jax.ShapeDtypeStruct(x.shape, x.dtype) for x in level]
    return pl.pallas_call(
        merge_kernel,
        out_shape=out_shape,
        in_specs=[WHOLE] * (2 + len(level)),
        out_specs=[WHOLE] * len(out_shape),
        compiler_params=params(),
        cost_estimate=cost(10**6),
        name="merge",
    )(keep, core, *level)


def join_kernel(sums_ref, moved_ref, straight_ref, level_ref, merged_ref, turned_ref):
    rows, width = merged_ref.shape
    merged_ref[...] = (sums_ref[:rows, :].astype(jnp.float32) + moved_ref[:rows, :].astype(jnp.float32)).astype(
        jnp.bfloat16
    )
    turned_ref[:rows, :] = straight_ref[...]
    turned_ref[rows:, :] = jnp.zeros((STEP, width), jnp.bfloat16)
    turned_ref[rows:, : level_ref.shape[1]] = in_parts(level_ref[...])


def run_join(sums, moved, straight, level):
    return pl.pallas_call(
        join_kernel,
        out_shape=[rows_of(straight.shape[0], straight), rows_of(straight.shape[0] + STEP, straight)],
        in_specs=[WHOLE] * 4,
        out_specs=[WHOLE] * 2,
        compiler_params=params(),
        cost_estimate=cost(10**6),
        name="join",
    )(sums, moved, straight, level)


def finish_kernel(
    place_ref, level_ref, norm_ref, direction_ref, keep_ref, core_ref, hop0_ref, hop1_ref, moved_ref,
    straight_ref, turned_ref, merged_ref, out_hbm, level_out_ref, out_near, sems,
):
    rows, width = out_near.shape
    half = rows // 2
    keeper = place_ref[1] // 2 == place_ref[0]
    other = jnp.where(keeper, moved_ref[half:, :rows].astype(jnp.float32), turned_ref[half:, :rows].astype(jnp.float32))
    level = (level_ref[...] + jnp.sum(other, axis=0, keepdims=True)) / norm_ref[0:1, 0:1]
    level_out_ref[...] = level
    direction = direction_ref[:, pl.ds(pl.multiple_of(place_ref[1] * width, LANES), width)]
    copies = []
    for i in range(2):
        here = slice(i * half, (i + 1) * half)
        column = jnp.transpose(jnp.broadcast_to(level[:, here], (LANES, half)))[:, 0:1]
        hop_ref = (hop0_ref, hop1_ref)[i]

        @pl.when(keeper)
        def _():
            total = keep_ref[here, :] + core_ref[here, :].astype(jnp.float32) + hop_ref[...].astype(jnp.float32)
            out_near[here, :] = (total - column * direction).astype(jnp.bfloat16)

        @pl.when(jnp.logical_not(keeper))
        def _():
            if i == 0:
                total = straight_ref[...].astype(jnp.float32) + turned_ref[:half, :].astype(jnp.float32)
            else:
                total = merged_ref[...].astype(jnp.float32)
            out_near[here, :] = (total - column * direction).astype(jnp.bfloat16)

        copies.append(pltpu.make_async_copy(out_near.at[here], out_hbm.at[here], sems.at[i]))
        copies[-1].start()
    for copy in copies:
        copy.wait()


def plane_plan(q, k, v, short_taps, decay_rate, residue, out_weight, direction):
    rows, width = q.shape
    blocks = width // LANES
    ctx, tp = lax.axis_index("ctx"), lax.axis_index("tp")
    axes = ("ctx", "tp")
    place = jnp.stack([ctx, tp]).astype(jnp.int32)

    forward = [(p, 4 + p) for p in range(4)]
    across = [(4 * c + p, 4 * (1 - c) + p) for c in range(2) for p in range(4)]
    sibling = [(4 * c + p, 4 * c + (p ^ 1)) for c in range(2) for p in range(4)]
    inward = [(4 * c + 2 * (1 - c) + a, 4 * c + 2 * c + a) for c in range(2) for a in range(2)]
    outward = [(4 * c + 2 * c + a, 4 * c + 2 * (1 - c) + a) for c in range(2) for a in range(2)]
    onward = [(4 * c + 2 * c + a, 4 * (1 - c) + 2 * c + a) for c in range(2) for a in range(2)]

    ended, signal, decay, taps, edge, rate, residue, q, weight, direction = run_front(
        q, k, v, short_taps, decay_rate.T, residue.T, (out_weight, direction.reshape(1, -1))
    )
    carry = lax.ppermute(ended, axes, forward)
    local, query, gain, parts, norm = run_local(
        q, signal, decay, taps, gains_of(rate, residue), place, direction, weight
    )
    whole = run_correct(carry, decay, gain, taps, edge, local, query, blocks, parts)
    far_whole = lax.ppermute(whole, axes, across)

    send, keep = run_project(place, weight, whole)
    core = lax.ppermute(send, axes, sibling)
    own0, own1 = run_merge(keep, core)
    hop0 = lax.ppermute(own0, axes, inward)

    send, far_keep, level = run_project(place, weight, after(far_whole, hop0), whole)
    sums0, sums1, level = run_merge(far_keep, lax.ppermute(send, axes, sibling), level)
    straight = lax.ppermute(sums0, axes, across)
    moved = lax.ppermute(sums1, axes, inward)
    merged, turned = run_join(sums1, moved, straight, level)
    merged = lax.ppermute(merged, axes, onward)
    turned = lax.ppermute(turned, axes, outward)
    hop1 = lax.ppermute(own1, axes, inward)

    ablated, level = pl.pallas_call(
        finish_kernel,
        out_shape=(rows_of(rows, keep), jax.ShapeDtypeStruct((1, rows), jnp.float32)),
        in_specs=[SCALARS] + [WHOLE] * 11,
        out_specs=[AWAY, WHOLE],
        scratch_shapes=[pltpu.VMEM(keep.shape, jnp.bfloat16), pltpu.SemaphoreType.DMA((2,))],
        compiler_params=params(),
        cost_estimate=cost(10**6),
        name="finish",
    )(place, level, norm, direction, keep, core, hop0, hop1, moved, straight, turned, merged)
    return ablated, level.reshape(rows)


def gather_plan(q, k, v, short_taps, decay_rate, residue, out_weight, direction):
    rows, width = q.shape
    blocks = width // LANES
    modes = decay_rate.shape[1]
    tp = lax.axis_index("tp")
    ctx_size = lax.axis_size("ctx")
    next_one = [(i, i + 1) for i in range(ctx_size - 1)]
    ended, signal, decay, taps, edge, rate, residue, q = run_front(q, k, v, short_taps, decay_rate.T, residue.T)
    halo = lax.ppermute(ended[modes * blocks :], "ctx", next_one)
    local, query, gain = run_local(q, signal, decay, taps, gains_of(rate, residue))
    k2, k1, v2, v1 = [halo[i * blocks : (i + 1) * blocks] for i in range(4)]
    tap = taps.reshape(9, blocks, LANES)
    key0, key1, value0, value1 = edge.reshape(4, blocks, LANES)
    extra0 = (key0 + tap[4] * k1 + tap[5] * k2) * (value0 + tap[7] * v1 + tap[8] * v2) - key0 * value0
    extra1 = (key1 + tap[5] * k1) * (value1 + tap[8] * v1) - key1 * value1
    wide_rate = decay_rate.T.reshape(modes, blocks, LANES)
    state = (
        ended[: modes * blocks].reshape(modes, blocks, LANES)
        + jnp.exp(-wide_rate * (rows - 1)) * extra0
        + jnp.exp(-wide_rate * (rows - 2)) * extra1
    )
    reach = 1
    while reach < ctx_size:
        earlier = lax.ppermute(state, "ctx", [(i, i + reach) for i in range(ctx_size - reach)])
        state = state + jnp.exp(-wide_rate * (rows * reach)) * earlier
        reach *= 2
    start = lax.ppermute(state, "ctx", next_one).reshape(modes * blocks, LANES)
    carry = jnp.concatenate([start, halo], axis=0)
    gated = run_correct(carry, decay, gain, taps, edge, local, query, blocks)
    partial_terms = lax.dot_general(
        gated,
        lax.all_gather(out_weight, "ctx", axis=1, tiled=True),
        (((1,), (0,)), ((), ())),
        preferred_element_type=jnp.float32,
    )
    summed = lax.psum_scatter(
        partial_terms.astype(jnp.bfloat16), "tp", scatter_dimension=1, tiled=True
    ).astype(jnp.float32)
    width_here = summed.shape[1]
    direction_here = lax.dynamic_slice_in_dim(direction, tp * width_here, width_here, 0)
    norm_total = jnp.sum(direction * direction) + EPSILON
    local_inner = jnp.dot(summed, direction_here, precision=HIGHEST)
    feature_level = lax.psum(local_inner, "tp") / norm_total
    ablated = (summed - feature_level[:, None] * direction_here[None, :]).astype(jnp.bfloat16)
    return ablated, feature_level


def solution(mesh):
    placed = (
        P(("dp", "ctx"), "tp"),
        P(("dp", "ctx"), "tp"),
        P(("dp", "ctx"), "tp"),
        P(None, None, "tp"),
        P("tp", None),
        P("tp", None),
        P("tp", "ctx"),
        P(),
    )
    plane = mesh.shape["ctx"] == 2 and mesh.shape["tp"] == 4
    return jax.shard_map(
        plane_plan if plane else gather_plan,
        mesh=mesh,
        in_specs=placed,
        out_specs=(P(("dp", "ctx"), "tp"), P(("dp", "ctx"))),
        check_vma=False,
    )
```

```python
import functools

import jax
import jax.numpy as jnp
from jax import lax
from jax.experimental import pallas as pl
from jax.experimental.pallas import tpu as pltpu
from jax.sharding import PartitionSpec as P

EPSILON = 1e-06
HIGHEST = lax.Precision.HIGHEST
LANES = 128
GROUP = 8
STEP = 16
WHOLE = pl.BlockSpec(memory_space=pltpu.VMEM)
SCALARS = pl.BlockSpec(memory_space=pltpu.SMEM)
AWAY = pl.BlockSpec(memory_space=pltpu.HBM)


def params(mebibytes=20):
    return pltpu.CompilerParams(vmem_limit_bytes=mebibytes * 1024 * 1024)


def cost(flops):
    return pl.CostEstimate(flops=flops, bytes_accessed=1024, transcendentals=0)


def spread(source, scratch, row, to):
    blocks = source.shape[1] // LANES
    for block in range(blocks):
        piece = source[pl.ds(row, STEP), block * LANES : (block + 1) * LANES].astype(jnp.float32)
        for half in range(STEP // GROUP):
            start = (half * blocks + block) * GROUP
            scratch[pl.ds(to + start, GROUP), :] = piece[half * GROUP : (half + 1) * GROUP]


def spread_rows(source, target):
    count, width = source.shape
    blocks = width // LANES
    for block in range(blocks):
        target[pl.ds(block, count, stride=blocks), :] = source[:, block * LANES : (block + 1) * LANES]


def place_of(index, blocks):
    return pl.ds((index // GROUP) * (blocks * GROUP) + index % GROUP, blocks, stride=GROUP)


def tile(ref, index, blocks):
    return ref[index * blocks : (index + 1) * blocks, :]


def moving_tile(index, blocks):
    return pl.ds(pl.multiple_of(index * blocks, blocks), blocks)


def front_kernel(*refs):
    k_hbm, v_hbm, q_hbm, taps_hbm, rate_hbm, residue_hbm = refs[:6]
    carry_ref, signal_ref, decay_ref, taps_ref, edge_ref, rate_ref, residue_ref, q_near = refs[6:14]
    k_near, v_near, taps_near, k_wide, v_wide, sems, late_sems = refs[-7:]
    rows, width = k_near.shape
    blocks = width // LANES
    modes = rate_ref.shape[0]
    pieces = sems.shape[0] // 2 - 1
    height = rows // pieces

    def part(i):
        here = pl.ds(i * height, height)
        return (
            pltpu.make_async_copy(k_hbm.at[here], k_near.at[here], sems.at[2 * i]),
            pltpu.make_async_copy(v_hbm.at[here], v_near.at[here], sems.at[2 * i + 1]),
        )

    rate_copy = pltpu.make_async_copy(rate_hbm, rate_ref, sems.at[2 * pieces])
    taps_copy = pltpu.make_async_copy(taps_hbm, taps_near, sems.at[2 * pieces + 1])
    late = [(residue_hbm, residue_ref), (q_hbm, q_near)]
    late = [pltpu.make_async_copy(source, target, late_sems.at[i]) for i, (source, target) in enumerate(late)]
    rate_copy.start()
    taps_copy.start()
    for i in range(pieces):
        for copy in part(i):
            copy.start()
    for copy in late:
        copy.start()
    rate_copy.wait()
    taps_copy.wait()
    spread_rows(jnp.exp(-rate_ref[...]), decay_ref)
    for i in range(3):
        for block in range(blocks):
            taps_ref[pl.ds(3 * i * blocks + block, 3, stride=blocks), :] = taps_near[
                i, :, block * LANES : (block + 1) * LANES
            ]
    zero = jnp.zeros((blocks, LANES), jnp.float32)
    key_taps = [tile(taps_ref, 3 + j, blocks) for j in range(3)]
    value_taps = [tile(taps_ref, 6 + j, blocks) for j in range(3)]
    decay = [tile(decay_ref, m, blocks) for m in range(modes)]

    def step(row, held, first):
        spread(k_near, k_wide, row, 0)
        spread(v_near, v_wide, row, 0)
        state, (k2, k1, v2, v1) = list(held[:modes]), held[modes:]
        for index in range(STEP):
            k0 = k_wide[place_of(index, blocks), :]
            v0 = v_wide[place_of(index, blocks), :]
            key = key_taps[0] * k0 + key_taps[1] * k1 + key_taps[2] * k2
            value = value_taps[0] * v0 + value_taps[1] * v1 + value_taps[2] * v2
            if first and index < 2:
                edge_ref[index * blocks : (index + 1) * blocks, :] = key
                edge_ref[(2 + index) * blocks : (3 + index) * blocks, :] = value
            signal = key * value
            signal_ref[moving_tile(row + index, blocks), :] = signal
            state = [decay[m] * state[m] + signal for m in range(modes)]
            k2, k1, v2, v1 = k1, k0, v1, v0
        return tuple(state) + (k2, k1, v2, v1)

    held = (zero,) * (modes + 4)
    for i in range(pieces):
        for copy in part(i):
            copy.wait()
        begin = 0
        if i == 0:
            held = step(0, held, True)
            begin = 1
        held = lax.fori_loop(
            begin,
            height // STEP,
            lambda j, held, i=i: step(pl.multiple_of(i * height + j * STEP, STEP), held, False),
            held,
        )
    for m in range(modes + 4):
        carry_ref[m * blocks : (m + 1) * blocks, :] = held[m]
    for copy in late:
        copy.wait()
    spread(q_near, k_wide, rows - STEP, 0)
    for i in range(2):
        start = (modes + 4 + i) * blocks
        carry_ref[start : start + blocks, :] = k_wide[place_of(STEP - 2 + i, blocks), :]


def far(x):
    return pltpu.with_memory_space_constraint(x, pltpu.HBM)


def run_front(q, k, v, short_taps, rate, residue):
    rows, width = k.shape
    modes = rate.shape[0]
    blocks = width // LANES
    pieces = 4

    def wide(n):
        return jax.ShapeDtypeStruct((n * blocks, LANES), jnp.float32)

    def like(x):
        return jax.ShapeDtypeStruct(x.shape, x.dtype)

    out_shape = [wide(modes + 6), wide(rows), wide(modes), wide(9), wide(4), like(rate), like(residue), like(q)]
    return pl.pallas_call(
        front_kernel,
        out_shape=out_shape,
        in_specs=[AWAY] * 6,
        out_specs=[WHOLE] * len(out_shape),
        scratch_shapes=[
            pltpu.VMEM((rows, width), jnp.bfloat16),
            pltpu.VMEM((rows, width), jnp.bfloat16),
            pltpu.VMEM(short_taps.shape, jnp.float32),
            pltpu.VMEM((STEP * blocks, LANES), jnp.float32),
            pltpu.VMEM((STEP * blocks, LANES), jnp.float32),
            pltpu.SemaphoreType.DMA((2 * pieces + 2,)),
            pltpu.SemaphoreType.DMA((2,)),
        ],
        compiler_params=params(),
        cost_estimate=cost(10**8),
        name="front",
    )(*[far(x) for x in (k, v, q, short_taps, rate, residue)])


def local_kernel(q_near, signal_ref, decay_ref, taps_ref, gain_near, *refs):
    with_weight = len(refs) > 4
    if with_weight:
        place_ref, direction_hbm, weight_hbm = refs[:3]
        parts_ref, norm_ref, direction_ref, weight_ref = refs[6:10]
        sems = refs[-1]
        refs = refs[3:6] + refs[10:-1]
        count = sems.shape[0] - 1
        depth = weight_ref.shape[0] // count
        copies = [pltpu.make_async_copy(direction_hbm, direction_ref, sems.at[count])]
        for i in range(count):
            here = pl.ds(i * depth, depth)
            copies.append(pltpu.make_async_copy(weight_hbm.at[here], weight_ref.at[here], sems.at[i]))
        for copy in copies:
            copy.start()
    out_ref, query_ref, gain_ref, q_wide = refs
    rows, width = q_near.shape
    blocks = width // LANES
    modes = gain_near.shape[0]
    spread_rows(gain_near[...], gain_ref)
    zero = jnp.zeros((blocks, LANES), jnp.float32)
    taps = [tile(taps_ref, j, blocks) for j in range(3)]
    decay = [tile(decay_ref, m, blocks) for m in range(modes)]
    gain = [tile(gain_ref, m, blocks) for m in range(modes)]

    def step(j, held):
        row = pl.multiple_of(j * STEP, STEP)
        spread(q_near, q_wide, row, 0)
        state, (q2, q1) = list(held[:modes]), held[modes:]
        for index in range(STEP):
            q0 = q_wide[place_of(index, blocks), :]
            here = moving_tile(row + index, blocks)
            signal = signal_ref[here, :]
            query_ref[here, :] = taps[0] * q0 + taps[1] * q1 + taps[2] * q2
            state = [decay[m] * state[m] + signal for m in range(modes)]
            sums = [gain[m] * state[m] for m in range(modes)]
            while len(sums) > 1:
                sums = [sums[i] + sums[i + 1] for i in range(0, len(sums), 2)]
            out_ref[here, :] = sums[0]
            q2, q1 = q1, q0
        return tuple(state) + (q2, q1)

    lax.fori_loop(0, rows // STEP, step, (zero,) * (modes + 2))
    if with_weight:
        for copy in copies:
            copy.wait()
        everything = direction_ref[...]
        norm_ref[...] = jnp.broadcast_to(
            jnp.sum(everything * everything, axis=1, keepdims=True) + EPSILON, norm_ref.shape
        )
        size = weight_ref.shape[1]
        here = direction_ref[:, pl.ds(pl.multiple_of(place_ref[0] * size, LANES), size)]
        parts_ref[...] = in_parts(dot_parts(in_parts(here), weight_ref[...]))


def run_local(q, signal, decay, taps, gain, *weight):
    rows, width = q.shape
    blocks = width // LANES
    wide = jax.ShapeDtypeStruct((rows * blocks, LANES), jnp.float32)
    out_shape = [wide, wide, jax.ShapeDtypeStruct(decay.shape, jnp.float32)]
    scratch_shapes = [pltpu.VMEM((STEP * blocks, LANES), jnp.float32)]
    if weight:
        out_shape += [jax.ShapeDtypeStruct((STEP, width), jnp.bfloat16), jax.ShapeDtypeStruct((1, LANES), jnp.float32)]
        out_shape += [jax.ShapeDtypeStruct(x.shape, x.dtype) for x in weight[1:]]
        scratch_shapes.append(pltpu.SemaphoreType.DMA((5,)))
        weight = (weight[0],) + tuple(far(x) for x in weight[1:])
    return pl.pallas_call(
        local_kernel,
        out_shape=out_shape,
        in_specs=[WHOLE] * 5 + ([SCALARS] + [AWAY] * 2 if weight else []),
        out_specs=[WHOLE] * len(out_shape),
        scratch_shapes=scratch_shapes,
        compiler_params=params(),
        cost_estimate=cost(10**6),
        name="local_filter",
    )(q, signal, decay, taps, gain, *weight)


def correct_kernel(blocks, carry_ref, decay_ref, gain_ref, taps_ref, edge_ref, local_ref, query_ref, *refs):
    wide, outs = refs[-1], refs[:-1]
    rows = local_ref.shape[0] // blocks
    if len(outs) > 1:
        outs = outs[1:]
        outs[1][rows // 2 :, :] = refs[0][...]
    modes = decay_ref.shape[0] // blocks
    k2, k1, v2, v1, q2, q1 = [tile(carry_ref, modes + i, blocks) for i in range(6)]
    tap = [tile(taps_ref, i, blocks) for i in range(9)]
    key0, key1, value0, value1 = [tile(edge_ref, i, blocks) for i in range(4)]
    extra = [
        (key0 + tap[4] * k1 + tap[5] * k2) * (value0 + tap[7] * v1 + tap[8] * v2) - key0 * value0,
        (key1 + tap[5] * k1) * (value1 + tap[8] * v1) - key1 * value1,
    ]
    query_extra = [tap[1] * q1 + tap[2] * q2, tap[2] * q1]
    state = [tile(gain_ref, m, blocks) * tile(carry_ref, m, blocks) for m in range(modes)]
    decay = [tile(decay_ref, m, blocks) for m in range(modes)]

    def step(row, state, first, piece_ref, start):
        state = list(state)
        for index in range(STEP):
            here = moving_tile(row + index, blocks)
            state = [decay[m] * state[m] for m in range(modes)]
            query = query_ref[here, :]
            if first and index < 2:
                state = [state[m] + tile(gain_ref, m, blocks) * extra[index] for m in range(modes)]
                query = query + query_extra[index]
            sums = state
            while len(sums) > 1:
                sums = [sums[i] + sums[i + 1] for i in range(0, len(sums), 2)]
            wide[place_of(index, blocks), :] = query * (local_ref[here, :] + sums[0])
        for block in range(blocks):
            halves = [
                wide[(half * blocks + block) * GROUP : (half * blocks + block + 1) * GROUP, :]
                for half in range(STEP // GROUP)
            ]
            rounded = jnp.concatenate(halves, axis=0).astype(jnp.bfloat16)
            columns = slice(block * LANES, (block + 1) * LANES)
            outs[-1][pl.ds(row, STEP), columns] = rounded
            if piece_ref is not None:
                piece_ref[pl.ds(pl.multiple_of(row - start, STEP), STEP), columns] = rounded
        return tuple(state)

    pieces = outs[:-1] or [None]
    height = rows // len(pieces)
    state = tuple(state)
    for i, piece_ref in enumerate(pieces):
        begin = i * height // STEP
        if i == 0:
            state = step(0, state, True, piece_ref, 0)
            begin = 1
        state = lax.fori_loop(
            begin,
            (i + 1) * height // STEP,
            lambda j, state, i=i, piece_ref=piece_ref: step(
                pl.multiple_of(j * STEP, STEP), state, False, piece_ref, i * height
            ),
            state,
        )


def run_correct(carry, decay, gain, taps, edge, local, query, blocks, *parts):
    rows = local.shape[0] // blocks
    width = blocks * LANES
    heights = [rows // 2, rows // 2 + STEP, rows] if parts else [rows]
    return pl.pallas_call(
        functools.partial(correct_kernel, blocks),
        out_shape=[jax.ShapeDtypeStruct((height, width), jnp.bfloat16) for height in heights],
        in_specs=[WHOLE] * (7 + len(parts)),
        out_specs=[WHOLE] * len(heights),
        scratch_shapes=[pltpu.VMEM((STEP * blocks, LANES), jnp.float32)],
        compiler_params=params(),
        cost_estimate=cost(10**8),
        name="carried_filter",
    )(carry, decay, gain, taps, edge, local, query, *parts)


def gains_of(rate, residue):
    return residue * jnp.sqrt(-jnp.expm1(-2.0 * rate)) * rate.shape[0] ** (-0.5)


def split_three(x):
    high = x.astype(jnp.bfloat16)
    rest = x - high.astype(jnp.float32)
    middle = rest.astype(jnp.bfloat16)
    low = (rest - middle.astype(jnp.float32)).astype(jnp.bfloat16)
    return high, middle, low


def in_parts(row):
    return jnp.concatenate(list(split_three(row)) + [jnp.zeros((13, row.shape[1]), jnp.bfloat16)], axis=0)


def dot_parts(parts, matrix):
    out = lax.dot_general(parts, matrix, (((1,), (1,)), ((), ())), preferred_element_type=jnp.float32)
    return out[0:1] + out[1:2] + out[2:3]


def idle_kernel(*refs):
    pass


def after(array, *others):
    return pl.pallas_call(
        idle_kernel,
        out_shape=jax.ShapeDtypeStruct(array.shape, array.dtype),
        in_specs=[pl.BlockSpec(memory_space=pl.ANY)] * (1 + len(others)),
        out_specs=pl.BlockSpec(memory_space=pl.ANY),
        input_output_aliases={0: 0},
        compiler_params=params(),
        cost_estimate=cost(1),
        name="after",
    )(array, *others)


def call(kernel, name, out_shape, in_specs, *operands):
    return pl.pallas_call(
        kernel,
        out_shape=out_shape,
        in_specs=in_specs,
        out_specs=[WHOLE] * len(out_shape),
        compiler_params=params(),
        cost_estimate=cost(10**6),
        name=name,
    )(*operands)


def rows_of(count, like, dtype=jnp.bfloat16):
    return jax.ShapeDtypeStruct((count, like.shape[1]), dtype)


def rows_of(count, like, dtype=jnp.bfloat16):
    return jax.ShapeDtypeStruct((count, like.shape[1]), dtype)


def call(kernel, name, out_shape, operands, scalars=False):
    return pl.pallas_call(
        kernel,
        out_shape=out_shape,
        in_specs=[SCALARS] * scalars + [WHOLE] * (len(operands) - scalars),
        out_specs=[WHOLE] * len(out_shape),
        compiler_params=params(),
        cost_estimate=cost(10**6),
        name=name,
    )(*operands)


def project_kernel(with_level, place_ref, weight_ref, piece_ref, *refs):
    if with_level:
        whole_ref, parts_ref, send_ref, keep_ref, level_ref = refs
    else:
        send_ref, keep_ref = refs
    rows, width = keep_ref.shape
    side = place_ref[1] % 2
    for which, ref in ((1 - side, send_ref), (side, keep_ref)):
        for part in range(0, width, 256):
            columns = pl.ds(pl.multiple_of(which * width + part, 256), 256)
            for row in range(0, rows, 128):
                here = slice(row, row + 128)
                out = jnp.dot(piece_ref[here, :], weight_ref[:, columns], preferred_element_type=jnp.float32)
                ref[here, part : part + 256] = out.astype(ref.dtype)
    if with_level:
        level = dot_parts(parts_ref[...], whole_ref[...]) + dot_parts(piece_ref[rows:, :], whole_ref[...])
        level_ref[...] = level
        send_ref[rows:, :] = jnp.zeros((STEP, width), jnp.bfloat16)
        send_ref[rows:, : level.shape[1]] = in_parts(level)


def run_project(place, weight, piece, *level_from):
    width = weight.shape[1] // 2
    out_shape = [rows_of(piece.shape[0], jax.ShapeDtypeStruct((1, width), jnp.bfloat16))]
    out_shape.append(jax.ShapeDtypeStruct((piece.shape[0] - STEP * bool(level_from), width), jnp.float32))
    if level_from:
        out_shape.append(jax.ShapeDtypeStruct((1, level_from[0].shape[0]), jnp.float32))
    kernel = functools.partial(project_kernel, bool(level_from))
    return call(kernel, "project", out_shape, (place, weight, piece, *level_from), True)


def merge_kernel(keep_ref, core_ref, *refs):
    outs = refs
    rows, width = keep_ref.shape
    if core_ref.shape[0] > rows:
        level_ref, *outs, total_ref = refs
        count = level_ref.shape[1]
        total_ref[...] = level_ref[...] + jnp.sum(core_ref[rows:, :count].astype(jnp.float32), axis=0, keepdims=True)
    height = rows // len(outs)
    for row in range(0, rows, STEP):
        here = slice(row, row + STEP)
        start = row % height
        outs[row // height][start : start + STEP, :] = (
            keep_ref[here, :] + core_ref[here, :].astype(jnp.float32)
        ).astype(jnp.bfloat16)


def run_merge(keep, core, count, *level):
    out_shape = [rows_of(keep.shape[0] // count, keep)] * count
    out_shape += [jax.ShapeDtypeStruct(x.shape, x.dtype) for x in level]
    return call(merge_kernel, "merge", out_shape, (keep, core, *level))


def choose_kernel(place_ref, straight_ref, own_ref, out_ref):
    keeper = place_ref[1] // 2 == place_ref[0]

    @pl.when(keeper)
    def _():
        out_ref[...] = straight_ref[...]

    @pl.when(jnp.logical_not(keeper))
    def _():
        out_ref[...] = own_ref[...]


def finish_kernel(
    index, place_ref, level_ref, other_ref, norm_ref, direction_ref, keep_ref, core_ref, straight_ref, turned_ref, *refs
):
    out_hbm, level_out_ref, out_near, sems = refs[-4:]
    half, width = out_near.shape
    start = index * half
    level = (level_ref[...] + other_ref[...]) / norm_ref[0:1, 0:1]
    level_out_ref[...] = level
    direction = direction_ref[:, pl.ds(pl.multiple_of(place_ref[1] * width, LANES), width)]
    keeper = place_ref[1] // 2 == place_ref[0]
    column = jnp.transpose(jnp.broadcast_to(level[:, start : start + half], (LANES, half)))
    copies = []
    cuts = sems.shape[0]
    for i in range(cuts):
        part = range(i * half // cuts, (i + 1) * half // cuts, STEP)

        @pl.when(keeper)
        def _():
            for row in part:
                here, there = slice(row, row + STEP), slice(start + row, start + row + STEP)
                total = keep_ref[there, :] + core_ref[there, :].astype(jnp.float32)
                total = total + turned_ref[here, :].astype(jnp.float32)
                out_near[here, :] = (total - column[here, 0:1] * direction).astype(jnp.bfloat16)

        @pl.when(jnp.logical_not(keeper))
        def _():
            for row in part:
                here = slice(row, row + STEP)
                total = straight_ref[here, :].astype(jnp.float32) + turned_ref[here, :].astype(jnp.float32)
                out_near[here, :] = (total - column[here, 0:1] * direction).astype(jnp.bfloat16)

        here = pl.ds(i * half // cuts, half // cuts)
        there = pl.ds(start + i * half // cuts, half // cuts)
        copies.append(pltpu.make_async_copy(out_near.at[here], out_hbm.at[there], sems.at[i]))
        copies[-1].start()
    for copy in copies:
        copy.wait()


def run_finish(index, place, level, other, norm, direction, keep, core, straight, turned, *before):
    rows, width = keep.shape
    operands = (place, level, other, norm, direction, keep, core, straight, turned, *before)
    return pl.pallas_call(
        functools.partial(finish_kernel, index),
        out_shape=(rows_of(rows, keep), jax.ShapeDtypeStruct((1, rows), jnp.float32)),
        in_specs=[SCALARS] + [WHOLE] * 8 + [AWAY] * len(before),
        out_specs=[AWAY, WHOLE],
        scratch_shapes=[pltpu.VMEM((rows // 2, width), jnp.bfloat16), pltpu.SemaphoreType.DMA((2,))],
        input_output_aliases={9: 0} if before else {},
        compiler_params=params(),
        cost_estimate=cost(10**6),
        name="finish",
    )(*operands)


def plane_plan(q, k, v, short_taps, decay_rate, residue, out_weight, direction):
    rows, width = q.shape
    half = rows // 2
    blocks = width // LANES
    ctx, tp = lax.axis_index("ctx"), lax.axis_index("tp")
    axes = ("ctx", "tp")
    place = jnp.stack([ctx, tp]).astype(jnp.int32)

    forward = [(p, 4 + p) for p in range(4)]
    across = [(4 * c + p, 4 * (1 - c) + p) for c in range(2) for p in range(4)]
    sibling = [(4 * c + p, 4 * c + (p ^ 1)) for c in range(2) for p in range(4)]
    pair = [(4 * c + p, 4 * c + (p ^ 2)) for c in range(2) for p in range(4)]

    ended, signal, decay, taps, edge, rate, residue, q = run_front(q, k, v, short_taps, decay_rate.T, residue.T)
    carry = lax.ppermute(ended, axes, forward)
    local, query, gain, parts, norm, direction, weight = run_local(
        q, signal, decay, taps, gains_of(rate, residue), place, direction.reshape(1, -1), out_weight
    )
    first, second, whole = run_correct(carry, decay, gain, taps, edge, local, query, blocks, parts)
    far_first = lax.ppermute(first, axes, across)
    far_second = lax.ppermute(second, axes, across)

    send, keep0 = run_project(place, weight, far_first)
    (sums0,) = run_merge(keep0, lax.ppermute(send, axes, sibling), 1)
    straight0 = lax.ppermute(sums0, axes, across)

    whole = after(whole, sums0)
    own_send, keep = run_project(place, weight, whole)
    send, keep1, level = run_project(place, weight, after(far_second, own_send), whole, parts)
    sums1, level = run_merge(keep1, lax.ppermute(send, axes, sibling), 1, level)
    straight1 = lax.ppermute(sums1, axes, across)
    other = lax.ppermute(level, axes, pair)

    core = lax.ppermute(own_send, axes, sibling)
    own0, own1 = run_merge(keep, core, 2)

    (moved,) = call(choose_kernel, "choose", [rows_of(half, keep)], (place, straight0, own0), True)
    turned0 = lax.ppermute(moved, axes, pair)
    (moved,) = call(choose_kernel, "choose", [rows_of(half, keep)], (place, straight1, own1), True)
    turned1 = lax.ppermute(moved, axes, pair)

    shared = (place, level, other, norm, direction, keep, core)
    ablated, _ = run_finish(0, *shared, straight0, turned0)
    ablated, level = run_finish(1, *shared, straight1, turned1, ablated)
    return ablated, level.reshape(rows)


def gather_plan(q, k, v, short_taps, decay_rate, residue, out_weight, direction):
    rows, width = q.shape
    blocks = width // LANES
    modes = decay_rate.shape[1]
    tp = lax.axis_index("tp")
    ctx_size = lax.axis_size("ctx")
    next_one = [(i, i + 1) for i in range(ctx_size - 1)]
    ended, signal, decay, taps, edge, rate, residue, q = run_front(q, k, v, short_taps, decay_rate.T, residue.T)
    halo = lax.ppermute(ended[modes * blocks :], "ctx", next_one)
    local, query, gain = run_local(q, signal, decay, taps, gains_of(rate, residue))
    k2, k1, v2, v1 = [halo[i * blocks : (i + 1) * blocks] for i in range(4)]
    tap = taps.reshape(9, blocks, LANES)
    key0, key1, value0, value1 = edge.reshape(4, blocks, LANES)
    extra0 = (key0 + tap[4] * k1 + tap[5] * k2) * (value0 + tap[7] * v1 + tap[8] * v2) - key0 * value0
    extra1 = (key1 + tap[5] * k1) * (value1 + tap[8] * v1) - key1 * value1
    wide_rate = decay_rate.T.reshape(modes, blocks, LANES)
    state = (
        ended[: modes * blocks].reshape(modes, blocks, LANES)
        + jnp.exp(-wide_rate * (rows - 1)) * extra0
        + jnp.exp(-wide_rate * (rows - 2)) * extra1
    )
    reach = 1
    while reach < ctx_size:
        earlier = lax.ppermute(state, "ctx", [(i, i + reach) for i in range(ctx_size - reach)])
        state = state + jnp.exp(-wide_rate * (rows * reach)) * earlier
        reach *= 2
    start = lax.ppermute(state, "ctx", next_one).reshape(modes * blocks, LANES)
    carry = jnp.concatenate([start, halo], axis=0)
    (gated,) = run_correct(carry, decay, gain, taps, edge, local, query, blocks)
    partial_terms = lax.dot_general(
        gated,
        lax.all_gather(out_weight, "ctx", axis=1, tiled=True),
        (((1,), (0,)), ((), ())),
        preferred_element_type=jnp.float32,
    )
    summed = lax.psum_scatter(
        partial_terms.astype(jnp.bfloat16), "tp", scatter_dimension=1, tiled=True
    ).astype(jnp.float32)
    width_here = summed.shape[1]
    direction_here = lax.dynamic_slice_in_dim(direction, tp * width_here, width_here, 0)
    norm_total = jnp.sum(direction * direction) + EPSILON
    local_inner = jnp.dot(summed, direction_here, precision=HIGHEST)
    feature_level = lax.psum(local_inner, "tp") / norm_total
    ablated = (summed - feature_level[:, None] * direction_here[None, :]).astype(jnp.bfloat16)
    return ablated, feature_level


def solution(mesh):
    placed = (
        P(("dp", "ctx"), "tp"),
        P(("dp", "ctx"), "tp"),
        P(("dp", "ctx"), "tp"),
        P(None, None, "tp"),
        P("tp", None),
        P("tp", None),
        P("tp", "ctx"),
        P(),
    )
    plane = mesh.shape["ctx"] == 2 and mesh.shape["tp"] == 4
    return jax.shard_map(
        plane_plan if plane else gather_plan,
        mesh=mesh,
        in_specs=placed,
        out_specs=(P(("dp", "ctx"), "tp"), P(("dp", "ctx"))),
        check_vma=False,
    )
```

```python
import functools

import jax
import jax.numpy as jnp
from jax import lax
from jax.experimental import pallas as pl
from jax.experimental.pallas import tpu as pltpu
from jax.sharding import PartitionSpec as P

EPSILON = 1e-06
HIGHEST = lax.Precision.HIGHEST
LANES = 128
GROUP = 8
STEP = 16
WHOLE = pl.BlockSpec(memory_space=pltpu.VMEM)
AWAY = pl.BlockSpec(memory_space=pltpu.HBM)


def params(mebibytes=20):
    return pltpu.CompilerParams(vmem_limit_bytes=mebibytes * 1024 * 1024)


def cost(flops):
    return pl.CostEstimate(flops=flops, bytes_accessed=1024, transcendentals=0)


def spread(source, scratch, row, to):
    blocks = source.shape[1] // LANES
    for block in range(blocks):
        piece = source[pl.ds(row, STEP), block * LANES : (block + 1) * LANES].astype(jnp.float32)
        for half in range(STEP // GROUP):
            start = (half * blocks + block) * GROUP
            scratch[pl.ds(to + start, GROUP), :] = piece[half * GROUP : (half + 1) * GROUP]


def spread_rows(source, target):
    count, width = source.shape
    blocks = width // LANES
    for block in range(blocks):
        target[pl.ds(block, count, stride=blocks), :] = source[:, block * LANES : (block + 1) * LANES]


def place_of(index, blocks):
    return pl.ds((index // GROUP) * (blocks * GROUP) + index % GROUP, blocks, stride=GROUP)


def tile(ref, index, blocks):
    return ref[index * blocks : (index + 1) * blocks, :]


def moving_tile(index, blocks):
    return pl.ds(pl.multiple_of(index * blocks, blocks), blocks)


def front_kernel(*refs):
    k_hbm, v_hbm, q_hbm, taps_hbm, rate_hbm, residue_hbm = refs[:6]
    carry_ref, signal_ref, decay_ref, taps_ref, edge_ref, rate_ref, residue_ref, q_near = refs[6:14]
    k_near, v_near, taps_near, k_wide, v_wide, sems, late_sems = refs[-7:]
    rows, width = k_near.shape
    blocks = width // LANES
    modes = rate_ref.shape[0]
    pieces = sems.shape[0] // 2 - 1
    height = rows // pieces

    def part(i):
        here = pl.ds(i * height, height)
        return (
            pltpu.make_async_copy(k_hbm.at[here], k_near.at[here], sems.at[2 * i]),
            pltpu.make_async_copy(v_hbm.at[here], v_near.at[here], sems.at[2 * i + 1]),
        )

    rate_copy = pltpu.make_async_copy(rate_hbm, rate_ref, sems.at[2 * pieces])
    taps_copy = pltpu.make_async_copy(taps_hbm, taps_near, sems.at[2 * pieces + 1])
    late = [(residue_hbm, residue_ref), (q_hbm, q_near)]
    late = [pltpu.make_async_copy(source, target, late_sems.at[i]) for i, (source, target) in enumerate(late)]
    rate_copy.start()
    taps_copy.start()
    for i in range(pieces):
        for copy in part(i):
            copy.start()
    for copy in late:
        copy.start()
    rate_copy.wait()
    taps_copy.wait()
    spread_rows(jnp.exp(-rate_ref[...]), decay_ref)
    for i in range(3):
        for block in range(blocks):
            taps_ref[pl.ds(3 * i * blocks + block, 3, stride=blocks), :] = taps_near[
                i, :, block * LANES : (block + 1) * LANES
            ]
    zero = jnp.zeros((blocks, LANES), jnp.float32)
    key_taps = [tile(taps_ref, 3 + j, blocks) for j in range(3)]
    value_taps = [tile(taps_ref, 6 + j, blocks) for j in range(3)]
    decay = [tile(decay_ref, m, blocks) for m in range(modes)]

    def step(row, held, first):
        spread(k_near, k_wide, row, 0)
        spread(v_near, v_wide, row, 0)
        state, (k2, k1, v2, v1) = list(held[:modes]), held[modes:]
        for index in range(STEP):
            k0 = k_wide[place_of(index, blocks), :]
            v0 = v_wide[place_of(index, blocks), :]
            key = key_taps[0] * k0 + key_taps[1] * k1 + key_taps[2] * k2
            value = value_taps[0] * v0 + value_taps[1] * v1 + value_taps[2] * v2
            if first and index < 2:
                edge_ref[index * blocks : (index + 1) * blocks, :] = key
                edge_ref[(2 + index) * blocks : (3 + index) * blocks, :] = value
            signal = key * value
            signal_ref[moving_tile(row + index, blocks), :] = signal
            state = [decay[m] * state[m] + signal for m in range(modes)]
            k2, k1, v2, v1 = k1, k0, v1, v0
        return tuple(state) + (k2, k1, v2, v1)

    held = (zero,) * (modes + 4)
    for i in range(pieces):
        for copy in part(i):
            copy.wait()
        begin = 0
        if i == 0:
            held = step(0, held, True)
            begin = 1
        held = lax.fori_loop(
            begin,
            height // STEP,
            lambda j, held, i=i: step(pl.multiple_of(i * height + j * STEP, STEP), held, False),
            held,
        )
    for m in range(modes + 4):
        carry_ref[m * blocks : (m + 1) * blocks, :] = held[m]
    for copy in late:
        copy.wait()
    spread(q_near, k_wide, rows - STEP, 0)
    for i in range(2):
        start = (modes + 4 + i) * blocks
        carry_ref[start : start + blocks, :] = k_wide[place_of(STEP - 2 + i, blocks), :]


def far(x):
    return pltpu.with_memory_space_constraint(x, pltpu.HBM)


def run_front(q, k, v, short_taps, rate, residue):
    rows, width = k.shape
    modes = rate.shape[0]
    blocks = width // LANES
    pieces = 4

    def wide(n):
        return jax.ShapeDtypeStruct((n * blocks, LANES), jnp.float32)

    def like(x):
        return jax.ShapeDtypeStruct(x.shape, x.dtype)

    out_shape = [wide(modes + 6), wide(rows), wide(modes), wide(9), wide(4), like(rate), like(residue), like(q)]
    return pl.pallas_call(
        front_kernel,
        out_shape=out_shape,
        in_specs=[AWAY] * 6,
        out_specs=[WHOLE] * len(out_shape),
        scratch_shapes=[
            pltpu.VMEM((rows, width), jnp.bfloat16),
            pltpu.VMEM((rows, width), jnp.bfloat16),
            pltpu.VMEM(short_taps.shape, jnp.float32),
            pltpu.VMEM((STEP * blocks, LANES), jnp.float32),
            pltpu.VMEM((STEP * blocks, LANES), jnp.float32),
            pltpu.SemaphoreType.DMA((2 * pieces + 2,)),
            pltpu.SemaphoreType.DMA((2,)),
        ],
        compiler_params=params(),
        cost_estimate=cost(10**8),
        name="front",
    )(*[far(x) for x in (k, v, q, short_taps, rate, residue)])


def local_kernel(q_near, signal_ref, decay_ref, taps_ref, gain_near, *refs):
    copies = []
    if len(refs) > 4:
        weight_hbm, weight_ref, sems = refs[0], refs[4], refs[-1]
        refs = refs[1:4] + refs[5:-1]
        count = sems.shape[0]
        depth = weight_ref.shape[0] // count
        for i in range(count):
            here = pl.ds(i * depth, depth)
            copies.append(pltpu.make_async_copy(weight_hbm.at[here], weight_ref.at[here], sems.at[i]))
            copies[-1].start()
    out_ref, query_ref, gain_ref, q_wide = refs
    rows, width = q_near.shape
    blocks = width // LANES
    modes = gain_near.shape[0]
    spread_rows(gain_near[...], gain_ref)
    zero = jnp.zeros((blocks, LANES), jnp.float32)
    taps = [tile(taps_ref, j, blocks) for j in range(3)]
    decay = [tile(decay_ref, m, blocks) for m in range(modes)]
    gain = [tile(gain_ref, m, blocks) for m in range(modes)]

    def step(j, held):
        row = pl.multiple_of(j * STEP, STEP)
        spread(q_near, q_wide, row, 0)
        state, (q2, q1) = list(held[:modes]), held[modes:]
        for index in range(STEP):
            q0 = q_wide[place_of(index, blocks), :]
            here = moving_tile(row + index, blocks)
            signal = signal_ref[here, :]
            query_ref[here, :] = taps[0] * q0 + taps[1] * q1 + taps[2] * q2
            state = [decay[m] * state[m] + signal for m in range(modes)]
            sums = [gain[m] * state[m] for m in range(modes)]
            while len(sums) > 1:
                sums = [sums[i] + sums[i + 1] for i in range(0, len(sums), 2)]
            out_ref[here, :] = sums[0]
            q2, q1 = q1, q0
        return tuple(state) + (q2, q1)

    lax.fori_loop(0, rows // STEP, step, (zero,) * (modes + 2))
    for copy in copies:
        copy.wait()


def run_local(q, signal, decay, taps, gain, *weight):
    rows, width = q.shape
    blocks = width // LANES
    wide = jax.ShapeDtypeStruct((rows * blocks, LANES), jnp.float32)
    out_shape = [wide, wide, jax.ShapeDtypeStruct(decay.shape, jnp.float32)]
    scratch_shapes = [pltpu.VMEM((STEP * blocks, LANES), jnp.float32)]
    if weight:
        out_shape += [jax.ShapeDtypeStruct(x.shape, x.dtype) for x in weight]
        scratch_shapes.append(pltpu.SemaphoreType.DMA((4,)))
        weight = tuple(far(x) for x in weight)
    return pl.pallas_call(
        local_kernel,
        out_shape=out_shape,
        in_specs=[WHOLE] * 5 + [AWAY] * len(weight),
        out_specs=[WHOLE] * len(out_shape),
        scratch_shapes=scratch_shapes,
        compiler_params=params(),
        cost_estimate=cost(10**6),
        name="local_filter",
    )(q, signal, decay, taps, gain, *weight)


def correct_kernel(blocks, carry_ref, decay_ref, gain_ref, taps_ref, edge_ref, local_ref, query_ref, *refs):
    wide, outs = refs[-1], refs[:-1]
    rows = local_ref.shape[0] // blocks
    modes = decay_ref.shape[0] // blocks
    k2, k1, v2, v1, q2, q1 = [tile(carry_ref, modes + i, blocks) for i in range(6)]
    tap = [tile(taps_ref, i, blocks) for i in range(9)]
    key0, key1, value0, value1 = [tile(edge_ref, i, blocks) for i in range(4)]
    extra = [
        (key0 + tap[4] * k1 + tap[5] * k2) * (value0 + tap[7] * v1 + tap[8] * v2) - key0 * value0,
        (key1 + tap[5] * k1) * (value1 + tap[8] * v1) - key1 * value1,
    ]
    query_extra = [tap[1] * q1 + tap[2] * q2, tap[2] * q1]
    state = [tile(gain_ref, m, blocks) * tile(carry_ref, m, blocks) for m in range(modes)]
    decay = [tile(decay_ref, m, blocks) for m in range(modes)]

    def step(row, state, first, piece_ref, start):
        state = list(state)
        for index in range(STEP):
            here = moving_tile(row + index, blocks)
            state = [decay[m] * state[m] for m in range(modes)]
            query = query_ref[here, :]
            if first and index < 2:
                state = [state[m] + tile(gain_ref, m, blocks) * extra[index] for m in range(modes)]
                query = query + query_extra[index]
            sums = state
            while len(sums) > 1:
                sums = [sums[i] + sums[i + 1] for i in range(0, len(sums), 2)]
            wide[place_of(index, blocks), :] = query * (local_ref[here, :] + sums[0])
        for block in range(blocks):
            halves = [
                wide[(half * blocks + block) * GROUP : (half * blocks + block + 1) * GROUP, :]
                for half in range(STEP // GROUP)
            ]
            rounded = jnp.concatenate(halves, axis=0).astype(jnp.bfloat16)
            columns = slice(block * LANES, (block + 1) * LANES)
            outs[-1][pl.ds(row, STEP), columns] = rounded
            if piece_ref is not None:
                piece_ref[pl.ds(pl.multiple_of(row - start, STEP), STEP), columns] = rounded
        return tuple(state)

    state = tuple(state)
    start = 0
    for piece_ref in outs[:-1] or [None]:
        end = start + (rows if piece_ref is None else piece_ref.shape[0])
        begin = start // STEP
        if start == 0:
            state = step(0, state, True, piece_ref, 0)
            begin = 1
        state = lax.fori_loop(
            begin,
            end // STEP,
            lambda j, state, start=start, piece_ref=piece_ref: step(
                pl.multiple_of(j * STEP, STEP), state, False, piece_ref, start
            ),
            state,
        )
        start = end


def run_correct(carry, decay, gain, taps, edge, local, query, blocks, *heights):
    rows = local.shape[0] // blocks
    width = blocks * LANES
    heights += (rows,)
    return pl.pallas_call(
        functools.partial(correct_kernel, blocks),
        out_shape=[jax.ShapeDtypeStruct((height, width), jnp.bfloat16) for height in heights],
        in_specs=[WHOLE] * 7,
        out_specs=[WHOLE] * len(heights),
        scratch_shapes=[pltpu.VMEM((STEP * blocks, LANES), jnp.float32)],
        compiler_params=params(),
        cost_estimate=cost(10**8),
        name="carried_filter",
    )(carry, decay, gain, taps, edge, local, query)


def gains_of(rate, residue):
    return residue * jnp.sqrt(-jnp.expm1(-2.0 * rate)) * rate.shape[0] ** (-0.5)


def split_three(x):
    high = x.astype(jnp.bfloat16)
    rest = x - high.astype(jnp.float32)
    middle = rest.astype(jnp.bfloat16)
    low = (rest - middle.astype(jnp.float32)).astype(jnp.bfloat16)
    return high, middle, low


def in_parts(row):
    return jnp.concatenate(list(split_three(row)) + [jnp.zeros((13, row.shape[1]), jnp.bfloat16)], axis=0)


def dot_parts(parts, matrix):
    out = lax.dot_general(parts, matrix, (((1,), (1,)), ((), ())), preferred_element_type=jnp.float32)
    return out[0:1] + out[1:2] + out[2:3]


def idle_kernel(*refs):
    pass


def after(array, *others):
    return pl.pallas_call(
        idle_kernel,
        out_shape=jax.ShapeDtypeStruct(array.shape, array.dtype),
        in_specs=[pl.BlockSpec(memory_space=pl.ANY)] * (1 + len(others)),
        out_specs=pl.BlockSpec(memory_space=pl.ANY),
        input_output_aliases={0: 0},
        compiler_params=params(),
        cost_estimate=cost(1),
        name="after",
    )(array, *others)


def rows_of(count, like, dtype=jnp.bfloat16):
    return jax.ShapeDtypeStruct((count, like.shape[1]), dtype)


def call(kernel, name, out_shape, *operands, tokens=()):
    def with_tokens(*refs):
        kernel(*refs[: len(operands)], *refs[len(operands) + len(tokens) :])

    return pl.pallas_call(
        with_tokens,
        out_shape=out_shape,
        in_specs=[WHOLE] * len(operands) + [pl.BlockSpec(memory_space=pl.ANY)] * len(tokens),
        out_specs=[WHOLE] * len(out_shape),
        compiler_params=params(),
        cost_estimate=cost(10**6),
        name=name,
    )(*operands, *tokens)


def inner_kernel(direction_hbm, weight_ref, parts_ref, norm_ref, here_ref, near, sem):
    copy = pltpu.make_async_copy(direction_hbm, near, sem)
    copy.start()
    copy.wait()
    everything = near[...]
    norm_ref[...] = jnp.broadcast_to(
        jnp.sum(everything * everything, axis=1, keepdims=True) + EPSILON, norm_ref.shape
    )
    size, width = weight_ref.shape[1], here_ref.shape[1]
    here_ref[...] = near[:, pl.ds(pl.multiple_of(lax.axis_index("tp") * width, LANES), width)]
    here = near[:, pl.ds(pl.multiple_of(lax.axis_index("ctx") * size, LANES), size)]
    parts_ref[...] = in_parts(dot_parts(in_parts(here), weight_ref[...]))


def run_inner(direction, weight):
    return pl.pallas_call(
        inner_kernel,
        out_shape=(
            jax.ShapeDtypeStruct((STEP, weight.shape[0]), jnp.bfloat16),
            jax.ShapeDtypeStruct((1, LANES), jnp.float32),
            jax.ShapeDtypeStruct((1, weight.shape[1] // 2), jnp.float32),
        ),
        in_specs=[AWAY, WHOLE],
        out_specs=[WHOLE] * 3,
        scratch_shapes=[pltpu.VMEM(direction.shape, jnp.float32), pltpu.SemaphoreType.DMA],
        compiler_params=params(),
        cost_estimate=cost(10**6),
        name="inner",
    )(far(direction), weight)


def project_kernel(weight_ref, piece_ref, send_ref, keep_ref):
    rows, width = keep_ref.shape
    side = lax.axis_index("tp") % 2
    for which, ref in ((1 - side, send_ref), (side, keep_ref)):
        for part in range(0, width, 256):
            columns = pl.ds(pl.multiple_of(which * width + part, 256), 256)
            size = rows if rows < 160 else 128
            for row in range(0, rows, size):
                here = slice(row, row + size)
                out = jnp.dot(piece_ref[here, :], weight_ref[:, columns], preferred_element_type=jnp.float32)
                ref[here, part : part + 256] = out.astype(ref.dtype)


def run_project(weight, piece, *tokens):
    keep = jax.ShapeDtypeStruct((piece.shape[0], weight.shape[1] // 2), jnp.float32)
    return call(project_kernel, "project", [rows_of(piece.shape[0], keep), keep], weight, piece, tokens=tokens)


def level_kernel(parts_ref, far_parts_ref, whole_ref, out_ref):
    out_ref[...] = dot_parts(parts_ref[...], whole_ref[...]) + dot_parts(far_parts_ref[...], whole_ref[...])


def merge_kernel(keep_ref, core_ref, *outs):
    start = 0
    for ref in outs:
        for row in range(0, ref.shape[0], STEP):
            here = slice(start + row, start + row + STEP)
            ref[row : row + STEP, :] = (keep_ref[here, :] + core_ref[here, :].astype(jnp.float32)).astype(jnp.bfloat16)
        start += ref.shape[0]


def run_merge(keep, core, *heights):
    return call(merge_kernel, "merge", [rows_of(height, keep) for height in heights], keep, core)


def is_keeper():
    return lax.axis_index("tp") // 2 == lax.axis_index("ctx")


def choose_kernel(straight_ref, own_ref, out_ref):
    keeper = is_keeper()

    @pl.when(keeper)
    def _():
        out_ref[...] = straight_ref[...]

    @pl.when(jnp.logical_not(keeper))
    def _():
        out_ref[...] = own_ref[...]


def run_choose(straight, own, *tokens):
    (out,) = call(choose_kernel, "choose", [rows_of(own.shape[0], own)], straight, own, tokens=tokens)
    return out


def finish_kernel(
    start, level_ref, other_ref, norm_ref, direction_ref, keep_ref, core_ref, straight_ref, turned_ref, *refs
):
    out_near, sems = refs[-2:]
    out_hbm = refs[-4 if start else -3]
    rows, width = out_near.shape
    level = (level_ref[...] + other_ref[...]) / norm_ref[0:1, 0:1]
    if start:
        refs[-3][...] = level
    direction = direction_ref[...]
    keeper = is_keeper()
    column = jnp.transpose(jnp.broadcast_to(level, (LANES, level.shape[1])))
    copies = []
    half = rows // 2 // STEP * STEP
    for i, (begin, end) in enumerate(((0, half), (half, rows))):

        @pl.when(keeper)
        def _():
            for row in range(begin, end, STEP):
                here, there = slice(row, row + STEP), slice(start + row, start + row + STEP)
                total = keep_ref[there, :] + core_ref[there, :].astype(jnp.float32)
                total = total + turned_ref[here, :].astype(jnp.float32)
                out_near[here, :] = (total - column[there, 0:1] * direction).astype(jnp.bfloat16)

        @pl.when(jnp.logical_not(keeper))
        def _():
            for row in range(begin, end, STEP):
                here, there = slice(row, row + STEP), slice(start + row, start + row + STEP)
                total = straight_ref[here, :].astype(jnp.float32) + turned_ref[here, :].astype(jnp.float32)
                out_near[here, :] = (total - column[there, 0:1] * direction).astype(jnp.bfloat16)

        here, there = pl.ds(begin, end - begin), pl.ds(start + begin, end - begin)
        copies.append(pltpu.make_async_copy(out_near.at[here], out_hbm.at[there], sems.at[i]))
        copies[-1].start()
    for copy in copies:
        copy.wait()


def run_finish(start, level, other, norm, direction, keep, core, straight, turned, *before):
    rows, width = keep.shape
    levels = [jax.ShapeDtypeStruct((1, rows), jnp.float32)] * (not before)
    return pl.pallas_call(
        functools.partial(finish_kernel, start),
        out_shape=[rows_of(rows, keep)] + levels,
        in_specs=[WHOLE] * 8 + [AWAY] * len(before),
        out_specs=[AWAY] + [WHOLE] * len(levels),
        scratch_shapes=[pltpu.VMEM(straight.shape, jnp.bfloat16), pltpu.SemaphoreType.DMA((2,))],
        input_output_aliases={8: 0} if before else {},
        compiler_params=params(),
        cost_estimate=cost(10**6),
        name="finish",
    )(level, other, norm, direction, keep, core, straight, turned, *before)


def plane_plan(q, k, v, short_taps, decay_rate, residue, out_weight, direction):
    rows, width = q.shape
    cut = rows // STEP * 7 // 16 * STEP
    blocks = width // LANES
    axes = ("ctx", "tp")
    forward = [(p, 4 + p) for p in range(4)]
    across = [(4 * c + p, 4 * (1 - c) + p) for c in range(2) for p in range(4)]
    sibling = [(4 * c + p, 4 * c + (p ^ 1)) for c in range(2) for p in range(4)]
    pair = [(4 * c + p, 4 * c + (p ^ 2)) for c in range(2) for p in range(4)]

    ended, signal, decay, taps, edge, rate, residue, q = run_front(q, k, v, short_taps, decay_rate.T, residue.T)
    carry = lax.ppermute(ended, axes, forward)
    local, query, gain, weight = run_local(q, signal, decay, taps, gains_of(rate, residue), out_weight)
    first, second, whole = run_correct(carry, decay, gain, taps, edge, local, query, blocks, cut, rows - cut)
    far_first = lax.ppermute(first, axes, across)
    far_second = lax.ppermute(second, axes, across)

    weight = after(weight, whole)
    parts, norm, direction = run_inner(direction.reshape(1, -1), weight)
    far_parts = lax.ppermute(parts, axes, across)
    send, keep0 = run_project(weight, far_first, parts)
    (sums0,) = run_merge(keep0, lax.ppermute(send, axes, sibling), cut)
    straight0 = lax.ppermute(sums0, axes, across)

    whole = after(whole, sums0)
    own_send, keep = run_project(weight, whole)
    send, keep1 = run_project(weight, after(far_second, own_send, far_parts))
    (sums1,) = run_merge(keep1, lax.ppermute(send, axes, sibling), rows - cut)
    straight1 = lax.ppermute(sums1, axes, across)
    core = lax.ppermute(own_send, axes, sibling)
    own0, own1 = run_merge(keep, core, cut, rows - cut)

    (level,) = call(
        level_kernel, "level", [jax.ShapeDtypeStruct((1, rows), jnp.float32)], parts, far_parts, whole, tokens=(sums1,)
    )
    level = level + lax.ppermute(level, axes, sibling)
    other = lax.ppermute(level, axes, pair)

    turned1 = lax.ppermute(run_choose(straight1, own1, other), axes, pair)
    turned0 = lax.ppermute(run_choose(straight0, own0), axes, pair)
    shared = (level, other, norm, direction, keep, core)
    ablated, level = run_finish(cut, *shared, straight1, turned1)
    (ablated,) = run_finish(0, *shared, straight0, turned0, ablated)
    return ablated, level.reshape(rows)


def gather_plan(q, k, v, short_taps, decay_rate, residue, out_weight, direction):
    rows, width = q.shape
    blocks = width // LANES
    modes = decay_rate.shape[1]
    tp = lax.axis_index("tp")
    ctx_size = lax.axis_size("ctx")
    next_one = [(i, i + 1) for i in range(ctx_size - 1)]
    ended, signal, decay, taps, edge, rate, residue, q = run_front(q, k, v, short_taps, decay_rate.T, residue.T)
    halo = lax.ppermute(ended[modes * blocks :], "ctx", next_one)
    local, query, gain = run_local(q, signal, decay, taps, gains_of(rate, residue))
    k2, k1, v2, v1 = [halo[i * blocks : (i + 1) * blocks] for i in range(4)]
    tap = taps.reshape(9, blocks, LANES)
    key0, key1, value0, value1 = edge.reshape(4, blocks, LANES)
    extra0 = (key0 + tap[4] * k1 + tap[5] * k2) * (value0 + tap[7] * v1 + tap[8] * v2) - key0 * value0
    extra1 = (key1 + tap[5] * k1) * (value1 + tap[8] * v1) - key1 * value1
    wide_rate = decay_rate.T.reshape(modes, blocks, LANES)
    state = (
        ended[: modes * blocks].reshape(modes, blocks, LANES)
        + jnp.exp(-wide_rate * (rows - 1)) * extra0
        + jnp.exp(-wide_rate * (rows - 2)) * extra1
    )
    reach = 1
    while reach < ctx_size:
        earlier = lax.ppermute(state, "ctx", [(i, i + reach) for i in range(ctx_size - reach)])
        state = state + jnp.exp(-wide_rate * (rows * reach)) * earlier
        reach *= 2
    start = lax.ppermute(state, "ctx", next_one).reshape(modes * blocks, LANES)
    carry = jnp.concatenate([start, halo], axis=0)
    (gated,) = run_correct(carry, decay, gain, taps, edge, local, query, blocks)
    partial_terms = lax.dot_general(
        gated,
        lax.all_gather(out_weight, "ctx", axis=1, tiled=True),
        (((1,), (0,)), ((), ())),
        preferred_element_type=jnp.float32,
    )
    summed = lax.psum_scatter(
        partial_terms.astype(jnp.bfloat16), "tp", scatter_dimension=1, tiled=True
    ).astype(jnp.float32)
    width_here = summed.shape[1]
    direction_here = lax.dynamic_slice_in_dim(direction, tp * width_here, width_here, 0)
    norm_total = jnp.sum(direction * direction) + EPSILON
    local_inner = jnp.dot(summed, direction_here, precision=HIGHEST)
    feature_level = lax.psum(local_inner, "tp") / norm_total
    ablated = (summed - feature_level[:, None] * direction_here[None, :]).astype(jnp.bfloat16)
    return ablated, feature_level


def solution(mesh):
    placed = (
        P(("dp", "ctx"), "tp"),
        P(("dp", "ctx"), "tp"),
        P(("dp", "ctx"), "tp"),
        P(None, None, "tp"),
        P("tp", None),
        P("tp", None),
        P("tp", "ctx"),
        P(),
    )
    plane = mesh.shape["ctx"] == 2 and mesh.shape["tp"] == 4
    return jax.shard_map(
        plane_plan if plane else gather_plan,
        mesh=mesh,
        in_specs=placed,
        out_specs=(P(("dp", "ctx"), "tp"), P(("dp", "ctx"))),
        check_vma=False,
    )
```

```python
import functools

import jax
import jax.numpy as jnp
from jax import lax
from jax.experimental import pallas as pl
from jax.experimental.pallas import tpu as pltpu
from jax.sharding import PartitionSpec as P

EPSILON = 1e-06
HIGHEST = lax.Precision.HIGHEST
LANES = 128
GROUP = 8
STEP = 16
WHOLE = pl.BlockSpec(memory_space=pltpu.VMEM)
AWAY = pl.BlockSpec(memory_space=pltpu.HBM)


def params(mebibytes=20):
    return pltpu.CompilerParams(vmem_limit_bytes=mebibytes * 1024 * 1024)


def cost(flops):
    return pl.CostEstimate(flops=flops, bytes_accessed=1024, transcendentals=0)


def spread(source, scratch, row, to):
    blocks = source.shape[1] // LANES
    for block in range(blocks):
        piece = source[pl.ds(row, STEP), block * LANES : (block + 1) * LANES].astype(jnp.float32)
        for half in range(STEP // GROUP):
            start = (half * blocks + block) * GROUP
            scratch[pl.ds(to + start, GROUP), :] = piece[half * GROUP : (half + 1) * GROUP]


def spread_rows(source, target):
    count, width = source.shape
    blocks = width // LANES
    for block in range(blocks):
        target[pl.ds(block, count, stride=blocks), :] = source[:, block * LANES : (block + 1) * LANES]


def place_of(index, blocks):
    return pl.ds((index // GROUP) * (blocks * GROUP) + index % GROUP, blocks, stride=GROUP)


def tile(ref, index, blocks):
    return ref[index * blocks : (index + 1) * blocks, :]


def moving_tile(index, blocks):
    return pl.ds(pl.multiple_of(index * blocks, blocks), blocks)


def front_kernel(*refs):
    k_hbm, v_hbm, q_hbm, taps_hbm, rate_hbm, residue_hbm = refs[:6]
    carry_ref, signal_ref, decay_ref, taps_ref, edge_ref, rate_ref, residue_ref, q_near = refs[6:14]
    k_near, v_near, taps_near, k_wide, v_wide, sems, late_sems = refs[-7:]
    rows, width = k_near.shape
    blocks = width // LANES
    modes = rate_ref.shape[0]
    pieces = sems.shape[0] // 2 - 1
    height = rows // pieces

    def part(i):
        here = pl.ds(i * height, height)
        return (
            pltpu.make_async_copy(k_hbm.at[here], k_near.at[here], sems.at[2 * i]),
            pltpu.make_async_copy(v_hbm.at[here], v_near.at[here], sems.at[2 * i + 1]),
        )

    rate_copy = pltpu.make_async_copy(rate_hbm, rate_ref, sems.at[2 * pieces])
    taps_copy = pltpu.make_async_copy(taps_hbm, taps_near, sems.at[2 * pieces + 1])
    late = [(residue_hbm, residue_ref), (q_hbm, q_near)]
    late = [pltpu.make_async_copy(source, target, late_sems.at[i]) for i, (source, target) in enumerate(late)]
    rate_copy.start()
    taps_copy.start()
    for i in range(pieces):
        for copy in part(i):
            copy.start()
    for copy in late:
        copy.start()
    rate_copy.wait()
    taps_copy.wait()
    spread_rows(jnp.exp(-rate_ref[...]), decay_ref)
    for i in range(3):
        for block in range(blocks):
            taps_ref[pl.ds(3 * i * blocks + block, 3, stride=blocks), :] = taps_near[
                i, :, block * LANES : (block + 1) * LANES
            ]
    zero = jnp.zeros((blocks, LANES), jnp.float32)
    key_taps = [tile(taps_ref, 3 + j, blocks) for j in range(3)]
    value_taps = [tile(taps_ref, 6 + j, blocks) for j in range(3)]
    decay = [tile(decay_ref, m, blocks) for m in range(modes)]

    def step(row, held, first):
        spread(k_near, k_wide, row, 0)
        spread(v_near, v_wide, row, 0)
        state, (k2, k1, v2, v1) = list(held[:modes]), held[modes:]
        for index in range(STEP):
            k0 = k_wide[place_of(index, blocks), :]
            v0 = v_wide[place_of(index, blocks), :]
            key = key_taps[0] * k0 + key_taps[1] * k1 + key_taps[2] * k2
            value = value_taps[0] * v0 + value_taps[1] * v1 + value_taps[2] * v2
            if first and index < 2:
                edge_ref[index * blocks : (index + 1) * blocks, :] = key
                edge_ref[(2 + index) * blocks : (3 + index) * blocks, :] = value
            signal = key * value
            signal_ref[moving_tile(row + index, blocks), :] = signal
            state = [decay[m] * state[m] + signal for m in range(modes)]
            k2, k1, v2, v1 = k1, k0, v1, v0
        return tuple(state) + (k2, k1, v2, v1)

    held = (zero,) * (modes + 4)
    for i in range(pieces):
        for copy in part(i):
            copy.wait()
        begin = 0
        if i == 0:
            held = step(0, held, True)
            begin = 1
        held = lax.fori_loop(
            begin,
            height // STEP,
            lambda j, held, i=i: step(pl.multiple_of(i * height + j * STEP, STEP), held, False),
            held,
        )
    for m in range(modes + 4):
        carry_ref[m * blocks : (m + 1) * blocks, :] = held[m]
    for copy in late:
        copy.wait()
    spread(q_near, k_wide, rows - STEP, 0)
    for i in range(2):
        start = (modes + 4 + i) * blocks
        carry_ref[start : start + blocks, :] = k_wide[place_of(STEP - 2 + i, blocks), :]


def far(x):
    return pltpu.with_memory_space_constraint(x, pltpu.HBM)


def run_front(q, k, v, short_taps, rate, residue):
    rows, width = k.shape
    modes = rate.shape[0]
    blocks = width // LANES
    pieces = 4

    def wide(n):
        return jax.ShapeDtypeStruct((n * blocks, LANES), jnp.float32)

    def like(x):
        return jax.ShapeDtypeStruct(x.shape, x.dtype)

    out_shape = [wide(modes + 6), wide(rows), wide(modes), wide(9), wide(4), like(rate), like(residue), like(q)]
    return pl.pallas_call(
        front_kernel,
        out_shape=out_shape,
        in_specs=[AWAY] * 6,
        out_specs=[WHOLE] * len(out_shape),
        scratch_shapes=[
            pltpu.VMEM((rows, width), jnp.bfloat16),
            pltpu.VMEM((rows, width), jnp.bfloat16),
            pltpu.VMEM(short_taps.shape, jnp.float32),
            pltpu.VMEM((STEP * blocks, LANES), jnp.float32),
            pltpu.VMEM((STEP * blocks, LANES), jnp.float32),
            pltpu.SemaphoreType.DMA((2 * pieces + 2,)),
            pltpu.SemaphoreType.DMA((2,)),
        ],
        compiler_params=params(),
        cost_estimate=cost(10**8),
        name="front",
    )(*[far(x) for x in (k, v, q, short_taps, rate, residue)])


def local_kernel(q_near, signal_ref, decay_ref, taps_ref, gain_near, *refs):
    copies = []
    if len(refs) > 4:
        weight_hbm, direction_hbm, weight_ref, direction_ref, sems = refs[:2] + refs[5:7] + refs[-1:]
        refs = refs[2:5] + refs[7:-1]
        count = sems.shape[0] - 1
        copies.append(pltpu.make_async_copy(direction_hbm, direction_ref, sems.at[count]))
        copies[-1].start()
        depth = weight_ref.shape[0] // count
        for i in range(count):
            here = pl.ds(i * depth, depth)
            copies.append(pltpu.make_async_copy(weight_hbm.at[here], weight_ref.at[here], sems.at[i]))
            copies[-1].start()
    out_ref, query_ref, gain_ref, q_wide = refs
    rows, width = q_near.shape
    blocks = width // LANES
    modes = gain_near.shape[0]
    spread_rows(gain_near[...], gain_ref)
    zero = jnp.zeros((blocks, LANES), jnp.float32)
    taps = [tile(taps_ref, j, blocks) for j in range(3)]
    decay = [tile(decay_ref, m, blocks) for m in range(modes)]
    gain = [tile(gain_ref, m, blocks) for m in range(modes)]

    def step(j, held):
        row = pl.multiple_of(j * STEP, STEP)
        spread(q_near, q_wide, row, 0)
        state, (q2, q1) = list(held[:modes]), held[modes:]
        for index in range(STEP):
            q0 = q_wide[place_of(index, blocks), :]
            here = moving_tile(row + index, blocks)
            signal = signal_ref[here, :]
            query_ref[here, :] = taps[0] * q0 + taps[1] * q1 + taps[2] * q2
            state = [decay[m] * state[m] + signal for m in range(modes)]
            sums = [gain[m] * state[m] for m in range(modes)]
            while len(sums) > 1:
                sums = [sums[i] + sums[i + 1] for i in range(0, len(sums), 2)]
            out_ref[here, :] = sums[0]
            q2, q1 = q1, q0
        return tuple(state) + (q2, q1)

    lax.fori_loop(0, rows // STEP, step, (zero,) * (modes + 2))
    for copy in copies:
        copy.wait()


def run_local(q, signal, decay, taps, gain, *weight):
    rows, width = q.shape
    blocks = width // LANES
    wide = jax.ShapeDtypeStruct((rows * blocks, LANES), jnp.float32)
    out_shape = [wide, wide, jax.ShapeDtypeStruct(decay.shape, jnp.float32)]
    scratch_shapes = [pltpu.VMEM((STEP * blocks, LANES), jnp.float32)]
    if weight:
        out_shape += [jax.ShapeDtypeStruct(x.shape, x.dtype) for x in weight]
        scratch_shapes.append(pltpu.SemaphoreType.DMA((5,)))
        weight = tuple(far(x) for x in weight)
    return pl.pallas_call(
        local_kernel,
        out_shape=out_shape,
        in_specs=[WHOLE] * 5 + [AWAY] * len(weight),
        out_specs=[WHOLE] * len(out_shape),
        scratch_shapes=scratch_shapes,
        compiler_params=params(),
        cost_estimate=cost(10**6),
        name="local_filter",
    )(q, signal, decay, taps, gain, *weight)


def correct_kernel(blocks, carry_ref, decay_ref, gain_ref, taps_ref, edge_ref, local_ref, query_ref, *refs):
    wide, outs = refs[-1], refs[:-1]
    rows = local_ref.shape[0] // blocks
    if len(outs) > 1:
        outs = outs[1:]
        outs[1][rows // 2 :, :] = refs[0][...]
    modes = decay_ref.shape[0] // blocks
    k2, k1, v2, v1, q2, q1 = [tile(carry_ref, modes + i, blocks) for i in range(6)]
    tap = [tile(taps_ref, i, blocks) for i in range(9)]
    key0, key1, value0, value1 = [tile(edge_ref, i, blocks) for i in range(4)]
    extra = [
        (key0 + tap[4] * k1 + tap[5] * k2) * (value0 + tap[7] * v1 + tap[8] * v2) - key0 * value0,
        (key1 + tap[5] * k1) * (value1 + tap[8] * v1) - key1 * value1,
    ]
    query_extra = [tap[1] * q1 + tap[2] * q2, tap[2] * q1]
    state = [tile(gain_ref, m, blocks) * tile(carry_ref, m, blocks) for m in range(modes)]
    decay = [tile(decay_ref, m, blocks) for m in range(modes)]

    def step(row, state, first, piece_ref, start):
        state = list(state)
        for index in range(STEP):
            here = moving_tile(row + index, blocks)
            state = [decay[m] * state[m] for m in range(modes)]
            query = query_ref[here, :]
            if first and index < 2:
                state = [state[m] + tile(gain_ref, m, blocks) * extra[index] for m in range(modes)]
                query = query + query_extra[index]
            sums = state
            while len(sums) > 1:
                sums = [sums[i] + sums[i + 1] for i in range(0, len(sums), 2)]
            wide[place_of(index, blocks), :] = query * (local_ref[here, :] + sums[0])
        for block in range(blocks):
            halves = [
                wide[(half * blocks + block) * GROUP : (half * blocks + block + 1) * GROUP, :]
                for half in range(STEP // GROUP)
            ]
            rounded = jnp.concatenate(halves, axis=0).astype(jnp.bfloat16)
            columns = slice(block * LANES, (block + 1) * LANES)
            outs[-1][pl.ds(row, STEP), columns] = rounded
            if piece_ref is not None:
                piece_ref[pl.ds(pl.multiple_of(row - start, STEP), STEP), columns] = rounded
        return tuple(state)

    state = tuple(state)
    start = 0
    for piece_ref in outs[:-1] or [None]:
        end = start + (rows if piece_ref is None else rows // 2)
        begin = start // STEP
        if start == 0:
            state = step(0, state, True, piece_ref, 0)
            begin = 1
        state = lax.fori_loop(
            begin,
            end // STEP,
            lambda j, state, start=start, piece_ref=piece_ref: step(
                pl.multiple_of(j * STEP, STEP), state, False, piece_ref, start
            ),
            state,
        )
        start = end


def run_correct(carry, decay, gain, taps, edge, local, query, blocks, *parts):
    rows = local.shape[0] // blocks
    width = blocks * LANES
    heights = ([rows // 2, rows // 2 + STEP] if parts else []) + [rows]
    return pl.pallas_call(
        functools.partial(correct_kernel, blocks),
        out_shape=[jax.ShapeDtypeStruct((height, width), jnp.bfloat16) for height in heights],
        in_specs=[WHOLE] * (7 + len(parts)),
        out_specs=[WHOLE] * len(heights),
        scratch_shapes=[pltpu.VMEM((STEP * blocks, LANES), jnp.float32)],
        compiler_params=params(),
        cost_estimate=cost(10**8),
        name="carried_filter",
    )(carry, decay, gain, taps, edge, local, query, *parts)


def gains_of(rate, residue):
    return residue * jnp.sqrt(-jnp.expm1(-2.0 * rate)) * rate.shape[0] ** (-0.5)


def split_three(x):
    high = x.astype(jnp.bfloat16)
    rest = x - high.astype(jnp.float32)
    middle = rest.astype(jnp.bfloat16)
    low = (rest - middle.astype(jnp.float32)).astype(jnp.bfloat16)
    return high, middle, low


def in_parts(row):
    return jnp.concatenate(list(split_three(row)) + [jnp.zeros((13, row.shape[1]), jnp.bfloat16)], axis=0)


def dot_parts(parts, matrix):
    out = lax.dot_general(parts, matrix, (((1,), (1,)), ((), ())), preferred_element_type=jnp.float32)
    return out[0:1] + out[1:2] + out[2:3]


def idle_kernel(*refs):
    pass


def after(array, *others):
    return pl.pallas_call(
        idle_kernel,
        out_shape=jax.ShapeDtypeStruct(array.shape, array.dtype),
        in_specs=[pl.BlockSpec(memory_space=pl.ANY)] * (1 + len(others)),
        out_specs=pl.BlockSpec(memory_space=pl.ANY),
        input_output_aliases={0: 0},
        compiler_params=params(),
        cost_estimate=cost(1),
        name="after",
    )(array, *others)


def rows_of(count, like, dtype=jnp.bfloat16):
    return jax.ShapeDtypeStruct((count, like.shape[1]), dtype)


def call(kernel, name, out_shape, *operands, tokens=()):
    def with_tokens(*refs):
        kernel(*refs[: len(operands)], *refs[len(operands) + len(tokens) :])

    return pl.pallas_call(
        with_tokens,
        out_shape=out_shape,
        in_specs=[WHOLE] * len(operands) + [pl.BlockSpec(memory_space=pl.ANY)] * len(tokens),
        out_specs=[WHOLE] * len(out_shape),
        compiler_params=params(),
        cost_estimate=cost(10**6),
        name=name,
    )(*operands, *tokens)


def inner_kernel(direction_ref, weight_ref, parts_ref, norm_ref, here_ref):
    everything = direction_ref[...]
    norm_ref[...] = jnp.broadcast_to(
        jnp.sum(everything * everything, axis=1, keepdims=True) + EPSILON, norm_ref.shape
    )
    size, width = weight_ref.shape[1], here_ref.shape[1]
    here_ref[...] = direction_ref[:, pl.ds(pl.multiple_of(lax.axis_index("tp") * width, LANES), width)]
    here = direction_ref[:, pl.ds(pl.multiple_of(lax.axis_index("ctx") * size, LANES), size)]
    parts_ref[...] = in_parts(dot_parts(in_parts(here), weight_ref[...]))


def run_inner(direction, weight):
    out_shape = [
        jax.ShapeDtypeStruct((STEP, weight.shape[0]), jnp.bfloat16),
        jax.ShapeDtypeStruct((1, LANES), jnp.float32),
        jax.ShapeDtypeStruct((1, weight.shape[1] // 2), jnp.float32),
    ]
    return call(inner_kernel, "inner", out_shape, direction, weight)


def project_kernel(begin, weight_ref, piece_ref, send_ref, keep_ref):
    rows, width = keep_ref.shape
    side = lax.axis_index("tp") % 2
    for which, ref in ((1 - side, send_ref), (side, keep_ref)):
        for part in range(0, width, 256):
            columns = pl.ds(pl.multiple_of(which * width + part, 256), 256)
            out = jnp.dot(piece_ref[begin : begin + rows, :], weight_ref[:, columns], preferred_element_type=jnp.float32)
            ref[:, part : part + 256] = out.astype(ref.dtype)


def run_project(weight, piece, begin, rows, *tokens):
    keep = jax.ShapeDtypeStruct((rows, weight.shape[1] // 2), jnp.float32)
    kernel = functools.partial(project_kernel, begin)
    return call(kernel, "project", [rows_of(rows, keep), keep], weight, piece, tokens=tokens)


def level_kernel(parts_ref, far_ref, whole_ref, out_ref):
    far_parts = far_ref[far_ref.shape[0] - STEP :, :]
    out_ref[...] = dot_parts(parts_ref[...], whole_ref[...]) + dot_parts(far_parts, whole_ref[...])


def merge_kernel(keep_ref, core_ref, out_ref):
    for row in range(0, out_ref.shape[0], STEP):
        here = slice(row, row + STEP)
        total = keep_ref[here, :].astype(jnp.float32) + core_ref[here, :].astype(jnp.float32)
        out_ref[here, :] = total.astype(jnp.bfloat16)


def run_merge(keep, core, *tokens):
    (out,) = call(merge_kernel, "merge", [rows_of(keep.shape[0], keep)], keep, core, tokens=tokens)
    return out


def is_keeper():
    return lax.axis_index("tp") // 2 == lax.axis_index("ctx")


def choose_kernel(straight_ref, own_ref, out_ref):
    keeper = is_keeper()

    @pl.when(keeper)
    def _():
        out_ref[: straight_ref.shape[0], :] = straight_ref[...]

    @pl.when(jnp.logical_not(keeper))
    def _():
        out_ref[...] = own_ref[...]


def run_choose(straight, own, *tokens):
    (out,) = call(choose_kernel, "choose", [rows_of(own.shape[0], own)], straight, own, tokens=tokens)
    return out


def finish_kernel(start, last, *refs):
    level_ref, other_ref, norm_ref, direction_ref = refs[:4]
    own, (straight_ref, turned_ref, merged_ref) = (refs[4:7], refs[7:10]), refs[10:13]
    out_near, sems = refs[-2:]
    rows, width = out_near.shape
    level = (level_ref[...] + other_ref[...]) / norm_ref[0:1, 0:1]
    if last:
        refs[-3][...] = level
    out_hbm = refs[-4 if last else -3]
    direction = direction_ref[...]
    keeper = is_keeper()
    column = jnp.transpose(jnp.broadcast_to(level, (LANES, level.shape[1])))
    copies = []
    half = rows // 2 // STEP * STEP

    def added(row, *pieces):
        total = pieces[0][row : row + STEP, :].astype(jnp.float32)
        for piece in pieces[1:]:
            total = total + piece[row : row + STEP, :].astype(jnp.float32)
        return total

    for i, (begin, end) in enumerate(((0, half), (half, rows))):

        @pl.when(keeper)
        def _():
            for row in range(start + begin, start + end, STEP):
                cut = own[0][0].shape[0]
                total = added(row, *own[0]) if row < cut else added(row - cut, *own[1])
                total = total - column[row : row + STEP, 0:1] * direction
                out_near[row - start : row - start + STEP, :] = total.astype(jnp.bfloat16)

        @pl.when(jnp.logical_not(keeper))
        def _():
            for row in range(start + begin, start + end, STEP):
                cut = straight_ref.shape[0]
                total = added(row, straight_ref, turned_ref) if row < cut else added(row - cut, merged_ref)
                total = total - column[row : row + STEP, 0:1] * direction
                out_near[row - start : row - start + STEP, :] = total.astype(jnp.bfloat16)

        here, there = pl.ds(begin, end - begin), pl.ds(start + begin, end - begin)
        copies.append(pltpu.make_async_copy(out_near.at[here], out_hbm.at[there], sems.at[i]))
        copies[-1].start()
    for copy in copies:
        copy.wait()


def run_finish(start, count, operands, before=()):
    level, keep = operands[0], operands[4]
    rows, width = level.shape[1], keep.shape[1]
    levels = [jax.ShapeDtypeStruct(level.shape, jnp.float32)] * len(before)
    return pl.pallas_call(
        functools.partial(finish_kernel, start, bool(before)),
        out_shape=[rows_of(rows, keep)] + levels,
        in_specs=[WHOLE] * len(operands) + [AWAY] * len(before),
        out_specs=[AWAY] + [WHOLE] * len(levels),
        scratch_shapes=[pltpu.VMEM((count, width), jnp.bfloat16), pltpu.SemaphoreType.DMA((2,))],
        input_output_aliases={len(operands): 0} if before else {},
        compiler_params=params(),
        cost_estimate=cost(10**6),
        name="finish",
    )(*operands, *before)


def plane_plan(q, k, v, short_taps, decay_rate, residue, out_weight, direction):
    rows, width = q.shape
    half = rows // 2
    early = rows * 3 // 8 // STEP * STEP
    blocks = width // LANES
    axes = ("ctx", "tp")
    forward = [(p, 4 + p) for p in range(4)]
    across = [(4 * c + p, 4 * (1 - c) + p) for c in range(2) for p in range(4)]
    sibling = [(4 * c + p, 4 * c + (p ^ 1)) for c in range(2) for p in range(4)]
    pair = [(4 * c + p, 4 * c + (p ^ 2)) for c in range(2) for p in range(4)]
    inward = [(4 * c + 2 * (1 - c) + a, 4 * c + 2 * c + a) for c in range(2) for a in range(2)]
    onward = [(4 * c + 2 * c + a, 4 * (1 - c) + 2 * c + a) for c in range(2) for a in range(2)]

    ended, signal, decay, taps, edge, rate, residue, q = run_front(q, k, v, short_taps, decay_rate.T, residue.T)
    carry = lax.ppermute(ended, axes, forward)
    local, query, gain, weight, direction = run_local(
        q, signal, decay, taps, gains_of(rate, residue), out_weight, direction.reshape(1, -1)
    )
    parts, norm, direction = run_inner(direction, weight)
    first, second, whole = run_correct(carry, decay, gain, taps, edge, local, query, blocks, parts)
    far_first = lax.ppermute(first, axes, across)
    far_second = lax.ppermute(second, axes, across)

    send, keep0 = run_project(weight, whole, 0, early)
    core0 = lax.ppermute(send, axes, sibling)
    hop0 = lax.ppermute(run_merge(keep0, core0), axes, inward)

    send, far_keep = run_project(weight, far_first, 0, half, hop0)
    sums0 = run_merge(far_keep, lax.ppermute(send, axes, sibling))
    straight = lax.ppermute(sums0, axes, across)

    whole = after(whole, sums0)
    own_send, keep1 = run_project(weight, whole, early, rows - early)
    far_second = after(far_second, own_send)
    send, far_keep = run_project(weight, far_second, 0, half)
    sums1 = run_merge(far_keep, lax.ppermute(send, axes, sibling))
    moved = lax.ppermute(sums1, axes, inward)
    core1 = lax.ppermute(own_send, axes, sibling)
    own1 = run_merge(keep1, core1)

    (level,) = call(
        level_kernel,
        "level",
        [jax.ShapeDtypeStruct((1, rows), jnp.float32)],
        parts,
        far_second,
        whole,
        tokens=(sums1,),
    )
    level = level + lax.ppermute(level, axes, sibling)
    other = lax.ppermute(level, axes, pair)

    merged = lax.ppermute(run_merge(sums1, moved), axes, onward)
    turned = lax.ppermute(run_choose(straight, own1, other), axes, pair)
    shared = (level, other, norm, direction, keep0, core0, hop0, keep1, core1, turned, straight, turned)
    before = run_finish(0, half, (*shared, straight))
    ablated, level = run_finish(half, half, (*shared, merged), before)
    return ablated, level.reshape(rows)


def gather_plan(q, k, v, short_taps, decay_rate, residue, out_weight, direction):
    rows, width = q.shape
    blocks = width // LANES
    modes = decay_rate.shape[1]
    tp = lax.axis_index("tp")
    ctx_size = lax.axis_size("ctx")
    next_one = [(i, i + 1) for i in range(ctx_size - 1)]
    ended, signal, decay, taps, edge, rate, residue, q = run_front(q, k, v, short_taps, decay_rate.T, residue.T)
    halo = lax.ppermute(ended[modes * blocks :], "ctx", next_one)
    local, query, gain = run_local(q, signal, decay, taps, gains_of(rate, residue))
    k2, k1, v2, v1 = [halo[i * blocks : (i + 1) * blocks] for i in range(4)]
    tap = taps.reshape(9, blocks, LANES)
    key0, key1, value0, value1 = edge.reshape(4, blocks, LANES)
    extra0 = (key0 + tap[4] * k1 + tap[5] * k2) * (value0 + tap[7] * v1 + tap[8] * v2) - key0 * value0
    extra1 = (key1 + tap[5] * k1) * (value1 + tap[8] * v1) - key1 * value1
    wide_rate = decay_rate.T.reshape(modes, blocks, LANES)
    state = (
        ended[: modes * blocks].reshape(modes, blocks, LANES)
        + jnp.exp(-wide_rate * (rows - 1)) * extra0
        + jnp.exp(-wide_rate * (rows - 2)) * extra1
    )
    reach = 1
    while reach < ctx_size:
        earlier = lax.ppermute(state, "ctx", [(i, i + reach) for i in range(ctx_size - reach)])
        state = state + jnp.exp(-wide_rate * (rows * reach)) * earlier
        reach *= 2
    start = lax.ppermute(state, "ctx", next_one).reshape(modes * blocks, LANES)
    carry = jnp.concatenate([start, halo], axis=0)
    (gated,) = run_correct(carry, decay, gain, taps, edge, local, query, blocks)
    partial_terms = lax.dot_general(
        gated,
        lax.all_gather(out_weight, "ctx", axis=1, tiled=True),
        (((1,), (0,)), ((), ())),
        preferred_element_type=jnp.float32,
    )
    summed = lax.psum_scatter(
        partial_terms.astype(jnp.bfloat16), "tp", scatter_dimension=1, tiled=True
    ).astype(jnp.float32)
    width_here = summed.shape[1]
    direction_here = lax.dynamic_slice_in_dim(direction, tp * width_here, width_here, 0)
    norm_total = jnp.sum(direction * direction) + EPSILON
    local_inner = jnp.dot(summed, direction_here, precision=HIGHEST)
    feature_level = lax.psum(local_inner, "tp") / norm_total
    ablated = (summed - feature_level[:, None] * direction_here[None, :]).astype(jnp.bfloat16)
    return ablated, feature_level


def solution(mesh):
    placed = (
        P(("dp", "ctx"), "tp"),
        P(("dp", "ctx"), "tp"),
        P(("dp", "ctx"), "tp"),
        P(None, None, "tp"),
        P("tp", None),
        P("tp", None),
        P("tp", "ctx"),
        P(),
    )
    plane = mesh.shape["ctx"] == 2 and mesh.shape["tp"] == 4
    return jax.shard_map(
        plane_plan if plane else gather_plan,
        mesh=mesh,
        in_specs=placed,
        out_specs=(P(("dp", "ctx"), "tp"), P(("dp", "ctx"))),
        check_vma=False,
    )
```

```python
import functools

import jax
import jax.numpy as jnp
from jax import lax
from jax.experimental import pallas as pl
from jax.experimental.pallas import tpu as pltpu
from jax.sharding import PartitionSpec as P

EPSILON = 1e-06
HIGHEST = lax.Precision.HIGHEST
LANES = 128
GROUP = 8
STEP = 16
WHOLE = pl.BlockSpec(memory_space=pltpu.VMEM)
AWAY = pl.BlockSpec(memory_space=pltpu.HBM)


def params(mebibytes=20):
    return pltpu.CompilerParams(vmem_limit_bytes=mebibytes * 1024 * 1024)


def cost(flops):
    return pl.CostEstimate(flops=flops, bytes_accessed=1024, transcendentals=0)


def spread(source, scratch, row, to):
    blocks = source.shape[1] // LANES
    for block in range(blocks):
        piece = source[pl.ds(row, STEP), block * LANES : (block + 1) * LANES].astype(jnp.float32)
        for half in range(STEP // GROUP):
            start = (half * blocks + block) * GROUP
            scratch[pl.ds(to + start, GROUP), :] = piece[half * GROUP : (half + 1) * GROUP]


def spread_rows(source, target):
    count, width = source.shape
    blocks = width // LANES
    for block in range(blocks):
        target[pl.ds(block, count, stride=blocks), :] = source[:, block * LANES : (block + 1) * LANES]


def place_of(index, blocks):
    return pl.ds((index // GROUP) * (blocks * GROUP) + index % GROUP, blocks, stride=GROUP)


def tile(ref, index, blocks):
    return ref[index * blocks : (index + 1) * blocks, :]


def moving_tile(index, blocks):
    return pl.ds(pl.multiple_of(index * blocks, blocks), blocks)


def front_kernel(*refs):
    k_hbm, v_hbm, q_hbm, taps_hbm, rate_hbm, residue_hbm = refs[:6]
    carry_ref, signal_ref, decay_ref, taps_ref, edge_ref, rate_ref, residue_ref, q_near = refs[6:14]
    k_near, v_near, taps_near, k_wide, v_wide, sems, late_sems = refs[-7:]
    rows, width = k_near.shape
    blocks = width // LANES
    modes = rate_ref.shape[0]
    pieces = sems.shape[0] // 2 - 1
    height = rows // pieces

    def part(i):
        here = pl.ds(i * height, height)
        return (
            pltpu.make_async_copy(k_hbm.at[here], k_near.at[here], sems.at[2 * i]),
            pltpu.make_async_copy(v_hbm.at[here], v_near.at[here], sems.at[2 * i + 1]),
        )

    rate_copy = pltpu.make_async_copy(rate_hbm, rate_ref, sems.at[2 * pieces])
    taps_copy = pltpu.make_async_copy(taps_hbm, taps_near, sems.at[2 * pieces + 1])
    late = [(residue_hbm, residue_ref), (q_hbm, q_near)]
    late = [pltpu.make_async_copy(source, target, late_sems.at[i]) for i, (source, target) in enumerate(late)]
    rate_copy.start()
    taps_copy.start()
    for i in range(pieces):
        for copy in part(i):
            copy.start()
    for copy in late:
        copy.start()
    rate_copy.wait()
    taps_copy.wait()
    spread_rows(jnp.exp(-rate_ref[...]), decay_ref)
    for i in range(3):
        for block in range(blocks):
            taps_ref[pl.ds(3 * i * blocks + block, 3, stride=blocks), :] = taps_near[
                i, :, block * LANES : (block + 1) * LANES
            ]
    zero = jnp.zeros((blocks, LANES), jnp.float32)
    key_taps = [tile(taps_ref, 3 + j, blocks) for j in range(3)]
    value_taps = [tile(taps_ref, 6 + j, blocks) for j in range(3)]
    decay = [tile(decay_ref, m, blocks) for m in range(modes)]

    def step(row, held, first):
        spread(k_near, k_wide, row, 0)
        spread(v_near, v_wide, row, 0)
        state, (k2, k1, v2, v1) = list(held[:modes]), held[modes:]
        for index in range(STEP):
            k0 = k_wide[place_of(index, blocks), :]
            v0 = v_wide[place_of(index, blocks), :]
            key = key_taps[0] * k0 + key_taps[1] * k1 + key_taps[2] * k2
            value = value_taps[0] * v0 + value_taps[1] * v1 + value_taps[2] * v2
            if first and index < 2:
                edge_ref[index * blocks : (index + 1) * blocks, :] = key
                edge_ref[(2 + index) * blocks : (3 + index) * blocks, :] = value
            signal = key * value
            signal_ref[moving_tile(row + index, blocks), :] = signal
            state = [decay[m] * state[m] + signal for m in range(modes)]
            k2, k1, v2, v1 = k1, k0, v1, v0
        return tuple(state) + (k2, k1, v2, v1)

    held = (zero,) * (modes + 4)
    for i in range(pieces):
        for copy in part(i):
            copy.wait()
        begin = 0
        if i == 0:
            held = step(0, held, True)
            begin = 1
        held = lax.fori_loop(
            begin,
            height // STEP,
            lambda j, held, i=i: step(pl.multiple_of(i * height + j * STEP, STEP), held, False),
            held,
        )
    for m in range(modes + 4):
        carry_ref[m * blocks : (m + 1) * blocks, :] = held[m]
    for copy in late:
        copy.wait()
    spread(q_near, k_wide, rows - STEP, 0)
    for i in range(2):
        start = (modes + 4 + i) * blocks
        carry_ref[start : start + blocks, :] = k_wide[place_of(STEP - 2 + i, blocks), :]


def far(x):
    return pltpu.with_memory_space_constraint(x, pltpu.HBM)


def run_front(q, k, v, short_taps, rate, residue):
    rows, width = k.shape
    modes = rate.shape[0]
    blocks = width // LANES
    pieces = 4

    def wide(n):
        return jax.ShapeDtypeStruct((n * blocks, LANES), jnp.float32)

    def like(x):
        return jax.ShapeDtypeStruct(x.shape, x.dtype)

    out_shape = [wide(modes + 6), wide(rows), wide(modes), wide(9), wide(4), like(rate), like(residue), like(q)]
    return pl.pallas_call(
        front_kernel,
        out_shape=out_shape,
        in_specs=[AWAY] * 6,
        out_specs=[WHOLE] * len(out_shape),
        scratch_shapes=[
            pltpu.VMEM((rows, width), jnp.bfloat16),
            pltpu.VMEM((rows, width), jnp.bfloat16),
            pltpu.VMEM(short_taps.shape, jnp.float32),
            pltpu.VMEM((STEP * blocks, LANES), jnp.float32),
            pltpu.VMEM((STEP * blocks, LANES), jnp.float32),
            pltpu.SemaphoreType.DMA((2 * pieces + 2,)),
            pltpu.SemaphoreType.DMA((2,)),
        ],
        compiler_params=params(),
        cost_estimate=cost(10**8),
        name="front",
    )(*[far(x) for x in (k, v, q, short_taps, rate, residue)])


def local_kernel(q_near, signal_ref, decay_ref, taps_ref, gain_near, *refs):
    copies = []
    if len(refs) > 4:
        weight_hbm, direction_hbm, weight_ref, direction_ref, sems = refs[:2] + refs[5:7] + refs[-1:]
        refs = refs[2:5] + refs[7:-1]
        count = sems.shape[0] - 1
        copies.append(pltpu.make_async_copy(direction_hbm, direction_ref, sems.at[count]))
        copies[-1].start()
        depth = weight_ref.shape[0] // count
        for i in range(count):
            here = pl.ds(i * depth, depth)
            copies.append(pltpu.make_async_copy(weight_hbm.at[here], weight_ref.at[here], sems.at[i]))
            copies[-1].start()
    out_ref, query_ref, gain_ref, q_wide = refs
    rows, width = q_near.shape
    blocks = width // LANES
    modes = gain_near.shape[0]
    spread_rows(gain_near[...], gain_ref)
    zero = jnp.zeros((blocks, LANES), jnp.float32)
    taps = [tile(taps_ref, j, blocks) for j in range(3)]
    decay = [tile(decay_ref, m, blocks) for m in range(modes)]
    gain = [tile(gain_ref, m, blocks) for m in range(modes)]

    def step(j, held):
        row = pl.multiple_of(j * STEP, STEP)
        spread(q_near, q_wide, row, 0)
        state, (q2, q1) = list(held[:modes]), held[modes:]
        for index in range(STEP):
            q0 = q_wide[place_of(index, blocks), :]
            here = moving_tile(row + index, blocks)
            signal = signal_ref[here, :]
            query_ref[here, :] = taps[0] * q0 + taps[1] * q1 + taps[2] * q2
            state = [decay[m] * state[m] + signal for m in range(modes)]
            sums = [gain[m] * state[m] for m in range(modes)]
            while len(sums) > 1:
                sums = [sums[i] + sums[i + 1] for i in range(0, len(sums), 2)]
            out_ref[here, :] = sums[0]
            q2, q1 = q1, q0
        return tuple(state) + (q2, q1)

    lax.fori_loop(0, rows // STEP, step, (zero,) * (modes + 2))
    for copy in copies:
        copy.wait()


def run_local(q, signal, decay, taps, gain, *weight):
    rows, width = q.shape
    blocks = width // LANES
    wide = jax.ShapeDtypeStruct((rows * blocks, LANES), jnp.float32)
    out_shape = [wide, wide, jax.ShapeDtypeStruct(decay.shape, jnp.float32)]
    scratch_shapes = [pltpu.VMEM((STEP * blocks, LANES), jnp.float32)]
    if weight:
        out_shape += [jax.ShapeDtypeStruct(x.shape, x.dtype) for x in weight]
        scratch_shapes.append(pltpu.SemaphoreType.DMA((5,)))
        weight = tuple(far(x) for x in weight)
    return pl.pallas_call(
        local_kernel,
        out_shape=out_shape,
        in_specs=[WHOLE] * 5 + [AWAY] * len(weight),
        out_specs=[WHOLE] * len(out_shape),
        scratch_shapes=scratch_shapes,
        compiler_params=params(),
        cost_estimate=cost(10**6),
        name="local_filter",
    )(q, signal, decay, taps, gain, *weight)


def correct_kernel(blocks, carry_ref, decay_ref, gain_ref, taps_ref, edge_ref, local_ref, query_ref, *refs):
    wide, outs = refs[-1], refs[:-1]
    rows = local_ref.shape[0] // blocks
    if len(outs) > 1:
        outs = outs[1:]
        outs[1][rows // 2 :, :] = refs[0][...]
    modes = decay_ref.shape[0] // blocks
    k2, k1, v2, v1, q2, q1 = [tile(carry_ref, modes + i, blocks) for i in range(6)]
    tap = [tile(taps_ref, i, blocks) for i in range(9)]
    key0, key1, value0, value1 = [tile(edge_ref, i, blocks) for i in range(4)]
    extra = [
        (key0 + tap[4] * k1 + tap[5] * k2) * (value0 + tap[7] * v1 + tap[8] * v2) - key0 * value0,
        (key1 + tap[5] * k1) * (value1 + tap[8] * v1) - key1 * value1,
    ]
    query_extra = [tap[1] * q1 + tap[2] * q2, tap[2] * q1]
    state = [tile(gain_ref, m, blocks) * tile(carry_ref, m, blocks) for m in range(modes)]
    decay = [tile(decay_ref, m, blocks) for m in range(modes)]

    def step(row, state, first, piece_ref, start):
        state = list(state)
        for index in range(STEP):
            here = moving_tile(row + index, blocks)
            state = [decay[m] * state[m] for m in range(modes)]
            query = query_ref[here, :]
            if first and index < 2:
                state = [state[m] + tile(gain_ref, m, blocks) * extra[index] for m in range(modes)]
                query = query + query_extra[index]
            sums = state
            while len(sums) > 1:
                sums = [sums[i] + sums[i + 1] for i in range(0, len(sums), 2)]
            wide[place_of(index, blocks), :] = query * (local_ref[here, :] + sums[0])
        for block in range(blocks):
            halves = [
                wide[(half * blocks + block) * GROUP : (half * blocks + block + 1) * GROUP, :]
                for half in range(STEP // GROUP)
            ]
            rounded = jnp.concatenate(halves, axis=0).astype(jnp.bfloat16)
            columns = slice(block * LANES, (block + 1) * LANES)
            outs[-1][pl.ds(row, STEP), columns] = rounded
            if piece_ref is not None:
                piece_ref[pl.ds(pl.multiple_of(row - start, STEP), STEP), columns] = rounded
        return tuple(state)

    state = tuple(state)
    start = 0
    for piece_ref in outs[:-1] or [None]:
        end = start + (rows if piece_ref is None else rows // 2)
        begin = start // STEP
        if start == 0:
            state = step(0, state, True, piece_ref, 0)
            begin = 1
        state = lax.fori_loop(
            begin,
            end // STEP,
            lambda j, state, start=start, piece_ref=piece_ref: step(
                pl.multiple_of(j * STEP, STEP), state, False, piece_ref, start
            ),
            state,
        )
        start = end


def run_correct(carry, decay, gain, taps, edge, local, query, blocks, *parts):
    rows = local.shape[0] // blocks
    width = blocks * LANES
    heights = ([rows // 2, rows // 2 + STEP] if parts else []) + [rows]
    return pl.pallas_call(
        functools.partial(correct_kernel, blocks),
        out_shape=[jax.ShapeDtypeStruct((height, width), jnp.bfloat16) for height in heights],
        in_specs=[WHOLE] * (7 + len(parts)),
        out_specs=[WHOLE] * len(heights),
        scratch_shapes=[pltpu.VMEM((STEP * blocks, LANES), jnp.float32)],
        compiler_params=params(),
        cost_estimate=cost(10**8),
        name="carried_filter",
    )(carry, decay, gain, taps, edge, local, query, *parts)


def gains_of(rate, residue):
    return residue * jnp.sqrt(-jnp.expm1(-2.0 * rate)) * rate.shape[0] ** (-0.5)


def split_three(x):
    high = x.astype(jnp.bfloat16)
    rest = x - high.astype(jnp.float32)
    middle = rest.astype(jnp.bfloat16)
    low = (rest - middle.astype(jnp.float32)).astype(jnp.bfloat16)
    return high, middle, low


def in_parts(row):
    return jnp.concatenate(list(split_three(row)) + [jnp.zeros((13, row.shape[1]), jnp.bfloat16)], axis=0)


def dot_parts(parts, matrix):
    out = lax.dot_general(parts, matrix, (((1,), (1,)), ((), ())), preferred_element_type=jnp.float32)
    return out[0:1] + out[1:2] + out[2:3]


def idle_kernel(*refs):
    pass


def after(array, *others):
    return pl.pallas_call(
        idle_kernel,
        out_shape=jax.ShapeDtypeStruct(array.shape, array.dtype),
        in_specs=[pl.BlockSpec(memory_space=pl.ANY)] * (1 + len(others)),
        out_specs=pl.BlockSpec(memory_space=pl.ANY),
        input_output_aliases={0: 0},
        compiler_params=params(),
        cost_estimate=cost(1),
        name="after",
    )(array, *others)


def rows_of(count, like, dtype=jnp.bfloat16):
    return jax.ShapeDtypeStruct((count, like.shape[1]), dtype)


def call(kernel, name, out_shape, *operands, tokens=()):
    def with_tokens(*refs):
        kernel(*refs[: len(operands)], *refs[len(operands) + len(tokens) :])

    return pl.pallas_call(
        with_tokens,
        out_shape=out_shape,
        in_specs=[WHOLE] * len(operands) + [pl.BlockSpec(memory_space=pl.ANY)] * len(tokens),
        out_specs=[WHOLE] * len(out_shape),
        compiler_params=params(),
        cost_estimate=cost(10**6),
        name=name,
    )(*operands, *tokens)


def inner_kernel(direction_ref, weight_ref, parts_ref, norm_ref, here_ref):
    everything = direction_ref[...]
    norm_ref[...] = jnp.broadcast_to(
        jnp.sum(everything * everything, axis=1, keepdims=True) + EPSILON, norm_ref.shape
    )
    size, width = weight_ref.shape[1], here_ref.shape[1]
    here_ref[...] = direction_ref[:, pl.ds(pl.multiple_of(lax.axis_index("tp") * width, LANES), width)]
    here = direction_ref[:, pl.ds(pl.multiple_of(lax.axis_index("ctx") * size, LANES), size)]
    parts_ref[...] = in_parts(dot_parts(in_parts(here), weight_ref[...]))


def run_inner(direction, weight):
    out_shape = [
        jax.ShapeDtypeStruct((STEP, weight.shape[0]), jnp.bfloat16),
        jax.ShapeDtypeStruct((1, LANES), jnp.float32),
        jax.ShapeDtypeStruct((1, weight.shape[1] // 2), jnp.float32),
    ]
    return call(inner_kernel, "inner", out_shape, direction, weight)


def project_kernel(begin, weight_ref, piece_ref, *outs):
    *sends, keep_ref = outs
    rows, width = keep_ref.shape
    cut = width // len(sends)
    side = lax.axis_index("tp") % 2
    for start in range(0, 2 * width, 256):
        away = start < width
        ref, to = (sends[start // cut], start % cut) if away else (keep_ref, start - width)
        which = 1 - side if away else side
        columns = pl.ds(pl.multiple_of(which * width + start % width, 256), 256)
        out = jnp.dot(piece_ref[begin : begin + rows, :], weight_ref[:, columns], preferred_element_type=jnp.float32)
        ref[:rows, to : to + 256] = out.astype(ref.dtype)


def run_project(weight, piece, begin, rows, count, *tokens):
    keep = jax.ShapeDtypeStruct((rows, weight.shape[1] // 2), jnp.float32)
    sends = [jax.ShapeDtypeStruct((rows, keep.shape[1] // count), jnp.bfloat16)] * count
    kernel = functools.partial(project_kernel, begin)
    *sends, keep = call(kernel, "project", [*sends, keep], weight, piece, tokens=tokens)
    return sends, keep


def put_behind(ref, rows, row):
    ref[rows:, :] = jnp.zeros((STEP, ref.shape[1]), jnp.bfloat16)
    ref[rows:, : row.shape[1]] = in_parts(row)


def take_behind(ref, rows, width):
    return jnp.sum(ref[rows:, :width].astype(jnp.float32), axis=0, keepdims=True)


def project_level_kernel(weight_ref, far_ref, whole_ref, parts_ref, send_ref, keep_ref, level_ref):
    project_kernel(0, weight_ref, far_ref, send_ref, keep_ref)
    level = dot_parts(parts_ref[...], whole_ref[...]) + dot_parts(far_ref[keep_ref.shape[0] :, :], whole_ref[...])
    level_ref[...] = level
    put_behind(send_ref, keep_ref.shape[0], level)


def merge_kernel(count, keep_ref, *refs):
    cores, outs = refs[:count], refs[count:]
    cut = outs[0].shape[1]
    for row in range(0, outs[0].shape[0], STEP):
        here = slice(row, row + STEP)
        for i, (core_ref, out_ref) in enumerate(zip(cores, outs)):
            total = keep_ref[here, i * cut : (i + 1) * cut].astype(jnp.float32) + core_ref[here, :].astype(jnp.float32)
            out_ref[here, :] = total.astype(jnp.bfloat16)


def run_merge(rows, keep, *cores):
    kernel = functools.partial(merge_kernel, len(cores))
    return call(kernel, "merge", [rows_of(rows, core) for core in cores], keep, *cores)


def merge_level_kernel(keep_ref, core_ref, level_ref, out_ref, total_ref):
    rows = keep_ref.shape[0]
    for row in range(0, rows, STEP):
        here = slice(row, row + STEP)
        out_ref[here, :] = (keep_ref[here, :] + core_ref[here, :].astype(jnp.float32)).astype(jnp.bfloat16)
    total = level_ref[...] + take_behind(core_ref, rows, level_ref.shape[1])
    total_ref[...] = total
    put_behind(out_ref, rows, total)


def is_keeper():
    return lax.axis_index("tp") // 2 == lax.axis_index("ctx")


def choose_kernel(straight_ref, level_ref, own_ref, out_ref):
    keeper = is_keeper()

    @pl.when(keeper)
    def _():
        rows = straight_ref.shape[0]
        out_ref[:rows, :] = straight_ref[...]
        put_behind(out_ref, rows, level_ref[...])

    @pl.when(jnp.logical_not(keeper))
    def _():
        out_ref[...] = own_ref[...]


def finish_kernel(start, *refs):
    level_ref, norm_ref, direction_ref, keep0_ref = refs[:4]
    own0, own1, (moved_ref, straight_ref) = refs[4:8], refs[8:11], refs[11:13]
    turned_ref = own1[-1]
    out_near, sems = refs[-2:]
    count, width = out_near.shape
    rows = level_ref.shape[1]
    keeper = is_keeper()
    if start:
        merged_ref, out_hbm = refs[13], refs[-3]
        level = level_ref[...]
    else:
        out_hbm, level_out_ref, level_near_ref = refs[-5:-2]
        behind = straight_ref.shape[0]
        other = jnp.where(keeper, take_behind(moved_ref, behind, rows), take_behind(turned_ref, behind, rows))
        level = (level_ref[...] + other) / norm_ref[0:1, 0:1]
        level_out_ref[...] = level
        level_near_ref[...] = level
    direction = direction_ref[...]
    column = jnp.transpose(jnp.broadcast_to(level, (LANES, rows)))

    def added(row, *pieces):
        total = pieces[0][row : row + STEP, :].astype(jnp.float32)
        for piece in pieces[1:]:
            total = total + piece[row : row + STEP, :].astype(jnp.float32)
        return total

    def put(row, total):
        total = total - column[row : row + STEP, 0:1] * direction
        out_near[row - start : row - start + STEP, :] = total.astype(jnp.bfloat16)

    copies = []
    half = count // 2
    for i in range(2):
        span = range(start + i * half, start + (i + 1) * half, STEP)

        @pl.when(keeper)
        def _():
            cut = keep0_ref.shape[0]
            for row in span:
                if row < cut:
                    here = slice(row, row + STEP)
                    core = jnp.concatenate([own0[0][here, :], own0[1][here, :]], axis=1).astype(jnp.float32)
                    hop = jnp.concatenate([own0[2][here, :], own0[3][here, :]], axis=1).astype(jnp.float32)
                    put(row, keep0_ref[here, :] + core + hop)
                else:
                    put(row, added(row - cut, *own1))

        @pl.when(jnp.logical_not(keeper))
        def _():
            cut = straight_ref.shape[0]
            for row in span:
                put(row, added(row, straight_ref, turned_ref) if row < cut else added(row - cut, merged_ref))

        here, there = pl.ds(i * half, half), pl.ds(start + i * half, half)
        copies.append(pltpu.make_async_copy(out_near.at[here], out_hbm.at[there], sems.at[i]))
        copies[-1].start()
    for copy in copies:
        copy.wait()


def run_finish(start, count, operands, before=()):
    level, keep = operands[0], operands[3]
    rows, width = level.shape[1], keep.shape[1]
    levels = [jax.ShapeDtypeStruct(level.shape, jnp.float32)] * (0 if before else 2)
    return pl.pallas_call(
        functools.partial(finish_kernel, start),
        out_shape=[pltpu.HBM((rows, width), jnp.bfloat16)] + levels,
        in_specs=[WHOLE] * len(operands) + [AWAY] * len(before),
        out_specs=[AWAY] + [WHOLE] * len(levels),
        scratch_shapes=[pltpu.VMEM((count, width), jnp.bfloat16), pltpu.SemaphoreType.DMA((2,))],
        input_output_aliases={len(operands): 0} if before else {},
        compiler_params=params(),
        cost_estimate=cost(10**6),
        name="finish",
    )(*operands, *[far(x) for x in before])


def plane_plan(q, k, v, short_taps, decay_rate, residue, out_weight, direction):
    rows, width = q.shape
    half = rows // 2
    early = half - STEP
    blocks = width // LANES
    axes = ("ctx", "tp")
    forward = [(p, 4 + p) for p in range(4)]
    across = [(4 * c + p, 4 * (1 - c) + p) for c in range(2) for p in range(4)]
    sibling = [(4 * c + p, 4 * c + (p ^ 1)) for c in range(2) for p in range(4)]
    pair = [(4 * c + p, 4 * c + (p ^ 2)) for c in range(2) for p in range(4)]
    inward = [(4 * c + 2 * (1 - c) + a, 4 * c + 2 * c + a) for c in range(2) for a in range(2)]
    onward = [(4 * c + 2 * c + a, 4 * (1 - c) + 2 * c + a) for c in range(2) for a in range(2)]

    ended, signal, decay, taps, edge, rate, residue, q = run_front(q, k, v, short_taps, decay_rate.T, residue.T)
    carry = lax.ppermute(ended, axes, forward)
    local, query, gain, weight, direction = run_local(
        q, signal, decay, taps, gains_of(rate, residue), out_weight, direction.reshape(1, -1)
    )
    parts, norm, direction = run_inner(direction, weight)
    first, second, whole = run_correct(carry, decay, gain, taps, edge, local, query, blocks, parts)
    far_first = lax.ppermute(first, axes, across)
    far_second = lax.ppermute(second, axes, across)

    def exchange(arrays, pairs):
        return [lax.ppermute(array, axes, pairs) for array in arrays]

    sends, keep0 = run_project(weight, whole, 0, early, 2)
    core0 = exchange(sends, sibling)
    hop0 = exchange(run_merge(early, keep0, *core0), inward)
    own_sends, keep1 = run_project(weight, whole, early, rows - early, 1)

    sends, far_keep = run_project(weight, far_first, 0, half, 1, *hop0, *own_sends)
    (sums0,) = run_merge(half, far_keep, *exchange(sends, sibling))
    (straight,) = exchange([sums0], across)

    one_row = jax.ShapeDtypeStruct((1, rows), jnp.float32)
    send, far_keep, level = call(
        project_level_kernel,
        "project",
        [rows_of(half + STEP, far_keep), far_keep, one_row],
        weight,
        after(far_second, sums0),
        whole,
        parts,
    )
    sums1, level = call(
        merge_level_kernel,
        "merge",
        [rows_of(half + STEP, far_keep), one_row],
        far_keep,
        *exchange([send], sibling),
        level,
    )
    (moved,) = exchange([sums1], inward)
    core1 = exchange(own_sends, sibling)
    (own1,) = run_merge(rows - early, keep1, *core1)

    (merged,) = exchange(run_merge(half, sums1, moved), onward)
    (turned,) = exchange(call(choose_kernel, "choose", [rows_of(rows - early, own1)], straight, level, own1), pair)
    own = (keep0, *core0, *hop0, keep1, *core1, turned)
    before, level, near = run_finish(0, half, (level, norm, direction, *own, moved, straight))
    (ablated,) = run_finish(half, half, (near, norm, direction, *own, moved, straight, merged), (before,))
    return ablated, level.reshape(rows)


def gather_plan(q, k, v, short_taps, decay_rate, residue, out_weight, direction):
    rows, width = q.shape
    blocks = width // LANES
    modes = decay_rate.shape[1]
    tp = lax.axis_index("tp")
    ctx_size = lax.axis_size("ctx")
    next_one = [(i, i + 1) for i in range(ctx_size - 1)]
    ended, signal, decay, taps, edge, rate, residue, q = run_front(q, k, v, short_taps, decay_rate.T, residue.T)
    halo = lax.ppermute(ended[modes * blocks :], "ctx", next_one)
    local, query, gain = run_local(q, signal, decay, taps, gains_of(rate, residue))
    k2, k1, v2, v1 = [halo[i * blocks : (i + 1) * blocks] for i in range(4)]
    tap = taps.reshape(9, blocks, LANES)
    key0, key1, value0, value1 = edge.reshape(4, blocks, LANES)
    extra0 = (key0 + tap[4] * k1 + tap[5] * k2) * (value0 + tap[7] * v1 + tap[8] * v2) - key0 * value0
    extra1 = (key1 + tap[5] * k1) * (value1 + tap[8] * v1) - key1 * value1
    wide_rate = decay_rate.T.reshape(modes, blocks, LANES)
    state = (
        ended[: modes * blocks].reshape(modes, blocks, LANES)
        + jnp.exp(-wide_rate * (rows - 1)) * extra0
        + jnp.exp(-wide_rate * (rows - 2)) * extra1
    )
    reach = 1
    while reach < ctx_size:
        earlier = lax.ppermute(state, "ctx", [(i, i + reach) for i in range(ctx_size - reach)])
        state = state + jnp.exp(-wide_rate * (rows * reach)) * earlier
        reach *= 2
    start = lax.ppermute(state, "ctx", next_one).reshape(modes * blocks, LANES)
    carry = jnp.concatenate([start, halo], axis=0)
    (gated,) = run_correct(carry, decay, gain, taps, edge, local, query, blocks)
    partial_terms = lax.dot_general(
        gated,
        lax.all_gather(out_weight, "ctx", axis=1, tiled=True),
        (((1,), (0,)), ((), ())),
        preferred_element_type=jnp.float32,
    )
    summed = lax.psum_scatter(
        partial_terms.astype(jnp.bfloat16), "tp", scatter_dimension=1, tiled=True
    ).astype(jnp.float32)
    width_here = summed.shape[1]
    direction_here = lax.dynamic_slice_in_dim(direction, tp * width_here, width_here, 0)
    norm_total = jnp.sum(direction * direction) + EPSILON
    local_inner = jnp.dot(summed, direction_here, precision=HIGHEST)
    feature_level = lax.psum(local_inner, "tp") / norm_total
    ablated = (summed - feature_level[:, None] * direction_here[None, :]).astype(jnp.bfloat16)
    return ablated, feature_level


def solution(mesh):
    placed = (
        P(("dp", "ctx"), "tp"),
        P(("dp", "ctx"), "tp"),
        P(("dp", "ctx"), "tp"),
        P(None, None, "tp"),
        P("tp", None),
        P("tp", None),
        P("tp", "ctx"),
        P(),
    )
    plane = mesh.shape["ctx"] == 2 and mesh.shape["tp"] == 4
    return jax.shard_map(
        plane_plan if plane else gather_plan,
        mesh=mesh,
        in_specs=placed,
        out_specs=(P(("dp", "ctx"), "tp"), P(("dp", "ctx"))),
        check_vma=False,
    )
```

```python
import functools

import jax
import jax.numpy as jnp
from jax import lax
from jax.experimental import pallas as pl
from jax.experimental.pallas import tpu as pltpu
from jax.sharding import PartitionSpec as P

EPSILON = 1e-06
HIGHEST = lax.Precision.HIGHEST
LANES = 128
GROUP = 8
STEP = 16
WHOLE = pl.BlockSpec(memory_space=pltpu.VMEM)
AWAY = pl.BlockSpec(memory_space=pltpu.HBM)


def params(mebibytes=20):
    return pltpu.CompilerParams(vmem_limit_bytes=mebibytes * 1024 * 1024)


def cost(flops):
    return pl.CostEstimate(flops=flops, bytes_accessed=1024, transcendentals=0)


def spread(source, scratch, row, to):
    blocks = source.shape[1] // LANES
    for block in range(blocks):
        piece = source[pl.ds(row, STEP), block * LANES : (block + 1) * LANES].astype(jnp.float32)
        for half in range(STEP // GROUP):
            start = (half * blocks + block) * GROUP
            scratch[pl.ds(to + start, GROUP), :] = piece[half * GROUP : (half + 1) * GROUP]


def spread_rows(source, target):
    count, width = source.shape
    blocks = width // LANES
    for block in range(blocks):
        target[pl.ds(block, count, stride=blocks), :] = source[:, block * LANES : (block + 1) * LANES]


def place_of(index, blocks):
    return pl.ds((index // GROUP) * (blocks * GROUP) + index % GROUP, blocks, stride=GROUP)


def tile(ref, index, blocks):
    return ref[index * blocks : (index + 1) * blocks, :]


def moving_tile(index, blocks):
    return pl.ds(pl.multiple_of(index * blocks, blocks), blocks)


def front_kernel(*refs):
    k_hbm, v_hbm, q_hbm, taps_hbm, rate_hbm, residue_hbm = refs[:6]
    carry_ref, signal_ref, decay_ref, taps_ref, edge_ref, rate_ref, residue_ref, q_near = refs[6:14]
    k_near, v_near, taps_near, k_wide, v_wide, sems, late_sems = refs[-7:]
    rows, width = k_near.shape
    blocks = width // LANES
    modes = rate_ref.shape[0]
    pieces = sems.shape[0] // 2 - 1
    height = rows // pieces

    def part(i):
        here = pl.ds(i * height, height)
        return (
            pltpu.make_async_copy(k_hbm.at[here], k_near.at[here], sems.at[2 * i]),
            pltpu.make_async_copy(v_hbm.at[here], v_near.at[here], sems.at[2 * i + 1]),
        )

    rate_copy = pltpu.make_async_copy(rate_hbm, rate_ref, sems.at[2 * pieces])
    taps_copy = pltpu.make_async_copy(taps_hbm, taps_near, sems.at[2 * pieces + 1])
    late = [(residue_hbm, residue_ref), (q_hbm, q_near)]
    late = [pltpu.make_async_copy(source, target, late_sems.at[i]) for i, (source, target) in enumerate(late)]
    rate_copy.start()
    taps_copy.start()
    for i in range(pieces):
        for copy in part(i):
            copy.start()
    for copy in late:
        copy.start()
    rate_copy.wait()
    taps_copy.wait()
    spread_rows(jnp.exp(-rate_ref[...]), decay_ref)
    for i in range(3):
        for block in range(blocks):
            taps_ref[pl.ds(3 * i * blocks + block, 3, stride=blocks), :] = taps_near[
                i, :, block * LANES : (block + 1) * LANES
            ]
    zero = jnp.zeros((blocks, LANES), jnp.float32)
    key_taps = [tile(taps_ref, 3 + j, blocks) for j in range(3)]
    value_taps = [tile(taps_ref, 6 + j, blocks) for j in range(3)]
    decay = [tile(decay_ref, m, blocks) for m in range(modes)]

    def step(row, held, first):
        spread(k_near, k_wide, row, 0)
        spread(v_near, v_wide, row, 0)
        state, (k2, k1, v2, v1) = list(held[:modes]), held[modes:]
        for index in range(STEP):
            k0 = k_wide[place_of(index, blocks), :]
            v0 = v_wide[place_of(index, blocks), :]
            key = key_taps[0] * k0 + key_taps[1] * k1 + key_taps[2] * k2
            value = value_taps[0] * v0 + value_taps[1] * v1 + value_taps[2] * v2
            if first and index < 2:
                edge_ref[index * blocks : (index + 1) * blocks, :] = key
                edge_ref[(2 + index) * blocks : (3 + index) * blocks, :] = value
            signal = key * value
            signal_ref[moving_tile(row + index, blocks), :] = signal
            state = [decay[m] * state[m] + signal for m in range(modes)]
            k2, k1, v2, v1 = k1, k0, v1, v0
        return tuple(state) + (k2, k1, v2, v1)

    held = (zero,) * (modes + 4)
    for i in range(pieces):
        for copy in part(i):
            copy.wait()
        begin = 0
        if i == 0:
            held = step(0, held, True)
            begin = 1
        held = lax.fori_loop(
            begin,
            height // STEP,
            lambda j, held, i=i: step(pl.multiple_of(i * height + j * STEP, STEP), held, False),
            held,
        )
    for m in range(modes + 4):
        carry_ref[m * blocks : (m + 1) * blocks, :] = held[m]
    for copy in late:
        copy.wait()
    spread(q_near, k_wide, rows - STEP, 0)
    for i in range(2):
        start = (modes + 4 + i) * blocks
        carry_ref[start : start + blocks, :] = k_wide[place_of(STEP - 2 + i, blocks), :]


def far(x):
    return pltpu.with_memory_space_constraint(x, pltpu.HBM)


def run_front(q, k, v, short_taps, rate, residue):
    rows, width = k.shape
    modes = rate.shape[0]
    blocks = width // LANES
    pieces = 4

    def wide(n):
        return jax.ShapeDtypeStruct((n * blocks, LANES), jnp.float32)

    def like(x):
        return jax.ShapeDtypeStruct(x.shape, x.dtype)

    out_shape = [wide(modes + 6), wide(rows), wide(modes), wide(9), wide(4), like(rate), like(residue), like(q)]
    return pl.pallas_call(
        front_kernel,
        out_shape=out_shape,
        in_specs=[AWAY] * 6,
        out_specs=[WHOLE] * len(out_shape),
        scratch_shapes=[
            pltpu.VMEM((rows, width), jnp.bfloat16),
            pltpu.VMEM((rows, width), jnp.bfloat16),
            pltpu.VMEM(short_taps.shape, jnp.float32),
            pltpu.VMEM((STEP * blocks, LANES), jnp.float32),
            pltpu.VMEM((STEP * blocks, LANES), jnp.float32),
            pltpu.SemaphoreType.DMA((2 * pieces + 2,)),
            pltpu.SemaphoreType.DMA((2,)),
        ],
        compiler_params=params(),
        cost_estimate=cost(10**8),
        name="front",
    )(*[far(x) for x in (k, v, q, short_taps, rate, residue)])


def local_kernel(q_near, signal_ref, decay_ref, taps_ref, gain_near, *refs):
    copies = []
    if len(refs) > 4:
        weight_hbm, direction_hbm, weight_ref, direction_ref, sems = refs[:2] + refs[5:7] + refs[-1:]
        refs = refs[2:5] + refs[7:-1]
        count = sems.shape[0] - 1
        copies.append(pltpu.make_async_copy(direction_hbm, direction_ref, sems.at[count]))
        copies[-1].start()
        depth = weight_ref.shape[0] // count
        for i in range(count):
            here = pl.ds(i * depth, depth)
            copies.append(pltpu.make_async_copy(weight_hbm.at[here], weight_ref.at[here], sems.at[i]))
            copies[-1].start()
    out_ref, query_ref, gain_ref, q_wide = refs
    rows, width = q_near.shape
    blocks = width // LANES
    modes = gain_near.shape[0]
    spread_rows(gain_near[...], gain_ref)
    zero = jnp.zeros((blocks, LANES), jnp.float32)
    taps = [tile(taps_ref, j, blocks) for j in range(3)]
    decay = [tile(decay_ref, m, blocks) for m in range(modes)]
    gain = [tile(gain_ref, m, blocks) for m in range(modes)]

    def step(j, held):
        row = pl.multiple_of(j * STEP, STEP)
        spread(q_near, q_wide, row, 0)
        state, (q2, q1) = list(held[:modes]), held[modes:]
        for index in range(STEP):
            q0 = q_wide[place_of(index, blocks), :]
            here = moving_tile(row + index, blocks)
            signal = signal_ref[here, :]
            query_ref[here, :] = taps[0] * q0 + taps[1] * q1 + taps[2] * q2
            state = [decay[m] * state[m] + signal for m in range(modes)]
            sums = [gain[m] * state[m] for m in range(modes)]
            while len(sums) > 1:
                sums = [sums[i] + sums[i + 1] for i in range(0, len(sums), 2)]
            out_ref[here, :] = sums[0]
            q2, q1 = q1, q0
        return tuple(state) + (q2, q1)

    lax.fori_loop(0, rows // STEP, step, (zero,) * (modes + 2))
    for copy in copies:
        copy.wait()


def run_local(q, signal, decay, taps, gain, *weight):
    rows, width = q.shape
    blocks = width // LANES
    wide = jax.ShapeDtypeStruct((rows * blocks, LANES), jnp.float32)
    out_shape = [wide, wide, jax.ShapeDtypeStruct(decay.shape, jnp.float32)]
    scratch_shapes = [pltpu.VMEM((STEP * blocks, LANES), jnp.float32)]
    if weight:
        out_shape += [jax.ShapeDtypeStruct(x.shape, x.dtype) for x in weight]
        scratch_shapes.append(pltpu.SemaphoreType.DMA((5,)))
        weight = tuple(far(x) for x in weight)
    return pl.pallas_call(
        local_kernel,
        out_shape=out_shape,
        in_specs=[WHOLE] * 5 + [AWAY] * len(weight),
        out_specs=[WHOLE] * len(out_shape),
        scratch_shapes=scratch_shapes,
        compiler_params=params(),
        cost_estimate=cost(10**6),
        name="local_filter",
    )(q, signal, decay, taps, gain, *weight)


def correct_kernel(blocks, carry_ref, decay_ref, gain_ref, taps_ref, edge_ref, local_ref, query_ref, *refs):
    wide, outs = refs[-1], refs[:-1]
    rows = local_ref.shape[0] // blocks
    if len(outs) > 1:
        outs = outs[1:]
        outs[1][rows // 2 :, :] = refs[0][...]
    modes = decay_ref.shape[0] // blocks
    k2, k1, v2, v1, q2, q1 = [tile(carry_ref, modes + i, blocks) for i in range(6)]
    tap = [tile(taps_ref, i, blocks) for i in range(9)]
    key0, key1, value0, value1 = [tile(edge_ref, i, blocks) for i in range(4)]
    extra = [
        (key0 + tap[4] * k1 + tap[5] * k2) * (value0 + tap[7] * v1 + tap[8] * v2) - key0 * value0,
        (key1 + tap[5] * k1) * (value1 + tap[8] * v1) - key1 * value1,
    ]
    query_extra = [tap[1] * q1 + tap[2] * q2, tap[2] * q1]
    state = [tile(gain_ref, m, blocks) * tile(carry_ref, m, blocks) for m in range(modes)]
    decay = [tile(decay_ref, m, blocks) for m in range(modes)]

    def step(row, state, first, piece_ref, start):
        state = list(state)
        for index in range(STEP):
            here = moving_tile(row + index, blocks)
            state = [decay[m] * state[m] for m in range(modes)]
            query = query_ref[here, :]
            if first and index < 2:
                state = [state[m] + tile(gain_ref, m, blocks) * extra[index] for m in range(modes)]
                query = query + query_extra[index]
            sums = state
            while len(sums) > 1:
                sums = [sums[i] + sums[i + 1] for i in range(0, len(sums), 2)]
            wide[place_of(index, blocks), :] = query * (local_ref[here, :] + sums[0])
        for block in range(blocks):
            halves = [
                wide[(half * blocks + block) * GROUP : (half * blocks + block + 1) * GROUP, :]
                for half in range(STEP // GROUP)
            ]
            rounded = jnp.concatenate(halves, axis=0).astype(jnp.bfloat16)
            columns = slice(block * LANES, (block + 1) * LANES)
            outs[-1][pl.ds(row, STEP), columns] = rounded
            if piece_ref is not None:
                piece_ref[pl.ds(pl.multiple_of(row - start, STEP), STEP), columns] = rounded
        return tuple(state)

    state = tuple(state)
    start = 0
    for piece_ref in outs[:-1] or [None]:
        end = start + (rows if piece_ref is None else rows // 2)
        begin = start // STEP
        if start == 0:
            state = step(0, state, True, piece_ref, 0)
            begin = 1
        state = lax.fori_loop(
            begin,
            end // STEP,
            lambda j, state, start=start, piece_ref=piece_ref: step(
                pl.multiple_of(j * STEP, STEP), state, False, piece_ref, start
            ),
            state,
        )
        start = end


def run_correct(carry, decay, gain, taps, edge, local, query, blocks, *parts):
    rows = local.shape[0] // blocks
    width = blocks * LANES
    heights = ([rows // 2, rows // 2 + STEP] if parts else []) + [rows]
    return pl.pallas_call(
        functools.partial(correct_kernel, blocks),
        out_shape=[jax.ShapeDtypeStruct((height, width), jnp.bfloat16) for height in heights],
        in_specs=[WHOLE] * (7 + len(parts)),
        out_specs=[WHOLE] * len(heights),
        scratch_shapes=[pltpu.VMEM((STEP * blocks, LANES), jnp.float32)],
        compiler_params=params(),
        cost_estimate=cost(10**8),
        name="carried_filter",
    )(carry, decay, gain, taps, edge, local, query, *parts)


def gains_of(rate, residue):
    return residue * jnp.sqrt(-jnp.expm1(-2.0 * rate)) * rate.shape[0] ** (-0.5)


def split_three(x):
    high = x.astype(jnp.bfloat16)
    rest = x - high.astype(jnp.float32)
    middle = rest.astype(jnp.bfloat16)
    low = (rest - middle.astype(jnp.float32)).astype(jnp.bfloat16)
    return high, middle, low


def in_parts(row):
    return jnp.concatenate(list(split_three(row)) + [jnp.zeros((13, row.shape[1]), jnp.bfloat16)], axis=0)


def dot_parts(parts, matrix):
    out = lax.dot_general(parts, matrix, (((1,), (1,)), ((), ())), preferred_element_type=jnp.float32)
    return out[0:1] + out[1:2] + out[2:3]


def idle_kernel(*refs):
    pass


def after(array, *others):
    return pl.pallas_call(
        idle_kernel,
        out_shape=jax.ShapeDtypeStruct(array.shape, array.dtype),
        in_specs=[pl.BlockSpec(memory_space=pl.ANY)] * (1 + len(others)),
        out_specs=pl.BlockSpec(memory_space=pl.ANY),
        input_output_aliases={0: 0},
        compiler_params=params(),
        cost_estimate=cost(1),
        name="after",
    )(array, *others)


def rows_of(count, like, dtype=jnp.bfloat16):
    return jax.ShapeDtypeStruct((count, like.shape[1]), dtype)


def call(kernel, name, out_shape, *operands, tokens=()):
    def with_tokens(*refs):
        kernel(*refs[: len(operands)], *refs[len(operands) + len(tokens) :])

    return pl.pallas_call(
        with_tokens,
        out_shape=out_shape,
        in_specs=[WHOLE] * len(operands) + [pl.BlockSpec(memory_space=pl.ANY)] * len(tokens),
        out_specs=[WHOLE] * len(out_shape),
        compiler_params=params(),
        cost_estimate=cost(10**6),
        name=name,
    )(*operands, *tokens)


def inner_kernel(direction_ref, weight_ref, parts_ref, norm_ref, here_ref):
    everything = direction_ref[...]
    norm_ref[...] = jnp.broadcast_to(
        jnp.sum(everything * everything, axis=1, keepdims=True) + EPSILON, norm_ref.shape
    )
    size, width = weight_ref.shape[1], here_ref.shape[1]
    here_ref[...] = direction_ref[:, pl.ds(pl.multiple_of(lax.axis_index("tp") * width, LANES), width)]
    here = direction_ref[:, pl.ds(pl.multiple_of(lax.axis_index("ctx") * size, LANES), size)]
    parts_ref[...] = in_parts(dot_parts(in_parts(here), weight_ref[...]))


def run_inner(direction, weight):
    out_shape = [
        jax.ShapeDtypeStruct((STEP, weight.shape[0]), jnp.bfloat16),
        jax.ShapeDtypeStruct((1, LANES), jnp.float32),
        jax.ShapeDtypeStruct((1, weight.shape[1] // 2), jnp.float32),
    ]
    return call(inner_kernel, "inner", out_shape, direction, weight)


def project_kernel(begin, weight_ref, piece_ref, *outs):
    *sends, keep_ref = outs
    rows, width = keep_ref.shape
    cut = width // len(sends)
    side = lax.axis_index("tp") % 2
    for start in range(0, 2 * width, 256):
        away = start < width
        ref, to = (sends[start // cut], start % cut) if away else (keep_ref, start - width)
        which = 1 - side if away else side
        columns = pl.ds(pl.multiple_of(which * width + start % width, 256), 256)
        out = jnp.dot(piece_ref[begin : begin + rows, :], weight_ref[:, columns], preferred_element_type=jnp.float32)
        ref[:rows, to : to + 256] = out.astype(ref.dtype)


def run_project(weight, piece, begin, rows, count, *tokens):
    keep = jax.ShapeDtypeStruct((rows, weight.shape[1] // 2), jnp.float32)
    sends = [jax.ShapeDtypeStruct((rows, keep.shape[1] // count), jnp.bfloat16)] * count
    kernel = functools.partial(project_kernel, begin)
    *sends, keep = call(kernel, "project", [*sends, keep], weight, piece, tokens=tokens)
    return sends, keep


def put_behind(ref, rows, row):
    here = slice(rows, rows + STEP)
    ref[here, :] = jnp.zeros((STEP, ref.shape[1]), jnp.bfloat16)
    ref[here, : row.shape[1]] = in_parts(row)


def take_behind(ref, rows, width):
    return jnp.sum(ref[rows : rows + STEP, :width].astype(jnp.float32), axis=0, keepdims=True)


def project_level_kernel(weight_ref, far_ref, whole_ref, parts_ref, *outs):
    *sends, keep_ref, level_ref = outs
    project_kernel(0, weight_ref, far_ref, *sends, keep_ref)
    level = dot_parts(parts_ref[...], whole_ref[...]) + dot_parts(far_ref[keep_ref.shape[0] :, :], whole_ref[...])
    level_ref[...] = level
    put_behind(sends[0], keep_ref.shape[0], level)


def merge_kernel(keep_ref, core_ref, out_ref):
    for row in range(0, out_ref.shape[0], STEP):
        here = slice(row, row + STEP)
        total = keep_ref[here, :].astype(jnp.float32) + core_ref[here, :].astype(jnp.float32)
        out_ref[here, :] = total.astype(jnp.bfloat16)


def run_merge(rows, keep, core):
    (out,) = call(merge_kernel, "merge", [rows_of(rows, keep)], keep, core)
    return out


def merge_level_kernel(keep_ref, level_ref, *refs):
    *cores, out_ref, total_ref = refs
    rows, width = keep_ref.shape
    cut = width // len(cores)
    for row in range(0, rows, STEP):
        here = slice(row, row + STEP)
        for i, core_ref in enumerate(cores):
            columns = slice(i * cut, (i + 1) * cut)
            total = keep_ref[here, columns] + core_ref[here, :].astype(jnp.float32)
            out_ref[here, columns] = total.astype(jnp.bfloat16)
    total = level_ref[...] + take_behind(cores[0], rows, level_ref.shape[1])
    total_ref[...] = total
    put_behind(out_ref, rows, total)


def is_keeper():
    return lax.axis_index("tp") // 2 == lax.axis_index("ctx")


def choose_kernel(straight_ref, level_ref, own_ref, out_ref):
    keeper = is_keeper()

    @pl.when(keeper)
    def _():
        rows = straight_ref.shape[0]
        out_ref[:rows, :] = straight_ref[...]
        put_behind(out_ref, rows, level_ref[...])

    @pl.when(jnp.logical_not(keeper))
    def _():
        out_ref[...] = own_ref[...]


def finish_kernel(*refs):
    level_ref, norm_ref, direction_ref = refs[:3]
    own0, own1, (moved_ref, straight_ref, merged_ref) = refs[3:6], refs[6:9], refs[9:12]
    out_hbm, level_out_ref, out_near, sems = refs[12:]
    turned_ref = own1[-1]
    rows, width = out_near.shape
    half = straight_ref.shape[0]
    keeper = is_keeper()
    other = jnp.where(keeper, take_behind(moved_ref, half, rows), take_behind(turned_ref, half, rows))
    level = (level_ref[...] + other) / norm_ref[0:1, 0:1]
    level_out_ref[...] = level
    direction = direction_ref[...]
    column = jnp.transpose(jnp.broadcast_to(level, (LANES, rows)))

    def put(row, cut, before, behind):
        pieces, start = (before, row) if row < cut else (behind, row - cut)
        total = pieces[0][start : start + STEP, :].astype(jnp.float32)
        for piece in pieces[1:]:
            total = total + piece[start : start + STEP, :].astype(jnp.float32)
        total = total - column[row : row + STEP, 0:1] * direction
        out_near[row : row + STEP, :] = total.astype(jnp.bfloat16)

    copies = []
    count = sems.shape[0]
    for i in range(count):
        begin, end = i * rows // count, (i + 1) * rows // count

        @pl.when(keeper)
        def _():
            for row in range(begin, end, STEP):
                put(row, own0[0].shape[0], own0, own1)

        @pl.when(jnp.logical_not(keeper))
        def _():
            for row in range(begin, end, STEP):
                put(row, half, (straight_ref, turned_ref), (merged_ref,))

        here = pl.ds(begin, end - begin)
        copies.append(pltpu.make_async_copy(out_near.at[here], out_hbm.at[here], sems.at[i]))
        copies[-1].start()
    for copy in copies:
        copy.wait()


def run_finish(*operands):
    rows, width = operands[0].shape[1], operands[2].shape[1]
    return pl.pallas_call(
        finish_kernel,
        out_shape=[
            jax.ShapeDtypeStruct((rows, width), jnp.bfloat16),
            jax.ShapeDtypeStruct((1, rows), jnp.float32),
        ],
        in_specs=[WHOLE] * len(operands),
        out_specs=[AWAY, WHOLE],
        scratch_shapes=[pltpu.VMEM((rows, width), jnp.bfloat16), pltpu.SemaphoreType.DMA((4,))],
        compiler_params=params(),
        cost_estimate=cost(10**6),
        name="finish",
    )(*operands)


def plane_plan(q, k, v, short_taps, decay_rate, residue, out_weight, direction):
    rows, width = q.shape
    half = rows // 2
    early = rows * 3 // 8 // STEP * STEP
    blocks = width // LANES
    axes = ("ctx", "tp")
    forward = [(p, 4 + p) for p in range(4)]
    across = [(4 * c + p, 4 * (1 - c) + p) for c in range(2) for p in range(4)]
    sibling = [(4 * c + p, 4 * c + (p ^ 1)) for c in range(2) for p in range(4)]
    pair = [(4 * c + p, 4 * c + (p ^ 2)) for c in range(2) for p in range(4)]
    inward = [(4 * c + 2 * (1 - c) + a, 4 * c + 2 * c + a) for c in range(2) for a in range(2)]
    onward = [(4 * c + 2 * c + a, 4 * (1 - c) + 2 * c + a) for c in range(2) for a in range(2)]

    ended, signal, decay, taps, edge, rate, residue, q = run_front(q, k, v, short_taps, decay_rate.T, residue.T)
    carry = lax.ppermute(ended, axes, forward)
    local, query, gain, weight, direction = run_local(
        q, signal, decay, taps, gains_of(rate, residue), out_weight, direction.reshape(1, -1)
    )
    parts, norm, direction = run_inner(direction, weight)
    first, second, whole = run_correct(carry, decay, gain, taps, edge, local, query, blocks, parts)
    far_first = lax.ppermute(first, axes, across)
    far_second = lax.ppermute(second, axes, across)

    def exchange(arrays, pairs):
        return [lax.ppermute(array, axes, pairs) for array in arrays]

    def exchange(array, pairs):
        return lax.ppermute(array, axes, pairs)

    (send,), keep0 = run_project(weight, whole, 0, early, 1)
    core0 = exchange(send, sibling)
    hop0 = exchange(run_merge(early, keep0, core0), inward)

    (send,), far_keep = run_project(weight, far_first, 0, half, 1)
    sums0 = run_merge(half, far_keep, exchange(send, sibling))
    straight = exchange(sums0, across)

    whole = after(whole, sums0)
    (own_send,), keep1 = run_project(weight, whole, early, rows - early, 1)
    one_row = jax.ShapeDtypeStruct((1, rows), jnp.float32)
    columns = far_keep.shape[1] // 4
    *sends, far_keep, level = call(
        project_level_kernel,
        "project",
        [jax.ShapeDtypeStruct((half + STEP * (i == 0), columns), jnp.bfloat16) for i in range(4)] + [far_keep, one_row],
        weight,
        after(far_second, own_send),
        whole,
        parts,
    )
    sums1, level = call(
        merge_level_kernel,
        "merge",
        [rows_of(half + STEP, far_keep), one_row],
        far_keep,
        level,
        *[exchange(send, sibling) for send in sends],
        tokens=(hop0,),
    )
    moved = exchange(sums1, inward)
    core1 = exchange(own_send, sibling)
    own1 = run_merge(rows - early, keep1, core1)

    merged = exchange(run_merge(half, sums1, moved), onward)
    (turned,) = call(choose_kernel, "choose", [rows_of(rows - early, own1)], straight, level, own1)
    turned = exchange(turned, pair)
    ablated, level = run_finish(
        level, norm, direction, keep0, core0, hop0, keep1, core1, turned, moved, straight, merged
    )
    return ablated, level.reshape(rows)


def gather_plan(q, k, v, short_taps, decay_rate, residue, out_weight, direction):
    rows, width = q.shape
    blocks = width // LANES
    modes = decay_rate.shape[1]
    tp = lax.axis_index("tp")
    ctx_size = lax.axis_size("ctx")
    next_one = [(i, i + 1) for i in range(ctx_size - 1)]
    ended, signal, decay, taps, edge, rate, residue, q = run_front(q, k, v, short_taps, decay_rate.T, residue.T)
    halo = lax.ppermute(ended[modes * blocks :], "ctx", next_one)
    local, query, gain = run_local(q, signal, decay, taps, gains_of(rate, residue))
    k2, k1, v2, v1 = [halo[i * blocks : (i + 1) * blocks] for i in range(4)]
    tap = taps.reshape(9, blocks, LANES)
    key0, key1, value0, value1 = edge.reshape(4, blocks, LANES)
    extra0 = (key0 + tap[4] * k1 + tap[5] * k2) * (value0 + tap[7] * v1 + tap[8] * v2) - key0 * value0
    extra1 = (key1 + tap[5] * k1) * (value1 + tap[8] * v1) - key1 * value1
    wide_rate = decay_rate.T.reshape(modes, blocks, LANES)
    state = (
        ended[: modes * blocks].reshape(modes, blocks, LANES)
        + jnp.exp(-wide_rate * (rows - 1)) * extra0
        + jnp.exp(-wide_rate * (rows - 2)) * extra1
    )
    reach = 1
    while reach < ctx_size:
        earlier = lax.ppermute(state, "ctx", [(i, i + reach) for i in range(ctx_size - reach)])
        state = state + jnp.exp(-wide_rate * (rows * reach)) * earlier
        reach *= 2
    start = lax.ppermute(state, "ctx", next_one).reshape(modes * blocks, LANES)
    carry = jnp.concatenate([start, halo], axis=0)
    (gated,) = run_correct(carry, decay, gain, taps, edge, local, query, blocks)
    partial_terms = lax.dot_general(
        gated,
        lax.all_gather(out_weight, "ctx", axis=1, tiled=True),
        (((1,), (0,)), ((), ())),
        preferred_element_type=jnp.float32,
    )
    summed = lax.psum_scatter(
        partial_terms.astype(jnp.bfloat16), "tp", scatter_dimension=1, tiled=True
    ).astype(jnp.float32)
    width_here = summed.shape[1]
    direction_here = lax.dynamic_slice_in_dim(direction, tp * width_here, width_here, 0)
    norm_total = jnp.sum(direction * direction) + EPSILON
    local_inner = jnp.dot(summed, direction_here, precision=HIGHEST)
    feature_level = lax.psum(local_inner, "tp") / norm_total
    ablated = (summed - feature_level[:, None] * direction_here[None, :]).astype(jnp.bfloat16)
    return ablated, feature_level


def solution(mesh):
    placed = (
        P(("dp", "ctx"), "tp"),
        P(("dp", "ctx"), "tp"),
        P(("dp", "ctx"), "tp"),
        P(None, None, "tp"),
        P("tp", None),
        P("tp", None),
        P("tp", "ctx"),
        P(),
    )
    plane = mesh.shape["ctx"] == 2 and mesh.shape["tp"] == 4
    return jax.shard_map(
        plane_plan if plane else gather_plan,
        mesh=mesh,
        in_specs=placed,
        out_specs=(P(("dp", "ctx"), "tp"), P(("dp", "ctx"))),
        check_vma=False,
    )
```

```python
import functools

import jax
import jax.numpy as jnp
from jax import lax
from jax.experimental import pallas as pl
from jax.experimental.pallas import tpu as pltpu
from jax.sharding import PartitionSpec as P

EPSILON = 1e-06
HIGHEST = lax.Precision.HIGHEST
LANES = 128
GROUP = 8
STEP = 16
WHOLE = pl.BlockSpec(memory_space=pltpu.VMEM)
AWAY = pl.BlockSpec(memory_space=pltpu.HBM)


def params(mebibytes=20):
    return pltpu.CompilerParams(vmem_limit_bytes=mebibytes * 1024 * 1024)


def cost(flops):
    return pl.CostEstimate(flops=flops, bytes_accessed=1024, transcendentals=0)


def spread(source, scratch, row, to):
    blocks = source.shape[1] // LANES
    for block in range(blocks):
        piece = source[pl.ds(row, STEP), block * LANES : (block + 1) * LANES].astype(jnp.float32)
        for half in range(STEP // GROUP):
            start = (half * blocks + block) * GROUP
            scratch[pl.ds(to + start, GROUP), :] = piece[half * GROUP : (half + 1) * GROUP]


def spread_rows(source, target):
    count, width = source.shape
    blocks = width // LANES
    for block in range(blocks):
        target[pl.ds(block, count, stride=blocks), :] = source[:, block * LANES : (block + 1) * LANES]


def place_of(index, blocks):
    return pl.ds((index // GROUP) * (blocks * GROUP) + index % GROUP, blocks, stride=GROUP)


def tile(ref, index, blocks):
    return ref[index * blocks : (index + 1) * blocks, :]


def moving_tile(index, blocks):
    return pl.ds(pl.multiple_of(index * blocks, blocks), blocks)


def front_kernel(*refs):
    k_hbm, v_hbm, q_hbm, taps_hbm, rate_hbm, residue_hbm = refs[:6]
    carry_ref, signal_ref, decay_ref, taps_ref, edge_ref, rate_ref, residue_ref, q_near = refs[6:14]
    k_near, v_near, taps_near, k_wide, v_wide, sems, late_sems = refs[-7:]
    rows, width = k_near.shape
    blocks = width // LANES
    modes = rate_ref.shape[0]
    pieces = sems.shape[0] // 2 - 1
    height = rows // pieces

    def part(i):
        here = pl.ds(i * height, height)
        return (
            pltpu.make_async_copy(k_hbm.at[here], k_near.at[here], sems.at[2 * i]),
            pltpu.make_async_copy(v_hbm.at[here], v_near.at[here], sems.at[2 * i + 1]),
        )

    rate_copy = pltpu.make_async_copy(rate_hbm, rate_ref, sems.at[2 * pieces])
    taps_copy = pltpu.make_async_copy(taps_hbm, taps_near, sems.at[2 * pieces + 1])
    late = [(residue_hbm, residue_ref), (q_hbm, q_near)]
    late = [pltpu.make_async_copy(source, target, late_sems.at[i]) for i, (source, target) in enumerate(late)]
    rate_copy.start()
    taps_copy.start()
    for i in range(pieces):
        for copy in part(i):
            copy.start()
    for copy in late:
        copy.start()
    rate_copy.wait()
    taps_copy.wait()
    spread_rows(jnp.exp(-rate_ref[...]), decay_ref)
    for i in range(3):
        for block in range(blocks):
            taps_ref[pl.ds(3 * i * blocks + block, 3, stride=blocks), :] = taps_near[
                i, :, block * LANES : (block + 1) * LANES
            ]
    zero = jnp.zeros((blocks, LANES), jnp.float32)
    key_taps = [tile(taps_ref, 3 + j, blocks) for j in range(3)]
    value_taps = [tile(taps_ref, 6 + j, blocks) for j in range(3)]
    decay = [tile(decay_ref, m, blocks) for m in range(modes)]

    def step(row, held, first):
        spread(k_near, k_wide, row, 0)
        spread(v_near, v_wide, row, 0)
        state, (k2, k1, v2, v1) = list(held[:modes]), held[modes:]
        for index in range(STEP):
            k0 = k_wide[place_of(index, blocks), :]
            v0 = v_wide[place_of(index, blocks), :]
            key = key_taps[0] * k0 + key_taps[1] * k1 + key_taps[2] * k2
            value = value_taps[0] * v0 + value_taps[1] * v1 + value_taps[2] * v2
            if first and index < 2:
                edge_ref[index * blocks : (index + 1) * blocks, :] = key
                edge_ref[(2 + index) * blocks : (3 + index) * blocks, :] = value
            signal = key * value
            signal_ref[moving_tile(row + index, blocks), :] = signal
            state = [decay[m] * state[m] + signal for m in range(modes)]
            k2, k1, v2, v1 = k1, k0, v1, v0
        return tuple(state) + (k2, k1, v2, v1)

    held = (zero,) * (modes + 4)
    for i in range(pieces):
        for copy in part(i):
            copy.wait()
        begin = 0
        if i == 0:
            held = step(0, held, True)
            begin = 1
        held = lax.fori_loop(
            begin,
            height // STEP,
            lambda j, held, i=i: step(pl.multiple_of(i * height + j * STEP, STEP), held, False),
            held,
        )
    for m in range(modes + 4):
        carry_ref[m * blocks : (m + 1) * blocks, :] = held[m]
    for copy in late:
        copy.wait()
    spread(q_near, k_wide, rows - STEP, 0)
    for i in range(2):
        start = (modes + 4 + i) * blocks
        carry_ref[start : start + blocks, :] = k_wide[place_of(STEP - 2 + i, blocks), :]


def far(x):
    return pltpu.with_memory_space_constraint(x, pltpu.HBM)


def run_front(q, k, v, short_taps, rate, residue):
    rows, width = k.shape
    modes = rate.shape[0]
    blocks = width // LANES
    pieces = 4

    def wide(n):
        return jax.ShapeDtypeStruct((n * blocks, LANES), jnp.float32)

    def like(x):
        return jax.ShapeDtypeStruct(x.shape, x.dtype)

    out_shape = [wide(modes + 6), wide(rows), wide(modes), wide(9), wide(4), like(rate), like(residue), like(q)]
    return pl.pallas_call(
        front_kernel,
        out_shape=out_shape,
        in_specs=[AWAY] * 6,
        out_specs=[WHOLE] * len(out_shape),
        scratch_shapes=[
            pltpu.VMEM((rows, width), jnp.bfloat16),
            pltpu.VMEM((rows, width), jnp.bfloat16),
            pltpu.VMEM(short_taps.shape, jnp.float32),
            pltpu.VMEM((STEP * blocks, LANES), jnp.float32),
            pltpu.VMEM((STEP * blocks, LANES), jnp.float32),
            pltpu.SemaphoreType.DMA((2 * pieces + 2,)),
            pltpu.SemaphoreType.DMA((2,)),
        ],
        compiler_params=params(),
        cost_estimate=cost(10**8),
        name="front",
    )(*[far(x) for x in (k, v, q, short_taps, rate, residue)])


def local_kernel(q_near, signal_ref, decay_ref, taps_ref, gain_near, *refs):
    copies = []
    if len(refs) > 4:
        weight_hbm, direction_hbm, weight_ref, direction_ref, sems = refs[:2] + refs[5:7] + refs[-1:]
        refs = refs[2:5] + refs[7:-1]
        count = sems.shape[0] - 1
        copies.append(pltpu.make_async_copy(direction_hbm, direction_ref, sems.at[count]))
        copies[-1].start()
        depth = weight_ref.shape[0] // count
        for i in range(count):
            here = pl.ds(i * depth, depth)
            copies.append(pltpu.make_async_copy(weight_hbm.at[here], weight_ref.at[here], sems.at[i]))
            copies[-1].start()
    out_ref, query_ref, gain_ref, q_wide = refs
    rows, width = q_near.shape
    blocks = width // LANES
    modes = gain_near.shape[0]
    spread_rows(gain_near[...], gain_ref)
    zero = jnp.zeros((blocks, LANES), jnp.float32)
    taps = [tile(taps_ref, j, blocks) for j in range(3)]
    decay = [tile(decay_ref, m, blocks) for m in range(modes)]
    gain = [tile(gain_ref, m, blocks) for m in range(modes)]

    def step(j, held):
        row = pl.multiple_of(j * STEP, STEP)
        spread(q_near, q_wide, row, 0)
        state, (q2, q1) = list(held[:modes]), held[modes:]
        for index in range(STEP):
            q0 = q_wide[place_of(index, blocks), :]
            here = moving_tile(row + index, blocks)
            signal = signal_ref[here, :]
            query_ref[here, :] = taps[0] * q0 + taps[1] * q1 + taps[2] * q2
            state = [decay[m] * state[m] + signal for m in range(modes)]
            sums = [gain[m] * state[m] for m in range(modes)]
            while len(sums) > 1:
                sums = [sums[i] + sums[i + 1] for i in range(0, len(sums), 2)]
            out_ref[here, :] = sums[0]
            q2, q1 = q1, q0
        return tuple(state) + (q2, q1)

    lax.fori_loop(0, rows // STEP, step, (zero,) * (modes + 2))
    for copy in copies:
        copy.wait()


def run_local(q, signal, decay, taps, gain, *weight):
    rows, width = q.shape
    blocks = width // LANES
    wide = jax.ShapeDtypeStruct((rows * blocks, LANES), jnp.float32)
    out_shape = [wide, wide, jax.ShapeDtypeStruct(decay.shape, jnp.float32)]
    scratch_shapes = [pltpu.VMEM((STEP * blocks, LANES), jnp.float32)]
    if weight:
        out_shape += [jax.ShapeDtypeStruct(x.shape, x.dtype) for x in weight]
        scratch_shapes.append(pltpu.SemaphoreType.DMA((5,)))
        weight = tuple(far(x) for x in weight)
    return pl.pallas_call(
        local_kernel,
        out_shape=out_shape,
        in_specs=[WHOLE] * 5 + [AWAY] * len(weight),
        out_specs=[WHOLE] * len(out_shape),
        scratch_shapes=scratch_shapes,
        compiler_params=params(),
        cost_estimate=cost(10**6),
        name="local_filter",
    )(q, signal, decay, taps, gain, *weight)


def correct_kernel(blocks, carry_ref, decay_ref, gain_ref, taps_ref, edge_ref, local_ref, query_ref, *refs):
    wide, outs = refs[-1], refs[:-1]
    rows = local_ref.shape[0] // blocks
    if len(outs) > 1:
        outs = outs[1:]
        outs[1][rows // 2 :, :] = refs[0][...]
    modes = decay_ref.shape[0] // blocks
    k2, k1, v2, v1, q2, q1 = [tile(carry_ref, modes + i, blocks) for i in range(6)]
    tap = [tile(taps_ref, i, blocks) for i in range(9)]
    key0, key1, value0, value1 = [tile(edge_ref, i, blocks) for i in range(4)]
    extra = [
        (key0 + tap[4] * k1 + tap[5] * k2) * (value0 + tap[7] * v1 + tap[8] * v2) - key0 * value0,
        (key1 + tap[5] * k1) * (value1 + tap[8] * v1) - key1 * value1,
    ]
    query_extra = [tap[1] * q1 + tap[2] * q2, tap[2] * q1]
    state = [tile(gain_ref, m, blocks) * tile(carry_ref, m, blocks) for m in range(modes)]
    decay = [tile(decay_ref, m, blocks) for m in range(modes)]

    def step(row, state, first, piece_ref, start):
        state = list(state)
        for index in range(STEP):
            here = moving_tile(row + index, blocks)
            state = [decay[m] * state[m] for m in range(modes)]
            query = query_ref[here, :]
            if first and index < 2:
                state = [state[m] + tile(gain_ref, m, blocks) * extra[index] for m in range(modes)]
                query = query + query_extra[index]
            sums = state
            while len(sums) > 1:
                sums = [sums[i] + sums[i + 1] for i in range(0, len(sums), 2)]
            wide[place_of(index, blocks), :] = query * (local_ref[here, :] + sums[0])
        for block in range(blocks):
            halves = [
                wide[(half * blocks + block) * GROUP : (half * blocks + block + 1) * GROUP, :]
                for half in range(STEP // GROUP)
            ]
            rounded = jnp.concatenate(halves, axis=0).astype(jnp.bfloat16)
            columns = slice(block * LANES, (block + 1) * LANES)
            outs[-1][pl.ds(row, STEP), columns] = rounded
            if piece_ref is not None:
                piece_ref[pl.ds(pl.multiple_of(row - start, STEP), STEP), columns] = rounded
        return tuple(state)

    state = tuple(state)
    start = 0
    for piece_ref in outs[:-1] or [None]:
        end = start + (rows if piece_ref is None else rows // 2)
        begin = start // STEP
        if start == 0:
            state = step(0, state, True, piece_ref, 0)
            begin = 1
        state = lax.fori_loop(
            begin,
            end // STEP,
            lambda j, state, start=start, piece_ref=piece_ref: step(
                pl.multiple_of(j * STEP, STEP), state, False, piece_ref, start
            ),
            state,
        )
        start = end


def run_correct(carry, decay, gain, taps, edge, local, query, blocks, *parts):
    rows = local.shape[0] // blocks
    width = blocks * LANES
    heights = ([rows // 2, rows // 2 + STEP] if parts else []) + [rows]
    return pl.pallas_call(
        functools.partial(correct_kernel, blocks),
        out_shape=[jax.ShapeDtypeStruct((height, width), jnp.bfloat16) for height in heights],
        in_specs=[WHOLE] * (7 + len(parts)),
        out_specs=[WHOLE] * len(heights),
        scratch_shapes=[pltpu.VMEM((STEP * blocks, LANES), jnp.float32)],
        compiler_params=params(),
        cost_estimate=cost(10**8),
        name="carried_filter",
    )(carry, decay, gain, taps, edge, local, query, *parts)


def gains_of(rate, residue):
    return residue * jnp.sqrt(-jnp.expm1(-2.0 * rate)) * rate.shape[0] ** (-0.5)


def split_three(x):
    high = x.astype(jnp.bfloat16)
    rest = x - high.astype(jnp.float32)
    middle = rest.astype(jnp.bfloat16)
    low = (rest - middle.astype(jnp.float32)).astype(jnp.bfloat16)
    return high, middle, low


def in_parts(row):
    return jnp.concatenate(list(split_three(row)) + [jnp.zeros((13, row.shape[1]), jnp.bfloat16)], axis=0)


def dot_parts(parts, matrix):
    out = lax.dot_general(parts, matrix, (((1,), (1,)), ((), ())), preferred_element_type=jnp.float32)
    return out[0:1] + out[1:2] + out[2:3]


def idle_kernel(*refs):
    pass


def after(array, *others):
    return pl.pallas_call(
        idle_kernel,
        out_shape=jax.ShapeDtypeStruct(array.shape, array.dtype),
        in_specs=[pl.BlockSpec(memory_space=pl.ANY)] * (1 + len(others)),
        out_specs=pl.BlockSpec(memory_space=pl.ANY),
        input_output_aliases={0: 0},
        compiler_params=params(),
        cost_estimate=cost(1),
        name="after",
    )(array, *others)


def rows_of(count, like, dtype=jnp.bfloat16):
    return jax.ShapeDtypeStruct((count, like.shape[1]), dtype)


def call(kernel, name, out_shape, *operands, tokens=()):
    def with_tokens(*refs):
        kernel(*refs[: len(operands)], *refs[len(operands) + len(tokens) :])

    return pl.pallas_call(
        with_tokens,
        out_shape=out_shape,
        in_specs=[WHOLE] * len(operands) + [pl.BlockSpec(memory_space=pl.ANY)] * len(tokens),
        out_specs=[WHOLE] * len(out_shape),
        compiler_params=params(),
        cost_estimate=cost(10**6),
        name=name,
    )(*operands, *tokens)


def inner_kernel(direction_ref, weight_ref, parts_ref, norm_ref, here_ref):
    everything = direction_ref[...]
    norm_ref[...] = jnp.broadcast_to(
        jnp.sum(everything * everything, axis=1, keepdims=True) + EPSILON, norm_ref.shape
    )
    size, width = weight_ref.shape[1], here_ref.shape[1]
    here_ref[...] = direction_ref[:, pl.ds(pl.multiple_of(lax.axis_index("tp") * width, LANES), width)]
    here = direction_ref[:, pl.ds(pl.multiple_of(lax.axis_index("ctx") * size, LANES), size)]
    parts_ref[...] = in_parts(dot_parts(in_parts(here), weight_ref[...]))


def run_inner(direction, weight):
    out_shape = [
        jax.ShapeDtypeStruct((STEP, weight.shape[0]), jnp.bfloat16),
        jax.ShapeDtypeStruct((1, LANES), jnp.float32),
        jax.ShapeDtypeStruct((1, weight.shape[1] // 2), jnp.float32),
    ]
    return call(inner_kernel, "inner", out_shape, direction, weight)


def project_kernel(begin, weight_ref, piece_ref, *outs):
    *sends, keep_ref = outs
    rows, width = keep_ref.shape
    cut = width // len(sends)
    side = lax.axis_index("tp") % 2
    for start in range(0, 2 * width, 256):
        away = start < width
        ref, to = (sends[start // cut], start % cut) if away else (keep_ref, start - width)
        which = 1 - side if away else side
        columns = pl.ds(pl.multiple_of(which * width + start % width, 256), 256)
        out = jnp.dot(piece_ref[begin : begin + rows, :], weight_ref[:, columns], preferred_element_type=jnp.float32)
        ref[:rows, to : to + 256] = out.astype(ref.dtype)


def run_project(weight, piece, begin, rows, count, *tokens):
    keep = jax.ShapeDtypeStruct((rows, weight.shape[1] // 2), jnp.float32)
    sends = [jax.ShapeDtypeStruct((rows, keep.shape[1] // count), jnp.bfloat16)] * count
    kernel = functools.partial(project_kernel, begin)
    *sends, keep = call(kernel, "project", [*sends, keep], weight, piece, tokens=tokens)
    return sends, keep


def put_behind(ref, rows, row):
    here = slice(rows, rows + STEP)
    ref[here, :] = jnp.zeros((STEP, ref.shape[1]), jnp.bfloat16)
    ref[here, : row.shape[1]] = in_parts(row)


def take_behind(ref, rows, width):
    return jnp.sum(ref[rows : rows + STEP, :width].astype(jnp.float32), axis=0, keepdims=True)


def project_level_kernel(weight_ref, far_ref, whole_ref, parts_ref, *outs):
    *sends, keep_ref, level_ref = outs
    project_kernel(0, weight_ref, far_ref, *sends, keep_ref)
    level = dot_parts(parts_ref[...], whole_ref[...]) + dot_parts(far_ref[keep_ref.shape[0] :, :], whole_ref[...])
    level_ref[...] = level
    put_behind(sends[0], keep_ref.shape[0], level)


def merge_kernel(keep_ref, core_ref, out_ref):
    for row in range(0, out_ref.shape[0], STEP):
        here = slice(row, row + STEP)
        total = keep_ref[here, :].astype(jnp.float32) + core_ref[here, :].astype(jnp.float32)
        out_ref[here, :] = total.astype(jnp.bfloat16)


def run_merge(rows, keep, core):
    (out,) = call(merge_kernel, "merge", [rows_of(rows, keep)], keep, core)
    return out


def merge_level_kernel(count, keep_ref, level_ref, *refs):
    cores, outs, total_ref = refs[:count], refs[count:-1], refs[-1]
    rows, width = keep_ref.shape
    cut, size = width // count, width // len(outs)
    for row in range(0, rows, STEP):
        here = slice(row, row + STEP)
        for i, core_ref in enumerate(cores):
            total = keep_ref[here, i * cut : (i + 1) * cut] + core_ref[here, :].astype(jnp.float32)
            to = i * cut % size
            outs[i * cut // size][here, to : to + cut] = total.astype(jnp.bfloat16)
    total = level_ref[...] + take_behind(cores[0], rows, level_ref.shape[1])
    total_ref[...] = total
    put_behind(outs[0], rows, total)


def join_kernel(*refs):
    out_ref = refs[-1]
    count = len(refs) // 2
    cut = out_ref.shape[1] // count
    for row in range(0, out_ref.shape[0], STEP):
        here = slice(row, row + STEP)
        for i in range(count):
            total = refs[i][here, :].astype(jnp.float32) + refs[count + i][here, :].astype(jnp.float32)
            out_ref[here, i * cut : (i + 1) * cut] = total.astype(jnp.bfloat16)


def is_keeper():
    return lax.axis_index("tp") // 2 == lax.axis_index("ctx")


def choose_kernel(straight_ref, level_ref, own_ref, out_ref):
    keeper = is_keeper()

    @pl.when(keeper)
    def _():
        rows = straight_ref.shape[0]
        out_ref[:rows, :] = straight_ref[...]
        put_behind(out_ref, rows, level_ref[...])

    @pl.when(jnp.logical_not(keeper))
    def _():
        out_ref[: own_ref.shape[0], :] = own_ref[...]


def finish_kernel(*refs):
    level_ref, norm_ref, direction_ref = refs[:3]
    own0, own1, (moved_ref, straight_ref, merged_ref) = refs[3:6], refs[6:9], refs[9:12]
    out_hbm, level_out_ref, out_near, sems = refs[12:]
    turned_ref = own1[-1]
    rows, width = out_near.shape
    half = straight_ref.shape[0]
    keeper = is_keeper()
    other = jnp.where(keeper, take_behind(moved_ref, half, rows), take_behind(turned_ref, half, rows))
    level = (level_ref[...] + other) / norm_ref[0:1, 0:1]
    level_out_ref[...] = level
    direction = direction_ref[...]
    column = jnp.transpose(jnp.broadcast_to(level, (LANES, rows)))

    def put(row, cut, before, behind):
        pieces, start = (before, row) if row < cut else (behind, row - cut)
        total = pieces[0][start : start + STEP, :].astype(jnp.float32)
        for piece in pieces[1:]:
            total = total + piece[start : start + STEP, :].astype(jnp.float32)
        total = total - column[row : row + STEP, 0:1] * direction
        out_near[row : row + STEP, :] = total.astype(jnp.bfloat16)

    copies = []
    count = sems.shape[0]
    for i in range(count):
        begin, end = i * rows // count, (i + 1) * rows // count

        @pl.when(keeper)
        def _():
            for row in range(begin, end, STEP):
                put(row, own0[0].shape[0], own0, own1)

        @pl.when(jnp.logical_not(keeper))
        def _():
            for row in range(begin, end, STEP):
                put(row, half, (straight_ref, turned_ref), (merged_ref,))

        here = pl.ds(begin, end - begin)
        copies.append(pltpu.make_async_copy(out_near.at[here], out_hbm.at[here], sems.at[i]))
        copies[-1].start()
    for copy in copies:
        copy.wait()


def run_finish(*operands):
    rows, width = operands[0].shape[1], operands[2].shape[1]
    return pl.pallas_call(
        finish_kernel,
        out_shape=[
            jax.ShapeDtypeStruct((rows, width), jnp.bfloat16),
            jax.ShapeDtypeStruct((1, rows), jnp.float32),
        ],
        in_specs=[WHOLE] * len(operands),
        out_specs=[AWAY, WHOLE],
        scratch_shapes=[pltpu.VMEM((rows, width), jnp.bfloat16), pltpu.SemaphoreType.DMA((4,))],
        compiler_params=params(),
        cost_estimate=cost(10**6),
        name="finish",
    )(*operands)


def plane_plan(q, k, v, short_taps, decay_rate, residue, out_weight, direction):
    rows, width = q.shape
    half = rows // 2
    early = half
    blocks = width // LANES
    axes = ("ctx", "tp")
    forward = [(p, 4 + p) for p in range(4)]
    across = [(4 * c + p, 4 * (1 - c) + p) for c in range(2) for p in range(4)]
    sibling = [(4 * c + p, 4 * c + (p ^ 1)) for c in range(2) for p in range(4)]
    pair = [(4 * c + p, 4 * c + (p ^ 2)) for c in range(2) for p in range(4)]
    inward = [(4 * c + 2 * (1 - c) + a, 4 * c + 2 * c + a) for c in range(2) for a in range(2)]
    onward = [(4 * c + 2 * c + a, 4 * (1 - c) + 2 * c + a) for c in range(2) for a in range(2)]

    ended, signal, decay, taps, edge, rate, residue, q = run_front(q, k, v, short_taps, decay_rate.T, residue.T)
    carry = lax.ppermute(ended, axes, forward)
    local, query, gain, weight, direction = run_local(
        q, signal, decay, taps, gains_of(rate, residue), out_weight, direction.reshape(1, -1)
    )
    parts, norm, direction = run_inner(direction, weight)
    first, second, whole = run_correct(carry, decay, gain, taps, edge, local, query, blocks, parts)
    far_first = lax.ppermute(first, axes, across)
    far_second = lax.ppermute(second, axes, across)

    def exchange(arrays, pairs):
        return [lax.ppermute(array, axes, pairs) for array in arrays]

    def exchange(array, pairs):
        return lax.ppermute(array, axes, pairs)

    (send,), keep0 = run_project(weight, whole, 0, early, 1)
    core0 = exchange(send, sibling)
    hop0 = exchange(run_merge(early, keep0, core0), inward)

    (send,), far_keep = run_project(weight, far_first, 0, half, 1)
    sums0 = run_merge(half, far_keep, exchange(send, sibling))
    straight = exchange(sums0, across)

    whole = after(whole, sums0)
    (own_send,), keep1 = run_project(weight, whole, early, rows - early, 1)
    one_row = jax.ShapeDtypeStruct((1, rows), jnp.float32)
    pieces, columns = 4, far_keep.shape[1] // 4
    *sends, far_keep, level = call(
        project_level_kernel,
        "project",
        [jax.ShapeDtypeStruct((half + STEP * (i == 0), columns), jnp.bfloat16) for i in range(pieces)] + [far_keep, one_row],
        weight,
        after(far_second, own_send),
        whole,
        parts,
    )
    columns = far_keep.shape[1] // 2
    *sums1, level = call(
        functools.partial(merge_level_kernel, pieces),
        "merge",
        [jax.ShapeDtypeStruct((half + STEP * (i == 0), columns), jnp.bfloat16) for i in range(2)] + [one_row],
        far_keep,
        level,
        *[exchange(send, sibling) for send in sends],
    )
    moved = [exchange(piece, inward) for piece in sums1]
    core1 = exchange(own_send, sibling)
    own1 = run_merge(rows - early, keep1, core1)

    (merged,) = call(join_kernel, "merge", [rows_of(half, far_keep)], *sums1, *moved)
    merged = exchange(merged, onward)
    payload = rows_of(max(half + STEP, rows - early), own1)
    (turned,) = call(choose_kernel, "choose", [payload], straight, level, own1, tokens=(hop0,))
    turned = exchange(turned, pair)
    ablated, level = run_finish(
        level, norm, direction, keep0, core0, hop0, keep1, core1, turned, moved[0], straight, merged
    )
    return ablated, level.reshape(rows)


def gather_plan(q, k, v, short_taps, decay_rate, residue, out_weight, direction):
    rows, width = q.shape
    blocks = width // LANES
    modes = decay_rate.shape[1]
    tp = lax.axis_index("tp")
    ctx_size = lax.axis_size("ctx")
    next_one = [(i, i + 1) for i in range(ctx_size - 1)]
    ended, signal, decay, taps, edge, rate, residue, q = run_front(q, k, v, short_taps, decay_rate.T, residue.T)
    halo = lax.ppermute(ended[modes * blocks :], "ctx", next_one)
    local, query, gain = run_local(q, signal, decay, taps, gains_of(rate, residue))
    k2, k1, v2, v1 = [halo[i * blocks : (i + 1) * blocks] for i in range(4)]
    tap = taps.reshape(9, blocks, LANES)
    key0, key1, value0, value1 = edge.reshape(4, blocks, LANES)
    extra0 = (key0 + tap[4] * k1 + tap[5] * k2) * (value0 + tap[7] * v1 + tap[8] * v2) - key0 * value0
    extra1 = (key1 + tap[5] * k1) * (value1 + tap[8] * v1) - key1 * value1
    wide_rate = decay_rate.T.reshape(modes, blocks, LANES)
    state = (
        ended[: modes * blocks].reshape(modes, blocks, LANES)
        + jnp.exp(-wide_rate * (rows - 1)) * extra0
        + jnp.exp(-wide_rate * (rows - 2)) * extra1
    )
    reach = 1
    while reach < ctx_size:
        earlier = lax.ppermute(state, "ctx", [(i, i + reach) for i in range(ctx_size - reach)])
        state = state + jnp.exp(-wide_rate * (rows * reach)) * earlier
        reach *= 2
    start = lax.ppermute(state, "ctx", next_one).reshape(modes * blocks, LANES)
    carry = jnp.concatenate([start, halo], axis=0)
    (gated,) = run_correct(carry, decay, gain, taps, edge, local, query, blocks)
    partial_terms = lax.dot_general(
        gated,
        lax.all_gather(out_weight, "ctx", axis=1, tiled=True),
        (((1,), (0,)), ((), ())),
        preferred_element_type=jnp.float32,
    )
    summed = lax.psum_scatter(
        partial_terms.astype(jnp.bfloat16), "tp", scatter_dimension=1, tiled=True
    ).astype(jnp.float32)
    width_here = summed.shape[1]
    direction_here = lax.dynamic_slice_in_dim(direction, tp * width_here, width_here, 0)
    norm_total = jnp.sum(direction * direction) + EPSILON
    local_inner = jnp.dot(summed, direction_here, precision=HIGHEST)
    feature_level = lax.psum(local_inner, "tp") / norm_total
    ablated = (summed - feature_level[:, None] * direction_here[None, :]).astype(jnp.bfloat16)
    return ablated, feature_level


def solution(mesh):
    placed = (
        P(("dp", "ctx"), "tp"),
        P(("dp", "ctx"), "tp"),
        P(("dp", "ctx"), "tp"),
        P(None, None, "tp"),
        P("tp", None),
        P("tp", None),
        P("tp", "ctx"),
        P(),
    )
    plane = mesh.shape["ctx"] == 2 and mesh.shape["tp"] == 4
    return jax.shard_map(
        plane_plan if plane else gather_plan,
        mesh=mesh,
        in_specs=placed,
        out_specs=(P(("dp", "ctx"), "tp"), P(("dp", "ctx"))),
        check_vma=False,
    )
```

```python
import functools

import jax
import jax.numpy as jnp
from jax import lax
from jax.experimental import pallas as pl
from jax.experimental.pallas import tpu as pltpu
from jax.sharding import PartitionSpec as P

EPSILON = 1e-06
HIGHEST = lax.Precision.HIGHEST
LANES = 128
GROUP = 8
STEP = 16
WHOLE = pl.BlockSpec(memory_space=pltpu.VMEM)
AWAY = pl.BlockSpec(memory_space=pltpu.HBM)


def params(mebibytes=20):
    return pltpu.CompilerParams(vmem_limit_bytes=mebibytes * 1024 * 1024)


def cost(flops):
    return pl.CostEstimate(flops=flops, bytes_accessed=1024, transcendentals=0)


def spread(source, scratch, row, to):
    blocks = source.shape[1] // LANES
    for block in range(blocks):
        piece = source[pl.ds(row, STEP), block * LANES : (block + 1) * LANES].astype(jnp.float32)
        for half in range(STEP // GROUP):
            start = (half * blocks + block) * GROUP
            scratch[pl.ds(to + start, GROUP), :] = piece[half * GROUP : (half + 1) * GROUP]


def spread_rows(source, target):
    count, width = source.shape
    blocks = width // LANES
    for block in range(blocks):
        target[pl.ds(block, count, stride=blocks), :] = source[:, block * LANES : (block + 1) * LANES]


def place_of(index, blocks):
    return pl.ds((index // GROUP) * (blocks * GROUP) + index % GROUP, blocks, stride=GROUP)


def tile(ref, index, blocks):
    return ref[index * blocks : (index + 1) * blocks, :]


def moving_tile(index, blocks):
    return pl.ds(pl.multiple_of(index * blocks, blocks), blocks)


def front_kernel(*refs):
    k_hbm, v_hbm, q_hbm, taps_hbm, rate_hbm, residue_hbm = refs[:6]
    carry_ref, signal_ref, decay_ref, taps_ref, edge_ref, rate_ref, residue_ref, q_near = refs[6:14]
    k_near, v_near, taps_near, k_wide, v_wide, sems, late_sems = refs[-7:]
    rows, width = k_near.shape
    blocks = width // LANES
    modes = rate_ref.shape[0]
    pieces = sems.shape[0] // 2 - 1
    height = rows // pieces

    def part(i):
        here = pl.ds(i * height, height)
        return (
            pltpu.make_async_copy(k_hbm.at[here], k_near.at[here], sems.at[2 * i]),
            pltpu.make_async_copy(v_hbm.at[here], v_near.at[here], sems.at[2 * i + 1]),
        )

    rate_copy = pltpu.make_async_copy(rate_hbm, rate_ref, sems.at[2 * pieces])
    taps_copy = pltpu.make_async_copy(taps_hbm, taps_near, sems.at[2 * pieces + 1])
    late = [(residue_hbm, residue_ref), (q_hbm, q_near)]
    late = [pltpu.make_async_copy(source, target, late_sems.at[i]) for i, (source, target) in enumerate(late)]
    rate_copy.start()
    taps_copy.start()
    for i in range(pieces):
        for copy in part(i):
            copy.start()
    for copy in late:
        copy.start()
    rate_copy.wait()
    taps_copy.wait()
    spread_rows(jnp.exp(-rate_ref[...]), decay_ref)
    for i in range(3):
        for block in range(blocks):
            taps_ref[pl.ds(3 * i * blocks + block, 3, stride=blocks), :] = taps_near[
                i, :, block * LANES : (block + 1) * LANES
            ]
    zero = jnp.zeros((blocks, LANES), jnp.float32)
    key_taps = [tile(taps_ref, 3 + j, blocks) for j in range(3)]
    value_taps = [tile(taps_ref, 6 + j, blocks) for j in range(3)]
    decay = [tile(decay_ref, m, blocks) for m in range(modes)]

    def step(row, held, first):
        spread(k_near, k_wide, row, 0)
        spread(v_near, v_wide, row, 0)
        state, (k2, k1, v2, v1) = list(held[:modes]), held[modes:]
        for index in range(STEP):
            k0 = k_wide[place_of(index, blocks), :]
            v0 = v_wide[place_of(index, blocks), :]
            key = key_taps[0] * k0 + key_taps[1] * k1 + key_taps[2] * k2
            value = value_taps[0] * v0 + value_taps[1] * v1 + value_taps[2] * v2
            if first and index < 2:
                edge_ref[index * blocks : (index + 1) * blocks, :] = key
                edge_ref[(2 + index) * blocks : (3 + index) * blocks, :] = value
            signal = key * value
            signal_ref[moving_tile(row + index, blocks), :] = signal
            state = [decay[m] * state[m] + signal for m in range(modes)]
            k2, k1, v2, v1 = k1, k0, v1, v0
        return tuple(state) + (k2, k1, v2, v1)

    held = (zero,) * (modes + 4)
    for i in range(pieces):
        for copy in part(i):
            copy.wait()
        begin = 0
        if i == 0:
            held = step(0, held, True)
            begin = 1
        held = lax.fori_loop(
            begin,
            height // STEP,
            lambda j, held, i=i: step(pl.multiple_of(i * height + j * STEP, STEP), held, False),
            held,
        )
    for m in range(modes + 4):
        carry_ref[m * blocks : (m + 1) * blocks, :] = held[m]
    for copy in late:
        copy.wait()
    spread(q_near, k_wide, rows - STEP, 0)
    for i in range(2):
        start = (modes + 4 + i) * blocks
        carry_ref[start : start + blocks, :] = k_wide[place_of(STEP - 2 + i, blocks), :]


def far(x):
    return pltpu.with_memory_space_constraint(x, pltpu.HBM)


def run_front(q, k, v, short_taps, rate, residue):
    rows, width = k.shape
    modes = rate.shape[0]
    blocks = width // LANES
    pieces = 4

    def wide(n):
        return jax.ShapeDtypeStruct((n * blocks, LANES), jnp.float32)

    def like(x):
        return jax.ShapeDtypeStruct(x.shape, x.dtype)

    out_shape = [wide(modes + 6), wide(rows), wide(modes), wide(9), wide(4), like(rate), like(residue), like(q)]
    return pl.pallas_call(
        front_kernel,
        out_shape=out_shape,
        in_specs=[AWAY] * 6,
        out_specs=[WHOLE] * len(out_shape),
        scratch_shapes=[
            pltpu.VMEM((rows, width), jnp.bfloat16),
            pltpu.VMEM((rows, width), jnp.bfloat16),
            pltpu.VMEM(short_taps.shape, jnp.float32),
            pltpu.VMEM((STEP * blocks, LANES), jnp.float32),
            pltpu.VMEM((STEP * blocks, LANES), jnp.float32),
            pltpu.SemaphoreType.DMA((2 * pieces + 2,)),
            pltpu.SemaphoreType.DMA((2,)),
        ],
        compiler_params=params(),
        cost_estimate=cost(10**8),
        name="front",
    )(*[far(x) for x in (k, v, q, short_taps, rate, residue)])


def local_kernel(q_near, signal_ref, decay_ref, taps_ref, gain_near, *refs):
    copies = []
    if len(refs) > 4:
        weight_hbm, direction_hbm, weight_ref, direction_ref, sems = refs[:2] + refs[5:7] + refs[-1:]
        refs = refs[2:5] + refs[7:-1]
        count = sems.shape[0] - 1
        copies.append(pltpu.make_async_copy(direction_hbm, direction_ref, sems.at[count]))
        copies[-1].start()
        depth = weight_ref.shape[0] // count
        for i in range(count):
            here = pl.ds(i * depth, depth)
            copies.append(pltpu.make_async_copy(weight_hbm.at[here], weight_ref.at[here], sems.at[i]))
            copies[-1].start()
    out_ref, query_ref, gain_ref, q_wide = refs
    rows, width = q_near.shape
    blocks = width // LANES
    modes = gain_near.shape[0]
    spread_rows(gain_near[...], gain_ref)
    zero = jnp.zeros((blocks, LANES), jnp.float32)
    taps = [tile(taps_ref, j, blocks) for j in range(3)]
    decay = [tile(decay_ref, m, blocks) for m in range(modes)]
    gain = [tile(gain_ref, m, blocks) for m in range(modes)]

    def step(j, held):
        row = pl.multiple_of(j * STEP, STEP)
        spread(q_near, q_wide, row, 0)
        state, (q2, q1) = list(held[:modes]), held[modes:]
        for index in range(STEP):
            q0 = q_wide[place_of(index, blocks), :]
            here = moving_tile(row + index, blocks)
            signal = signal_ref[here, :]
            query_ref[here, :] = taps[0] * q0 + taps[1] * q1 + taps[2] * q2
            state = [decay[m] * state[m] + signal for m in range(modes)]
            sums = [gain[m] * state[m] for m in range(modes)]
            while len(sums) > 1:
                sums = [sums[i] + sums[i + 1] for i in range(0, len(sums), 2)]
            out_ref[here, :] = sums[0]
            q2, q1 = q1, q0
        return tuple(state) + (q2, q1)

    lax.fori_loop(0, rows // STEP, step, (zero,) * (modes + 2))
    for copy in copies:
        copy.wait()


def run_local(q, signal, decay, taps, gain, *weight):
    rows, width = q.shape
    blocks = width // LANES
    wide = jax.ShapeDtypeStruct((rows * blocks, LANES), jnp.float32)
    out_shape = [wide, wide, jax.ShapeDtypeStruct(decay.shape, jnp.float32)]
    scratch_shapes = [pltpu.VMEM((STEP * blocks, LANES), jnp.float32)]
    if weight:
        out_shape += [jax.ShapeDtypeStruct(x.shape, x.dtype) for x in weight]
        scratch_shapes.append(pltpu.SemaphoreType.DMA((5,)))
        weight = tuple(far(x) for x in weight)
    return pl.pallas_call(
        local_kernel,
        out_shape=out_shape,
        in_specs=[WHOLE] * 5 + [AWAY] * len(weight),
        out_specs=[WHOLE] * len(out_shape),
        scratch_shapes=scratch_shapes,
        compiler_params=params(),
        cost_estimate=cost(10**6),
        name="local_filter",
    )(q, signal, decay, taps, gain, *weight)


def correct_kernel(blocks, carry_ref, decay_ref, gain_ref, taps_ref, edge_ref, local_ref, query_ref, *refs):
    wide, outs = refs[-1], refs[:-1]
    rows = local_ref.shape[0] // blocks
    if len(outs) > 1:
        outs = outs[1:]
        outs[1][rows // 2 :, :] = refs[0][...]
    modes = decay_ref.shape[0] // blocks
    carried = jnp.where(lax.axis_index("ctx") > 0, 1.0, 0.0)
    k2, k1, v2, v1, q2, q1 = [carried * tile(carry_ref, modes + i, blocks) for i in range(6)]
    tap = [tile(taps_ref, i, blocks) for i in range(9)]
    key0, key1, value0, value1 = [tile(edge_ref, i, blocks) for i in range(4)]
    extra = [
        (key0 + tap[4] * k1 + tap[5] * k2) * (value0 + tap[7] * v1 + tap[8] * v2) - key0 * value0,
        (key1 + tap[5] * k1) * (value1 + tap[8] * v1) - key1 * value1,
    ]
    query_extra = [tap[1] * q1 + tap[2] * q2, tap[2] * q1]
    state = [tile(gain_ref, m, blocks) * (carried * tile(carry_ref, m, blocks)) for m in range(modes)]
    decay = [tile(decay_ref, m, blocks) for m in range(modes)]

    def step(row, state, first, piece_ref, start):
        state = list(state)
        for index in range(STEP):
            here = moving_tile(row + index, blocks)
            state = [decay[m] * state[m] for m in range(modes)]
            query = query_ref[here, :]
            if first and index < 2:
                state = [state[m] + tile(gain_ref, m, blocks) * extra[index] for m in range(modes)]
                query = query + query_extra[index]
            sums = state
            while len(sums) > 1:
                sums = [sums[i] + sums[i + 1] for i in range(0, len(sums), 2)]
            wide[place_of(index, blocks), :] = query * (local_ref[here, :] + sums[0])
        for block in range(blocks):
            halves = [
                wide[(half * blocks + block) * GROUP : (half * blocks + block + 1) * GROUP, :]
                for half in range(STEP // GROUP)
            ]
            rounded = jnp.concatenate(halves, axis=0).astype(jnp.bfloat16)
            columns = slice(block * LANES, (block + 1) * LANES)
            outs[-1][pl.ds(row, STEP), columns] = rounded
            if piece_ref is not None:
                piece_ref[pl.ds(pl.multiple_of(row - start, STEP), STEP), columns] = rounded
        return tuple(state)

    state = tuple(state)
    start = 0
    for piece_ref in outs[:-1] or [None]:
        end = start + (rows if piece_ref is None else rows // 2)
        begin = start // STEP
        if start == 0:
            state = step(0, state, True, piece_ref, 0)
            begin = 1
        state = lax.fori_loop(
            begin,
            end // STEP,
            lambda j, state, start=start, piece_ref=piece_ref: step(
                pl.multiple_of(j * STEP, STEP), state, False, piece_ref, start
            ),
            state,
        )
        start = end


def run_correct(carry, decay, gain, taps, edge, local, query, blocks, *parts):
    rows = local.shape[0] // blocks
    width = blocks * LANES
    heights = ([rows // 2, rows // 2 + STEP] if parts else []) + [rows]
    return pl.pallas_call(
        functools.partial(correct_kernel, blocks),
        out_shape=[jax.ShapeDtypeStruct((height, width), jnp.bfloat16) for height in heights],
        in_specs=[WHOLE] * (7 + len(parts)),
        out_specs=[WHOLE] * len(heights),
        scratch_shapes=[pltpu.VMEM((STEP * blocks, LANES), jnp.float32)],
        compiler_params=params(),
        cost_estimate=cost(10**8),
        name="carried_filter",
    )(carry, decay, gain, taps, edge, local, query, *parts)


def gains_of(rate, residue):
    return residue * jnp.sqrt(-jnp.expm1(-2.0 * rate)) * rate.shape[0] ** (-0.5)


def split_three(x):
    high = x.astype(jnp.bfloat16)
    rest = x - high.astype(jnp.float32)
    middle = rest.astype(jnp.bfloat16)
    low = (rest - middle.astype(jnp.float32)).astype(jnp.bfloat16)
    return high, middle, low


def in_parts(row):
    return jnp.concatenate(list(split_three(row)) + [jnp.zeros((13, row.shape[1]), jnp.bfloat16)], axis=0)


def dot_parts(parts, matrix):
    out = lax.dot_general(parts, matrix, (((1,), (1,)), ((), ())), preferred_element_type=jnp.float32)
    return out[0:1] + out[1:2] + out[2:3]


def idle_kernel(*refs):
    pass


def after(array, *others):
    return pl.pallas_call(
        idle_kernel,
        out_shape=jax.ShapeDtypeStruct(array.shape, array.dtype),
        in_specs=[pl.BlockSpec(memory_space=pl.ANY)] * (1 + len(others)),
        out_specs=pl.BlockSpec(memory_space=pl.ANY),
        input_output_aliases={0: 0},
        compiler_params=params(),
        cost_estimate=cost(1),
        name="after",
    )(array, *others)


def rows_of(count, like, dtype=jnp.bfloat16):
    return jax.ShapeDtypeStruct((count, like.shape[1]), dtype)


def call(kernel, name, out_shape, *operands, tokens=()):
    def with_tokens(*refs):
        kernel(*refs[: len(operands)], *refs[len(operands) + len(tokens) :])

    return pl.pallas_call(
        with_tokens,
        out_shape=out_shape,
        in_specs=[WHOLE] * len(operands) + [pl.BlockSpec(memory_space=pl.ANY)] * len(tokens),
        out_specs=[WHOLE] * len(out_shape),
        compiler_params=params(),
        cost_estimate=cost(10**6),
        name=name,
    )(*operands, *tokens)


def inner_kernel(direction_ref, weight_ref, parts_ref, norm_ref, here_ref):
    everything = direction_ref[...]
    norm_ref[...] = jnp.broadcast_to(
        jnp.sum(everything * everything, axis=1, keepdims=True) + EPSILON, norm_ref.shape
    )
    size, width = weight_ref.shape[1], here_ref.shape[1]
    here_ref[...] = direction_ref[:, pl.ds(pl.multiple_of(lax.axis_index("tp") * width, LANES), width)]
    here = direction_ref[:, pl.ds(pl.multiple_of(lax.axis_index("ctx") * size, LANES), size)]
    parts_ref[...] = in_parts(dot_parts(in_parts(here), weight_ref[...]))


def run_inner(direction, weight):
    out_shape = [
        jax.ShapeDtypeStruct((STEP, weight.shape[0]), jnp.bfloat16),
        jax.ShapeDtypeStruct((1, LANES), jnp.float32),
        jax.ShapeDtypeStruct((1, weight.shape[1] // 2), jnp.float32),
    ]
    return call(inner_kernel, "inner", out_shape, direction, weight)


def project_kernel(begin, weight_ref, piece_ref, *outs):
    *sends, keep_ref = outs
    rows, width = keep_ref.shape
    cut = width // len(sends)
    side = lax.axis_index("tp") % 2
    for start in range(0, 2 * width, 256):
        away = start < width
        ref, to = (sends[start // cut], start % cut) if away else (keep_ref, start - width)
        which = 1 - side if away else side
        columns = pl.ds(pl.multiple_of(which * width + start % width, 256), 256)
        out = jnp.dot(piece_ref[begin : begin + rows, :], weight_ref[:, columns], preferred_element_type=jnp.float32)
        ref[:rows, to : to + 256] = out.astype(ref.dtype)


def run_project(weight, piece, begin, rows, count, *tokens):
    keep = jax.ShapeDtypeStruct((rows, weight.shape[1] // 2), jnp.float32)
    sends = [jax.ShapeDtypeStruct((rows, keep.shape[1] // count), jnp.bfloat16)] * count
    kernel = functools.partial(project_kernel, begin)
    *sends, keep = call(kernel, "project", [*sends, keep], weight, piece, tokens=tokens)
    return sends, keep


def put_behind(ref, rows, row):
    here = slice(rows, rows + STEP)
    ref[here, :] = jnp.zeros((STEP, ref.shape[1]), jnp.bfloat16)
    ref[here, : row.shape[1]] = in_parts(row)


def take_behind(ref, rows, width):
    return jnp.sum(ref[rows : rows + STEP, :width].astype(jnp.float32), axis=0, keepdims=True)


def project_level_kernel(weight_ref, far_ref, whole_ref, parts_ref, *outs):
    *sends, keep_ref, level_ref = outs
    project_kernel(0, weight_ref, far_ref, *sends, keep_ref)
    level = dot_parts(parts_ref[...], whole_ref[...]) + dot_parts(far_ref[keep_ref.shape[0] :, :], whole_ref[...])
    level_ref[...] = level
    put_behind(sends[0], keep_ref.shape[0], level)


def merge_kernel(keep_ref, core_ref, out_ref):
    for row in range(0, out_ref.shape[0], STEP):
        here = slice(row, row + STEP)
        total = keep_ref[here, :].astype(jnp.float32) + core_ref[here, :].astype(jnp.float32)
        out_ref[here, :] = total.astype(jnp.bfloat16)


def run_merge(rows, keep, core):
    (out,) = call(merge_kernel, "merge", [rows_of(rows, keep)], keep, core)
    return out


def merge_level_kernel(count, keep_ref, level_ref, *refs):
    cores, outs, total_ref = refs[:count], refs[count:-1], refs[-1]
    rows, width = keep_ref.shape
    cut, size = width // count, width // len(outs)
    for row in range(0, rows, STEP):
        here = slice(row, row + STEP)
        for i, core_ref in enumerate(cores):
            total = keep_ref[here, i * cut : (i + 1) * cut] + core_ref[here, :].astype(jnp.float32)
            to = i * cut % size
            outs[i * cut // size][here, to : to + cut] = total.astype(jnp.bfloat16)
    total = level_ref[...] + take_behind(cores[0], rows, level_ref.shape[1])
    total_ref[...] = total
    put_behind(outs[0], rows, total)


def join_kernel(*refs):
    out_ref = refs[-1]
    count = len(refs) // 2
    cut = out_ref.shape[1] // count
    for row in range(0, out_ref.shape[0], STEP):
        here = slice(row, row + STEP)
        for i in range(count):
            total = refs[i][here, :].astype(jnp.float32) + refs[count + i][here, :].astype(jnp.float32)
            out_ref[here, i * cut : (i + 1) * cut] = total.astype(jnp.bfloat16)


def is_keeper():
    return lax.axis_index("tp") // 2 == lax.axis_index("ctx")


def choose_kernel(straight_ref, level_ref, own_ref, out_ref):
    keeper = is_keeper()

    @pl.when(keeper)
    def _():
        rows = straight_ref.shape[0]
        out_ref[:rows, :] = straight_ref[...]
        put_behind(out_ref, rows, level_ref[...])

    @pl.when(jnp.logical_not(keeper))
    def _():
        out_ref[: own_ref.shape[0], :] = own_ref[...]


def finish_kernel(*refs):
    level_ref, norm_ref, direction_ref = refs[:3]
    own0, own1, (moved_ref, straight_ref, merged_ref) = refs[3:6], refs[6:9], refs[9:12]
    out_hbm, level_out_ref, out_near, sems = refs[12:]
    turned_ref = own1[-1]
    rows, width = out_near.shape
    half = straight_ref.shape[0]
    keeper = is_keeper()
    other = jnp.where(keeper, take_behind(moved_ref, half, rows), take_behind(turned_ref, half, rows))
    level = (level_ref[...] + other) / norm_ref[0:1, 0:1]
    level_out_ref[...] = level
    direction = direction_ref[...]
    column = jnp.transpose(jnp.broadcast_to(level, (LANES, rows)))

    def put(row, cut, before, behind):
        pieces, start = (before, row) if row < cut else (behind, row - cut)
        total = pieces[0][start : start + STEP, :].astype(jnp.float32)
        for piece in pieces[1:]:
            total = total + piece[start : start + STEP, :].astype(jnp.float32)
        total = total - column[row : row + STEP, 0:1] * direction
        out_near[row : row + STEP, :] = total.astype(jnp.bfloat16)

    copies = []
    count = sems.shape[0]
    for i in range(count):
        begin, end = i * rows // count, (i + 1) * rows // count

        @pl.when(keeper)
        def _():
            for row in range(begin, end, STEP):
                put(row, own0[0].shape[0], own0, own1)

        @pl.when(jnp.logical_not(keeper))
        def _():
            for row in range(begin, end, STEP):
                put(row, half, (straight_ref, turned_ref), (merged_ref,))

        here = pl.ds(begin, end - begin)
        copies.append(pltpu.make_async_copy(out_near.at[here], out_hbm.at[here], sems.at[i]))
        copies[-1].start()
    for copy in copies:
        copy.wait()


def run_finish(*operands):
    rows, width = operands[0].shape[1], operands[2].shape[1]
    return pl.pallas_call(
        finish_kernel,
        out_shape=[
            jax.ShapeDtypeStruct((rows, width), jnp.bfloat16),
            jax.ShapeDtypeStruct((1, rows), jnp.float32),
        ],
        in_specs=[WHOLE] * len(operands),
        out_specs=[AWAY, WHOLE],
        scratch_shapes=[pltpu.VMEM((rows, width), jnp.bfloat16), pltpu.SemaphoreType.DMA((4,))],
        compiler_params=params(),
        cost_estimate=cost(10**6),
        name="finish",
    )(*operands)


def plane_plan(q, k, v, short_taps, decay_rate, residue, out_weight, direction):
    rows, width = q.shape
    half = rows // 2
    early = half
    blocks = width // LANES
    axes = ("ctx", "tp")
    across = [(4 * c + p, 4 * (1 - c) + p) for c in range(2) for p in range(4)]
    sibling = [(4 * c + p, 4 * c + (p ^ 1)) for c in range(2) for p in range(4)]
    pair = [(4 * c + p, 4 * c + (p ^ 2)) for c in range(2) for p in range(4)]

    ended, signal, decay, taps, edge, rate, residue, q = run_front(q, k, v, short_taps, decay_rate.T, residue.T)
    carry = lax.ppermute(ended, axes, across)
    local, query, gain, weight, direction = run_local(
        q, signal, decay, taps, gains_of(rate, residue), out_weight, direction.reshape(1, -1)
    )
    parts, norm, direction = run_inner(direction, weight)
    first, second, whole = run_correct(carry, decay, gain, taps, edge, local, query, blocks, parts)
    far_first = lax.ppermute(first, axes, across)
    far_second = lax.ppermute(second, axes, across)

    def exchange(arrays, pairs):
        return [lax.ppermute(array, axes, pairs) for array in arrays]

    def exchange(array, pairs):
        return lax.ppermute(array, axes, pairs)

    (send,), keep0 = run_project(weight, whole, 0, early, 1)
    core0 = exchange(send, sibling)
    hop0 = exchange(run_merge(early, keep0, core0), pair)

    (send,), far_keep = run_project(weight, far_first, 0, half, 1)
    sums0 = run_merge(half, far_keep, exchange(send, sibling))
    straight = exchange(sums0, across)

    whole = after(whole, sums0)
    (own_send,), keep1 = run_project(weight, whole, early, rows - early, 1)
    one_row = jax.ShapeDtypeStruct((1, rows), jnp.float32)
    pieces, columns = 4, far_keep.shape[1] // 4
    *sends, far_keep, level = call(
        project_level_kernel,
        "project",
        [jax.ShapeDtypeStruct((half + STEP * (i == 0), columns), jnp.bfloat16) for i in range(pieces)] + [far_keep, one_row],
        weight,
        after(far_second, own_send),
        whole,
        parts,
    )
    columns = far_keep.shape[1] // 2
    *sums1, level = call(
        functools.partial(merge_level_kernel, pieces),
        "merge",
        [jax.ShapeDtypeStruct((half + STEP * (i == 0), columns), jnp.bfloat16) for i in range(2)] + [one_row],
        far_keep,
        level,
        *[exchange(send, sibling) for send in sends],
    )
    moved = [exchange(piece, pair) for piece in sums1]
    core1 = exchange(own_send, sibling)
    own1 = run_merge(rows - early, keep1, core1)

    (merged,) = call(join_kernel, "merge", [rows_of(half, far_keep)], *sums1, *moved)
    merged = exchange(merged, across)
    payload = rows_of(max(half + STEP, rows - early), own1)
    (turned,) = call(choose_kernel, "choose", [payload], straight, level, own1, tokens=(hop0,))
    turned = exchange(turned, pair)
    ablated, level = run_finish(
        level, norm, direction, keep0, core0, hop0, keep1, core1, turned, moved[0], straight, merged
    )
    return ablated, level.reshape(rows)


def gather_plan(q, k, v, short_taps, decay_rate, residue, out_weight, direction):
    rows, width = q.shape
    blocks = width // LANES
    modes = decay_rate.shape[1]
    tp = lax.axis_index("tp")
    ctx_size = lax.axis_size("ctx")
    next_one = [(i, i + 1) for i in range(ctx_size - 1)]
    ended, signal, decay, taps, edge, rate, residue, q = run_front(q, k, v, short_taps, decay_rate.T, residue.T)
    halo = lax.ppermute(ended[modes * blocks :], "ctx", next_one)
    local, query, gain = run_local(q, signal, decay, taps, gains_of(rate, residue))
    k2, k1, v2, v1 = [halo[i * blocks : (i + 1) * blocks] for i in range(4)]
    tap = taps.reshape(9, blocks, LANES)
    key0, key1, value0, value1 = edge.reshape(4, blocks, LANES)
    extra0 = (key0 + tap[4] * k1 + tap[5] * k2) * (value0 + tap[7] * v1 + tap[8] * v2) - key0 * value0
    extra1 = (key1 + tap[5] * k1) * (value1 + tap[8] * v1) - key1 * value1
    wide_rate = decay_rate.T.reshape(modes, blocks, LANES)
    state = (
        ended[: modes * blocks].reshape(modes, blocks, LANES)
        + jnp.exp(-wide_rate * (rows - 1)) * extra0
        + jnp.exp(-wide_rate * (rows - 2)) * extra1
    )
    reach = 1
    while reach < ctx_size:
        earlier = lax.ppermute(state, "ctx", [(i, i + reach) for i in range(ctx_size - reach)])
        state = state + jnp.exp(-wide_rate * (rows * reach)) * earlier
        reach *= 2
    start = lax.ppermute(state, "ctx", next_one).reshape(modes * blocks, LANES)
    carry = jnp.concatenate([start, halo], axis=0)
    (gated,) = run_correct(carry, decay, gain, taps, edge, local, query, blocks)
    partial_terms = lax.dot_general(
        gated,
        lax.all_gather(out_weight, "ctx", axis=1, tiled=True),
        (((1,), (0,)), ((), ())),
        preferred_element_type=jnp.float32,
    )
    summed = lax.psum_scatter(
        partial_terms.astype(jnp.bfloat16), "tp", scatter_dimension=1, tiled=True
    ).astype(jnp.float32)
    width_here = summed.shape[1]
    direction_here = lax.dynamic_slice_in_dim(direction, tp * width_here, width_here, 0)
    norm_total = jnp.sum(direction * direction) + EPSILON
    local_inner = jnp.dot(summed, direction_here, precision=HIGHEST)
    feature_level = lax.psum(local_inner, "tp") / norm_total
    ablated = (summed - feature_level[:, None] * direction_here[None, :]).astype(jnp.bfloat16)
    return ablated, feature_level


def solution(mesh):
    placed = (
        P(("dp", "ctx"), "tp"),
        P(("dp", "ctx"), "tp"),
        P(("dp", "ctx"), "tp"),
        P(None, None, "tp"),
        P("tp", None),
        P("tp", None),
        P("tp", "ctx"),
        P(),
    )
    plane = mesh.shape["ctx"] == 2 and mesh.shape["tp"] == 4
    return jax.shard_map(
        plane_plan if plane else gather_plan,
        mesh=mesh,
        in_specs=placed,
        out_specs=(P(("dp", "ctx"), "tp"), P(("dp", "ctx"))),
        check_vma=False,
    )
```

```python
import functools

import jax
import jax.numpy as jnp
from jax import lax
from jax.experimental import pallas as pl
from jax.experimental.pallas import tpu as pltpu
from jax.sharding import PartitionSpec as P

EPSILON = 1e-06
HIGHEST = lax.Precision.HIGHEST
LANES = 128
GROUP = 8
STEP = 16
WHOLE = pl.BlockSpec(memory_space=pltpu.VMEM)
AWAY = pl.BlockSpec(memory_space=pltpu.HBM)


def params(mebibytes=20):
    return pltpu.CompilerParams(vmem_limit_bytes=mebibytes * 1024 * 1024)


def cost(flops):
    return pl.CostEstimate(flops=flops, bytes_accessed=1024, transcendentals=0)


def spread(source, scratch, row, to):
    blocks = source.shape[1] // LANES
    for block in range(blocks):
        piece = source[pl.ds(row, STEP), block * LANES : (block + 1) * LANES].astype(jnp.float32)
        for half in range(STEP // GROUP):
            start = (half * blocks + block) * GROUP
            scratch[pl.ds(to + start, GROUP), :] = piece[half * GROUP : (half + 1) * GROUP]


def spread_rows(source, target):
    count, width = source.shape
    blocks = width // LANES
    for block in range(blocks):
        target[pl.ds(block, count, stride=blocks), :] = source[:, block * LANES : (block + 1) * LANES]


def place_of(index, blocks):
    return pl.ds((index // GROUP) * (blocks * GROUP) + index % GROUP, blocks, stride=GROUP)


def tile(ref, index, blocks):
    return ref[index * blocks : (index + 1) * blocks, :]


def moving_tile(index, blocks):
    return pl.ds(pl.multiple_of(index * blocks, blocks), blocks)


def front_kernel(*refs):
    k_hbm, v_hbm, q_hbm, taps_hbm, rate_hbm, residue_hbm = refs[:6]
    carry_ref, signal_ref, decay_ref, taps_ref, edge_ref, rate_ref, residue_ref, q_near = refs[6:14]
    k_near, v_near, taps_near, k_wide, v_wide, sems, late_sems = refs[-7:]
    rows, width = k_near.shape
    blocks = width // LANES
    modes = rate_ref.shape[0]
    pieces = sems.shape[0] // 2 - 1
    height = rows // pieces

    def part(i):
        here = pl.ds(i * height, height)
        return (
            pltpu.make_async_copy(k_hbm.at[here], k_near.at[here], sems.at[2 * i]),
            pltpu.make_async_copy(v_hbm.at[here], v_near.at[here], sems.at[2 * i + 1]),
        )

    rate_copy = pltpu.make_async_copy(rate_hbm, rate_ref, sems.at[2 * pieces])
    taps_copy = pltpu.make_async_copy(taps_hbm, taps_near, sems.at[2 * pieces + 1])
    late = [(residue_hbm, residue_ref), (q_hbm, q_near)]
    late = [pltpu.make_async_copy(source, target, late_sems.at[i]) for i, (source, target) in enumerate(late)]
    rate_copy.start()
    taps_copy.start()
    for i in range(pieces):
        for copy in part(i):
            copy.start()
    for copy in late:
        copy.start()
    rate_copy.wait()
    taps_copy.wait()
    spread_rows(jnp.exp(-rate_ref[...]), decay_ref)
    for i in range(3):
        for block in range(blocks):
            taps_ref[pl.ds(3 * i * blocks + block, 3, stride=blocks), :] = taps_near[
                i, :, block * LANES : (block + 1) * LANES
            ]
    zero = jnp.zeros((blocks, LANES), jnp.float32)
    key_taps = [tile(taps_ref, 3 + j, blocks) for j in range(3)]
    value_taps = [tile(taps_ref, 6 + j, blocks) for j in range(3)]
    decay = [tile(decay_ref, m, blocks) for m in range(modes)]

    def step(row, held, first):
        spread(k_near, k_wide, row, 0)
        spread(v_near, v_wide, row, 0)
        state, (k2, k1, v2, v1) = list(held[:modes]), held[modes:]
        for index in range(STEP):
            k0 = k_wide[place_of(index, blocks), :]
            v0 = v_wide[place_of(index, blocks), :]
            key = key_taps[0] * k0 + key_taps[1] * k1 + key_taps[2] * k2
            value = value_taps[0] * v0 + value_taps[1] * v1 + value_taps[2] * v2
            if first and index < 2:
                edge_ref[index * blocks : (index + 1) * blocks, :] = key
                edge_ref[(2 + index) * blocks : (3 + index) * blocks, :] = value
            signal = key * value
            signal_ref[moving_tile(row + index, blocks), :] = signal
            state = [decay[m] * state[m] + signal for m in range(modes)]
            k2, k1, v2, v1 = k1, k0, v1, v0
        return tuple(state) + (k2, k1, v2, v1)

    held = (zero,) * (modes + 4)
    for i in range(pieces):
        for copy in part(i):
            copy.wait()
        begin = 0
        if i == 0:
            held = step(0, held, True)
            begin = 1
        held = lax.fori_loop(
            begin,
            height // STEP,
            lambda j, held, i=i: step(pl.multiple_of(i * height + j * STEP, STEP), held, False),
            held,
        )
    for m in range(modes + 4):
        carry_ref[m * blocks : (m + 1) * blocks, :] = held[m]
    for copy in late:
        copy.wait()
    spread(q_near, k_wide, rows - STEP, 0)
    for i in range(2):
        start = (modes + 4 + i) * blocks
        carry_ref[start : start + blocks, :] = k_wide[place_of(STEP - 2 + i, blocks), :]


def far(x):
    return pltpu.with_memory_space_constraint(x, pltpu.HBM)


def run_front(q, k, v, short_taps, rate, residue):
    rows, width = k.shape
    modes = rate.shape[0]
    blocks = width // LANES
    pieces = 4

    def wide(n):
        return jax.ShapeDtypeStruct((n * blocks, LANES), jnp.float32)

    def like(x):
        return jax.ShapeDtypeStruct(x.shape, x.dtype)

    out_shape = [wide(modes + 6), wide(rows), wide(modes), wide(9), wide(4), like(rate), like(residue), like(q)]
    return pl.pallas_call(
        front_kernel,
        out_shape=out_shape,
        in_specs=[AWAY] * 6,
        out_specs=[WHOLE] * len(out_shape),
        scratch_shapes=[
            pltpu.VMEM((rows, width), jnp.bfloat16),
            pltpu.VMEM((rows, width), jnp.bfloat16),
            pltpu.VMEM(short_taps.shape, jnp.float32),
            pltpu.VMEM((STEP * blocks, LANES), jnp.float32),
            pltpu.VMEM((STEP * blocks, LANES), jnp.float32),
            pltpu.SemaphoreType.DMA((2 * pieces + 2,)),
            pltpu.SemaphoreType.DMA((2,)),
        ],
        compiler_params=params(),
        cost_estimate=cost(10**8),
        name="front",
    )(*[far(x) for x in (k, v, q, short_taps, rate, residue)])


def local_kernel(q_near, signal_ref, decay_ref, taps_ref, gain_near, *refs):
    copies = []
    if len(refs) > 4:
        weight_hbm, direction_hbm, weight_ref, direction_ref, sems = refs[:2] + refs[5:7] + refs[-1:]
        refs = refs[2:5] + refs[7:-1]
        count = sems.shape[0] - 1
        copies.append(pltpu.make_async_copy(direction_hbm, direction_ref, sems.at[count]))
        copies[-1].start()
        depth = weight_ref.shape[0] // count
        for i in range(count):
            here = pl.ds(i * depth, depth)
            copies.append(pltpu.make_async_copy(weight_hbm.at[here], weight_ref.at[here], sems.at[i]))
            copies[-1].start()
    out_ref, query_ref, gain_ref, q_wide = refs
    rows, width = q_near.shape
    blocks = width // LANES
    modes = gain_near.shape[0]
    spread_rows(gain_near[...], gain_ref)
    zero = jnp.zeros((blocks, LANES), jnp.float32)
    taps = [tile(taps_ref, j, blocks) for j in range(3)]
    decay = [tile(decay_ref, m, blocks) for m in range(modes)]
    gain = [tile(gain_ref, m, blocks) for m in range(modes)]

    def step(j, held):
        row = pl.multiple_of(j * STEP, STEP)
        spread(q_near, q_wide, row, 0)
        state, (q2, q1) = list(held[:modes]), held[modes:]
        for index in range(STEP):
            q0 = q_wide[place_of(index, blocks), :]
            here = moving_tile(row + index, blocks)
            signal = signal_ref[here, :]
            query_ref[here, :] = taps[0] * q0 + taps[1] * q1 + taps[2] * q2
            state = [decay[m] * state[m] + signal for m in range(modes)]
            sums = [gain[m] * state[m] for m in range(modes)]
            while len(sums) > 1:
                sums = [sums[i] + sums[i + 1] for i in range(0, len(sums), 2)]
            out_ref[here, :] = sums[0]
            q2, q1 = q1, q0
        return tuple(state) + (q2, q1)

    lax.fori_loop(0, rows // STEP, step, (zero,) * (modes + 2))
    for copy in copies:
        copy.wait()


def run_local(q, signal, decay, taps, gain, *weight):
    rows, width = q.shape
    blocks = width // LANES
    wide = jax.ShapeDtypeStruct((rows * blocks, LANES), jnp.float32)
    out_shape = [wide, wide, jax.ShapeDtypeStruct(decay.shape, jnp.float32)]
    scratch_shapes = [pltpu.VMEM((STEP * blocks, LANES), jnp.float32)]
    if weight:
        out_shape += [jax.ShapeDtypeStruct(x.shape, x.dtype) for x in weight]
        scratch_shapes.append(pltpu.SemaphoreType.DMA((5,)))
        weight = tuple(far(x) for x in weight)
    return pl.pallas_call(
        local_kernel,
        out_shape=out_shape,
        in_specs=[WHOLE] * 5 + [AWAY] * len(weight),
        out_specs=[WHOLE] * len(out_shape),
        scratch_shapes=scratch_shapes,
        compiler_params=params(),
        cost_estimate=cost(10**6),
        name="local_filter",
    )(q, signal, decay, taps, gain, *weight)


def correct_kernel(blocks, carry_ref, decay_ref, gain_ref, taps_ref, edge_ref, local_ref, query_ref, *refs):
    wide, outs = refs[-1], refs[:-1]
    rows = local_ref.shape[0] // blocks
    modes = decay_ref.shape[0] // blocks
    carried = jnp.where(lax.axis_index("ctx") > 0, 1.0, 0.0)
    k2, k1, v2, v1, q2, q1 = [carried * tile(carry_ref, modes + i, blocks) for i in range(6)]
    tap = [tile(taps_ref, i, blocks) for i in range(9)]
    key0, key1, value0, value1 = [tile(edge_ref, i, blocks) for i in range(4)]
    extra = [
        (key0 + tap[4] * k1 + tap[5] * k2) * (value0 + tap[7] * v1 + tap[8] * v2) - key0 * value0,
        (key1 + tap[5] * k1) * (value1 + tap[8] * v1) - key1 * value1,
    ]
    query_extra = [tap[1] * q1 + tap[2] * q2, tap[2] * q1]
    state = [tile(gain_ref, m, blocks) * (carried * tile(carry_ref, m, blocks)) for m in range(modes)]
    decay = [tile(decay_ref, m, blocks) for m in range(modes)]

    def step(row, state, first, piece_ref, start):
        state = list(state)
        for index in range(STEP):
            here = moving_tile(row + index, blocks)
            state = [decay[m] * state[m] for m in range(modes)]
            query = query_ref[here, :]
            if first and index < 2:
                state = [state[m] + tile(gain_ref, m, blocks) * extra[index] for m in range(modes)]
                query = query + query_extra[index]
            sums = state
            while len(sums) > 1:
                sums = [sums[i] + sums[i + 1] for i in range(0, len(sums), 2)]
            wide[place_of(index, blocks), :] = query * (local_ref[here, :] + sums[0])
        for block in range(blocks):
            halves = [
                wide[(half * blocks + block) * GROUP : (half * blocks + block + 1) * GROUP, :]
                for half in range(STEP // GROUP)
            ]
            rounded = jnp.concatenate(halves, axis=0).astype(jnp.bfloat16)
            columns = slice(block * LANES, (block + 1) * LANES)
            outs[-1][pl.ds(row, STEP), columns] = rounded
            if piece_ref is not None:
                piece_ref[pl.ds(pl.multiple_of(row - start, STEP), STEP), columns] = rounded
        return tuple(state)

    state = tuple(state)
    start = 0
    for piece_ref in outs[:-1] or [None]:
        end = start + (rows if piece_ref is None else piece_ref.shape[0])
        begin = start // STEP
        if start == 0:
            state = step(0, state, True, piece_ref, 0)
            begin = 1
        state = lax.fori_loop(
            begin,
            end // STEP,
            lambda j, state, start=start, piece_ref=piece_ref: step(
                pl.multiple_of(j * STEP, STEP), state, False, piece_ref, start
            ),
            state,
        )
        start = end


def run_correct(carry, decay, gain, taps, edge, local, query, blocks, *heights):
    rows = local.shape[0] // blocks
    width = blocks * LANES
    heights += (rows,)
    return pl.pallas_call(
        functools.partial(correct_kernel, blocks),
        out_shape=[jax.ShapeDtypeStruct((height, width), jnp.bfloat16) for height in heights],
        in_specs=[WHOLE] * 7,
        out_specs=[WHOLE] * len(heights),
        scratch_shapes=[pltpu.VMEM((STEP * blocks, LANES), jnp.float32)],
        compiler_params=params(),
        cost_estimate=cost(10**8),
        name="carried_filter",
    )(carry, decay, gain, taps, edge, local, query)


def gains_of(rate, residue):
    return residue * jnp.sqrt(-jnp.expm1(-2.0 * rate)) * rate.shape[0] ** (-0.5)


def split_three(x):
    high = x.astype(jnp.bfloat16)
    rest = x - high.astype(jnp.float32)
    middle = rest.astype(jnp.bfloat16)
    low = (rest - middle.astype(jnp.float32)).astype(jnp.bfloat16)
    return high, middle, low


def in_parts(row):
    return jnp.concatenate(list(split_three(row)) + [jnp.zeros((13, row.shape[1]), jnp.bfloat16)], axis=0)


def dot_parts(parts, matrix):
    out = lax.dot_general(parts, matrix, (((1,), (1,)), ((), ())), preferred_element_type=jnp.float32)
    return out[0:1] + out[1:2] + out[2:3]


def idle_kernel(*refs):
    pass


def after(array, *others):
    return pl.pallas_call(
        idle_kernel,
        out_shape=jax.ShapeDtypeStruct(array.shape, array.dtype),
        in_specs=[pl.BlockSpec(memory_space=pl.ANY)] * (1 + len(others)),
        out_specs=pl.BlockSpec(memory_space=pl.ANY),
        input_output_aliases={0: 0},
        compiler_params=params(),
        cost_estimate=cost(1),
        name="after",
    )(array, *others)


def rows_of(count, like, dtype=jnp.bfloat16):
    return jax.ShapeDtypeStruct((count, like.shape[1]), dtype)


def call(kernel, name, out_shape, *operands, tokens=()):
    def with_tokens(*refs):
        kernel(*refs[: len(operands)], *refs[len(operands) + len(tokens) :])

    return pl.pallas_call(
        with_tokens,
        out_shape=out_shape,
        in_specs=[WHOLE] * len(operands) + [pl.BlockSpec(memory_space=pl.ANY)] * len(tokens),
        out_specs=[WHOLE] * len(out_shape),
        compiler_params=params(),
        cost_estimate=cost(10**6),
        name=name,
    )(*operands, *tokens)


def inner_kernel(direction_ref, weight_ref, parts_ref, norm_ref, here_ref):
    everything = direction_ref[...]
    norm_ref[...] = jnp.broadcast_to(
        jnp.sum(everything * everything, axis=1, keepdims=True) + EPSILON, norm_ref.shape
    )
    size, width = weight_ref.shape[1], here_ref.shape[1]
    here_ref[...] = direction_ref[:, pl.ds(pl.multiple_of(lax.axis_index("tp") * width, LANES), width)]
    here = direction_ref[:, pl.ds(pl.multiple_of(lax.axis_index("ctx") * size, LANES), size)]
    parts_ref[...] = in_parts(dot_parts(in_parts(here), weight_ref[...]))


def run_inner(direction, weight):
    out_shape = [
        jax.ShapeDtypeStruct((STEP, weight.shape[0]), jnp.bfloat16),
        jax.ShapeDtypeStruct((1, LANES), jnp.float32),
        jax.ShapeDtypeStruct((1, weight.shape[1] // 2), jnp.float32),
    ]
    return call(inner_kernel, "inner", out_shape, direction, weight)


def project_kernel(begin, weight_ref, piece_ref, *outs):
    *sends, keep_ref = outs
    rows, width = keep_ref.shape
    cut = width // len(sends)
    side = lax.axis_index("tp") % 2
    for start in range(0, 2 * width, 256):
        away = start < width
        ref, to = (sends[start // cut], start % cut) if away else (keep_ref, start - width)
        which = 1 - side if away else side
        columns = pl.ds(pl.multiple_of(which * width + start % width, 256), 256)
        out = jnp.dot(piece_ref[begin : begin + rows, :], weight_ref[:, columns], preferred_element_type=jnp.float32)
        ref[:rows, to : to + 256] = out.astype(ref.dtype)


def run_project(weight, piece, begin, rows, count, *tokens):
    keep = jax.ShapeDtypeStruct((rows, weight.shape[1] // 2), jnp.float32)
    sends = [jax.ShapeDtypeStruct((rows, keep.shape[1] // count), jnp.bfloat16)] * count
    kernel = functools.partial(project_kernel, begin)
    *sends, keep = call(kernel, "project", [*sends, keep], weight, piece, tokens=tokens)
    return sends, keep


def put_behind(ref, rows, row):
    here = slice(rows, rows + STEP)
    ref[here, :] = jnp.zeros((STEP, ref.shape[1]), jnp.bfloat16)
    ref[here, : row.shape[1]] = in_parts(row)


def take_behind(ref, rows, width):
    return jnp.sum(ref[rows : rows + STEP, :width].astype(jnp.float32), axis=0, keepdims=True)


def level_kernel(parts_ref, far_ref, whole_ref, out_ref):
    far_parts = far_ref[far_ref.shape[0] - STEP :, :]
    out_ref[...] = dot_parts(parts_ref[...], whole_ref[...]) + dot_parts(far_parts, whole_ref[...])


def add_shares(lefts, rights, outs):
    width = sum(ref.shape[1] for ref in lefts)
    rows = lefts[0].shape[0]
    step = min(ref.shape[1] for ref in (*lefts, *rights, *outs))

    def at(pieces, row, column):
        size = pieces[0].shape[1]
        return pieces[column // size].at[row : row + STEP, column % size : column % size + step]

    for row in range(0, rows, STEP):
        for column in range(0, width, step):
            left = at(lefts, row, column)[...].astype(jnp.float32)
            right = at(rights, row, column)[...].astype(jnp.float32)
            at(outs, row, column)[...] = (left + right).astype(jnp.bfloat16)


def merge_kernel(left, right, *refs):
    add_shares(refs[:left], refs[left : left + right], refs[left + right :])


def run_merge(lefts, rights, count):
    rows, width = lefts[0].shape[0], sum(x.shape[1] for x in lefts)
    kernel = functools.partial(merge_kernel, len(lefts), len(rights))
    out_shape = [jax.ShapeDtypeStruct((rows, width // count), jnp.bfloat16)] * count
    return call(kernel, "merge", out_shape, *lefts, *rights)


def merge_parts_kernel(keep_ref, parts_ref, *refs):
    add_shares((keep_ref,), refs[:-1], refs[-1:])
    refs[-1][keep_ref.shape[0] :, :] = parts_ref[...]


def is_keeper():
    return lax.axis_index("tp") // 2 == lax.axis_index("ctx")


def choose_kernel(straight_ref, own_ref, level_ref, other_ref, out_ref, total_ref):
    keeper = is_keeper()
    rows = own_ref.shape[0]

    @pl.when(keeper)
    def _():
        out_ref[:rows, :] = straight_ref[:rows, :]

    @pl.when(jnp.logical_not(keeper))
    def _():
        out_ref[:rows, :] = own_ref[...]

    total = level_ref[...] + other_ref[...]
    total_ref[...] = total
    put_behind(out_ref, rows, total)


def finish_kernel(*refs):
    level_ref, norm_ref, direction_ref = refs[:3]
    own0, own1, (straight_ref, merged_ref) = refs[3:6], refs[6:9], refs[9:11]
    out_hbm, level_out_ref, out_near, sems = refs[11:]
    turned_ref = own1[-1]
    rows, width = out_near.shape
    half = straight_ref.shape[0] - STEP
    keeper = is_keeper()
    level = (level_ref[...] + take_behind(turned_ref, turned_ref.shape[0] - STEP, rows)) / norm_ref[0:1, 0:1]
    level_out_ref[...] = level
    direction = direction_ref[...]
    column = jnp.transpose(jnp.broadcast_to(level, (LANES, rows)))

    def put(row, cut, before, behind):
        pieces, start = (before, row) if row < cut else (behind, row - cut)
        total = pieces[0][start : start + STEP, :].astype(jnp.float32)
        for piece in pieces[1:]:
            total = total + piece[start : start + STEP, :].astype(jnp.float32)
        total = total - column[row : row + STEP, 0:1] * direction
        out_near[row : row + STEP, :] = total.astype(jnp.bfloat16)

    copies = []
    count = sems.shape[0]
    for i in range(count):
        begin, end = i * rows // count, (i + 1) * rows // count

        @pl.when(keeper)
        def _():
            for row in range(begin, end, STEP):
                put(row, own0[0].shape[0], own0, own1)

        @pl.when(jnp.logical_not(keeper))
        def _():
            for row in range(begin, end, STEP):
                put(row, half, (straight_ref, turned_ref), (merged_ref,))

        here = pl.ds(begin, end - begin)
        copies.append(pltpu.make_async_copy(out_near.at[here], out_hbm.at[here], sems.at[i]))
        copies[-1].start()
    for copy in copies:
        copy.wait()


def run_finish(*operands):
    rows, width = operands[0].shape[1], operands[2].shape[1]
    return pl.pallas_call(
        finish_kernel,
        out_shape=[
            jax.ShapeDtypeStruct((rows, width), jnp.bfloat16),
            jax.ShapeDtypeStruct((1, rows), jnp.float32),
        ],
        in_specs=[WHOLE] * len(operands),
        out_specs=[AWAY, WHOLE],
        scratch_shapes=[pltpu.VMEM((rows, width), jnp.bfloat16), pltpu.SemaphoreType.DMA((4,))],
        compiler_params=params(),
        cost_estimate=cost(10**6),
        name="finish",
    )(*operands)


def plane_plan(q, k, v, short_taps, decay_rate, residue, out_weight, direction):
    rows, width = q.shape
    half = rows // 2
    blocks = width // LANES
    axes = ("ctx", "tp")
    across = [(4 * c + p, 4 * (1 - c) + p) for c in range(2) for p in range(4)]
    sibling = [(4 * c + p, 4 * c + (p ^ 1)) for c in range(2) for p in range(4)]
    pair = [(4 * c + p, 4 * c + (p ^ 2)) for c in range(2) for p in range(4)]

    ended, signal, decay, taps, edge, rate, residue, q = run_front(q, k, v, short_taps, decay_rate.T, residue.T)
    carry = lax.ppermute(ended, axes, across)
    local, query, gain, weight, direction = run_local(
        q, signal, decay, taps, gains_of(rate, residue), out_weight, direction.reshape(1, -1)
    )
    first, second, whole = run_correct(carry, decay, gain, taps, edge, local, query, blocks, half, half)
    far_first = lax.ppermute(first, axes, across)
    far_second = lax.ppermute(second, axes, across)

    def exchange(arrays, pairs):
        return [lax.ppermute(array, axes, pairs) for array in arrays]

    weight = after(weight, whole)
    parts, norm, direction = run_inner(direction, weight)
    sends0, keep0 = run_project(weight, whole, 0, half, 1)
    sends1, keep1 = run_project(weight, whole, half, half, 1)
    (core0,) = exchange(sends0, sibling)
    (hop0,) = exchange(run_merge((keep0,), (core0,), 1), pair)

    sends, far_keep = run_project(weight, far_first, 0, half, 2, parts, *sends0, *sends1)
    (sums0,) = call(
        merge_parts_kernel, "merge", [rows_of(half + STEP, far_keep)], far_keep, parts, *exchange(sends, sibling)
    )
    (straight,) = exchange([sums0], across)

    sends, far_keep = run_project(weight, after(far_second, sums0), 0, half, 2)
    sums1 = run_merge((far_keep,), exchange(sends, sibling), 2)
    moved = exchange(sums1, pair)
    (core1,) = exchange(sends1, sibling)
    (own1,) = run_merge((keep1,), (core1,), 1)

    one_row = jax.ShapeDtypeStruct((1, rows), jnp.float32)
    (level,) = call(level_kernel, "level", [one_row], parts, straight, whole)
    payload = rows_of(half + STEP, far_keep)
    turned, level = call(
        choose_kernel,
        "choose",
        [payload, one_row],
        straight,
        own1,
        level,
        *exchange([level], sibling),
        tokens=(hop0,),
    )
    (turned,) = exchange([turned], pair)
    (merged,) = exchange(run_merge(sums1, moved, 1), across)
    ablated, level = run_finish(
        level, norm, direction, keep0, core0, hop0, keep1, core1, turned, straight, merged
    )
    return ablated, level.reshape(rows)


def gather_plan(q, k, v, short_taps, decay_rate, residue, out_weight, direction):
    rows, width = q.shape
    blocks = width // LANES
    modes = decay_rate.shape[1]
    tp = lax.axis_index("tp")
    ctx_size = lax.axis_size("ctx")
    next_one = [(i, i + 1) for i in range(ctx_size - 1)]
    ended, signal, decay, taps, edge, rate, residue, q = run_front(q, k, v, short_taps, decay_rate.T, residue.T)
    halo = lax.ppermute(ended[modes * blocks :], "ctx", next_one)
    local, query, gain = run_local(q, signal, decay, taps, gains_of(rate, residue))
    k2, k1, v2, v1 = [halo[i * blocks : (i + 1) * blocks] for i in range(4)]
    tap = taps.reshape(9, blocks, LANES)
    key0, key1, value0, value1 = edge.reshape(4, blocks, LANES)
    extra0 = (key0 + tap[4] * k1 + tap[5] * k2) * (value0 + tap[7] * v1 + tap[8] * v2) - key0 * value0
    extra1 = (key1 + tap[5] * k1) * (value1 + tap[8] * v1) - key1 * value1
    wide_rate = decay_rate.T.reshape(modes, blocks, LANES)
    state = (
        ended[: modes * blocks].reshape(modes, blocks, LANES)
        + jnp.exp(-wide_rate * (rows - 1)) * extra0
        + jnp.exp(-wide_rate * (rows - 2)) * extra1
    )
    reach = 1
    while reach < ctx_size:
        earlier = lax.ppermute(state, "ctx", [(i, i + reach) for i in range(ctx_size - reach)])
        state = state + jnp.exp(-wide_rate * (rows * reach)) * earlier
        reach *= 2
    start = lax.ppermute(state, "ctx", next_one).reshape(modes * blocks, LANES)
    carry = jnp.concatenate([start, halo], axis=0)
    (gated,) = run_correct(carry, decay, gain, taps, edge, local, query, blocks)
    partial_terms = lax.dot_general(
        gated,
        lax.all_gather(out_weight, "ctx", axis=1, tiled=True),
        (((1,), (0,)), ((), ())),
        preferred_element_type=jnp.float32,
    )
    summed = lax.psum_scatter(
        partial_terms.astype(jnp.bfloat16), "tp", scatter_dimension=1, tiled=True
    ).astype(jnp.float32)
    width_here = summed.shape[1]
    direction_here = lax.dynamic_slice_in_dim(direction, tp * width_here, width_here, 0)
    norm_total = jnp.sum(direction * direction) + EPSILON
    local_inner = jnp.dot(summed, direction_here, precision=HIGHEST)
    feature_level = lax.psum(local_inner, "tp") / norm_total
    ablated = (summed - feature_level[:, None] * direction_here[None, :]).astype(jnp.bfloat16)
    return ablated, feature_level


def solution(mesh):
    placed = (
        P(("dp", "ctx"), "tp"),
        P(("dp", "ctx"), "tp"),
        P(("dp", "ctx"), "tp"),
        P(None, None, "tp"),
        P("tp", None),
        P("tp", None),
        P("tp", "ctx"),
        P(),
    )
    plane = mesh.shape["ctx"] == 2 and mesh.shape["tp"] == 4
    return jax.shard_map(
        plane_plan if plane else gather_plan,
        mesh=mesh,
        in_specs=placed,
        out_specs=(P(("dp", "ctx"), "tp"), P(("dp", "ctx"))),
        check_vma=False,
    )
```

```python
import functools

import jax
import jax.numpy as jnp
from jax import lax
from jax.experimental import pallas as pl
from jax.experimental.pallas import tpu as pltpu
from jax.sharding import PartitionSpec as P

EPSILON = 1e-06
HIGHEST = lax.Precision.HIGHEST
LANES = 128
GROUP = 8
STEP = 16
WHOLE = pl.BlockSpec(memory_space=pltpu.VMEM)
AWAY = pl.BlockSpec(memory_space=pltpu.HBM)


def params(mebibytes=20):
    return pltpu.CompilerParams(vmem_limit_bytes=mebibytes * 1024 * 1024)


def cost(flops):
    return pl.CostEstimate(flops=flops, bytes_accessed=1024, transcendentals=0)


def spread(source, scratch, row, to):
    blocks = source.shape[1] // LANES
    for block in range(blocks):
        piece = source[pl.ds(row, STEP), block * LANES : (block + 1) * LANES].astype(jnp.float32)
        for half in range(STEP // GROUP):
            start = (half * blocks + block) * GROUP
            scratch[pl.ds(to + start, GROUP), :] = piece[half * GROUP : (half + 1) * GROUP]


def spread_rows(source, target):
    count, width = source.shape
    blocks = width // LANES
    for block in range(blocks):
        target[pl.ds(block, count, stride=blocks), :] = source[:, block * LANES : (block + 1) * LANES]


def place_of(index, blocks):
    return pl.ds((index // GROUP) * (blocks * GROUP) + index % GROUP, blocks, stride=GROUP)


def tile(ref, index, blocks):
    return ref[index * blocks : (index + 1) * blocks, :]


def moving_tile(index, blocks):
    return pl.ds(pl.multiple_of(index * blocks, blocks), blocks)


def front_kernel(*refs):
    k_hbm, v_hbm, q_hbm, taps_hbm, rate_hbm, residue_hbm = refs[:6]
    carry_ref, signal_ref, decay_ref, taps_ref, edge_ref, rate_ref, residue_ref, q_near = refs[6:14]
    k_near, v_near, taps_near, *wides, sems, late_sems = refs[-9:]
    wides = (wides[:2], wides[2:])
    rows, width = k_near.shape
    blocks = width // LANES
    modes = rate_ref.shape[0]
    pieces = sems.shape[0] // 2 - 1
    height = rows // pieces

    def part(i):
        here = pl.ds(i * height, height)
        return (
            pltpu.make_async_copy(k_hbm.at[here], k_near.at[here], sems.at[2 * i]),
            pltpu.make_async_copy(v_hbm.at[here], v_near.at[here], sems.at[2 * i + 1]),
        )

    rate_copy = pltpu.make_async_copy(rate_hbm, rate_ref, sems.at[2 * pieces])
    taps_copy = pltpu.make_async_copy(taps_hbm, taps_near, sems.at[2 * pieces + 1])
    late = [(residue_hbm, residue_ref), (q_hbm, q_near)]
    late = [pltpu.make_async_copy(source, target, late_sems.at[i]) for i, (source, target) in enumerate(late)]
    rate_copy.start()
    taps_copy.start()
    for i in range(pieces):
        for copy in part(i):
            copy.start()
    for copy in late:
        copy.start()
    rate_copy.wait()
    taps_copy.wait()
    spread_rows(jnp.exp(-rate_ref[...]), decay_ref)
    for i in range(3):
        for block in range(blocks):
            taps_ref[pl.ds(3 * i * blocks + block, 3, stride=blocks), :] = taps_near[
                i, :, block * LANES : (block + 1) * LANES
            ]
    zero = jnp.zeros((blocks, LANES), jnp.float32)
    key_taps = [tile(taps_ref, 3 + j, blocks) for j in range(3)]
    value_taps = [tile(taps_ref, 6 + j, blocks) for j in range(3)]
    decay = [tile(decay_ref, m, blocks) for m in range(modes)]

    def step(row, held):
        state, (k2, k1, v2, v1) = list(held[:modes]), held[modes:]
        for half, (k_wide, v_wide) in enumerate(wides):
            spread(k_near, k_wide, row + half * STEP, 0)
            spread(v_near, v_wide, row + half * STEP, 0)
        for half, (k_wide, v_wide) in enumerate(wides):
            for index in range(STEP):
                k0 = k_wide[place_of(index, blocks), :]
                v0 = v_wide[place_of(index, blocks), :]
                key = key_taps[0] * k0 + key_taps[1] * k1 + key_taps[2] * k2
                value = value_taps[0] * v0 + value_taps[1] * v1 + value_taps[2] * v2
                signal = key * value
                signal_ref[moving_tile(row + half * STEP + index, blocks), :] = signal
                state = [decay[m] * state[m] + signal for m in range(modes)]
                k2, k1, v2, v1 = k1, k0, v1, v0
        return tuple(state) + (k2, k1, v2, v1)

    held = (zero,) * (modes + 4)
    for i in range(pieces):
        for copy in part(i):
            copy.wait()
        if i == 0:
            spread(k_near, wides[0][0], 0, 0)
            spread(v_near, wides[0][1], 0, 0)
            for wide, taps, place in ((wides[0][0], key_taps, 0), (wides[0][1], value_taps, 2)):
                x0, x1 = wide[place_of(0, blocks), :], wide[place_of(1, blocks), :]
                edge_ref[place * blocks : (place + 1) * blocks, :] = taps[0] * x0
                edge_ref[(place + 1) * blocks : (place + 2) * blocks, :] = taps[0] * x1 + taps[1] * x0
        held = lax.fori_loop(
            0,
            height // (2 * STEP),
            lambda j, held, i=i: step(pl.multiple_of(i * height + j * 2 * STEP, 2 * STEP), held),
            held,
        )
    for m in range(modes + 4):
        carry_ref[m * blocks : (m + 1) * blocks, :] = held[m]
    for copy in late:
        copy.wait()
    k_wide = wides[0][0]
    spread(q_near, k_wide, rows - STEP, 0)
    for i in range(2):
        start = (modes + 4 + i) * blocks
        carry_ref[start : start + blocks, :] = k_wide[place_of(STEP - 2 + i, blocks), :]


def far(x):
    return pltpu.with_memory_space_constraint(x, pltpu.HBM)


def run_front(q, k, v, short_taps, rate, residue):
    rows, width = k.shape
    modes = rate.shape[0]
    blocks = width // LANES
    pieces = 4

    def wide(n):
        return jax.ShapeDtypeStruct((n * blocks, LANES), jnp.float32)

    def like(x):
        return jax.ShapeDtypeStruct(x.shape, x.dtype)

    out_shape = [wide(modes + 6), wide(rows), wide(modes), wide(9), wide(4), like(rate), like(residue), like(q)]
    return pl.pallas_call(
        front_kernel,
        out_shape=out_shape,
        in_specs=[AWAY] * 6,
        out_specs=[WHOLE] * len(out_shape),
        scratch_shapes=[
            pltpu.VMEM((rows, width), jnp.bfloat16),
            pltpu.VMEM((rows, width), jnp.bfloat16),
            pltpu.VMEM(short_taps.shape, jnp.float32),
            *[pltpu.VMEM((STEP * blocks, LANES), jnp.float32)] * 4,
            pltpu.SemaphoreType.DMA((2 * pieces + 2,)),
            pltpu.SemaphoreType.DMA((2,)),
        ],
        compiler_params=params(),
        cost_estimate=cost(10**8),
        name="front",
    )(*[far(x) for x in (k, v, q, short_taps, rate, residue)])


def local_kernel(q_near, signal_ref, decay_ref, taps_ref, gain_near, *refs):
    copies = []
    if len(refs) > 5:
        weight_hbm, direction_hbm, weight_ref, direction_ref, sems = refs[:2] + refs[5:7] + refs[-1:]
        refs = refs[2:5] + refs[7:-1]
        count = sems.shape[0] - 1
        copies.append(pltpu.make_async_copy(direction_hbm, direction_ref, sems.at[count]))
        copies[-1].start()
        depth = weight_ref.shape[0] // count
        for i in range(count):
            here = pl.ds(i * depth, depth)
            copies.append(pltpu.make_async_copy(weight_hbm.at[here], weight_ref.at[here], sems.at[i]))
            copies[-1].start()
    out_ref, query_ref, gain_ref, *wides = refs
    rows, width = q_near.shape
    blocks = width // LANES
    modes = gain_near.shape[0]
    spread_rows(gain_near[...], gain_ref)
    zero = jnp.zeros((blocks, LANES), jnp.float32)
    taps = [tile(taps_ref, j, blocks) for j in range(3)]
    decay = [tile(decay_ref, m, blocks) for m in range(modes)]
    gain = [tile(gain_ref, m, blocks) for m in range(modes)]

    def step(j, held):
        row = pl.multiple_of(j * 2 * STEP, 2 * STEP)
        state, (q2, q1) = list(held[:modes]), held[modes:]
        for half, q_wide in enumerate(wides):
            spread(q_near, q_wide, row + half * STEP, 0)
        for half, q_wide in enumerate(wides):
            for index in range(STEP):
                q0 = q_wide[place_of(index, blocks), :]
                here = moving_tile(row + half * STEP + index, blocks)
                signal = signal_ref[here, :]
                query_ref[here, :] = taps[0] * q0 + taps[1] * q1 + taps[2] * q2
                state = [decay[m] * state[m] + signal for m in range(modes)]
                sums = [gain[m] * state[m] for m in range(modes)]
                while len(sums) > 1:
                    sums = [sums[i] + sums[i + 1] for i in range(0, len(sums), 2)]
                out_ref[here, :] = sums[0]
                q2, q1 = q1, q0
        return tuple(state) + (q2, q1)

    lax.fori_loop(0, rows // (2 * STEP), step, (zero,) * (modes + 2))
    for copy in copies:
        copy.wait()


def run_local(q, signal, decay, taps, gain, *weight):
    rows, width = q.shape
    blocks = width // LANES
    wide = jax.ShapeDtypeStruct((rows * blocks, LANES), jnp.float32)
    out_shape = [wide, wide, jax.ShapeDtypeStruct(decay.shape, jnp.float32)]
    scratch_shapes = [pltpu.VMEM((STEP * blocks, LANES), jnp.float32)] * 2
    if weight:
        out_shape += [jax.ShapeDtypeStruct(x.shape, x.dtype) for x in weight]
        scratch_shapes.append(pltpu.SemaphoreType.DMA((5,)))
        weight = tuple(far(x) for x in weight)
    return pl.pallas_call(
        local_kernel,
        out_shape=out_shape,
        in_specs=[WHOLE] * 5 + [AWAY] * len(weight),
        out_specs=[WHOLE] * len(out_shape),
        scratch_shapes=scratch_shapes,
        compiler_params=params(),
        cost_estimate=cost(10**6),
        name="local_filter",
    )(q, signal, decay, taps, gain, *weight)


def correct_kernel(blocks, carry_ref, decay_ref, gain_ref, taps_ref, edge_ref, local_ref, query_ref, *refs):
    wide, outs = refs[-1], refs[:-1]
    rows = local_ref.shape[0] // blocks
    modes = decay_ref.shape[0] // blocks
    carried = jnp.where(lax.axis_index("ctx") > 0, 1.0, 0.0)
    k2, k1, v2, v1, q2, q1 = [carried * tile(carry_ref, modes + i, blocks) for i in range(6)]
    tap = [tile(taps_ref, i, blocks) for i in range(9)]
    key0, key1, value0, value1 = [tile(edge_ref, i, blocks) for i in range(4)]
    extra = [
        (key0 + tap[4] * k1 + tap[5] * k2) * (value0 + tap[7] * v1 + tap[8] * v2) - key0 * value0,
        (key1 + tap[5] * k1) * (value1 + tap[8] * v1) - key1 * value1,
    ]
    query_extra = [tap[1] * q1 + tap[2] * q2, tap[2] * q1]
    state = [tile(gain_ref, m, blocks) * (carried * tile(carry_ref, m, blocks)) for m in range(modes)]
    decay = [tile(decay_ref, m, blocks) for m in range(modes)]

    def step(row, state, first, piece_ref, start):
        state = list(state)
        for index in range(STEP):
            here = moving_tile(row + index, blocks)
            state = [decay[m] * state[m] for m in range(modes)]
            query = query_ref[here, :]
            if first and index < 2:
                state = [state[m] + tile(gain_ref, m, blocks) * extra[index] for m in range(modes)]
                query = query + query_extra[index]
            sums = state
            while len(sums) > 1:
                sums = [sums[i] + sums[i + 1] for i in range(0, len(sums), 2)]
            wide[place_of(index, blocks), :] = query * (local_ref[here, :] + sums[0])
        for block in range(blocks):
            halves = [
                wide[(half * blocks + block) * GROUP : (half * blocks + block + 1) * GROUP, :]
                for half in range(STEP // GROUP)
            ]
            rounded = jnp.concatenate(halves, axis=0).astype(jnp.bfloat16)
            columns = slice(block * LANES, (block + 1) * LANES)
            outs[-1][pl.ds(row, STEP), columns] = rounded
            if piece_ref is not None:
                piece_ref[pl.ds(pl.multiple_of(row - start, STEP), STEP), columns] = rounded
        return tuple(state)

    state = tuple(state)
    start = 0
    for piece_ref in outs[:-1] or [None]:
        end = start + (rows if piece_ref is None else piece_ref.shape[0])
        begin = start // STEP
        if start == 0:
            state = step(0, state, True, piece_ref, 0)
            begin = 1
        state = lax.fori_loop(
            begin,
            end // STEP,
            lambda j, state, start=start, piece_ref=piece_ref: step(
                pl.multiple_of(j * STEP, STEP), state, False, piece_ref, start
            ),
            state,
        )
        start = end


def run_correct(carry, decay, gain, taps, edge, local, query, blocks, *heights):
    rows = local.shape[0] // blocks
    width = blocks * LANES
    heights += (rows,)
    return pl.pallas_call(
        functools.partial(correct_kernel, blocks),
        out_shape=[jax.ShapeDtypeStruct((height, width), jnp.bfloat16) for height in heights],
        in_specs=[WHOLE] * 7,
        out_specs=[WHOLE] * len(heights),
        scratch_shapes=[pltpu.VMEM((STEP * blocks, LANES), jnp.float32)],
        compiler_params=params(),
        cost_estimate=cost(10**8),
        name="carried_filter",
    )(carry, decay, gain, taps, edge, local, query)


def gains_of(rate, residue):
    return residue * jnp.sqrt(-jnp.expm1(-2.0 * rate)) * rate.shape[0] ** (-0.5)


def split_three(x):
    high = x.astype(jnp.bfloat16)
    rest = x - high.astype(jnp.float32)
    middle = rest.astype(jnp.bfloat16)
    low = (rest - middle.astype(jnp.float32)).astype(jnp.bfloat16)
    return high, middle, low


def in_parts(row):
    return jnp.concatenate(list(split_three(row)) + [jnp.zeros((13, row.shape[1]), jnp.bfloat16)], axis=0)


def dot_parts(parts, matrix):
    out = lax.dot_general(parts, matrix, (((1,), (1,)), ((), ())), preferred_element_type=jnp.float32)
    return out[0:1] + out[1:2] + out[2:3]


def idle_kernel(*refs):
    pass


def after(array, *others):
    return pl.pallas_call(
        idle_kernel,
        out_shape=jax.ShapeDtypeStruct(array.shape, array.dtype),
        in_specs=[pl.BlockSpec(memory_space=pl.ANY)] * (1 + len(others)),
        out_specs=pl.BlockSpec(memory_space=pl.ANY),
        input_output_aliases={0: 0},
        compiler_params=params(),
        cost_estimate=cost(1),
        name="after",
    )(array, *others)


def rows_of(count, like, dtype=jnp.bfloat16):
    return jax.ShapeDtypeStruct((count, like.shape[1]), dtype)


def call(kernel, name, out_shape, *operands, tokens=()):
    def with_tokens(*refs):
        kernel(*refs[: len(operands)], *refs[len(operands) + len(tokens) :])

    return pl.pallas_call(
        with_tokens,
        out_shape=out_shape,
        in_specs=[WHOLE] * len(operands) + [pl.BlockSpec(memory_space=pl.ANY)] * len(tokens),
        out_specs=[WHOLE] * len(out_shape),
        compiler_params=params(),
        cost_estimate=cost(10**6),
        name=name,
    )(*operands, *tokens)


def inner_kernel(direction_ref, weight_ref, parts_ref, norm_ref, here_ref):
    everything = direction_ref[...]
    norm_ref[...] = jnp.broadcast_to(
        jnp.sum(everything * everything, axis=1, keepdims=True) + EPSILON, norm_ref.shape
    )
    size, width = weight_ref.shape[1], here_ref.shape[1]
    here_ref[...] = direction_ref[:, pl.ds(pl.multiple_of(lax.axis_index("tp") * width, LANES), width)]
    here = direction_ref[:, pl.ds(pl.multiple_of(lax.axis_index("ctx") * size, LANES), size)]
    parts_ref[...] = in_parts(dot_parts(in_parts(here), weight_ref[...]))


def run_inner(direction, weight):
    out_shape = [
        jax.ShapeDtypeStruct((STEP, weight.shape[0]), jnp.bfloat16),
        jax.ShapeDtypeStruct((1, LANES), jnp.float32),
        jax.ShapeDtypeStruct((1, weight.shape[1] // 2), jnp.float32),
    ]
    return call(inner_kernel, "inner", out_shape, direction, weight)


def project_kernel(begin, weight_ref, piece_ref, *outs):
    *sends, keep_ref = outs
    rows, width = keep_ref.shape
    cut = width // len(sends)
    side = lax.axis_index("tp") % 2
    for start in range(0, 2 * width, 256):
        away = start < width
        ref, to = (sends[start // cut], start % cut) if away else (keep_ref, start - width)
        which = 1 - side if away else side
        columns = pl.ds(pl.multiple_of(which * width + start % width, 256), 256)
        out = jnp.dot(piece_ref[begin : begin + rows, :], weight_ref[:, columns], preferred_element_type=jnp.float32)
        ref[:rows, to : to + 256] = out.astype(ref.dtype)


def run_project(weight, piece, begin, rows, count, *tokens):
    keep = jax.ShapeDtypeStruct((rows, weight.shape[1] // 2), jnp.float32)
    sends = [jax.ShapeDtypeStruct((rows, keep.shape[1] // count), jnp.bfloat16)] * count
    kernel = functools.partial(project_kernel, begin)
    *sends, keep = call(kernel, "project", [*sends, keep], weight, piece, tokens=tokens)
    return sends, keep


def put_behind(ref, rows, row):
    here = slice(rows, rows + STEP)
    ref[here, :] = jnp.zeros((STEP, ref.shape[1]), jnp.bfloat16)
    ref[here, : row.shape[1]] = in_parts(row)


def take_behind(ref, rows, width):
    return jnp.sum(ref[rows : rows + STEP, :width].astype(jnp.float32), axis=0, keepdims=True)


def level_kernel(parts_ref, far_ref, whole_ref, out_ref):
    far_parts = far_ref[far_ref.shape[0] - STEP :, :]
    out_ref[...] = dot_parts(parts_ref[...], whole_ref[...]) + dot_parts(far_parts, whole_ref[...])


def add_shares(lefts, rights, outs):
    width = sum(ref.shape[1] for ref in lefts)
    rows = lefts[0].shape[0]
    step = min(ref.shape[1] for ref in (*lefts, *rights, *outs))

    def at(pieces, row, column):
        size = pieces[0].shape[1]
        return pieces[column // size].at[row : row + STEP, column % size : column % size + step]

    for row in range(0, rows, STEP):
        for column in range(0, width, step):
            left = at(lefts, row, column)[...].astype(jnp.float32)
            right = at(rights, row, column)[...].astype(jnp.float32)
            at(outs, row, column)[...] = (left + right).astype(jnp.bfloat16)


def merge_kernel(left, right, *refs):
    add_shares(refs[:left], refs[left : left + right], refs[left + right :])


def run_merge(lefts, rights, count):
    rows, width = lefts[0].shape[0], sum(x.shape[1] for x in lefts)
    kernel = functools.partial(merge_kernel, len(lefts), len(rights))
    out_shape = [jax.ShapeDtypeStruct((rows, width // count), jnp.bfloat16)] * count
    return call(kernel, "merge", out_shape, *lefts, *rights)


def merge_parts_kernel(keep_ref, parts_ref, *refs):
    add_shares((keep_ref,), refs[:-1], refs[-1:])
    refs[-1][keep_ref.shape[0] :, :] = parts_ref[...]


def is_keeper():
    return lax.axis_index("tp") // 2 == lax.axis_index("ctx")


def choose_kernel(straight_ref, own_ref, level_ref, other_ref, out_ref, total_ref):
    keeper = is_keeper()

    @pl.when(keeper)
    def _():
        rows = straight_ref.shape[0] - STEP
        out_ref[:rows, :] = straight_ref[:rows, :]

    @pl.when(jnp.logical_not(keeper))
    def _():
        out_ref[: own_ref.shape[0], :] = own_ref[...]

    total = level_ref[...] + other_ref[...]
    total_ref[...] = total
    put_behind(out_ref, out_ref.shape[0] - STEP, total)


def finish_kernel(*refs):
    level_ref, norm_ref, direction_ref = refs[:3]
    own0, own1, (straight_ref, merged_ref) = refs[3:6], refs[6:9], refs[9:11]
    out_hbm, level_hbm, out_near, level_near, sems = refs[11:]
    turned_ref = own1[-1]
    rows, width = out_near.shape
    half = straight_ref.shape[0] - STEP
    keeper = is_keeper()
    level = (level_ref[...] + take_behind(turned_ref, turned_ref.shape[0] - STEP, rows)) / norm_ref[0:1, 0:1]
    level_near[...] = level
    copies = [pltpu.make_async_copy(level_near, level_hbm, sems.at[sems.shape[0] - 1])]
    copies[0].start()
    direction = direction_ref[...]
    column = jnp.transpose(jnp.broadcast_to(level, (LANES, rows)))

    def put(row, cut, before, behind):
        pieces, start = (before, row) if row < cut else (behind, row - cut)
        total = pieces[0][start : start + STEP, :].astype(jnp.float32)
        for piece in pieces[1:]:
            total = total + piece[start : start + STEP, :].astype(jnp.float32)
        total = total - column[row : row + STEP, 0:1] * direction
        out_near[row : row + STEP, :] = total.astype(jnp.bfloat16)

    count = sems.shape[0] - 1
    for i in range(count):
        begin, end = i * rows // count, (i + 1) * rows // count

        @pl.when(keeper)
        def _():
            for row in range(begin, end, STEP):
                put(row, own0[0].shape[0], own0, own1)

        @pl.when(jnp.logical_not(keeper))
        def _():
            for row in range(begin, end, STEP):
                put(row, half, (straight_ref, turned_ref), (merged_ref,))

        here = pl.ds(begin, end - begin)
        copies.append(pltpu.make_async_copy(out_near.at[here], out_hbm.at[here], sems.at[i]))
        copies[-1].start()
    for copy in copies:
        copy.wait()


def run_finish(*operands):
    rows, width = operands[0].shape[1], operands[2].shape[1]
    return pl.pallas_call(
        finish_kernel,
        out_shape=[pltpu.HBM((rows, width), jnp.bfloat16), pltpu.HBM((1, rows), jnp.float32)],
        in_specs=[WHOLE] * len(operands),
        out_specs=[AWAY] * 2,
        scratch_shapes=[
            pltpu.VMEM((rows, width), jnp.bfloat16),
            pltpu.VMEM((1, rows), jnp.float32),
            pltpu.SemaphoreType.DMA((5,)),
        ],
        compiler_params=params(),
        cost_estimate=cost(10**6),
        name="finish",
    )(*operands)


def plane_plan(q, k, v, short_taps, decay_rate, residue, out_weight, direction):
    rows, width = q.shape
    cut, early = rows * 8 // 16, rows * 7 // 16
    blocks = width // LANES
    axes = ("ctx", "tp")
    across = [(4 * c + p, 4 * (1 - c) + p) for c in range(2) for p in range(4)]
    sibling = [(4 * c + p, 4 * c + (p ^ 1)) for c in range(2) for p in range(4)]
    pair = [(4 * c + p, 4 * c + (p ^ 2)) for c in range(2) for p in range(4)]

    ended, signal, decay, taps, edge, rate, residue, q = run_front(q, k, v, short_taps, decay_rate.T, residue.T)
    carry = lax.ppermute(ended, axes, across)
    local, query, gain, weight, direction = run_local(
        q, signal, decay, taps, gains_of(rate, residue), out_weight, direction.reshape(1, -1)
    )
    first, second, whole = run_correct(carry, decay, gain, taps, edge, local, query, blocks, cut, rows - cut)
    far_first = lax.ppermute(first, axes, across)
    far_second = lax.ppermute(second, axes, across)

    def exchange(arrays, pairs):
        return [lax.ppermute(array, axes, pairs) for array in arrays]

    weight = after(weight, whole)
    parts, norm, direction = run_inner(direction, weight)
    sends0, keep0 = run_project(weight, whole, 0, early, 1)
    sends1, keep1 = run_project(weight, whole, early, rows - early, 1)
    (core0,) = exchange(sends0, sibling)
    (hop0,) = exchange(run_merge((keep0,), (core0,), 1), pair)

    sends, far_keep = run_project(weight, far_first, 0, cut, 2, parts, *sends0, *sends1)
    (sums0,) = call(
        merge_parts_kernel, "merge", [rows_of(cut + STEP, far_keep)], far_keep, parts, *exchange(sends, sibling)
    )
    (straight,) = exchange([sums0], across)

    sends, far_keep = run_project(weight, after(far_second, sums0), 0, rows - cut, 2)
    sums1 = run_merge((far_keep,), exchange(sends, sibling), 2)
    moved = exchange(sums1, pair)
    (core1,) = exchange(sends1, sibling)
    (own1,) = run_merge((keep1,), (core1,), 1)

    one_row = jax.ShapeDtypeStruct((1, rows), jnp.float32)
    (level,) = call(level_kernel, "level", [one_row], parts, straight, whole)
    payload = rows_of(max(cut, rows - early) + STEP, far_keep)
    turned, level = call(
        choose_kernel,
        "choose",
        [payload, one_row],
        straight,
        own1,
        level,
        *exchange([level], sibling),
        tokens=(hop0,),
    )
    (turned,) = exchange([turned], pair)
    (merged,) = exchange(run_merge(sums1, moved, 1), across)
    ablated, level = run_finish(
        level, norm, direction, keep0, core0, hop0, keep1, core1, turned, straight, merged
    )
    return ablated, level.reshape(rows)


def gather_plan(q, k, v, short_taps, decay_rate, residue, out_weight, direction):
    rows, width = q.shape
    blocks = width // LANES
    modes = decay_rate.shape[1]
    tp = lax.axis_index("tp")
    ctx_size = lax.axis_size("ctx")
    next_one = [(i, i + 1) for i in range(ctx_size - 1)]
    ended, signal, decay, taps, edge, rate, residue, q = run_front(q, k, v, short_taps, decay_rate.T, residue.T)
    halo = lax.ppermute(ended[modes * blocks :], "ctx", next_one)
    local, query, gain = run_local(q, signal, decay, taps, gains_of(rate, residue))
    k2, k1, v2, v1 = [halo[i * blocks : (i + 1) * blocks] for i in range(4)]
    tap = taps.reshape(9, blocks, LANES)
    key0, key1, value0, value1 = edge.reshape(4, blocks, LANES)
    extra0 = (key0 + tap[4] * k1 + tap[5] * k2) * (value0 + tap[7] * v1 + tap[8] * v2) - key0 * value0
    extra1 = (key1 + tap[5] * k1) * (value1 + tap[8] * v1) - key1 * value1
    wide_rate = decay_rate.T.reshape(modes, blocks, LANES)
    state = (
        ended[: modes * blocks].reshape(modes, blocks, LANES)
        + jnp.exp(-wide_rate * (rows - 1)) * extra0
        + jnp.exp(-wide_rate * (rows - 2)) * extra1
    )
    reach = 1
    while reach < ctx_size:
        earlier = lax.ppermute(state, "ctx", [(i, i + reach) for i in range(ctx_size - reach)])
        state = state + jnp.exp(-wide_rate * (rows * reach)) * earlier
        reach *= 2
    start = lax.ppermute(state, "ctx", next_one).reshape(modes * blocks, LANES)
    carry = jnp.concatenate([start, halo], axis=0)
    (gated,) = run_correct(carry, decay, gain, taps, edge, local, query, blocks)
    partial_terms = lax.dot_general(
        gated,
        lax.all_gather(out_weight, "ctx", axis=1, tiled=True),
        (((1,), (0,)), ((), ())),
        preferred_element_type=jnp.float32,
    )
    summed = lax.psum_scatter(
        partial_terms.astype(jnp.bfloat16), "tp", scatter_dimension=1, tiled=True
    ).astype(jnp.float32)
    width_here = summed.shape[1]
    direction_here = lax.dynamic_slice_in_dim(direction, tp * width_here, width_here, 0)
    norm_total = jnp.sum(direction * direction) + EPSILON
    local_inner = jnp.dot(summed, direction_here, precision=HIGHEST)
    feature_level = lax.psum(local_inner, "tp") / norm_total
    ablated = (summed - feature_level[:, None] * direction_here[None, :]).astype(jnp.bfloat16)
    return ablated, feature_level


def solution(mesh):
    placed = (
        P(("dp", "ctx"), "tp"),
        P(("dp", "ctx"), "tp"),
        P(("dp", "ctx"), "tp"),
        P(None, None, "tp"),
        P("tp", None),
        P("tp", None),
        P("tp", "ctx"),
        P(),
    )
    plane = mesh.shape["ctx"] == 2 and mesh.shape["tp"] == 4
    return jax.shard_map(
        plane_plan if plane else gather_plan,
        mesh=mesh,
        in_specs=placed,
        out_specs=(P(("dp", "ctx"), "tp"), P(("dp", "ctx"))),
        check_vma=False,
    )
```

```python
import functools

import jax
import jax.numpy as jnp
from jax import lax
from jax.experimental import pallas as pl
from jax.experimental.pallas import tpu as pltpu
from jax.sharding import PartitionSpec as P

EPSILON = 1e-06
HIGHEST = lax.Precision.HIGHEST
LANES = 128
GROUP = 8
STEP = 16
WHOLE = pl.BlockSpec(memory_space=pltpu.VMEM)
AWAY = pl.BlockSpec(memory_space=pltpu.HBM)


def params(mebibytes=20):
    return pltpu.CompilerParams(vmem_limit_bytes=mebibytes * 1024 * 1024)


def cost(flops):
    return pl.CostEstimate(flops=flops, bytes_accessed=1024, transcendentals=0)


def spread(source, scratch, row, to):
    blocks = source.shape[1] // LANES
    for block in range(blocks):
        piece = source[pl.ds(row, STEP), block * LANES : (block + 1) * LANES].astype(jnp.float32)
        for half in range(STEP // GROUP):
            start = (half * blocks + block) * GROUP
            scratch[pl.ds(to + start, GROUP), :] = piece[half * GROUP : (half + 1) * GROUP]


def spread_rows(source, target):
    count, width = source.shape
    blocks = width // LANES
    for block in range(blocks):
        target[pl.ds(block, count, stride=blocks), :] = source[:, block * LANES : (block + 1) * LANES]


def place_of(index, blocks):
    return pl.ds((index // GROUP) * (blocks * GROUP) + index % GROUP, blocks, stride=GROUP)


def tile(ref, index, blocks):
    return ref[index * blocks : (index + 1) * blocks, :]


def moving_tile(index, blocks):
    return pl.ds(pl.multiple_of(index * blocks, blocks), blocks)


def front_kernel(*refs):
    k_hbm, v_hbm, q_hbm, taps_hbm, rate_hbm, residue_hbm = refs[:6]
    carry_ref, signal_ref, decay_ref, taps_ref, edge_ref, rate_ref, residue_ref, q_near = refs[6:14]
    k_near, v_near, taps_near, *wides, sems, late_sems = refs[-9:]
    wides = (wides[:2], wides[2:])
    rows, width = k_near.shape
    blocks = width // LANES
    modes = rate_ref.shape[0]
    pieces = sems.shape[0] // 2 - 1
    height = rows // pieces

    def part(i):
        here = pl.ds(i * height, height)
        return (
            pltpu.make_async_copy(k_hbm.at[here], k_near.at[here], sems.at[2 * i]),
            pltpu.make_async_copy(v_hbm.at[here], v_near.at[here], sems.at[2 * i + 1]),
        )

    rate_copy = pltpu.make_async_copy(rate_hbm, rate_ref, sems.at[2 * pieces])
    taps_copy = pltpu.make_async_copy(taps_hbm, taps_near, sems.at[2 * pieces + 1])
    late = [(residue_hbm, residue_ref), (q_hbm, q_near)]
    late = [pltpu.make_async_copy(source, target, late_sems.at[i]) for i, (source, target) in enumerate(late)]
    rate_copy.start()
    taps_copy.start()
    for i in range(pieces):
        for copy in part(i):
            copy.start()
    for copy in late:
        copy.start()
    rate_copy.wait()
    taps_copy.wait()
    spread_rows(jnp.exp(-rate_ref[...]), decay_ref)
    for i in range(3):
        for block in range(blocks):
            taps_ref[pl.ds(3 * i * blocks + block, 3, stride=blocks), :] = taps_near[
                i, :, block * LANES : (block + 1) * LANES
            ]
    zero = jnp.zeros((blocks, LANES), jnp.float32)
    key_taps = [tile(taps_ref, 3 + j, blocks) for j in range(3)]
    value_taps = [tile(taps_ref, 6 + j, blocks) for j in range(3)]
    decay = [tile(decay_ref, m, blocks) for m in range(modes)]

    def step(row, held):
        state, (k2, k1, v2, v1) = list(held[:modes]), held[modes:]
        for half, (k_wide, v_wide) in enumerate(wides):
            spread(k_near, k_wide, row + half * STEP, 0)
            spread(v_near, v_wide, row + half * STEP, 0)
        for half, (k_wide, v_wide) in enumerate(wides):
            for index in range(STEP):
                k0 = k_wide[place_of(index, blocks), :]
                v0 = v_wide[place_of(index, blocks), :]
                key = key_taps[0] * k0 + key_taps[1] * k1 + key_taps[2] * k2
                value = value_taps[0] * v0 + value_taps[1] * v1 + value_taps[2] * v2
                signal = key * value
                signal_ref[moving_tile(row + half * STEP + index, blocks), :] = signal
                state = [decay[m] * state[m] + signal for m in range(modes)]
                k2, k1, v2, v1 = k1, k0, v1, v0
        return tuple(state) + (k2, k1, v2, v1)

    held = (zero,) * (modes + 4)
    for i in range(pieces):
        for copy in part(i):
            copy.wait()
        if i == 0:
            spread(k_near, wides[0][0], 0, 0)
            spread(v_near, wides[0][1], 0, 0)
            for wide, taps, place in ((wides[0][0], key_taps, 0), (wides[0][1], value_taps, 2)):
                x0, x1 = wide[place_of(0, blocks), :], wide[place_of(1, blocks), :]
                edge_ref[place * blocks : (place + 1) * blocks, :] = taps[0] * x0
                edge_ref[(place + 1) * blocks : (place + 2) * blocks, :] = taps[0] * x1 + taps[1] * x0
        held = lax.fori_loop(
            0,
            height // (2 * STEP),
            lambda j, held, i=i: step(pl.multiple_of(i * height + j * 2 * STEP, 2 * STEP), held),
            held,
        )
    for m in range(modes + 4):
        carry_ref[m * blocks : (m + 1) * blocks, :] = held[m]
    for copy in late:
        copy.wait()
    k_wide = wides[0][0]
    spread(q_near, k_wide, rows - STEP, 0)
    for i in range(2):
        start = (modes + 4 + i) * blocks
        carry_ref[start : start + blocks, :] = k_wide[place_of(STEP - 2 + i, blocks), :]


def far(x):
    return pltpu.with_memory_space_constraint(x, pltpu.HBM)


def run_front(q, k, v, short_taps, rate, residue):
    rows, width = k.shape
    modes = rate.shape[0]
    blocks = width // LANES
    pieces = 4

    def wide(n):
        return jax.ShapeDtypeStruct((n * blocks, LANES), jnp.float32)

    def like(x):
        return jax.ShapeDtypeStruct(x.shape, x.dtype)

    out_shape = [wide(modes + 6), wide(rows), wide(modes), wide(9), wide(4), like(rate), like(residue), like(q)]
    return pl.pallas_call(
        front_kernel,
        out_shape=out_shape,
        in_specs=[AWAY] * 6,
        out_specs=[WHOLE] * len(out_shape),
        scratch_shapes=[
            pltpu.VMEM((rows, width), jnp.bfloat16),
            pltpu.VMEM((rows, width), jnp.bfloat16),
            pltpu.VMEM(short_taps.shape, jnp.float32),
            *[pltpu.VMEM((STEP * blocks, LANES), jnp.float32)] * 4,
            pltpu.SemaphoreType.DMA((2 * pieces + 2,)),
            pltpu.SemaphoreType.DMA((2,)),
        ],
        compiler_params=params(),
        cost_estimate=cost(10**8),
        name="front",
    )(*[far(x) for x in (k, v, q, short_taps, rate, residue)])


def local_kernel(q_near, signal_ref, decay_ref, taps_ref, gain_near, *refs):
    copies = []
    if len(refs) > 5:
        weight_hbm, direction_hbm, weight_ref, direction_ref, sems = refs[:2] + refs[5:7] + refs[-1:]
        refs = refs[2:5] + refs[7:-1]
        count = sems.shape[0] - 1
        copies.append(pltpu.make_async_copy(direction_hbm, direction_ref, sems.at[count]))
        copies[-1].start()
        depth = weight_ref.shape[0] // count
        for i in range(count):
            here = pl.ds(i * depth, depth)
            copies.append(pltpu.make_async_copy(weight_hbm.at[here], weight_ref.at[here], sems.at[i]))
            copies[-1].start()
    out_ref, query_ref, gain_ref, *wides = refs
    rows, width = q_near.shape
    blocks = width // LANES
    modes = gain_near.shape[0]
    spread_rows(gain_near[...], gain_ref)
    zero = jnp.zeros((blocks, LANES), jnp.float32)
    taps = [tile(taps_ref, j, blocks) for j in range(3)]
    decay = [tile(decay_ref, m, blocks) for m in range(modes)]
    gain = [tile(gain_ref, m, blocks) for m in range(modes)]

    def step(j, held):
        row = pl.multiple_of(j * 2 * STEP, 2 * STEP)
        state, (q2, q1) = list(held[:modes]), held[modes:]
        for half, q_wide in enumerate(wides):
            spread(q_near, q_wide, row + half * STEP, 0)
        for half, q_wide in enumerate(wides):
            for index in range(STEP):
                q0 = q_wide[place_of(index, blocks), :]
                here = moving_tile(row + half * STEP + index, blocks)
                signal = signal_ref[here, :]
                query_ref[here, :] = taps[0] * q0 + taps[1] * q1 + taps[2] * q2
                state = [decay[m] * state[m] + signal for m in range(modes)]
                sums = [gain[m] * state[m] for m in range(modes)]
                while len(sums) > 1:
                    sums = [sums[i] + sums[i + 1] for i in range(0, len(sums), 2)]
                out_ref[here, :] = sums[0]
                q2, q1 = q1, q0
        return tuple(state) + (q2, q1)

    lax.fori_loop(0, rows // (2 * STEP), step, (zero,) * (modes + 2))
    for copy in copies:
        copy.wait()


def run_local(q, signal, decay, taps, gain, *weight):
    rows, width = q.shape
    blocks = width // LANES
    wide = jax.ShapeDtypeStruct((rows * blocks, LANES), jnp.float32)
    out_shape = [wide, wide, jax.ShapeDtypeStruct(decay.shape, jnp.float32)]
    scratch_shapes = [pltpu.VMEM((STEP * blocks, LANES), jnp.float32)] * 2
    if weight:
        out_shape += [jax.ShapeDtypeStruct(x.shape, x.dtype) for x in weight]
        scratch_shapes.append(pltpu.SemaphoreType.DMA((5,)))
        weight = tuple(far(x) for x in weight)
    return pl.pallas_call(
        local_kernel,
        out_shape=out_shape,
        in_specs=[WHOLE] * 5 + [AWAY] * len(weight),
        out_specs=[WHOLE] * len(out_shape),
        scratch_shapes=scratch_shapes,
        compiler_params=params(),
        cost_estimate=cost(10**6),
        name="local_filter",
    )(q, signal, decay, taps, gain, *weight)


def correct_kernel(blocks, carry_ref, decay_ref, gain_ref, taps_ref, edge_ref, local_ref, query_ref, *refs):
    wide, outs = refs[-1], refs[:-1]
    rows = local_ref.shape[0] // blocks
    weight_ref = None
    if len(outs) > 1:
        weight_ref, *outs, send_ref, keep_ref = outs
    modes = decay_ref.shape[0] // blocks
    carried = jnp.where(lax.axis_index("ctx") > 0, 1.0, 0.0)
    k2, k1, v2, v1, q2, q1 = [carried * tile(carry_ref, modes + i, blocks) for i in range(6)]
    tap = [tile(taps_ref, i, blocks) for i in range(9)]
    key0, key1, value0, value1 = [tile(edge_ref, i, blocks) for i in range(4)]
    extra = [
        (key0 + tap[4] * k1 + tap[5] * k2) * (value0 + tap[7] * v1 + tap[8] * v2) - key0 * value0,
        (key1 + tap[5] * k1) * (value1 + tap[8] * v1) - key1 * value1,
    ]
    query_extra = [tap[1] * q1 + tap[2] * q2, tap[2] * q1]
    state = [tile(gain_ref, m, blocks) * (carried * tile(carry_ref, m, blocks)) for m in range(modes)]
    decay = [tile(decay_ref, m, blocks) for m in range(modes)]

    def step(row, state, first, piece_ref, start):
        state = list(state)
        for index in range(STEP):
            here = moving_tile(row + index, blocks)
            state = [decay[m] * state[m] for m in range(modes)]
            query = query_ref[here, :]
            if first and index < 2:
                state = [state[m] + tile(gain_ref, m, blocks) * extra[index] for m in range(modes)]
                query = query + query_extra[index]
            sums = state
            while len(sums) > 1:
                sums = [sums[i] + sums[i + 1] for i in range(0, len(sums), 2)]
            wide[place_of(index, blocks), :] = query * (local_ref[here, :] + sums[0])
        for block in range(blocks):
            halves = [
                wide[(half * blocks + block) * GROUP : (half * blocks + block + 1) * GROUP, :]
                for half in range(STEP // GROUP)
            ]
            rounded = jnp.concatenate(halves, axis=0).astype(jnp.bfloat16)
            columns = slice(block * LANES, (block + 1) * LANES)
            outs[-1][pl.ds(row, STEP), columns] = rounded
            if piece_ref is not None:
                piece_ref[pl.ds(pl.multiple_of(row - start, STEP), STEP), columns] = rounded
        return tuple(state)

    def products(j, which, ref):
        columns = pl.ds(pl.multiple_of(which * ref.shape[1] + j * 256, 256), 256)
        out = jnp.dot(outs[0][...], weight_ref[:, columns], preferred_element_type=jnp.float32)
        ref[:, pl.ds(pl.multiple_of(j * 256, 256), 256)] = out.astype(ref.dtype)

    def run(state, begin, end, piece_ref, start, beside):
        def body(j, state):
            if beside is not None:
                products(j - begin, *beside)
            return step(pl.multiple_of(j * STEP, STEP), state, False, piece_ref, start)

        return lax.fori_loop(begin, end, body, state)

    count = rows // STEP
    if weight_ref is None:
        run(step(0, tuple(state), True, None, 0), 1, count, None, 0, None)
    else:
        cut = outs[0].shape[0] // STEP
        parts = keep_ref.shape[1] // 256
        side = lax.axis_index("tp") % 2
        state = run(step(0, tuple(state), True, outs[0], 0), 1, cut, outs[0], 0, None)
        state = run(state, cut, cut + parts, outs[1], cut * STEP, (1 - side, send_ref))
        state = run(state, cut + parts, cut + 2 * parts, outs[1], cut * STEP, (side, keep_ref))
        run(state, cut + 2 * parts, count, outs[1], cut * STEP, None)


def run_correct(carry, decay, gain, taps, edge, local, query, blocks, cut=0, *weight):
    rows, width = local.shape[0] // blocks, blocks * LANES
    heights = [cut, rows - cut, rows] if weight else [rows]
    out_shape = [jax.ShapeDtypeStruct((height, width), jnp.bfloat16) for height in heights]
    for x in weight:
        out_shape.append(jax.ShapeDtypeStruct((cut, x.shape[1] // 2), jnp.bfloat16))
        out_shape.append(jax.ShapeDtypeStruct((cut, x.shape[1] // 2), jnp.float32))
    return pl.pallas_call(
        functools.partial(correct_kernel, blocks),
        out_shape=out_shape,
        in_specs=[WHOLE] * (7 + len(weight)),
        out_specs=[WHOLE] * len(out_shape),
        scratch_shapes=[pltpu.VMEM((STEP * blocks, LANES), jnp.float32)],
        compiler_params=params(),
        cost_estimate=cost(10**8),
        name="carried_filter",
    )(carry, decay, gain, taps, edge, local, query, *weight)


def gains_of(rate, residue):
    return residue * jnp.sqrt(-jnp.expm1(-2.0 * rate)) * rate.shape[0] ** (-0.5)


def split_three(x):
    high = x.astype(jnp.bfloat16)
    rest = x - high.astype(jnp.float32)
    middle = rest.astype(jnp.bfloat16)
    low = (rest - middle.astype(jnp.float32)).astype(jnp.bfloat16)
    return high, middle, low


def in_parts(row):
    return jnp.concatenate(list(split_three(row)) + [jnp.zeros((13, row.shape[1]), jnp.bfloat16)], axis=0)


def dot_parts(parts, matrix):
    out = lax.dot_general(parts, matrix, (((1,), (1,)), ((), ())), preferred_element_type=jnp.float32)
    return out[0:1] + out[1:2] + out[2:3]


def idle_kernel(*refs):
    pass


def after(array, *others):
    return pl.pallas_call(
        idle_kernel,
        out_shape=jax.ShapeDtypeStruct(array.shape, array.dtype),
        in_specs=[pl.BlockSpec(memory_space=pl.ANY)] * (1 + len(others)),
        out_specs=pl.BlockSpec(memory_space=pl.ANY),
        input_output_aliases={0: 0},
        compiler_params=params(),
        cost_estimate=cost(1),
        name="after",
    )(array, *others)


def rows_of(count, like, dtype=jnp.bfloat16):
    return jax.ShapeDtypeStruct((count, like.shape[1]), dtype)


def call(kernel, name, out_shape, *operands, tokens=()):
    def with_tokens(*refs):
        kernel(*refs[: len(operands)], *refs[len(operands) + len(tokens) :])

    return pl.pallas_call(
        with_tokens,
        out_shape=out_shape,
        in_specs=[WHOLE] * len(operands) + [pl.BlockSpec(memory_space=pl.ANY)] * len(tokens),
        out_specs=[WHOLE] * len(out_shape),
        compiler_params=params(),
        cost_estimate=cost(10**6),
        name=name,
    )(*operands, *tokens)


def inner_kernel(direction_ref, weight_ref, parts_ref, norm_ref, here_ref):
    everything = direction_ref[...]
    norm_ref[...] = jnp.broadcast_to(
        jnp.sum(everything * everything, axis=1, keepdims=True) + EPSILON, norm_ref.shape
    )
    size, width = weight_ref.shape[1], here_ref.shape[1]
    here_ref[...] = direction_ref[:, pl.ds(pl.multiple_of(lax.axis_index("tp") * width, LANES), width)]
    here = direction_ref[:, pl.ds(pl.multiple_of(lax.axis_index("ctx") * size, LANES), size)]
    parts_ref[...] = in_parts(dot_parts(in_parts(here), weight_ref[...]))


def run_inner(direction, weight):
    out_shape = [
        jax.ShapeDtypeStruct((STEP, weight.shape[0]), jnp.bfloat16),
        jax.ShapeDtypeStruct((1, LANES), jnp.float32),
        jax.ShapeDtypeStruct((1, weight.shape[1] // 2), jnp.float32),
    ]
    return call(inner_kernel, "inner", out_shape, direction, weight)


def project_kernel(begin, rows, away, weight_ref, piece_ref, *outs):
    cut = outs[0].shape[1]
    width = cut * len(outs)
    side = lax.axis_index("tp") % 2
    which = 1 - side if away else side
    for start in range(0, width, 256):
        columns = pl.ds(pl.multiple_of(which * width + start, 256), 256)
        out = jnp.dot(piece_ref[begin : begin + rows, :], weight_ref[:, columns], preferred_element_type=jnp.float32)
        ref, to = outs[start // cut], start % cut
        ref[:, to : to + 256] = out.astype(ref.dtype)


def run_project(weight, piece, begin, rows, count, *tokens):
    width = weight.shape[1] // 2
    sends = [jax.ShapeDtypeStruct((rows, width // count), jnp.bfloat16)] * count
    keep = [jax.ShapeDtypeStruct((rows, width), jnp.float32)]
    away, here = [functools.partial(project_kernel, begin, rows, x) for x in (True, False)]
    sends = call(away, "project", sends, weight, piece, tokens=tokens)
    return sends, call(here, "project", keep, weight, piece, tokens=tokens)[0]


def put_behind(ref, rows, row):
    here = slice(rows, rows + STEP)
    ref[here, :] = jnp.zeros((STEP, ref.shape[1]), jnp.bfloat16)
    ref[here, : row.shape[1]] = in_parts(row)


def take_behind(ref, rows, width):
    return jnp.sum(ref[rows : rows + STEP, :width].astype(jnp.float32), axis=0, keepdims=True)


def level_kernel(parts_ref, far_ref, whole_ref, out_ref):
    far_parts = far_ref[far_ref.shape[0] - STEP :, :]
    out_ref[...] = dot_parts(parts_ref[...], whole_ref[...]) + dot_parts(far_parts, whole_ref[...])


def add_shares(lefts, rights, outs):
    width = sum(ref.shape[1] for ref in lefts)
    rows = lefts[0].shape[0]
    step = min(ref.shape[1] for ref in (*lefts, *rights, *outs))

    def at(pieces, row, column):
        size = pieces[0].shape[1]
        return pieces[column // size].at[row : row + STEP, column % size : column % size + step]

    for row in range(0, rows, STEP):
        for column in range(0, width, step):
            left = at(lefts, row, column)[...].astype(jnp.float32)
            right = at(rights, row, column)[...].astype(jnp.float32)
            at(outs, row, column)[...] = (left + right).astype(jnp.bfloat16)


def merge_kernel(left, right, *refs):
    add_shares(refs[:left], refs[left : left + right], refs[left + right :])


def run_merge(lefts, rights, count):
    rows, width = lefts[0].shape[0], sum(x.shape[1] for x in lefts)
    kernel = functools.partial(merge_kernel, len(lefts), len(rights))
    out_shape = [jax.ShapeDtypeStruct((rows, width // count), jnp.bfloat16)] * count
    return call(kernel, "merge", out_shape, *lefts, *rights)


def merge_parts_kernel(keep_ref, parts_ref, *refs):
    add_shares((keep_ref,), refs[:-1], refs[-1:])
    refs[-1][keep_ref.shape[0] :, :] = parts_ref[...]


def is_keeper():
    return lax.axis_index("tp") // 2 == lax.axis_index("ctx")


def choose_kernel(straight_ref, own_ref, level_ref, other_ref, out_ref, total_ref):
    keeper = is_keeper()

    @pl.when(keeper)
    def _():
        rows = straight_ref.shape[0] - STEP
        out_ref[:rows, :] = straight_ref[:rows, :]

    @pl.when(jnp.logical_not(keeper))
    def _():
        out_ref[: own_ref.shape[0], :] = own_ref[...]

    total = level_ref[...] + other_ref[...]
    total_ref[...] = total
    put_behind(out_ref, out_ref.shape[0] - STEP, total)


def finish_kernel(*refs):
    level_ref, norm_ref, direction_ref = refs[:3]
    own0, own1, (straight_ref, merged_ref) = refs[3:6], refs[6:9], refs[9:11]
    out_hbm, level_hbm, out_near, level_near, sems = refs[11:]
    turned_ref = own1[-1]
    rows, width = out_near.shape
    half = straight_ref.shape[0] - STEP
    keeper = is_keeper()
    level = (level_ref[...] + take_behind(turned_ref, turned_ref.shape[0] - STEP, rows)) / norm_ref[0:1, 0:1]
    level_near[...] = level
    copies = [pltpu.make_async_copy(level_near, level_hbm, sems.at[sems.shape[0] - 1])]
    copies[0].start()
    direction = direction_ref[...]
    column = jnp.transpose(jnp.broadcast_to(level, (LANES, rows)))

    def put(row, cut, before, behind):
        pieces, start = (before, row) if row < cut else (behind, row - cut)
        total = pieces[0][start : start + STEP, :].astype(jnp.float32)
        for piece in pieces[1:]:
            total = total + piece[start : start + STEP, :].astype(jnp.float32)
        total = total - column[row : row + STEP, 0:1] * direction
        out_near[row : row + STEP, :] = total.astype(jnp.bfloat16)

    count = sems.shape[0] - 1
    for i in range(count):
        begin, end = i * rows // count, (i + 1) * rows // count

        @pl.when(keeper)
        def _():
            for row in range(begin, end, STEP):
                put(row, own0[0].shape[0], own0, own1)

        @pl.when(jnp.logical_not(keeper))
        def _():
            for row in range(begin, end, STEP):
                put(row, half, (straight_ref, turned_ref), (merged_ref,))

        here = pl.ds(begin, end - begin)
        copies.append(pltpu.make_async_copy(out_near.at[here], out_hbm.at[here], sems.at[i]))
        copies[-1].start()
    for copy in copies:
        copy.wait()


def run_finish(*operands):
    rows, width = operands[0].shape[1], operands[2].shape[1]
    return pl.pallas_call(
        finish_kernel,
        out_shape=[pltpu.HBM((rows, width), jnp.bfloat16), pltpu.HBM((1, rows), jnp.float32)],
        in_specs=[WHOLE] * len(operands),
        out_specs=[AWAY] * 2,
        scratch_shapes=[
            pltpu.VMEM((rows, width), jnp.bfloat16),
            pltpu.VMEM((1, rows), jnp.float32),
            pltpu.SemaphoreType.DMA((5,)),
        ],
        compiler_params=params(),
        cost_estimate=cost(10**6),
        name="finish",
    )(*operands)


def plane_plan(q, k, v, short_taps, decay_rate, residue, out_weight, direction):
    rows, width = q.shape
    cut = early = rows // 2
    blocks = width // LANES
    axes = ("ctx", "tp")
    across = [(4 * c + p, 4 * (1 - c) + p) for c in range(2) for p in range(4)]
    sibling = [(4 * c + p, 4 * c + (p ^ 1)) for c in range(2) for p in range(4)]
    pair = [(4 * c + p, 4 * c + (p ^ 2)) for c in range(2) for p in range(4)]

    ended, signal, decay, taps, edge, rate, residue, q = run_front(q, k, v, short_taps, decay_rate.T, residue.T)
    carry = lax.ppermute(ended, axes, across)
    local, query, gain, weight, direction = run_local(
        q, signal, decay, taps, gains_of(rate, residue), out_weight, direction.reshape(1, -1)
    )
    first, second, whole, send0, keep0 = run_correct(
        carry, decay, gain, taps, edge, local, query, blocks, cut, weight
    )
    far_first = lax.ppermute(first, axes, across)
    far_second = lax.ppermute(second, axes, across)

    def exchange(arrays, pairs):
        return [lax.ppermute(array, axes, pairs) for array in arrays]

    weight = after(weight, whole)
    parts, norm, direction = run_inner(direction, weight)
    sends1, keep1 = run_project(weight, whole, early, rows - early, 1)
    (core0,) = exchange([send0], sibling)
    (hop0,) = exchange(run_merge((keep0,), (core0,), 1), pair)

    sends, far_keep = run_project(weight, far_first, 0, cut, 2, parts, *sends1)
    (sums0,) = call(
        merge_parts_kernel, "merge", [rows_of(cut + STEP, far_keep)], far_keep, parts, *exchange(sends, sibling)
    )
    (straight,) = exchange([sums0], across)

    sends, far_keep = run_project(weight, after(far_second, sums0, hop0), 0, rows - cut, 2)
    sums1 = run_merge((far_keep,), exchange(sends, sibling), 2)
    moved = exchange(sums1, pair)
    (core1,) = exchange(sends1, sibling)
    (own1,) = run_merge((keep1,), (core1,), 1)

    one_row = jax.ShapeDtypeStruct((1, rows), jnp.float32)
    (level,) = call(level_kernel, "level", [one_row], parts, straight, whole)
    payload = rows_of(max(cut, rows - early) + STEP, far_keep)
    turned, level = call(
        choose_kernel,
        "choose",
        [payload, one_row],
        straight,
        own1,
        level,
        *exchange([level], sibling),
    )
    (turned,) = exchange([turned], pair)
    (merged,) = exchange(run_merge(sums1, moved, 1), across)
    ablated, level = run_finish(
        level, norm, direction, keep0, core0, hop0, keep1, core1, turned, straight, merged
    )
    return ablated, level.reshape(rows)


def gather_plan(q, k, v, short_taps, decay_rate, residue, out_weight, direction):
    rows, width = q.shape
    blocks = width // LANES
    modes = decay_rate.shape[1]
    tp = lax.axis_index("tp")
    ctx_size = lax.axis_size("ctx")
    next_one = [(i, i + 1) for i in range(ctx_size - 1)]
    ended, signal, decay, taps, edge, rate, residue, q = run_front(q, k, v, short_taps, decay_rate.T, residue.T)
    halo = lax.ppermute(ended[modes * blocks :], "ctx", next_one)
    local, query, gain = run_local(q, signal, decay, taps, gains_of(rate, residue))
    k2, k1, v2, v1 = [halo[i * blocks : (i + 1) * blocks] for i in range(4)]
    tap = taps.reshape(9, blocks, LANES)
    key0, key1, value0, value1 = edge.reshape(4, blocks, LANES)
    extra0 = (key0 + tap[4] * k1 + tap[5] * k2) * (value0 + tap[7] * v1 + tap[8] * v2) - key0 * value0
    extra1 = (key1 + tap[5] * k1) * (value1 + tap[8] * v1) - key1 * value1
    wide_rate = decay_rate.T.reshape(modes, blocks, LANES)
    state = (
        ended[: modes * blocks].reshape(modes, blocks, LANES)
        + jnp.exp(-wide_rate * (rows - 1)) * extra0
        + jnp.exp(-wide_rate * (rows - 2)) * extra1
    )
    reach = 1
    while reach < ctx_size:
        earlier = lax.ppermute(state, "ctx", [(i, i + reach) for i in range(ctx_size - reach)])
        state = state + jnp.exp(-wide_rate * (rows * reach)) * earlier
        reach *= 2
    start = lax.ppermute(state, "ctx", next_one).reshape(modes * blocks, LANES)
    carry = jnp.concatenate([start, halo], axis=0)
    (gated,) = run_correct(carry, decay, gain, taps, edge, local, query, blocks)
    partial_terms = lax.dot_general(
        gated,
        lax.all_gather(out_weight, "ctx", axis=1, tiled=True),
        (((1,), (0,)), ((), ())),
        preferred_element_type=jnp.float32,
    )
    summed = lax.psum_scatter(
        partial_terms.astype(jnp.bfloat16), "tp", scatter_dimension=1, tiled=True
    ).astype(jnp.float32)
    width_here = summed.shape[1]
    direction_here = lax.dynamic_slice_in_dim(direction, tp * width_here, width_here, 0)
    norm_total = jnp.sum(direction * direction) + EPSILON
    local_inner = jnp.dot(summed, direction_here, precision=HIGHEST)
    feature_level = lax.psum(local_inner, "tp") / norm_total
    ablated = (summed - feature_level[:, None] * direction_here[None, :]).astype(jnp.bfloat16)
    return ablated, feature_level


def solution(mesh):
    placed = (
        P(("dp", "ctx"), "tp"),
        P(("dp", "ctx"), "tp"),
        P(("dp", "ctx"), "tp"),
        P(None, None, "tp"),
        P("tp", None),
        P("tp", None),
        P("tp", "ctx"),
        P(),
    )
    plane = mesh.shape["ctx"] == 2 and mesh.shape["tp"] == 4
    return jax.shard_map(
        plane_plan if plane else gather_plan,
        mesh=mesh,
        in_specs=placed,
        out_specs=(P(("dp", "ctx"), "tp"), P(("dp", "ctx"))),
        check_vma=False,
    )
```

```python
import functools

import jax
import jax.numpy as jnp
from jax import lax
from jax.experimental import pallas as pl
from jax.experimental.pallas import tpu as pltpu
from jax.sharding import PartitionSpec as P

EPSILON = 1e-06
HIGHEST = lax.Precision.HIGHEST
LANES = 128
GROUP = 8
STEP = 16
WHOLE = pl.BlockSpec(memory_space=pltpu.VMEM)
AWAY = pl.BlockSpec(memory_space=pltpu.HBM)


def params(mebibytes=20):
    return pltpu.CompilerParams(vmem_limit_bytes=mebibytes * 1024 * 1024)


def cost(flops):
    return pl.CostEstimate(flops=flops, bytes_accessed=1024, transcendentals=0)


def spread(source, scratch, row, to):
    blocks = source.shape[1] // LANES
    for block in range(blocks):
        piece = source[pl.ds(row, STEP), block * LANES : (block + 1) * LANES].astype(jnp.float32)
        for half in range(STEP // GROUP):
            start = (half * blocks + block) * GROUP
            scratch[pl.ds(to + start, GROUP), :] = piece[half * GROUP : (half + 1) * GROUP]


def spread_rows(source, target):
    count, width = source.shape
    blocks = width // LANES
    for block in range(blocks):
        target[pl.ds(block, count, stride=blocks), :] = source[:, block * LANES : (block + 1) * LANES]


def place_of(index, blocks):
    return pl.ds((index // GROUP) * (blocks * GROUP) + index % GROUP, blocks, stride=GROUP)


def tile(ref, index, blocks):
    return ref[index * blocks : (index + 1) * blocks, :]


def moving_tile(index, blocks):
    return pl.ds(pl.multiple_of(index * blocks, blocks), blocks)


def front_kernel(*refs):
    k_hbm, v_hbm, q_hbm, taps_hbm, rate_hbm, residue_hbm = refs[:6]
    carry_ref, signal_ref, decay_ref, taps_ref, edge_ref, rate_ref, residue_ref, q_near = refs[6:14]
    k_near, v_near, taps_near, *wides, sems, late_sems = refs[-9:]
    wides = (wides[:2], wides[2:])
    rows, width = k_near.shape
    blocks = width // LANES
    modes = rate_ref.shape[0]
    pieces = sems.shape[0] // 2 - 1
    height = rows // pieces

    def part(i):
        here = pl.ds(i * height, height)
        return (
            pltpu.make_async_copy(k_hbm.at[here], k_near.at[here], sems.at[2 * i]),
            pltpu.make_async_copy(v_hbm.at[here], v_near.at[here], sems.at[2 * i + 1]),
        )

    rate_copy = pltpu.make_async_copy(rate_hbm, rate_ref, sems.at[2 * pieces])
    taps_copy = pltpu.make_async_copy(taps_hbm, taps_near, sems.at[2 * pieces + 1])
    late = [(residue_hbm, residue_ref), (q_hbm, q_near)]
    late = [pltpu.make_async_copy(source, target, late_sems.at[i]) for i, (source, target) in enumerate(late)]
    rate_copy.start()
    taps_copy.start()
    for i in range(pieces):
        for copy in part(i):
            copy.start()
    for copy in late:
        copy.start()
    rate_copy.wait()
    taps_copy.wait()
    spread_rows(jnp.exp(-rate_ref[...]), decay_ref)
    for i in range(3):
        for block in range(blocks):
            taps_ref[pl.ds(3 * i * blocks + block, 3, stride=blocks), :] = taps_near[
                i, :, block * LANES : (block + 1) * LANES
            ]
    zero = jnp.zeros((blocks, LANES), jnp.float32)
    key_taps = [tile(taps_ref, 3 + j, blocks) for j in range(3)]
    value_taps = [tile(taps_ref, 6 + j, blocks) for j in range(3)]
    decay = [tile(decay_ref, m, blocks) for m in range(modes)]

    def step(row, held):
        state, (k2, k1, v2, v1) = list(held[:modes]), held[modes:]
        for half, (k_wide, v_wide) in enumerate(wides):
            spread(k_near, k_wide, row + half * STEP, 0)
            spread(v_near, v_wide, row + half * STEP, 0)
        for half, (k_wide, v_wide) in enumerate(wides):
            for index in range(STEP):
                k0 = k_wide[place_of(index, blocks), :]
                v0 = v_wide[place_of(index, blocks), :]
                key = key_taps[0] * k0 + key_taps[1] * k1 + key_taps[2] * k2
                value = value_taps[0] * v0 + value_taps[1] * v1 + value_taps[2] * v2
                signal = key * value
                signal_ref[moving_tile(row + half * STEP + index, blocks), :] = signal
                state = [decay[m] * state[m] + signal for m in range(modes)]
                k2, k1, v2, v1 = k1, k0, v1, v0
        return tuple(state) + (k2, k1, v2, v1)

    held = (zero,) * (modes + 4)
    for i in range(pieces):
        for copy in part(i):
            copy.wait()
        if i == 0:
            spread(k_near, wides[0][0], 0, 0)
            spread(v_near, wides[0][1], 0, 0)
            for wide, taps, place in ((wides[0][0], key_taps, 0), (wides[0][1], value_taps, 2)):
                x0, x1 = wide[place_of(0, blocks), :], wide[place_of(1, blocks), :]
                edge_ref[place * blocks : (place + 1) * blocks, :] = taps[0] * x0
                edge_ref[(place + 1) * blocks : (place + 2) * blocks, :] = taps[0] * x1 + taps[1] * x0
        held = lax.fori_loop(
            0,
            height // (2 * STEP),
            lambda j, held, i=i: step(pl.multiple_of(i * height + j * 2 * STEP, 2 * STEP), held),
            held,
        )
    for m in range(modes + 4):
        carry_ref[m * blocks : (m + 1) * blocks, :] = held[m]
    for copy in late:
        copy.wait()
    k_wide = wides[0][0]
    spread(q_near, k_wide, rows - STEP, 0)
    for i in range(2):
        start = (modes + 4 + i) * blocks
        carry_ref[start : start + blocks, :] = k_wide[place_of(STEP - 2 + i, blocks), :]


def far(x):
    return pltpu.with_memory_space_constraint(x, pltpu.HBM)


def run_front(q, k, v, short_taps, rate, residue):
    rows, width = k.shape
    modes = rate.shape[0]
    blocks = width // LANES
    pieces = 4

    def wide(n):
        return jax.ShapeDtypeStruct((n * blocks, LANES), jnp.float32)

    def like(x):
        return jax.ShapeDtypeStruct(x.shape, x.dtype)

    out_shape = [wide(modes + 6), wide(rows), wide(modes), wide(9), wide(4), like(rate), like(residue), like(q)]
    return pl.pallas_call(
        front_kernel,
        out_shape=out_shape,
        in_specs=[AWAY] * 6,
        out_specs=[WHOLE] * len(out_shape),
        scratch_shapes=[
            pltpu.VMEM((rows, width), jnp.bfloat16),
            pltpu.VMEM((rows, width), jnp.bfloat16),
            pltpu.VMEM(short_taps.shape, jnp.float32),
            *[pltpu.VMEM((STEP * blocks, LANES), jnp.float32)] * 4,
            pltpu.SemaphoreType.DMA((2 * pieces + 2,)),
            pltpu.SemaphoreType.DMA((2,)),
        ],
        compiler_params=params(),
        cost_estimate=cost(10**8),
        name="front",
    )(*[far(x) for x in (k, v, q, short_taps, rate, residue)])


def local_kernel(q_near, signal_ref, decay_ref, taps_ref, gain_near, *refs):
    copies = []
    if len(refs) > 5:
        weight_hbm, direction_hbm, weight_ref, direction_ref, sems = refs[:2] + refs[5:7] + refs[-1:]
        refs = refs[2:5] + refs[7:-1]
        count = sems.shape[0] - 1
        copies.append(pltpu.make_async_copy(direction_hbm, direction_ref, sems.at[count]))
        copies[-1].start()
        depth = weight_ref.shape[0] // count
        for i in range(count):
            here = pl.ds(i * depth, depth)
            copies.append(pltpu.make_async_copy(weight_hbm.at[here], weight_ref.at[here], sems.at[i]))
            copies[-1].start()
    out_ref, query_ref, gain_ref, *wides = refs
    rows, width = q_near.shape
    blocks = width // LANES
    modes = gain_near.shape[0]
    spread_rows(gain_near[...], gain_ref)
    zero = jnp.zeros((blocks, LANES), jnp.float32)
    taps = [tile(taps_ref, j, blocks) for j in range(3)]
    decay = [tile(decay_ref, m, blocks) for m in range(modes)]
    gain = [tile(gain_ref, m, blocks) for m in range(modes)]

    def step(j, held):
        row = pl.multiple_of(j * 2 * STEP, 2 * STEP)
        state, (q2, q1) = list(held[:modes]), held[modes:]
        for half, q_wide in enumerate(wides):
            spread(q_near, q_wide, row + half * STEP, 0)
        for half, q_wide in enumerate(wides):
            for index in range(STEP):
                q0 = q_wide[place_of(index, blocks), :]
                here = moving_tile(row + half * STEP + index, blocks)
                signal = signal_ref[here, :]
                query_ref[here, :] = taps[0] * q0 + taps[1] * q1 + taps[2] * q2
                state = [decay[m] * state[m] + signal for m in range(modes)]
                sums = [gain[m] * state[m] for m in range(modes)]
                while len(sums) > 1:
                    sums = [sums[i] + sums[i + 1] for i in range(0, len(sums), 2)]
                out_ref[here, :] = sums[0]
                q2, q1 = q1, q0
        return tuple(state) + (q2, q1)

    lax.fori_loop(0, rows // (2 * STEP), step, (zero,) * (modes + 2))
    for copy in copies:
        copy.wait()


def run_local(q, signal, decay, taps, gain, *weight):
    rows, width = q.shape
    blocks = width // LANES
    wide = jax.ShapeDtypeStruct((rows * blocks, LANES), jnp.float32)
    out_shape = [wide, wide, jax.ShapeDtypeStruct(decay.shape, jnp.float32)]
    scratch_shapes = [pltpu.VMEM((STEP * blocks, LANES), jnp.float32)] * 2
    if weight:
        out_shape += [jax.ShapeDtypeStruct(x.shape, x.dtype) for x in weight]
        scratch_shapes.append(pltpu.SemaphoreType.DMA((5,)))
        weight = tuple(far(x) for x in weight)
    return pl.pallas_call(
        local_kernel,
        out_shape=out_shape,
        in_specs=[WHOLE] * 5 + [AWAY] * len(weight),
        out_specs=[WHOLE] * len(out_shape),
        scratch_shapes=scratch_shapes,
        compiler_params=params(),
        cost_estimate=cost(10**6),
        name="local_filter",
    )(q, signal, decay, taps, gain, *weight)


def correct_kernel(blocks, carry_ref, decay_ref, gain_ref, taps_ref, edge_ref, local_ref, query_ref, *refs):
    wide, outs = refs[-1], refs[:-1]
    rows = local_ref.shape[0] // blocks
    modes = decay_ref.shape[0] // blocks
    carried = jnp.where(lax.axis_index("ctx") > 0, 1.0, 0.0)
    k2, k1, v2, v1, q2, q1 = [carried * tile(carry_ref, modes + i, blocks) for i in range(6)]
    tap = [tile(taps_ref, i, blocks) for i in range(9)]
    key0, key1, value0, value1 = [tile(edge_ref, i, blocks) for i in range(4)]
    extra = [
        (key0 + tap[4] * k1 + tap[5] * k2) * (value0 + tap[7] * v1 + tap[8] * v2) - key0 * value0,
        (key1 + tap[5] * k1) * (value1 + tap[8] * v1) - key1 * value1,
    ]
    query_extra = [tap[1] * q1 + tap[2] * q2, tap[2] * q1]
    state = [tile(gain_ref, m, blocks) * (carried * tile(carry_ref, m, blocks)) for m in range(modes)]
    decay = [tile(decay_ref, m, blocks) for m in range(modes)]

    def step(row, state, first, piece_ref, start):
        state = list(state)
        for index in range(STEP):
            here = moving_tile(row + index, blocks)
            state = [decay[m] * state[m] for m in range(modes)]
            query = query_ref[here, :]
            if first and index < 2:
                state = [state[m] + tile(gain_ref, m, blocks) * extra[index] for m in range(modes)]
                query = query + query_extra[index]
            sums = state
            while len(sums) > 1:
                sums = [sums[i] + sums[i + 1] for i in range(0, len(sums), 2)]
            wide[place_of(index, blocks), :] = query * (local_ref[here, :] + sums[0])
        for block in range(blocks):
            halves = [
                wide[(half * blocks + block) * GROUP : (half * blocks + block + 1) * GROUP, :]
                for half in range(STEP // GROUP)
            ]
            rounded = jnp.concatenate(halves, axis=0).astype(jnp.bfloat16)
            columns = slice(block * LANES, (block + 1) * LANES)
            outs[-1][pl.ds(row, STEP), columns] = rounded
            if piece_ref is not None:
                piece_ref[pl.ds(pl.multiple_of(row - start, STEP), STEP), columns] = rounded
        return tuple(state)

    state = tuple(state)
    start = 0
    for piece_ref in outs[:-1] or [None]:
        end = start + (rows if piece_ref is None else piece_ref.shape[0])
        begin = start // STEP
        if start == 0:
            state = step(0, state, True, piece_ref, 0)
            begin = 1
        state = lax.fori_loop(
            begin,
            end // STEP,
            lambda j, state, start=start, piece_ref=piece_ref: step(
                pl.multiple_of(j * STEP, STEP), state, False, piece_ref, start
            ),
            state,
        )
        start = end


def run_correct(carry, decay, gain, taps, edge, local, query, blocks, *heights):
    rows = local.shape[0] // blocks
    width = blocks * LANES
    heights += (rows,)
    return pl.pallas_call(
        functools.partial(correct_kernel, blocks),
        out_shape=[jax.ShapeDtypeStruct((height, width), jnp.bfloat16) for height in heights],
        in_specs=[WHOLE] * 7,
        out_specs=[WHOLE] * len(heights),
        scratch_shapes=[pltpu.VMEM((STEP * blocks, LANES), jnp.float32)],
        compiler_params=params(),
        cost_estimate=cost(10**8),
        name="carried_filter",
    )(carry, decay, gain, taps, edge, local, query)


def gains_of(rate, residue):
    return residue * jnp.sqrt(-jnp.expm1(-2.0 * rate)) * rate.shape[0] ** (-0.5)


def split_three(x):
    high = x.astype(jnp.bfloat16)
    rest = x - high.astype(jnp.float32)
    middle = rest.astype(jnp.bfloat16)
    low = (rest - middle.astype(jnp.float32)).astype(jnp.bfloat16)
    return high, middle, low


def in_parts(row):
    return jnp.concatenate(list(split_three(row)) + [jnp.zeros((13, row.shape[1]), jnp.bfloat16)], axis=0)


def dot_parts(parts, matrix):
    out = lax.dot_general(parts, matrix, (((1,), (1,)), ((), ())), preferred_element_type=jnp.float32)
    return out[0:1] + out[1:2] + out[2:3]


def idle_kernel(*refs):
    pass


def after(array, *others):
    return pl.pallas_call(
        idle_kernel,
        out_shape=jax.ShapeDtypeStruct(array.shape, array.dtype),
        in_specs=[pl.BlockSpec(memory_space=pl.ANY)] * (1 + len(others)),
        out_specs=pl.BlockSpec(memory_space=pl.ANY),
        input_output_aliases={0: 0},
        compiler_params=params(),
        cost_estimate=cost(1),
        name="after",
    )(array, *others)


def rows_of(count, like, dtype=jnp.bfloat16):
    return jax.ShapeDtypeStruct((count, like.shape[1]), dtype)


def call(kernel, name, out_shape, *operands, tokens=()):
    def with_tokens(*refs):
        kernel(*refs[: len(operands)], *refs[len(operands) + len(tokens) :])

    return pl.pallas_call(
        with_tokens,
        out_shape=out_shape,
        in_specs=[WHOLE] * len(operands) + [pl.BlockSpec(memory_space=pl.ANY)] * len(tokens),
        out_specs=[WHOLE] * len(out_shape),
        compiler_params=params(),
        cost_estimate=cost(10**6),
        name=name,
    )(*operands, *tokens)


def inner_kernel(direction_ref, weight_ref, parts_ref, norm_ref, here_ref):
    everything = direction_ref[...]
    norm_ref[...] = jnp.broadcast_to(
        jnp.sum(everything * everything, axis=1, keepdims=True) + EPSILON, norm_ref.shape
    )
    size, width = weight_ref.shape[1], here_ref.shape[1]
    here_ref[...] = direction_ref[:, pl.ds(pl.multiple_of(lax.axis_index("tp") * width, LANES), width)]
    here = direction_ref[:, pl.ds(pl.multiple_of(lax.axis_index("ctx") * size, LANES), size)]
    parts_ref[...] = in_parts(dot_parts(in_parts(here), weight_ref[...]))


def run_inner(direction, weight):
    out_shape = [
        jax.ShapeDtypeStruct((STEP, weight.shape[0]), jnp.bfloat16),
        jax.ShapeDtypeStruct((1, LANES), jnp.float32),
        jax.ShapeDtypeStruct((1, weight.shape[1] // 2), jnp.float32),
    ]
    return call(inner_kernel, "inner", out_shape, direction, weight)


def project_kernel(begin, rows, away, weight_ref, piece_ref, *outs):
    cut = outs[0].shape[1]
    width = cut * len(outs)
    side = lax.axis_index("tp") % 2
    which = 1 - side if away else side
    for start in range(0, width, 256):
        columns = pl.ds(pl.multiple_of(which * width + start, 256), 256)
        out = jnp.dot(piece_ref[begin : begin + rows, :], weight_ref[:, columns], preferred_element_type=jnp.float32)
        ref, to = outs[start // cut], start % cut
        ref[:, to : to + 256] = out.astype(ref.dtype)


def run_project(weight, piece, begin, rows, count, *tokens):
    width = weight.shape[1] // 2
    sends = [jax.ShapeDtypeStruct((rows, width // count), jnp.bfloat16)] * count
    keep = [jax.ShapeDtypeStruct((rows, width), jnp.float32)]
    away, here = [functools.partial(project_kernel, begin, rows, x) for x in (True, False)]
    sends = call(away, "project", sends, weight, piece, tokens=tokens)
    return sends, call(here, "project", keep, weight, piece, tokens=tokens)[0]


def put_behind(ref, rows, row):
    here = slice(rows, rows + STEP)
    ref[here, :] = jnp.zeros((STEP, ref.shape[1]), jnp.bfloat16)
    ref[here, : row.shape[1]] = in_parts(row)


def take_behind(ref, rows, width):
    return jnp.sum(ref[rows : rows + STEP, :width].astype(jnp.float32), axis=0, keepdims=True)


def level_kernel(parts_ref, far_ref, whole_ref, out_ref):
    far_parts = far_ref[far_ref.shape[0] - STEP :, :]
    out_ref[...] = dot_parts(parts_ref[...], whole_ref[...]) + dot_parts(far_parts, whole_ref[...])


def add_shares(lefts, rights, outs):
    width = sum(ref.shape[1] for ref in lefts)
    rows = lefts[0].shape[0]
    step = min(ref.shape[1] for ref in (*lefts, *rights, *outs))

    def at(pieces, row, column):
        size = pieces[0].shape[1]
        return pieces[column // size].at[row : row + STEP, column % size : column % size + step]

    for row in range(0, rows, STEP):
        for column in range(0, width, step):
            left = at(lefts, row, column)[...].astype(jnp.float32)
            right = at(rights, row, column)[...].astype(jnp.float32)
            at(outs, row, column)[...] = (left + right).astype(jnp.bfloat16)


def merge_kernel(left, right, *refs):
    add_shares(refs[:left], refs[left : left + right], refs[left + right :])


def run_merge(lefts, rights, count):
    rows, width = lefts[0].shape[0], sum(x.shape[1] for x in lefts)
    kernel = functools.partial(merge_kernel, len(lefts), len(rights))
    out_shape = [jax.ShapeDtypeStruct((rows, width // count), jnp.bfloat16)] * count
    return call(kernel, "merge", out_shape, *lefts, *rights)


def merge_parts_kernel(keep_ref, parts_ref, *refs):
    add_shares((keep_ref,), refs[:-1], refs[-1:])
    refs[-1][keep_ref.shape[0] :, :] = parts_ref[...]


def is_keeper():
    return lax.axis_index("tp") // 2 == lax.axis_index("ctx")


def choose_kernel(straight_ref, own_ref, level_ref, other_ref, out_ref, total_ref):
    keeper = is_keeper()

    @pl.when(keeper)
    def _():
        rows = straight_ref.shape[0] - STEP
        out_ref[:rows, :] = straight_ref[:rows, :]

    @pl.when(jnp.logical_not(keeper))
    def _():
        out_ref[: own_ref.shape[0], :] = own_ref[...]

    total = level_ref[...] + other_ref[...]
    total_ref[...] = total
    put_behind(out_ref, out_ref.shape[0] - STEP, total)


def finish_kernel(*refs):
    level_ref, norm_ref, direction_ref = refs[:3]
    own0, own1, (straight_ref, merged_ref) = refs[3:6], refs[6:9], refs[9:11]
    out_hbm, level_hbm, out_near, level_near, sems = refs[11:]
    turned_ref = own1[-1]
    rows, width = out_near.shape
    half = straight_ref.shape[0] - STEP
    keeper = is_keeper()
    level = (level_ref[...] + take_behind(turned_ref, turned_ref.shape[0] - STEP, rows)) / norm_ref[0:1, 0:1]
    level_near[...] = level
    copies = [pltpu.make_async_copy(level_near, level_hbm, sems.at[sems.shape[0] - 1])]
    copies[0].start()
    direction = direction_ref[...]
    column = jnp.transpose(jnp.broadcast_to(level, (LANES, rows)))

    def put(row, cut, before, behind):
        pieces, start = (before, row) if row < cut else (behind, row - cut)
        total = pieces[0][start : start + STEP, :].astype(jnp.float32)
        for piece in pieces[1:]:
            total = total + piece[start : start + STEP, :].astype(jnp.float32)
        total = total - column[row : row + STEP, 0:1] * direction
        out_near[row : row + STEP, :] = total.astype(jnp.bfloat16)

    count = sems.shape[0] - 1
    for i in range(count):
        begin, end = i * rows // count, (i + 1) * rows // count

        @pl.when(keeper)
        def _():
            for row in range(begin, end, STEP):
                put(row, own0[0].shape[0], own0, own1)

        @pl.when(jnp.logical_not(keeper))
        def _():
            for row in range(begin, end, STEP):
                put(row, half, (straight_ref, turned_ref), (merged_ref,))

        here = pl.ds(begin, end - begin)
        copies.append(pltpu.make_async_copy(out_near.at[here], out_hbm.at[here], sems.at[i]))
        copies[-1].start()
    for copy in copies:
        copy.wait()


def run_finish(*operands):
    rows, width = operands[0].shape[1], operands[2].shape[1]
    return pl.pallas_call(
        finish_kernel,
        out_shape=[pltpu.HBM((rows, width), jnp.bfloat16), pltpu.HBM((1, rows), jnp.float32)],
        in_specs=[WHOLE] * len(operands),
        out_specs=[AWAY] * 2,
        scratch_shapes=[
            pltpu.VMEM((rows, width), jnp.bfloat16),
            pltpu.VMEM((1, rows), jnp.float32),
            pltpu.SemaphoreType.DMA((5,)),
        ],
        compiler_params=params(),
        cost_estimate=cost(10**6),
        name="finish",
    )(*operands)


def plane_plan(q, k, v, short_taps, decay_rate, residue, out_weight, direction):
    rows, width = q.shape
    cut, early = rows * 8 // 16, rows * 8 // 16
    blocks = width // LANES
    axes = ("ctx", "tp")
    across = [(4 * c + p, 4 * (1 - c) + p) for c in range(2) for p in range(4)]
    sibling = [(4 * c + p, 4 * c + (p ^ 1)) for c in range(2) for p in range(4)]
    pair = [(4 * c + p, 4 * c + (p ^ 2)) for c in range(2) for p in range(4)]

    ended, signal, decay, taps, edge, rate, residue, q = run_front(q, k, v, short_taps, decay_rate.T, residue.T)
    carry = lax.ppermute(ended, axes, across)
    local, query, gain, weight, direction = run_local(
        q, signal, decay, taps, gains_of(rate, residue), out_weight, direction.reshape(1, -1)
    )
    first, second, whole = run_correct(carry, decay, gain, taps, edge, local, query, blocks, cut, rows - cut)
    far_first = lax.ppermute(first, axes, across)
    far_second = lax.ppermute(second, axes, across)

    def exchange(arrays, pairs):
        return [lax.ppermute(array, axes, pairs) for array in arrays]

    weight = after(weight, whole)
    parts, norm, direction = run_inner(direction, weight)
    sends0, keep0 = run_project(weight, whole, 0, early, 1)
    sends1, keep1 = run_project(weight, whole, early, rows - early, 1)
    (core0,) = exchange(sends0, sibling)
    (hop0,) = exchange(run_merge((keep0,), (core0,), 1), pair)

    sends, far_keep = run_project(weight, far_first, 0, cut, 2, parts, *sends0, *sends1)
    (sums0,) = call(
        merge_parts_kernel, "merge", [rows_of(cut + STEP, far_keep)], far_keep, parts, *exchange(sends, sibling)
    )
    (straight,) = exchange([sums0], across)

    sends, far_keep = run_project(weight, after(far_second, sums0, hop0), 0, rows - cut, 2)
    sums1 = run_merge((far_keep,), exchange(sends, sibling), 2)
    moved = exchange(sums1, pair)
    (core1,) = exchange(sends1, sibling)
    (own1,) = run_merge((keep1,), (core1,), 1)

    one_row = jax.ShapeDtypeStruct((1, rows), jnp.float32)
    (level,) = call(level_kernel, "level", [one_row], parts, straight, whole)
    payload = rows_of(max(cut, rows - early) + STEP, far_keep)
    turned, level = call(
        choose_kernel,
        "choose",
        [payload, one_row],
        straight,
        own1,
        level,
        *exchange([level], sibling),
    )
    (turned,) = exchange([turned], pair)
    (merged,) = exchange(run_merge(sums1, moved, 1), across)
    ablated, level = run_finish(
        level, norm, direction, keep0, core0, hop0, keep1, core1, turned, straight, merged
    )
    return ablated, level.reshape(rows)


def gather_plan(q, k, v, short_taps, decay_rate, residue, out_weight, direction):
    rows, width = q.shape
    blocks = width // LANES
    modes = decay_rate.shape[1]
    tp = lax.axis_index("tp")
    ctx_size = lax.axis_size("ctx")
    next_one = [(i, i + 1) for i in range(ctx_size - 1)]
    ended, signal, decay, taps, edge, rate, residue, q = run_front(q, k, v, short_taps, decay_rate.T, residue.T)
    halo = lax.ppermute(ended[modes * blocks :], "ctx", next_one)
    local, query, gain = run_local(q, signal, decay, taps, gains_of(rate, residue))
    k2, k1, v2, v1 = [halo[i * blocks : (i + 1) * blocks] for i in range(4)]
    tap = taps.reshape(9, blocks, LANES)
    key0, key1, value0, value1 = edge.reshape(4, blocks, LANES)
    extra0 = (key0 + tap[4] * k1 + tap[5] * k2) * (value0 + tap[7] * v1 + tap[8] * v2) - key0 * value0
    extra1 = (key1 + tap[5] * k1) * (value1 + tap[8] * v1) - key1 * value1
    wide_rate = decay_rate.T.reshape(modes, blocks, LANES)
    state = (
        ended[: modes * blocks].reshape(modes, blocks, LANES)
        + jnp.exp(-wide_rate * (rows - 1)) * extra0
        + jnp.exp(-wide_rate * (rows - 2)) * extra1
    )
    reach = 1
    while reach < ctx_size:
        earlier = lax.ppermute(state, "ctx", [(i, i + reach) for i in range(ctx_size - reach)])
        state = state + jnp.exp(-wide_rate * (rows * reach)) * earlier
        reach *= 2
    start = lax.ppermute(state, "ctx", next_one).reshape(modes * blocks, LANES)
    carry = jnp.concatenate([start, halo], axis=0)
    (gated,) = run_correct(carry, decay, gain, taps, edge, local, query, blocks)
    partial_terms = lax.dot_general(
        gated,
        lax.all_gather(out_weight, "ctx", axis=1, tiled=True),
        (((1,), (0,)), ((), ())),
        preferred_element_type=jnp.float32,
    )
    summed = lax.psum_scatter(
        partial_terms.astype(jnp.bfloat16), "tp", scatter_dimension=1, tiled=True
    ).astype(jnp.float32)
    width_here = summed.shape[1]
    direction_here = lax.dynamic_slice_in_dim(direction, tp * width_here, width_here, 0)
    norm_total = jnp.sum(direction * direction) + EPSILON
    local_inner = jnp.dot(summed, direction_here, precision=HIGHEST)
    feature_level = lax.psum(local_inner, "tp") / norm_total
    ablated = (summed - feature_level[:, None] * direction_here[None, :]).astype(jnp.bfloat16)
    return ablated, feature_level


def solution(mesh):
    placed = (
        P(("dp", "ctx"), "tp"),
        P(("dp", "ctx"), "tp"),
        P(("dp", "ctx"), "tp"),
        P(None, None, "tp"),
        P("tp", None),
        P("tp", None),
        P("tp", "ctx"),
        P(),
    )
    plane = mesh.shape["ctx"] == 2 and mesh.shape["tp"] == 4
    return jax.shard_map(
        plane_plan if plane else gather_plan,
        mesh=mesh,
        in_specs=placed,
        out_specs=(P(("dp", "ctx"), "tp"), P(("dp", "ctx"))),
        check_vma=False,
    )
```

```python
import functools

import jax
import jax.numpy as jnp
from jax import lax
from jax.experimental import pallas as pl
from jax.experimental.pallas import tpu as pltpu
from jax.sharding import PartitionSpec as P

EPSILON = 1e-06
HIGHEST = lax.Precision.HIGHEST
LANES = 128
GROUP = 8
STEP = 16
WHOLE = pl.BlockSpec(memory_space=pltpu.VMEM)
AWAY = pl.BlockSpec(memory_space=pltpu.HBM)


def params(mebibytes=20):
    return pltpu.CompilerParams(vmem_limit_bytes=mebibytes * 1024 * 1024)


def cost(flops):
    return pl.CostEstimate(flops=flops, bytes_accessed=1024, transcendentals=0)


def spread(source, scratch, row, to):
    blocks = source.shape[1] // LANES
    for block in range(blocks):
        piece = source[pl.ds(row, STEP), block * LANES : (block + 1) * LANES].astype(jnp.float32)
        for half in range(STEP // GROUP):
            start = (half * blocks + block) * GROUP
            scratch[pl.ds(to + start, GROUP), :] = piece[half * GROUP : (half + 1) * GROUP]


def spread_rows(source, target):
    count, width = source.shape
    blocks = width // LANES
    for block in range(blocks):
        target[pl.ds(block, count, stride=blocks), :] = source[:, block * LANES : (block + 1) * LANES]


def place_of(index, blocks):
    return pl.ds((index // GROUP) * (blocks * GROUP) + index % GROUP, blocks, stride=GROUP)


def tile(ref, index, blocks):
    return ref[index * blocks : (index + 1) * blocks, :]


def moving_tile(index, blocks):
    return pl.ds(pl.multiple_of(index * blocks, blocks), blocks)


def front_kernel(*refs):
    k_hbm, v_hbm, q_hbm, taps_hbm, rate_hbm, residue_hbm = refs[:6]
    carry_ref, signal_ref, decay_ref, taps_ref, edge_ref, rate_ref, residue_ref, q_near = refs[6:14]
    k_near, v_near, taps_near, *wides, sems, late_sems = refs[-9:]
    wides = (wides[:2], wides[2:])
    rows, width = k_near.shape
    blocks = width // LANES
    modes = rate_ref.shape[0]
    pieces = sems.shape[0] // 2 - 1
    height = rows // pieces

    def part(i):
        here = pl.ds(i * height, height)
        return (
            pltpu.make_async_copy(k_hbm.at[here], k_near.at[here], sems.at[2 * i]),
            pltpu.make_async_copy(v_hbm.at[here], v_near.at[here], sems.at[2 * i + 1]),
        )

    rate_copy = pltpu.make_async_copy(rate_hbm, rate_ref, sems.at[2 * pieces])
    taps_copy = pltpu.make_async_copy(taps_hbm, taps_near, sems.at[2 * pieces + 1])
    late = [(residue_hbm, residue_ref), (q_hbm, q_near)]
    late = [pltpu.make_async_copy(source, target, late_sems.at[i]) for i, (source, target) in enumerate(late)]
    rate_copy.start()
    taps_copy.start()
    for i in range(pieces):
        for copy in part(i):
            copy.start()
    for copy in late:
        copy.start()
    rate_copy.wait()
    taps_copy.wait()
    spread_rows(jnp.exp(-rate_ref[...]), decay_ref)
    for i in range(3):
        for block in range(blocks):
            taps_ref[pl.ds(3 * i * blocks + block, 3, stride=blocks), :] = taps_near[
                i, :, block * LANES : (block + 1) * LANES
            ]
    zero = jnp.zeros((blocks, LANES), jnp.float32)
    key_taps = [tile(taps_ref, 3 + j, blocks) for j in range(3)]
    value_taps = [tile(taps_ref, 6 + j, blocks) for j in range(3)]
    decay = [tile(decay_ref, m, blocks) for m in range(modes)]

    def step(row, held):
        state, (k2, k1, v2, v1) = list(held[:modes]), held[modes:]
        for half, (k_wide, v_wide) in enumerate(wides):
            spread(k_near, k_wide, row + half * STEP, 0)
            spread(v_near, v_wide, row + half * STEP, 0)
        for half, (k_wide, v_wide) in enumerate(wides):
            for index in range(STEP):
                k0 = k_wide[place_of(index, blocks), :]
                v0 = v_wide[place_of(index, blocks), :]
                key = key_taps[0] * k0 + key_taps[1] * k1 + key_taps[2] * k2
                value = value_taps[0] * v0 + value_taps[1] * v1 + value_taps[2] * v2
                signal = key * value
                signal_ref[moving_tile(row + half * STEP + index, blocks), :] = signal
                state = [decay[m] * state[m] + signal for m in range(modes)]
                k2, k1, v2, v1 = k1, k0, v1, v0
        return tuple(state) + (k2, k1, v2, v1)

    held = (zero,) * (modes + 4)
    for i in range(pieces):
        for copy in part(i):
            copy.wait()
        if i == 0:
            spread(k_near, wides[0][0], 0, 0)
            spread(v_near, wides[0][1], 0, 0)
            for wide, taps, place in ((wides[0][0], key_taps, 0), (wides[0][1], value_taps, 2)):
                x0, x1 = wide[place_of(0, blocks), :], wide[place_of(1, blocks), :]
                edge_ref[place * blocks : (place + 1) * blocks, :] = taps[0] * x0
                edge_ref[(place + 1) * blocks : (place + 2) * blocks, :] = taps[0] * x1 + taps[1] * x0
        held = lax.fori_loop(
            0,
            height // (2 * STEP),
            lambda j, held, i=i: step(pl.multiple_of(i * height + j * 2 * STEP, 2 * STEP), held),
            held,
        )
    for m in range(modes + 4):
        carry_ref[m * blocks : (m + 1) * blocks, :] = held[m]
    for copy in late:
        copy.wait()
    k_wide = wides[0][0]
    spread(q_near, k_wide, rows - STEP, 0)
    for i in range(2):
        start = (modes + 4 + i) * blocks
        carry_ref[start : start + blocks, :] = k_wide[place_of(STEP - 2 + i, blocks), :]


def far(x):
    return pltpu.with_memory_space_constraint(x, pltpu.HBM)


def run_front(q, k, v, short_taps, rate, residue):
    rows, width = k.shape
    modes = rate.shape[0]
    blocks = width // LANES
    pieces = 4

    def wide(n):
        return jax.ShapeDtypeStruct((n * blocks, LANES), jnp.float32)

    def like(x):
        return jax.ShapeDtypeStruct(x.shape, x.dtype)

    out_shape = [wide(modes + 6), wide(rows), wide(modes), wide(9), wide(4), like(rate), like(residue), like(q)]
    return pl.pallas_call(
        front_kernel,
        out_shape=out_shape,
        in_specs=[AWAY] * 6,
        out_specs=[WHOLE] * len(out_shape),
        scratch_shapes=[
            pltpu.VMEM((rows, width), jnp.bfloat16),
            pltpu.VMEM((rows, width), jnp.bfloat16),
            pltpu.VMEM(short_taps.shape, jnp.float32),
            *[pltpu.VMEM((STEP * blocks, LANES), jnp.float32)] * 4,
            pltpu.SemaphoreType.DMA((2 * pieces + 2,)),
            pltpu.SemaphoreType.DMA((2,)),
        ],
        compiler_params=params(),
        cost_estimate=cost(10**8),
        name="front",
    )(*[far(x) for x in (k, v, q, short_taps, rate, residue)])


def local_kernel(q_near, signal_ref, decay_ref, taps_ref, gain_near, *refs):
    copies = []
    if len(refs) > 5:
        weight_hbm, direction_hbm, weight_ref, direction_ref, sems = refs[:2] + refs[5:7] + refs[-1:]
        refs = refs[2:5] + refs[7:-1]
        count = sems.shape[0] - 1
        copies.append(pltpu.make_async_copy(direction_hbm, direction_ref, sems.at[count]))
        copies[-1].start()
        depth = weight_ref.shape[0] // count
        for i in range(count):
            here = pl.ds(i * depth, depth)
            copies.append(pltpu.make_async_copy(weight_hbm.at[here], weight_ref.at[here], sems.at[i]))
            copies[-1].start()
    out_ref, query_ref, gain_ref, *wides = refs
    rows, width = q_near.shape
    blocks = width // LANES
    modes = gain_near.shape[0]
    spread_rows(gain_near[...], gain_ref)
    zero = jnp.zeros((blocks, LANES), jnp.float32)
    taps = [tile(taps_ref, j, blocks) for j in range(3)]
    decay = [tile(decay_ref, m, blocks) for m in range(modes)]
    gain = [tile(gain_ref, m, blocks) for m in range(modes)]

    def step(j, held):
        row = pl.multiple_of(j * 2 * STEP, 2 * STEP)
        state, (q2, q1) = list(held[:modes]), held[modes:]
        for half, q_wide in enumerate(wides):
            spread(q_near, q_wide, row + half * STEP, 0)
        for half, q_wide in enumerate(wides):
            for index in range(STEP):
                q0 = q_wide[place_of(index, blocks), :]
                here = moving_tile(row + half * STEP + index, blocks)
                signal = signal_ref[here, :]
                query_ref[here, :] = taps[0] * q0 + taps[1] * q1 + taps[2] * q2
                state = [decay[m] * state[m] + signal for m in range(modes)]
                sums = [gain[m] * state[m] for m in range(modes)]
                while len(sums) > 1:
                    sums = [sums[i] + sums[i + 1] for i in range(0, len(sums), 2)]
                out_ref[here, :] = sums[0]
                q2, q1 = q1, q0
        return tuple(state) + (q2, q1)

    lax.fori_loop(0, rows // (2 * STEP), step, (zero,) * (modes + 2))
    for copy in copies:
        copy.wait()


def run_local(q, signal, decay, taps, gain, *weight):
    rows, width = q.shape
    blocks = width // LANES
    wide = jax.ShapeDtypeStruct((rows * blocks, LANES), jnp.float32)
    out_shape = [wide, wide, jax.ShapeDtypeStruct(decay.shape, jnp.float32)]
    scratch_shapes = [pltpu.VMEM((STEP * blocks, LANES), jnp.float32)] * 2
    if weight:
        out_shape += [jax.ShapeDtypeStruct(x.shape, x.dtype) for x in weight]
        scratch_shapes.append(pltpu.SemaphoreType.DMA((5,)))
        weight = tuple(far(x) for x in weight)
    return pl.pallas_call(
        local_kernel,
        out_shape=out_shape,
        in_specs=[WHOLE] * 5 + [AWAY] * len(weight),
        out_specs=[WHOLE] * len(out_shape),
        scratch_shapes=scratch_shapes,
        compiler_params=params(),
        cost_estimate=cost(10**6),
        name="local_filter",
    )(q, signal, decay, taps, gain, *weight)


def correct_kernel(blocks, start, decay_ref, gain_ref, local_ref, query_ref, *refs):
    out_ref, state_out_ref, wide = refs[-3:]
    rows = out_ref.shape[0]
    modes = decay_ref.shape[0] // blocks
    decay = [tile(decay_ref, m, blocks) for m in range(modes)]
    extra = query_extra = ()
    if start:
        state = tuple(tile(refs[0], m, blocks) for m in range(modes))
    else:
        carry_ref, taps_ref, edge_ref = refs[:3]
        carried = jnp.where(lax.axis_index("ctx") > 0, 1.0, 0.0)
        k2, k1, v2, v1, q2, q1 = [carried * tile(carry_ref, modes + i, blocks) for i in range(6)]
        tap = [tile(taps_ref, i, blocks) for i in range(9)]
        key0, key1, value0, value1 = [tile(edge_ref, i, blocks) for i in range(4)]
        extra = (
            (key0 + tap[4] * k1 + tap[5] * k2) * (value0 + tap[7] * v1 + tap[8] * v2) - key0 * value0,
            (key1 + tap[5] * k1) * (value1 + tap[8] * v1) - key1 * value1,
        )
        query_extra = (tap[1] * q1 + tap[2] * q2, tap[2] * q1)
        state = tuple(tile(gain_ref, m, blocks) * (carried * tile(carry_ref, m, blocks)) for m in range(modes))

    def step(row, state, first):
        state = list(state)
        for index in range(STEP):
            here = moving_tile(start + row + index, blocks)
            state = [decay[m] * state[m] for m in range(modes)]
            query = query_ref[here, :]
            if first and index < 2:
                state = [state[m] + tile(gain_ref, m, blocks) * extra[index] for m in range(modes)]
                query = query + query_extra[index]
            sums = state
            while len(sums) > 1:
                sums = [sums[i] + sums[i + 1] for i in range(0, len(sums), 2)]
            wide[place_of(index, blocks), :] = query * (local_ref[here, :] + sums[0])
        for block in range(blocks):
            halves = [
                wide[(half * blocks + block) * GROUP : (half * blocks + block + 1) * GROUP, :]
                for half in range(STEP // GROUP)
            ]
            out_ref[pl.ds(row, STEP), block * LANES : (block + 1) * LANES] = jnp.concatenate(
                halves, axis=0
            ).astype(jnp.bfloat16)
        return tuple(state)

    begin = 0
    if start == 0:
        state = step(0, state, True)
        begin = 1
    state = lax.fori_loop(
        begin, rows // STEP, lambda j, state: step(pl.multiple_of(j * STEP, STEP), state, False), state
    )
    for m in range(modes):
        state_out_ref[m * blocks : (m + 1) * blocks, :] = state[m]


def run_correct(start, rows, decay, gain, local, query, blocks, *before):
    return pl.pallas_call(
        functools.partial(correct_kernel, blocks, start),
        out_shape=[
            jax.ShapeDtypeStruct((rows, blocks * LANES), jnp.bfloat16),
            jax.ShapeDtypeStruct(decay.shape, jnp.float32),
        ],
        in_specs=[WHOLE] * (4 + len(before)),
        out_specs=[WHOLE] * 2,
        scratch_shapes=[pltpu.VMEM((STEP * blocks, LANES), jnp.float32)],
        compiler_params=params(),
        cost_estimate=cost(10**8),
        name="carried_filter",
    )(decay, gain, local, query, *before)


def gains_of(rate, residue):
    return residue * jnp.sqrt(-jnp.expm1(-2.0 * rate)) * rate.shape[0] ** (-0.5)


def split_three(x):
    high = x.astype(jnp.bfloat16)
    rest = x - high.astype(jnp.float32)
    middle = rest.astype(jnp.bfloat16)
    low = (rest - middle.astype(jnp.float32)).astype(jnp.bfloat16)
    return high, middle, low


def in_parts(row):
    return jnp.concatenate(list(split_three(row)) + [jnp.zeros((13, row.shape[1]), jnp.bfloat16)], axis=0)


def dot_parts(parts, matrix):
    out = lax.dot_general(parts, matrix, (((1,), (1,)), ((), ())), preferred_element_type=jnp.float32)
    return out[0:1] + out[1:2] + out[2:3]


def idle_kernel(*refs):
    pass


def after(array, *others):
    return pl.pallas_call(
        idle_kernel,
        out_shape=jax.ShapeDtypeStruct(array.shape, array.dtype),
        in_specs=[pl.BlockSpec(memory_space=pl.ANY)] * (1 + len(others)),
        out_specs=pl.BlockSpec(memory_space=pl.ANY),
        input_output_aliases={0: 0},
        compiler_params=params(),
        cost_estimate=cost(1),
        name="after",
    )(array, *others)


def rows_of(count, like, dtype=jnp.bfloat16):
    return jax.ShapeDtypeStruct((count, like.shape[1]), dtype)


def call(kernel, name, out_shape, *operands, tokens=()):
    def with_tokens(*refs):
        kernel(*refs[: len(operands)], *refs[len(operands) + len(tokens) :])

    return pl.pallas_call(
        with_tokens,
        out_shape=out_shape,
        in_specs=[WHOLE] * len(operands) + [pl.BlockSpec(memory_space=pl.ANY)] * len(tokens),
        out_specs=[WHOLE] * len(out_shape),
        compiler_params=params(),
        cost_estimate=cost(10**6),
        name=name,
    )(*operands, *tokens)


def inner_kernel(direction_ref, weight_ref, parts_ref, norm_ref, here_ref):
    everything = direction_ref[...]
    norm_ref[...] = jnp.broadcast_to(
        jnp.sum(everything * everything, axis=1, keepdims=True) + EPSILON, norm_ref.shape
    )
    size, width = weight_ref.shape[1], here_ref.shape[1]
    here_ref[...] = direction_ref[:, pl.ds(pl.multiple_of(lax.axis_index("tp") * width, LANES), width)]
    here = direction_ref[:, pl.ds(pl.multiple_of(lax.axis_index("ctx") * size, LANES), size)]
    parts_ref[...] = in_parts(dot_parts(in_parts(here), weight_ref[...]))


def run_inner(direction, weight):
    out_shape = [
        jax.ShapeDtypeStruct((STEP, weight.shape[0]), jnp.bfloat16),
        jax.ShapeDtypeStruct((1, LANES), jnp.float32),
        jax.ShapeDtypeStruct((1, weight.shape[1] // 2), jnp.float32),
    ]
    return call(inner_kernel, "inner", out_shape, direction, weight)


def project_kernel(begin, rows, away, weight_ref, piece_ref, *outs):
    cut = outs[0].shape[1]
    width = cut * len(outs)
    side = lax.axis_index("tp") % 2
    which = 1 - side if away else side
    for start in range(0, width, 256):
        columns = pl.ds(pl.multiple_of(which * width + start, 256), 256)
        out = jnp.dot(piece_ref[begin : begin + rows, :], weight_ref[:, columns], preferred_element_type=jnp.float32)
        ref, to = outs[start // cut], start % cut
        ref[:, to : to + 256] = out.astype(ref.dtype)


def run_project(weight, piece, begin, rows, count, *tokens):
    width = weight.shape[1] // 2
    sends = [jax.ShapeDtypeStruct((rows, width // count), jnp.bfloat16)] * count
    keep = [jax.ShapeDtypeStruct((rows, width), jnp.float32)]
    away, here = [functools.partial(project_kernel, begin, rows, x) for x in (True, False)]
    sends = call(away, "project", sends, weight, piece, tokens=tokens)
    return sends, call(here, "project", keep, weight, piece, tokens=tokens)[0]


def put_behind(ref, rows, row):
    here = slice(rows, rows + STEP)
    ref[here, :] = jnp.zeros((STEP, ref.shape[1]), jnp.bfloat16)
    ref[here, : row.shape[1]] = in_parts(row)


def take_behind(ref, rows, width):
    return jnp.sum(ref[rows : rows + STEP, :width].astype(jnp.float32), axis=0, keepdims=True)


def level_kernel(parts_ref, far_ref, *refs):
    *pieces, out_ref = refs
    far_parts = far_ref[far_ref.shape[0] - STEP :, :]
    start = 0
    for piece in pieces:
        end = start + piece.shape[0]
        out_ref[:, start:end] = dot_parts(parts_ref[...], piece[...]) + dot_parts(far_parts, piece[...])
        start = end


def add_shares(lefts, rights, outs):
    width = sum(ref.shape[1] for ref in lefts)
    rows = lefts[0].shape[0]
    step = min(ref.shape[1] for ref in (*lefts, *rights, *outs))

    def at(pieces, row, column):
        size = pieces[0].shape[1]
        return pieces[column // size].at[row : row + STEP, column % size : column % size + step]

    for row in range(0, rows, STEP):
        for column in range(0, width, step):
            left = at(lefts, row, column)[...].astype(jnp.float32)
            right = at(rights, row, column)[...].astype(jnp.float32)
            at(outs, row, column)[...] = (left + right).astype(jnp.bfloat16)


def merge_kernel(left, right, *refs):
    add_shares(refs[:left], refs[left : left + right], refs[left + right :])


def run_merge(lefts, rights, count):
    rows, width = lefts[0].shape[0], sum(x.shape[1] for x in lefts)
    kernel = functools.partial(merge_kernel, len(lefts), len(rights))
    out_shape = [jax.ShapeDtypeStruct((rows, width // count), jnp.bfloat16)] * count
    return call(kernel, "merge", out_shape, *lefts, *rights)


def merge_parts_kernel(keep_ref, parts_ref, *refs):
    add_shares((keep_ref,), refs[:-1], refs[-1:])
    refs[-1][keep_ref.shape[0] :, :] = parts_ref[...]


def is_keeper():
    return lax.axis_index("tp") // 2 == lax.axis_index("ctx")


def choose_kernel(straight_ref, own_ref, level_ref, other_ref, out_ref, total_ref):
    keeper = is_keeper()

    @pl.when(keeper)
    def _():
        rows = straight_ref.shape[0] - STEP
        out_ref[:rows, :] = straight_ref[:rows, :]

    @pl.when(jnp.logical_not(keeper))
    def _():
        out_ref[: own_ref.shape[0], :] = own_ref[...]

    total = level_ref[...] + other_ref[...]
    total_ref[...] = total
    put_behind(out_ref, out_ref.shape[0] - STEP, total)


def finish_kernel(*refs):
    level_ref, norm_ref, direction_ref = refs[:3]
    own0, own1, (straight_ref, merged_ref) = refs[3:6], refs[6:9], refs[9:11]
    out_hbm, level_hbm, out_near, level_near, sems = refs[11:]
    turned_ref = own1[-1]
    rows, width = out_near.shape
    half = straight_ref.shape[0] - STEP
    keeper = is_keeper()
    level = (level_ref[...] + take_behind(turned_ref, turned_ref.shape[0] - STEP, rows)) / norm_ref[0:1, 0:1]
    level_near[...] = level
    copies = [pltpu.make_async_copy(level_near, level_hbm, sems.at[sems.shape[0] - 1])]
    copies[0].start()
    direction = direction_ref[...]
    column = jnp.transpose(jnp.broadcast_to(level, (LANES, rows)))

    def put(row, cut, before, behind):
        pieces, start = (before, row) if row < cut else (behind, row - cut)
        total = pieces[0][start : start + STEP, :].astype(jnp.float32)
        for piece in pieces[1:]:
            total = total + piece[start : start + STEP, :].astype(jnp.float32)
        total = total - column[row : row + STEP, 0:1] * direction
        out_near[row : row + STEP, :] = total.astype(jnp.bfloat16)

    count = sems.shape[0] - 1
    for i in range(count):
        begin, end = i * rows // count, (i + 1) * rows // count

        @pl.when(keeper)
        def _():
            for row in range(begin, end, STEP):
                put(row, own0[0].shape[0], own0, own1)

        @pl.when(jnp.logical_not(keeper))
        def _():
            for row in range(begin, end, STEP):
                put(row, half, (straight_ref, turned_ref), (merged_ref,))

        here = pl.ds(begin, end - begin)
        copies.append(pltpu.make_async_copy(out_near.at[here], out_hbm.at[here], sems.at[i]))
        copies[-1].start()
    for copy in copies:
        copy.wait()


def run_finish(*operands):
    rows, width = operands[0].shape[1], operands[2].shape[1]
    return pl.pallas_call(
        finish_kernel,
        out_shape=[pltpu.HBM((rows, width), jnp.bfloat16), pltpu.HBM((1, rows), jnp.float32)],
        in_specs=[WHOLE] * len(operands),
        out_specs=[AWAY] * 2,
        scratch_shapes=[
            pltpu.VMEM((rows, width), jnp.bfloat16),
            pltpu.VMEM((1, rows), jnp.float32),
            pltpu.SemaphoreType.DMA((5,)),
        ],
        compiler_params=params(),
        cost_estimate=cost(10**6),
        name="finish",
    )(*operands)


def plane_plan(q, k, v, short_taps, decay_rate, residue, out_weight, direction):
    rows, width = q.shape
    cut = rows // 2
    blocks = width // LANES
    axes = ("ctx", "tp")
    across = [(4 * c + p, 4 * (1 - c) + p) for c in range(2) for p in range(4)]
    sibling = [(4 * c + p, 4 * c + (p ^ 1)) for c in range(2) for p in range(4)]
    pair = [(4 * c + p, 4 * c + (p ^ 2)) for c in range(2) for p in range(4)]

    ended, signal, decay, taps, edge, rate, residue, q = run_front(q, k, v, short_taps, decay_rate.T, residue.T)
    carry = lax.ppermute(ended, axes, across)
    local, query, gain, weight, direction = run_local(
        q, signal, decay, taps, gains_of(rate, residue), out_weight, direction.reshape(1, -1)
    )
    first, state = run_correct(0, cut, decay, gain, local, query, blocks, carry, taps, edge)
    second, _ = run_correct(cut, rows - cut, decay, gain, local, query, blocks, state)
    far_first = lax.ppermute(first, axes, across)
    far_second = lax.ppermute(second, axes, across)

    def exchange(arrays, pairs):
        return [lax.ppermute(array, axes, pairs) for array in arrays]

    weight = after(weight, first)
    parts, norm, direction = run_inner(direction, weight)
    sends0, keep0 = run_project(weight, first, 0, cut, 1)
    sends1, keep1 = run_project(weight, second, 0, rows - cut, 1)
    (core0,) = exchange(sends0, sibling)
    (hop0,) = exchange(run_merge((keep0,), (core0,), 1), pair)

    sends, far_keep = run_project(weight, far_first, 0, cut, 2, parts, *sends0, *sends1)
    (sums0,) = call(
        merge_parts_kernel, "merge", [rows_of(cut + STEP, far_keep)], far_keep, parts, *exchange(sends, sibling)
    )
    (straight,) = exchange([sums0], across)

    sends, far_keep = run_project(weight, after(far_second, sums0, hop0), 0, rows - cut, 2)
    sums1 = run_merge((far_keep,), exchange(sends, sibling), 2)
    moved = exchange(sums1, pair)
    (core1,) = exchange(sends1, sibling)
    (own1,) = run_merge((keep1,), (core1,), 1)

    one_row = jax.ShapeDtypeStruct((1, rows), jnp.float32)
    (level,) = call(level_kernel, "level", [one_row], parts, straight, first, second)
    payload = rows_of(max(cut, rows - cut) + STEP, far_keep)
    turned, level = call(
        choose_kernel,
        "choose",
        [payload, one_row],
        straight,
        own1,
        level,
        *exchange([level], sibling),
    )
    (turned,) = exchange([turned], pair)
    (merged,) = exchange(run_merge(sums1, moved, 1), across)
    ablated, level = run_finish(
        level, norm, direction, keep0, core0, hop0, keep1, core1, turned, straight, merged
    )
    return ablated, level.reshape(rows)


def gather_plan(q, k, v, short_taps, decay_rate, residue, out_weight, direction):
    rows, width = q.shape
    blocks = width // LANES
    modes = decay_rate.shape[1]
    tp = lax.axis_index("tp")
    ctx_size = lax.axis_size("ctx")
    next_one = [(i, i + 1) for i in range(ctx_size - 1)]
    ended, signal, decay, taps, edge, rate, residue, q = run_front(q, k, v, short_taps, decay_rate.T, residue.T)
    halo = lax.ppermute(ended[modes * blocks :], "ctx", next_one)
    local, query, gain = run_local(q, signal, decay, taps, gains_of(rate, residue))
    k2, k1, v2, v1 = [halo[i * blocks : (i + 1) * blocks] for i in range(4)]
    tap = taps.reshape(9, blocks, LANES)
    key0, key1, value0, value1 = edge.reshape(4, blocks, LANES)
    extra0 = (key0 + tap[4] * k1 + tap[5] * k2) * (value0 + tap[7] * v1 + tap[8] * v2) - key0 * value0
    extra1 = (key1 + tap[5] * k1) * (value1 + tap[8] * v1) - key1 * value1
    wide_rate = decay_rate.T.reshape(modes, blocks, LANES)
    state = (
        ended[: modes * blocks].reshape(modes, blocks, LANES)
        + jnp.exp(-wide_rate * (rows - 1)) * extra0
        + jnp.exp(-wide_rate * (rows - 2)) * extra1
    )
    reach = 1
    while reach < ctx_size:
        earlier = lax.ppermute(state, "ctx", [(i, i + reach) for i in range(ctx_size - reach)])
        state = state + jnp.exp(-wide_rate * (rows * reach)) * earlier
        reach *= 2
    start = lax.ppermute(state, "ctx", next_one).reshape(modes * blocks, LANES)
    carry = jnp.concatenate([start, halo], axis=0)
    gated, _ = run_correct(0, rows, decay, gain, local, query, blocks, carry, taps, edge)
    partial_terms = lax.dot_general(
        gated,
        lax.all_gather(out_weight, "ctx", axis=1, tiled=True),
        (((1,), (0,)), ((), ())),
        preferred_element_type=jnp.float32,
    )
    summed = lax.psum_scatter(
        partial_terms.astype(jnp.bfloat16), "tp", scatter_dimension=1, tiled=True
    ).astype(jnp.float32)
    width_here = summed.shape[1]
    direction_here = lax.dynamic_slice_in_dim(direction, tp * width_here, width_here, 0)
    norm_total = jnp.sum(direction * direction) + EPSILON
    local_inner = jnp.dot(summed, direction_here, precision=HIGHEST)
    feature_level = lax.psum(local_inner, "tp") / norm_total
    ablated = (summed - feature_level[:, None] * direction_here[None, :]).astype(jnp.bfloat16)
    return ablated, feature_level


def solution(mesh):
    placed = (
        P(("dp", "ctx"), "tp"),
        P(("dp", "ctx"), "tp"),
        P(("dp", "ctx"), "tp"),
        P(None, None, "tp"),
        P("tp", None),
        P("tp", None),
        P("tp", "ctx"),
        P(),
    )
    plane = mesh.shape["ctx"] == 2 and mesh.shape["tp"] == 4
    return jax.shard_map(
        plane_plan if plane else gather_plan,
        mesh=mesh,
        in_specs=placed,
        out_specs=(P(("dp", "ctx"), "tp"), P(("dp", "ctx"))),
        check_vma=False,
    )
```

```python
import functools

import jax
import jax.numpy as jnp
from jax import lax
from jax.experimental import pallas as pl
from jax.experimental.pallas import tpu as pltpu
from jax.sharding import PartitionSpec as P

EPSILON = 1e-06
HIGHEST = lax.Precision.HIGHEST
LANES = 128
GROUP = 8
STEP = 16
WHOLE = pl.BlockSpec(memory_space=pltpu.VMEM)
AWAY = pl.BlockSpec(memory_space=pltpu.HBM)


def params(mebibytes=20):
    return pltpu.CompilerParams(vmem_limit_bytes=mebibytes * 1024 * 1024)


def cost(flops):
    return pl.CostEstimate(flops=flops, bytes_accessed=1024, transcendentals=0)


def spread(source, scratch, row, to):
    blocks = source.shape[1] // LANES
    for block in range(blocks):
        piece = source[pl.ds(row, STEP), block * LANES : (block + 1) * LANES].astype(jnp.float32)
        for half in range(STEP // GROUP):
            start = (half * blocks + block) * GROUP
            scratch[pl.ds(to + start, GROUP), :] = piece[half * GROUP : (half + 1) * GROUP]


def spread_rows(source, target):
    count, width = source.shape
    blocks = width // LANES
    for block in range(blocks):
        target[pl.ds(block, count, stride=blocks), :] = source[:, block * LANES : (block + 1) * LANES]


def place_of(index, blocks):
    return pl.ds((index // GROUP) * (blocks * GROUP) + index % GROUP, blocks, stride=GROUP)


def tile(ref, index, blocks):
    return ref[index * blocks : (index + 1) * blocks, :]


def moving_tile(index, blocks):
    return pl.ds(pl.multiple_of(index * blocks, blocks), blocks)


def front_kernel(*refs):
    k_hbm, v_hbm, q_hbm, taps_hbm, rate_hbm, residue_hbm = refs[:6]
    carry_ref, signal_ref, decay_ref, taps_ref, edge_ref, rate_ref, residue_ref, q_near = refs[6:14]
    k_near, v_near, taps_near, *wides, sems, late_sems = refs[-9:]
    wides = (wides[:2], wides[2:])
    rows, width = k_near.shape
    blocks = width // LANES
    modes = rate_ref.shape[0]
    pieces = sems.shape[0] // 2 - 1
    height = rows // pieces

    def part(i):
        here = pl.ds(i * height, height)
        return (
            pltpu.make_async_copy(k_hbm.at[here], k_near.at[here], sems.at[2 * i]),
            pltpu.make_async_copy(v_hbm.at[here], v_near.at[here], sems.at[2 * i + 1]),
        )

    rate_copy = pltpu.make_async_copy(rate_hbm, rate_ref, sems.at[2 * pieces])
    taps_copy = pltpu.make_async_copy(taps_hbm, taps_near, sems.at[2 * pieces + 1])
    late = [(residue_hbm, residue_ref), (q_hbm, q_near)]
    late = [pltpu.make_async_copy(source, target, late_sems.at[i]) for i, (source, target) in enumerate(late)]
    rate_copy.start()
    taps_copy.start()
    for i in range(pieces):
        for copy in part(i):
            copy.start()
    for copy in late:
        copy.start()
    rate_copy.wait()
    taps_copy.wait()
    spread_rows(jnp.exp(-rate_ref[...]), decay_ref)
    for i in range(3):
        for block in range(blocks):
            taps_ref[pl.ds(3 * i * blocks + block, 3, stride=blocks), :] = taps_near[
                i, :, block * LANES : (block + 1) * LANES
            ]
    zero = jnp.zeros((blocks, LANES), jnp.float32)
    key_taps = [tile(taps_ref, 3 + j, blocks) for j in range(3)]
    value_taps = [tile(taps_ref, 6 + j, blocks) for j in range(3)]
    decay = [tile(decay_ref, m, blocks) for m in range(modes)]

    def step(row, held):
        state, (k2, k1, v2, v1) = list(held[:modes]), held[modes:]
        for half, (k_wide, v_wide) in enumerate(wides):
            spread(k_near, k_wide, row + half * STEP, 0)
            spread(v_near, v_wide, row + half * STEP, 0)
        for half, (k_wide, v_wide) in enumerate(wides):
            for index in range(STEP):
                k0 = k_wide[place_of(index, blocks), :]
                v0 = v_wide[place_of(index, blocks), :]
                key = key_taps[0] * k0 + key_taps[1] * k1 + key_taps[2] * k2
                value = value_taps[0] * v0 + value_taps[1] * v1 + value_taps[2] * v2
                signal = key * value
                signal_ref[moving_tile(row + half * STEP + index, blocks), :] = signal
                state = [decay[m] * state[m] + signal for m in range(modes)]
                k2, k1, v2, v1 = k1, k0, v1, v0
        return tuple(state) + (k2, k1, v2, v1)

    held = (zero,) * (modes + 4)
    for i in range(pieces):
        for copy in part(i):
            copy.wait()
        if i == 0:
            spread(k_near, wides[0][0], 0, 0)
            spread(v_near, wides[0][1], 0, 0)
            for wide, taps, place in ((wides[0][0], key_taps, 0), (wides[0][1], value_taps, 2)):
                x0, x1 = wide[place_of(0, blocks), :], wide[place_of(1, blocks), :]
                edge_ref[place * blocks : (place + 1) * blocks, :] = taps[0] * x0
                edge_ref[(place + 1) * blocks : (place + 2) * blocks, :] = taps[0] * x1 + taps[1] * x0
        held = lax.fori_loop(
            0,
            height // (2 * STEP),
            lambda j, held, i=i: step(pl.multiple_of(i * height + j * 2 * STEP, 2 * STEP), held),
            held,
        )
    for m in range(modes + 4):
        carry_ref[m * blocks : (m + 1) * blocks, :] = held[m]
    for copy in late:
        copy.wait()
    k_wide = wides[0][0]
    spread(q_near, k_wide, rows - STEP, 0)
    for i in range(2):
        start = (modes + 4 + i) * blocks
        carry_ref[start : start + blocks, :] = k_wide[place_of(STEP - 2 + i, blocks), :]


def far(x):
    return pltpu.with_memory_space_constraint(x, pltpu.HBM)


def run_front(q, k, v, short_taps, rate, residue):
    rows, width = k.shape
    modes = rate.shape[0]
    blocks = width // LANES
    pieces = 4

    def wide(n):
        return jax.ShapeDtypeStruct((n * blocks, LANES), jnp.float32)

    def like(x):
        return jax.ShapeDtypeStruct(x.shape, x.dtype)

    out_shape = [wide(modes + 6), wide(rows), wide(modes), wide(9), wide(4), like(rate), like(residue), like(q)]
    return pl.pallas_call(
        front_kernel,
        out_shape=out_shape,
        in_specs=[AWAY] * 6,
        out_specs=[WHOLE] * len(out_shape),
        scratch_shapes=[
            pltpu.VMEM((rows, width), jnp.bfloat16),
            pltpu.VMEM((rows, width), jnp.bfloat16),
            pltpu.VMEM(short_taps.shape, jnp.float32),
            *[pltpu.VMEM((STEP * blocks, LANES), jnp.float32)] * 4,
            pltpu.SemaphoreType.DMA((2 * pieces + 2,)),
            pltpu.SemaphoreType.DMA((2,)),
        ],
        compiler_params=params(),
        cost_estimate=cost(10**8),
        name="front",
    )(*[far(x) for x in (k, v, q, short_taps, rate, residue)])


def local_kernel(q_near, signal_ref, decay_ref, taps_ref, gain_near, *refs):
    copies = []
    if len(refs) > 5:
        weight_hbm, direction_hbm, weight_ref, direction_ref, sems = refs[:2] + refs[5:7] + refs[-1:]
        refs = refs[2:5] + refs[7:-1]
        count = sems.shape[0] - 1
        copies.append(pltpu.make_async_copy(direction_hbm, direction_ref, sems.at[count]))
        copies[-1].start()
        depth = weight_ref.shape[0] // count
        for i in range(count):
            here = pl.ds(i * depth, depth)
            copies.append(pltpu.make_async_copy(weight_hbm.at[here], weight_ref.at[here], sems.at[i]))
            copies[-1].start()
    out_ref, query_ref, gain_ref, *wides = refs
    rows, width = q_near.shape
    blocks = width // LANES
    modes = gain_near.shape[0]
    spread_rows(gain_near[...], gain_ref)
    zero = jnp.zeros((blocks, LANES), jnp.float32)
    taps = [tile(taps_ref, j, blocks) for j in range(3)]
    decay = [tile(decay_ref, m, blocks) for m in range(modes)]
    gain = [tile(gain_ref, m, blocks) for m in range(modes)]

    def step(j, held):
        row = pl.multiple_of(j * 2 * STEP, 2 * STEP)
        state, (q2, q1) = list(held[:modes]), held[modes:]
        for half, q_wide in enumerate(wides):
            spread(q_near, q_wide, row + half * STEP, 0)
        for half, q_wide in enumerate(wides):
            for index in range(STEP):
                q0 = q_wide[place_of(index, blocks), :]
                here = moving_tile(row + half * STEP + index, blocks)
                signal = signal_ref[here, :]
                query_ref[here, :] = taps[0] * q0 + taps[1] * q1 + taps[2] * q2
                state = [decay[m] * state[m] + signal for m in range(modes)]
                sums = [gain[m] * state[m] for m in range(modes)]
                while len(sums) > 1:
                    sums = [sums[i] + sums[i + 1] for i in range(0, len(sums), 2)]
                out_ref[here, :] = sums[0]
                q2, q1 = q1, q0
        return tuple(state) + (q2, q1)

    lax.fori_loop(0, rows // (2 * STEP), step, (zero,) * (modes + 2))
    for copy in copies:
        copy.wait()


def run_local(q, signal, decay, taps, gain, *weight):
    rows, width = q.shape
    blocks = width // LANES
    wide = jax.ShapeDtypeStruct((rows * blocks, LANES), jnp.float32)
    out_shape = [wide, wide, jax.ShapeDtypeStruct(decay.shape, jnp.float32)]
    scratch_shapes = [pltpu.VMEM((STEP * blocks, LANES), jnp.float32)] * 2
    if weight:
        out_shape += [jax.ShapeDtypeStruct(x.shape, x.dtype) for x in weight]
        scratch_shapes.append(pltpu.SemaphoreType.DMA((5,)))
        weight = tuple(far(x) for x in weight)
    return pl.pallas_call(
        local_kernel,
        out_shape=out_shape,
        in_specs=[WHOLE] * 5 + [AWAY] * len(weight),
        out_specs=[WHOLE] * len(out_shape),
        scratch_shapes=scratch_shapes,
        compiler_params=params(),
        cost_estimate=cost(10**6),
        name="local_filter",
    )(q, signal, decay, taps, gain, *weight)


def correct_kernel(blocks, start, decay_ref, gain_ref, local_ref, query_ref, *refs):
    out_ref, state_out_ref, wide = refs[-3:]
    rows = out_ref.shape[0]
    modes = decay_ref.shape[0] // blocks
    decay = [tile(decay_ref, m, blocks) for m in range(modes)]
    extra = query_extra = ()
    if start:
        state = tuple(tile(refs[0], m, blocks) for m in range(modes))
    else:
        carry_ref, taps_ref, edge_ref = refs[:3]
        carried = jnp.where(lax.axis_index("ctx") > 0, 1.0, 0.0)
        k2, k1, v2, v1, q2, q1 = [carried * tile(carry_ref, modes + i, blocks) for i in range(6)]
        tap = [tile(taps_ref, i, blocks) for i in range(9)]
        key0, key1, value0, value1 = [tile(edge_ref, i, blocks) for i in range(4)]
        extra = (
            (key0 + tap[4] * k1 + tap[5] * k2) * (value0 + tap[7] * v1 + tap[8] * v2) - key0 * value0,
            (key1 + tap[5] * k1) * (value1 + tap[8] * v1) - key1 * value1,
        )
        query_extra = (tap[1] * q1 + tap[2] * q2, tap[2] * q1)
        state = tuple(tile(gain_ref, m, blocks) * (carried * tile(carry_ref, m, blocks)) for m in range(modes))

    def step(row, state, first):
        state = list(state)
        for index in range(STEP):
            here = moving_tile(start + row + index, blocks)
            state = [decay[m] * state[m] for m in range(modes)]
            query = query_ref[here, :]
            if first and index < 2:
                state = [state[m] + tile(gain_ref, m, blocks) * extra[index] for m in range(modes)]
                query = query + query_extra[index]
            sums = state
            while len(sums) > 1:
                sums = [sums[i] + sums[i + 1] for i in range(0, len(sums), 2)]
            wide[place_of(index, blocks), :] = query * (local_ref[here, :] + sums[0])
        for block in range(blocks):
            halves = [
                wide[(half * blocks + block) * GROUP : (half * blocks + block + 1) * GROUP, :]
                for half in range(STEP // GROUP)
            ]
            out_ref[pl.ds(row, STEP), block * LANES : (block + 1) * LANES] = jnp.concatenate(
                halves, axis=0
            ).astype(jnp.bfloat16)
        return tuple(state)

    begin = 0
    if start == 0:
        state = step(0, state, True)
        begin = 1
    state = lax.fori_loop(
        begin, rows // STEP, lambda j, state: step(pl.multiple_of(j * STEP, STEP), state, False), state
    )
    for m in range(modes):
        state_out_ref[m * blocks : (m + 1) * blocks, :] = state[m]


def run_correct(start, rows, decay, gain, local, query, blocks, *before):
    return pl.pallas_call(
        functools.partial(correct_kernel, blocks, start),
        out_shape=[
            jax.ShapeDtypeStruct((rows, blocks * LANES), jnp.bfloat16),
            jax.ShapeDtypeStruct(decay.shape, jnp.float32),
        ],
        in_specs=[WHOLE] * (4 + len(before)),
        out_specs=[WHOLE] * 2,
        scratch_shapes=[pltpu.VMEM((STEP * blocks, LANES), jnp.float32)],
        compiler_params=params(),
        cost_estimate=cost(10**8),
        name="carried_filter",
    )(decay, gain, local, query, *before)


def gains_of(rate, residue):
    return residue * jnp.sqrt(-jnp.expm1(-2.0 * rate)) * rate.shape[0] ** (-0.5)


def split_three(x):
    high = x.astype(jnp.bfloat16)
    rest = x - high.astype(jnp.float32)
    middle = rest.astype(jnp.bfloat16)
    low = (rest - middle.astype(jnp.float32)).astype(jnp.bfloat16)
    return high, middle, low


def in_parts(row):
    return jnp.concatenate(list(split_three(row)) + [jnp.zeros((13, row.shape[1]), jnp.bfloat16)], axis=0)


def dot_parts(parts, matrix):
    out = lax.dot_general(parts, matrix, (((1,), (1,)), ((), ())), preferred_element_type=jnp.float32)
    return out[0:1] + out[1:2] + out[2:3]


def idle_kernel(*refs):
    pass


def after(array, *others):
    return pl.pallas_call(
        idle_kernel,
        out_shape=jax.ShapeDtypeStruct(array.shape, array.dtype),
        in_specs=[pl.BlockSpec(memory_space=pl.ANY)] * (1 + len(others)),
        out_specs=pl.BlockSpec(memory_space=pl.ANY),
        input_output_aliases={0: 0},
        compiler_params=params(),
        cost_estimate=cost(1),
        name="after",
    )(array, *others)


def rows_of(count, like, dtype=jnp.bfloat16):
    return jax.ShapeDtypeStruct((count, like.shape[1]), dtype)


def call(kernel, name, out_shape, *operands, tokens=()):
    def with_tokens(*refs):
        kernel(*refs[: len(operands)], *refs[len(operands) + len(tokens) :])

    return pl.pallas_call(
        with_tokens,
        out_shape=out_shape,
        in_specs=[WHOLE] * len(operands) + [pl.BlockSpec(memory_space=pl.ANY)] * len(tokens),
        out_specs=[WHOLE] * len(out_shape),
        compiler_params=params(),
        cost_estimate=cost(10**6),
        name=name,
    )(*operands, *tokens)


def inner_kernel(direction_ref, weight_ref, parts_ref, norm_ref, here_ref):
    everything = direction_ref[...]
    norm_ref[...] = jnp.broadcast_to(
        jnp.sum(everything * everything, axis=1, keepdims=True) + EPSILON, norm_ref.shape
    )
    size, width = weight_ref.shape[1], here_ref.shape[1]
    here_ref[...] = direction_ref[:, pl.ds(pl.multiple_of(lax.axis_index("tp") * width, LANES), width)]
    here = direction_ref[:, pl.ds(pl.multiple_of(lax.axis_index("ctx") * size, LANES), size)]
    parts_ref[...] = in_parts(dot_parts(in_parts(here), weight_ref[...]))


def run_inner(direction, weight):
    out_shape = [
        jax.ShapeDtypeStruct((STEP, weight.shape[0]), jnp.bfloat16),
        jax.ShapeDtypeStruct((1, LANES), jnp.float32),
        jax.ShapeDtypeStruct((1, weight.shape[1] // 2), jnp.float32),
    ]
    return call(inner_kernel, "inner", out_shape, direction, weight)


def project_kernel(begin, rows, away, weight_ref, piece_ref, *outs):
    cut = outs[0].shape[1]
    width = cut * len(outs)
    side = lax.axis_index("tp") % 2
    which = 1 - side if away else side
    for start in range(0, width, 256):
        columns = pl.ds(pl.multiple_of(which * width + start, 256), 256)
        out = jnp.dot(piece_ref[begin : begin + rows, :], weight_ref[:, columns], preferred_element_type=jnp.float32)
        ref, to = outs[start // cut], start % cut
        ref[:, to : to + 256] = out.astype(ref.dtype)


def run_project(weight, piece, begin, rows, count, *tokens):
    width = weight.shape[1] // 2
    sends = [jax.ShapeDtypeStruct((rows, width // count), jnp.bfloat16)] * count
    keep = [jax.ShapeDtypeStruct((rows, width), jnp.float32)]
    away, here = [functools.partial(project_kernel, begin, rows, x) for x in (True, False)]
    sends = call(away, "project", sends, weight, piece, tokens=tokens)
    return sends, call(here, "project", keep, weight, piece, tokens=tokens)[0]


def put_behind(ref, rows, row):
    here = slice(rows, rows + STEP)
    ref[here, :] = jnp.zeros((STEP, ref.shape[1]), jnp.bfloat16)
    ref[here, : row.shape[1]] = in_parts(row)


def take_behind(ref, rows, width):
    return jnp.sum(ref[rows : rows + STEP, :width].astype(jnp.float32), axis=0, keepdims=True)


def level_kernel(parts_ref, far_ref, *refs):
    *pieces, out_ref = refs
    far_parts = far_ref[far_ref.shape[0] - STEP :, :]
    start = 0
    for piece in pieces:
        end = start + piece.shape[0]
        out_ref[:, start:end] = dot_parts(parts_ref[...], piece[...]) + dot_parts(far_parts, piece[...])
        start = end


def add_shares(lefts, rights, outs):
    width = sum(ref.shape[1] for ref in lefts)
    rows = lefts[0].shape[0]
    step = min(ref.shape[1] for ref in (*lefts, *rights, *outs))

    def at(pieces, row, column):
        size = pieces[0].shape[1]
        return pieces[column // size].at[row : row + STEP, column % size : column % size + step]

    for row in range(0, rows, STEP):
        for column in range(0, width, step):
            left = at(lefts, row, column)[...].astype(jnp.float32)
            right = at(rights, row, column)[...].astype(jnp.float32)
            at(outs, row, column)[...] = (left + right).astype(jnp.bfloat16)


def merge_kernel(left, right, *refs):
    add_shares(refs[:left], refs[left : left + right], refs[left + right :])


def run_merge(lefts, rights, count):
    rows, width = lefts[0].shape[0], sum(x.shape[1] for x in lefts)
    kernel = functools.partial(merge_kernel, len(lefts), len(rights))
    out_shape = [jax.ShapeDtypeStruct((rows, width // count), jnp.bfloat16)] * count
    return call(kernel, "merge", out_shape, *lefts, *rights)


def merge_parts_kernel(keep_ref, parts_ref, *refs):
    add_shares((keep_ref,), refs[:-1], refs[-1:])
    refs[-1][keep_ref.shape[0] :, :] = parts_ref[...]


def is_keeper():
    return lax.axis_index("tp") // 2 == lax.axis_index("ctx")


def choose_kernel(straight_ref, own_ref, level_ref, other_ref, out_ref, total_ref):
    keeper = is_keeper()

    @pl.when(keeper)
    def _():
        rows = straight_ref.shape[0] - STEP
        out_ref[:rows, :] = straight_ref[:rows, :]

    @pl.when(jnp.logical_not(keeper))
    def _():
        out_ref[: own_ref.shape[0], :] = own_ref[...]

    total = level_ref[...] + other_ref[...]
    total_ref[...] = total
    put_behind(out_ref, out_ref.shape[0] - STEP, total)


def finish_kernel(start, count, *refs):
    level_ref, norm_ref, direction_ref, keep_ref, core_ref, hop_ref, first_ref = refs[:7]
    second_ref = None if start else refs[7]
    rows = level_ref.shape[1]
    if start:
        out_hbm, out_near, sems = refs[-3:]
        level = level_ref[...]
        copies = []
    else:
        out_hbm, level_hbm, level_near, level_out, out_near, sems = refs[-6:]
        level = level_ref[...] + take_behind(second_ref, second_ref.shape[0] - STEP, rows)
        level = level / norm_ref[0:1, 0:1]
        level_near[...] = level
        level_out[...] = level
        copies = [pltpu.make_async_copy(level_out, level_hbm, sems.at[2])]
        copies[0].start()
    direction = direction_ref[...]
    keeper = is_keeper()
    column = jnp.transpose(jnp.broadcast_to(level, (LANES, rows)))

    def put(row, *pieces):
        here = slice(row, row + STEP)
        total = pieces[0][here, :].astype(jnp.float32)
        for piece in pieces[1:]:
            total = total + piece[here, :].astype(jnp.float32)
        total = total - column[start + row : start + row + STEP, 0:1] * direction
        out_near[here, :] = total.astype(jnp.bfloat16)

    for i in range(2):
        begin, end = i * count // 2, (i + 1) * count // 2

        @pl.when(keeper)
        def _():
            for row in range(begin, end, STEP):
                put(row, keep_ref, core_ref, hop_ref)

        @pl.when(jnp.logical_not(keeper))
        def _():
            for row in range(begin, end, STEP):
                put(row, *((first_ref,) if start else (first_ref, second_ref)))

        here, there = pl.ds(begin, end - begin), pl.ds(start + begin, end - begin)
        copies.append(pltpu.make_async_copy(out_near.at[here], out_hbm.at[there], sems.at[i]))
        copies[-1].start()
    for copy in copies:
        copy.wait()


def run_finish(start, rows, operands, before=()):
    count, width = operands[3].shape
    one_row = jax.ShapeDtypeStruct((1, rows), jnp.float32)
    out_shape, out_specs = [pltpu.HBM((rows, width), jnp.bfloat16)], [AWAY]
    scratch_shapes = [pltpu.VMEM((count, width), jnp.bfloat16), pltpu.SemaphoreType.DMA((3,))]
    if not before:
        out_shape += [pltpu.HBM(one_row.shape, one_row.dtype), one_row]
        out_specs += [AWAY, WHOLE]
        scratch_shapes = [pltpu.VMEM(one_row.shape, one_row.dtype)] + scratch_shapes
    return pl.pallas_call(
        functools.partial(finish_kernel, start, count),
        out_shape=out_shape,
        in_specs=[WHOLE] * len(operands) + [AWAY] * len(before),
        out_specs=out_specs,
        scratch_shapes=scratch_shapes,
        input_output_aliases={len(operands): 0} if before else {},
        compiler_params=params(),
        cost_estimate=cost(10**6),
        name="finish",
    )(*operands, *[far(x) for x in before])


def plane_plan(q, k, v, short_taps, decay_rate, residue, out_weight, direction):
    rows, width = q.shape
    cut = rows // 2
    blocks = width // LANES
    axes = ("ctx", "tp")
    across = [(4 * c + p, 4 * (1 - c) + p) for c in range(2) for p in range(4)]
    sibling = [(4 * c + p, 4 * c + (p ^ 1)) for c in range(2) for p in range(4)]
    pair = [(4 * c + p, 4 * c + (p ^ 2)) for c in range(2) for p in range(4)]

    ended, signal, decay, taps, edge, rate, residue, q = run_front(q, k, v, short_taps, decay_rate.T, residue.T)
    carry = lax.ppermute(ended, axes, across)
    local, query, gain, weight, direction = run_local(
        q, signal, decay, taps, gains_of(rate, residue), out_weight, direction.reshape(1, -1)
    )
    first, state = run_correct(0, cut, decay, gain, local, query, blocks, carry, taps, edge)
    second, _ = run_correct(cut, rows - cut, decay, gain, local, query, blocks, state)
    far_first = lax.ppermute(first, axes, across)
    far_second = lax.ppermute(second, axes, across)

    def exchange(arrays, pairs):
        return [lax.ppermute(array, axes, pairs) for array in arrays]

    weight = after(weight, first)
    parts, norm, direction = run_inner(direction, weight)
    sends0, keep0 = run_project(weight, first, 0, cut, 1)
    sends1, keep1 = run_project(weight, second, 0, rows - cut, 1)
    (core0,) = exchange(sends0, sibling)
    (hop0,) = exchange(run_merge((keep0,), (core0,), 1), pair)

    sends, far_keep = run_project(weight, far_first, 0, cut, 2, parts, *sends0, *sends1)
    (sums0,) = call(
        merge_parts_kernel, "merge", [rows_of(cut + STEP, far_keep)], far_keep, parts, *exchange(sends, sibling)
    )
    (straight,) = exchange([sums0], across)

    sends, far_keep = run_project(weight, after(far_second, sums0, hop0), 0, rows - cut, 2)
    sums1 = run_merge((far_keep,), exchange(sends, sibling), 2)
    moved = exchange(sums1, pair)
    (core1,) = exchange(sends1, sibling)
    (own1,) = run_merge((keep1,), (core1,), 1)

    one_row = jax.ShapeDtypeStruct((1, rows), jnp.float32)
    (level,) = call(level_kernel, "level", [one_row], parts, straight, first, second)
    payload = rows_of(max(cut, rows - cut) + STEP, far_keep)
    turned, level = call(
        choose_kernel,
        "choose",
        [payload, one_row],
        straight,
        own1,
        level,
        *exchange([level], sibling),
    )
    (turned,) = exchange([turned], pair)
    (merged,) = exchange(run_merge(sums1, moved, 1), across)
    shared = (norm, direction)
    before, level, near = run_finish(0, rows, (level, *shared, keep0, core0, hop0, straight, turned))
    (ablated,) = run_finish(cut, rows, (near, *shared, keep1, core1, turned, merged), (before,))
    return ablated, level.reshape(rows)


def gather_plan(q, k, v, short_taps, decay_rate, residue, out_weight, direction):
    rows, width = q.shape
    blocks = width // LANES
    modes = decay_rate.shape[1]
    tp = lax.axis_index("tp")
    ctx_size = lax.axis_size("ctx")
    next_one = [(i, i + 1) for i in range(ctx_size - 1)]
    ended, signal, decay, taps, edge, rate, residue, q = run_front(q, k, v, short_taps, decay_rate.T, residue.T)
    halo = lax.ppermute(ended[modes * blocks :], "ctx", next_one)
    local, query, gain = run_local(q, signal, decay, taps, gains_of(rate, residue))
    k2, k1, v2, v1 = [halo[i * blocks : (i + 1) * blocks] for i in range(4)]
    tap = taps.reshape(9, blocks, LANES)
    key0, key1, value0, value1 = edge.reshape(4, blocks, LANES)
    extra0 = (key0 + tap[4] * k1 + tap[5] * k2) * (value0 + tap[7] * v1 + tap[8] * v2) - key0 * value0
    extra1 = (key1 + tap[5] * k1) * (value1 + tap[8] * v1) - key1 * value1
    wide_rate = decay_rate.T.reshape(modes, blocks, LANES)
    state = (
        ended[: modes * blocks].reshape(modes, blocks, LANES)
        + jnp.exp(-wide_rate * (rows - 1)) * extra0
        + jnp.exp(-wide_rate * (rows - 2)) * extra1
    )
    reach = 1
    while reach < ctx_size:
        earlier = lax.ppermute(state, "ctx", [(i, i + reach) for i in range(ctx_size - reach)])
        state = state + jnp.exp(-wide_rate * (rows * reach)) * earlier
        reach *= 2
    start = lax.ppermute(state, "ctx", next_one).reshape(modes * blocks, LANES)
    carry = jnp.concatenate([start, halo], axis=0)
    gated, _ = run_correct(0, rows, decay, gain, local, query, blocks, carry, taps, edge)
    partial_terms = lax.dot_general(
        gated,
        lax.all_gather(out_weight, "ctx", axis=1, tiled=True),
        (((1,), (0,)), ((), ())),
        preferred_element_type=jnp.float32,
    )
    summed = lax.psum_scatter(
        partial_terms.astype(jnp.bfloat16), "tp", scatter_dimension=1, tiled=True
    ).astype(jnp.float32)
    width_here = summed.shape[1]
    direction_here = lax.dynamic_slice_in_dim(direction, tp * width_here, width_here, 0)
    norm_total = jnp.sum(direction * direction) + EPSILON
    local_inner = jnp.dot(summed, direction_here, precision=HIGHEST)
    feature_level = lax.psum(local_inner, "tp") / norm_total
    ablated = (summed - feature_level[:, None] * direction_here[None, :]).astype(jnp.bfloat16)
    return ablated, feature_level


def solution(mesh):
    placed = (
        P(("dp", "ctx"), "tp"),
        P(("dp", "ctx"), "tp"),
        P(("dp", "ctx"), "tp"),
        P(None, None, "tp"),
        P("tp", None),
        P("tp", None),
        P("tp", "ctx"),
        P(),
    )
    plane = mesh.shape["ctx"] == 2 and mesh.shape["tp"] == 4
    return jax.shard_map(
        plane_plan if plane else gather_plan,
        mesh=mesh,
        in_specs=placed,
        out_specs=(P(("dp", "ctx"), "tp"), P(("dp", "ctx"))),
        check_vma=False,
    )
```

```python
import functools

import jax
import jax.numpy as jnp
from jax import lax
from jax.experimental import pallas as pl
from jax.experimental.pallas import tpu as pltpu
from jax.sharding import PartitionSpec as P

EPSILON = 1e-06
HIGHEST = lax.Precision.HIGHEST
LANES = 128
GROUP = 8
STEP = 16
WHOLE = pl.BlockSpec(memory_space=pltpu.VMEM)
AWAY = pl.BlockSpec(memory_space=pltpu.HBM)


def params(mebibytes=20):
    return pltpu.CompilerParams(vmem_limit_bytes=mebibytes * 1024 * 1024)


def cost(flops):
    return pl.CostEstimate(flops=flops, bytes_accessed=1024, transcendentals=0)


def spread(source, scratch, row, to):
    blocks = source.shape[1] // LANES
    for block in range(blocks):
        piece = source[pl.ds(row, STEP), block * LANES : (block + 1) * LANES].astype(jnp.float32)
        for half in range(STEP // GROUP):
            start = (half * blocks + block) * GROUP
            scratch[pl.ds(to + start, GROUP), :] = piece[half * GROUP : (half + 1) * GROUP]


def spread_rows(source, target):
    count, width = source.shape
    blocks = width // LANES
    for block in range(blocks):
        target[pl.ds(block, count, stride=blocks), :] = source[:, block * LANES : (block + 1) * LANES]


def place_of(index, blocks):
    return pl.ds((index // GROUP) * (blocks * GROUP) + index % GROUP, blocks, stride=GROUP)


def tile(ref, index, blocks):
    return ref[index * blocks : (index + 1) * blocks, :]


def moving_tile(index, blocks):
    return pl.ds(pl.multiple_of(index * blocks, blocks), blocks)


def front_kernel(*refs):
    k_hbm, v_hbm, q_hbm, taps_hbm, rate_hbm, residue_hbm = refs[:6]
    carry_ref, signal_ref, decay_ref, taps_ref, edge_ref, rate_ref, residue_ref, q_near = refs[6:14]
    k_near, v_near, taps_near, *wides, sems, late_sems = refs[-9:]
    wides = (wides[:2], wides[2:])
    rows, width = k_near.shape
    blocks = width // LANES
    modes = rate_ref.shape[0]
    pieces = sems.shape[0] // 2 - 1
    height = rows // pieces

    def part(i):
        here = pl.ds(i * height, height)
        return (
            pltpu.make_async_copy(k_hbm.at[here], k_near.at[here], sems.at[2 * i]),
            pltpu.make_async_copy(v_hbm.at[here], v_near.at[here], sems.at[2 * i + 1]),
        )

    rate_copy = pltpu.make_async_copy(rate_hbm, rate_ref, sems.at[2 * pieces])
    taps_copy = pltpu.make_async_copy(taps_hbm, taps_near, sems.at[2 * pieces + 1])
    late = [(residue_hbm, residue_ref), (q_hbm, q_near)]
    late = [pltpu.make_async_copy(source, target, late_sems.at[i]) for i, (source, target) in enumerate(late)]
    rate_copy.start()
    taps_copy.start()
    for i in range(pieces):
        for copy in part(i):
            copy.start()
    for copy in late:
        copy.start()
    rate_copy.wait()
    taps_copy.wait()
    spread_rows(jnp.exp(-rate_ref[...]), decay_ref)
    for i in range(3):
        for block in range(blocks):
            taps_ref[pl.ds(3 * i * blocks + block, 3, stride=blocks), :] = taps_near[
                i, :, block * LANES : (block + 1) * LANES
            ]
    zero = jnp.zeros((blocks, LANES), jnp.float32)
    key_taps = [tile(taps_ref, 3 + j, blocks) for j in range(3)]
    value_taps = [tile(taps_ref, 6 + j, blocks) for j in range(3)]
    decay = [tile(decay_ref, m, blocks) for m in range(modes)]

    def step(row, held):
        state, (k2, k1, v2, v1) = list(held[:modes]), held[modes:]
        for half, (k_wide, v_wide) in enumerate(wides):
            spread(k_near, k_wide, row + half * STEP, 0)
            spread(v_near, v_wide, row + half * STEP, 0)
        for half, (k_wide, v_wide) in enumerate(wides):
            for index in range(STEP):
                k0 = k_wide[place_of(index, blocks), :]
                v0 = v_wide[place_of(index, blocks), :]
                key = key_taps[0] * k0 + key_taps[1] * k1 + key_taps[2] * k2
                value = value_taps[0] * v0 + value_taps[1] * v1 + value_taps[2] * v2
                signal = key * value
                signal_ref[moving_tile(row + half * STEP + index, blocks), :] = signal
                state = [decay[m] * state[m] + signal for m in range(modes)]
                k2, k1, v2, v1 = k1, k0, v1, v0
        return tuple(state) + (k2, k1, v2, v1)

    held = (zero,) * (modes + 4)
    for i in range(pieces):
        for copy in part(i):
            copy.wait()
        if i == 0:
            spread(k_near, wides[0][0], 0, 0)
            spread(v_near, wides[0][1], 0, 0)
            for wide, taps, place in ((wides[0][0], key_taps, 0), (wides[0][1], value_taps, 2)):
                x0, x1 = wide[place_of(0, blocks), :], wide[place_of(1, blocks), :]
                edge_ref[place * blocks : (place + 1) * blocks, :] = taps[0] * x0
                edge_ref[(place + 1) * blocks : (place + 2) * blocks, :] = taps[0] * x1 + taps[1] * x0
        held = lax.fori_loop(
            0,
            height // (2 * STEP),
            lambda j, held, i=i: step(pl.multiple_of(i * height + j * 2 * STEP, 2 * STEP), held),
            held,
        )
    for m in range(modes + 4):
        carry_ref[m * blocks : (m + 1) * blocks, :] = held[m]
    for copy in late:
        copy.wait()
    k_wide = wides[0][0]
    spread(q_near, k_wide, rows - STEP, 0)
    for i in range(2):
        start = (modes + 4 + i) * blocks
        carry_ref[start : start + blocks, :] = k_wide[place_of(STEP - 2 + i, blocks), :]


def far(x):
    return pltpu.with_memory_space_constraint(x, pltpu.HBM)


def run_front(q, k, v, short_taps, rate, residue):
    rows, width = k.shape
    modes = rate.shape[0]
    blocks = width // LANES
    pieces = 4

    def wide(n):
        return jax.ShapeDtypeStruct((n * blocks, LANES), jnp.float32)

    def like(x):
        return jax.ShapeDtypeStruct(x.shape, x.dtype)

    out_shape = [wide(modes + 6), wide(rows), wide(modes), wide(9), wide(4), like(rate), like(residue), like(q)]
    return pl.pallas_call(
        front_kernel,
        out_shape=out_shape,
        in_specs=[AWAY] * 6,
        out_specs=[WHOLE] * len(out_shape),
        scratch_shapes=[
            pltpu.VMEM((rows, width), jnp.bfloat16),
            pltpu.VMEM((rows, width), jnp.bfloat16),
            pltpu.VMEM(short_taps.shape, jnp.float32),
            *[pltpu.VMEM((STEP * blocks, LANES), jnp.float32)] * 4,
            pltpu.SemaphoreType.DMA((2 * pieces + 2,)),
            pltpu.SemaphoreType.DMA((2,)),
        ],
        compiler_params=params(),
        cost_estimate=cost(10**8),
        name="front",
    )(*[far(x) for x in (k, v, q, short_taps, rate, residue)])


def local_kernel(q_near, signal_ref, decay_ref, taps_ref, gain_near, *refs):
    copies = []
    if len(refs) > 5:
        weight_hbm, direction_hbm, weight_ref, direction_ref, sems = refs[:2] + refs[5:7] + refs[-1:]
        refs = refs[2:5] + refs[7:-1]
        count = sems.shape[0] - 1
        copies.append(pltpu.make_async_copy(direction_hbm, direction_ref, sems.at[count]))
        copies[-1].start()
        depth = weight_ref.shape[0] // count
        for i in range(count):
            here = pl.ds(i * depth, depth)
            copies.append(pltpu.make_async_copy(weight_hbm.at[here], weight_ref.at[here], sems.at[i]))
            copies[-1].start()
    out_ref, query_ref, gain_ref, *wides = refs
    rows, width = q_near.shape
    blocks = width // LANES
    modes = gain_near.shape[0]
    spread_rows(gain_near[...], gain_ref)
    zero = jnp.zeros((blocks, LANES), jnp.float32)
    taps = [tile(taps_ref, j, blocks) for j in range(3)]
    decay = [tile(decay_ref, m, blocks) for m in range(modes)]
    gain = [tile(gain_ref, m, blocks) for m in range(modes)]

    def step(j, held):
        row = pl.multiple_of(j * 2 * STEP, 2 * STEP)
        state, (q2, q1) = list(held[:modes]), held[modes:]
        for half, q_wide in enumerate(wides):
            spread(q_near, q_wide, row + half * STEP, 0)
        for half, q_wide in enumerate(wides):
            for index in range(STEP):
                q0 = q_wide[place_of(index, blocks), :]
                here = moving_tile(row + half * STEP + index, blocks)
                signal = signal_ref[here, :]
                query_ref[here, :] = taps[0] * q0 + taps[1] * q1 + taps[2] * q2
                state = [decay[m] * state[m] + signal for m in range(modes)]
                sums = [gain[m] * state[m] for m in range(modes)]
                while len(sums) > 1:
                    sums = [sums[i] + sums[i + 1] for i in range(0, len(sums), 2)]
                out_ref[here, :] = sums[0]
                q2, q1 = q1, q0
        return tuple(state) + (q2, q1)

    lax.fori_loop(0, rows // (2 * STEP), step, (zero,) * (modes + 2))
    for copy in copies:
        copy.wait()


def run_local(q, signal, decay, taps, gain, *weight):
    rows, width = q.shape
    blocks = width // LANES
    wide = jax.ShapeDtypeStruct((rows * blocks, LANES), jnp.float32)
    out_shape = [wide, wide, jax.ShapeDtypeStruct(decay.shape, jnp.float32)]
    scratch_shapes = [pltpu.VMEM((STEP * blocks, LANES), jnp.float32)] * 2
    if weight:
        out_shape += [jax.ShapeDtypeStruct(x.shape, x.dtype) for x in weight]
        scratch_shapes.append(pltpu.SemaphoreType.DMA((5,)))
        weight = tuple(far(x) for x in weight)
    return pl.pallas_call(
        local_kernel,
        out_shape=out_shape,
        in_specs=[WHOLE] * 5 + [AWAY] * len(weight),
        out_specs=[WHOLE] * len(out_shape),
        scratch_shapes=scratch_shapes,
        compiler_params=params(),
        cost_estimate=cost(10**6),
        name="local_filter",
    )(q, signal, decay, taps, gain, *weight)


def correct_kernel(blocks, start, decay_ref, gain_ref, local_ref, query_ref, *refs):
    out_ref, state_out_ref, wide = refs[-3:]
    rows = out_ref.shape[0]
    modes = decay_ref.shape[0] // blocks
    decay = [tile(decay_ref, m, blocks) for m in range(modes)]
    extra = query_extra = ()
    if start:
        state = tuple(tile(refs[0], m, blocks) for m in range(modes))
    else:
        carry_ref, taps_ref, edge_ref = refs[:3]
        carried = jnp.where(lax.axis_index("ctx") > 0, 1.0, 0.0)
        k2, k1, v2, v1, q2, q1 = [carried * tile(carry_ref, modes + i, blocks) for i in range(6)]
        tap = [tile(taps_ref, i, blocks) for i in range(9)]
        key0, key1, value0, value1 = [tile(edge_ref, i, blocks) for i in range(4)]
        extra = (
            (key0 + tap[4] * k1 + tap[5] * k2) * (value0 + tap[7] * v1 + tap[8] * v2) - key0 * value0,
            (key1 + tap[5] * k1) * (value1 + tap[8] * v1) - key1 * value1,
        )
        query_extra = (tap[1] * q1 + tap[2] * q2, tap[2] * q1)
        state = tuple(tile(gain_ref, m, blocks) * (carried * tile(carry_ref, m, blocks)) for m in range(modes))

    def step(row, state, first):
        state = list(state)
        for index in range(STEP):
            here = moving_tile(start + row + index, blocks)
            state = [decay[m] * state[m] for m in range(modes)]
            query = query_ref[here, :]
            if first and index < 2:
                state = [state[m] + tile(gain_ref, m, blocks) * extra[index] for m in range(modes)]
                query = query + query_extra[index]
            sums = state
            while len(sums) > 1:
                sums = [sums[i] + sums[i + 1] for i in range(0, len(sums), 2)]
            wide[place_of(index, blocks), :] = query * (local_ref[here, :] + sums[0])
        for block in range(blocks):
            halves = [
                wide[(half * blocks + block) * GROUP : (half * blocks + block + 1) * GROUP, :]
                for half in range(STEP // GROUP)
            ]
            out_ref[pl.ds(row, STEP), block * LANES : (block + 1) * LANES] = jnp.concatenate(
                halves, axis=0
            ).astype(jnp.bfloat16)
        return tuple(state)

    begin = 0
    if start == 0:
        state = step(0, state, True)
        begin = 1
    state = lax.fori_loop(
        begin, rows // STEP, lambda j, state: step(pl.multiple_of(j * STEP, STEP), state, False), state
    )
    for m in range(modes):
        state_out_ref[m * blocks : (m + 1) * blocks, :] = state[m]


def run_correct(start, rows, decay, gain, local, query, blocks, *before):
    return pl.pallas_call(
        functools.partial(correct_kernel, blocks, start),
        out_shape=[
            jax.ShapeDtypeStruct((rows, blocks * LANES), jnp.bfloat16),
            jax.ShapeDtypeStruct(decay.shape, jnp.float32),
        ],
        in_specs=[WHOLE] * (4 + len(before)),
        out_specs=[WHOLE] * 2,
        scratch_shapes=[pltpu.VMEM((STEP * blocks, LANES), jnp.float32)],
        compiler_params=params(),
        cost_estimate=cost(10**8),
        name="carried_filter",
    )(decay, gain, local, query, *before)


def gains_of(rate, residue):
    return residue * jnp.sqrt(-jnp.expm1(-2.0 * rate)) * rate.shape[0] ** (-0.5)


def split_three(x):
    high = x.astype(jnp.bfloat16)
    rest = x - high.astype(jnp.float32)
    middle = rest.astype(jnp.bfloat16)
    low = (rest - middle.astype(jnp.float32)).astype(jnp.bfloat16)
    return high, middle, low


def in_parts(row):
    return jnp.concatenate(list(split_three(row)) + [jnp.zeros((13, row.shape[1]), jnp.bfloat16)], axis=0)


def dot_parts(parts, matrix):
    out = lax.dot_general(parts, matrix, (((1,), (1,)), ((), ())), preferred_element_type=jnp.float32)
    return out[0:1] + out[1:2] + out[2:3]


def idle_kernel(*refs):
    pass


def after(array, *others):
    return pl.pallas_call(
        idle_kernel,
        out_shape=jax.ShapeDtypeStruct(array.shape, array.dtype),
        in_specs=[pl.BlockSpec(memory_space=pl.ANY)] * (1 + len(others)),
        out_specs=pl.BlockSpec(memory_space=pl.ANY),
        input_output_aliases={0: 0},
        compiler_params=params(),
        cost_estimate=cost(1),
        name="after",
    )(array, *others)


def rows_of(count, like, dtype=jnp.bfloat16):
    return jax.ShapeDtypeStruct((count, like.shape[1]), dtype)


def call(kernel, name, out_shape, *operands, tokens=()):
    def with_tokens(*refs):
        kernel(*refs[: len(operands)], *refs[len(operands) + len(tokens) :])

    return pl.pallas_call(
        with_tokens,
        out_shape=out_shape,
        in_specs=[WHOLE] * len(operands) + [pl.BlockSpec(memory_space=pl.ANY)] * len(tokens),
        out_specs=[WHOLE] * len(out_shape),
        compiler_params=params(),
        cost_estimate=cost(10**6),
        name=name,
    )(*operands, *tokens)


def inner_kernel(direction_ref, weight_ref, parts_ref, norm_ref, here_ref):
    everything = direction_ref[...]
    norm_ref[...] = jnp.broadcast_to(
        jnp.sum(everything * everything, axis=1, keepdims=True) + EPSILON, norm_ref.shape
    )
    size, width = weight_ref.shape[1], here_ref.shape[1]
    here_ref[...] = direction_ref[:, pl.ds(pl.multiple_of(lax.axis_index("tp") * width, LANES), width)]
    here = direction_ref[:, pl.ds(pl.multiple_of(lax.axis_index("ctx") * size, LANES), size)]
    parts_ref[...] = in_parts(dot_parts(in_parts(here), weight_ref[...]))


def run_inner(direction, weight):
    out_shape = [
        jax.ShapeDtypeStruct((STEP, weight.shape[0]), jnp.bfloat16),
        jax.ShapeDtypeStruct((1, LANES), jnp.float32),
        jax.ShapeDtypeStruct((1, weight.shape[1] // 2), jnp.float32),
    ]
    return call(inner_kernel, "inner", out_shape, direction, weight)


def project_kernel(begin, rows, away, weight_ref, piece_ref, *outs):
    cut = outs[0].shape[1]
    width = cut * len(outs)
    side = lax.axis_index("tp") % 2
    which = 1 - side if away else side
    for start in range(0, width, 256):
        columns = pl.ds(pl.multiple_of(which * width + start, 256), 256)
        out = jnp.dot(piece_ref[begin : begin + rows, :], weight_ref[:, columns], preferred_element_type=jnp.float32)
        ref, to = outs[start // cut], start % cut
        ref[:, to : to + 256] = out.astype(ref.dtype)


def run_project(weight, piece, begin, rows, count, *tokens):
    width = weight.shape[1] // 2
    sends = [jax.ShapeDtypeStruct((rows, width // count), jnp.bfloat16)] * count
    keep = [jax.ShapeDtypeStruct((rows, width), jnp.float32)]
    away, here = [functools.partial(project_kernel, begin, rows, x) for x in (True, False)]
    sends = call(away, "project", sends, weight, piece, tokens=tokens)
    return sends, call(here, "project", keep, weight, piece, tokens=tokens)[0]


def put_behind(ref, rows, row):
    here = slice(rows, rows + STEP)
    ref[here, :] = jnp.zeros((STEP, ref.shape[1]), jnp.bfloat16)
    ref[here, : row.shape[1]] = in_parts(row)


def take_behind(ref, rows, width):
    return jnp.sum(ref[rows : rows + STEP, :width].astype(jnp.float32), axis=0, keepdims=True)


def level_kernel(parts_ref, far_ref, *refs):
    *pieces, out_ref = refs
    far_parts = far_ref[far_ref.shape[0] - STEP :, :]
    start = 0
    for piece in pieces:
        end = start + piece.shape[0]
        out_ref[:, start:end] = dot_parts(parts_ref[...], piece[...]) + dot_parts(far_parts, piece[...])
        start = end


def add_shares(lefts, rights, outs):
    width = sum(ref.shape[1] for ref in lefts)
    rows = lefts[0].shape[0]
    step = min(ref.shape[1] for ref in (*lefts, *rights, *outs))

    def at(pieces, row, column):
        size = pieces[0].shape[1]
        return pieces[column // size].at[row : row + STEP, column % size : column % size + step]

    for row in range(0, rows, STEP):
        for column in range(0, width, step):
            left = at(lefts, row, column)[...].astype(jnp.float32)
            right = at(rights, row, column)[...].astype(jnp.float32)
            at(outs, row, column)[...] = (left + right).astype(jnp.bfloat16)


def merge_kernel(left, right, *refs):
    add_shares(refs[:left], refs[left : left + right], refs[left + right :])


def run_merge(lefts, rights, count):
    rows, width = lefts[0].shape[0], sum(x.shape[1] for x in lefts)
    kernel = functools.partial(merge_kernel, len(lefts), len(rights))
    out_shape = [jax.ShapeDtypeStruct((rows, width // count), jnp.bfloat16)] * count
    return call(kernel, "merge", out_shape, *lefts, *rights)


def merge_parts_kernel(keep_ref, parts_ref, *refs):
    add_shares((keep_ref,), refs[:-1], refs[-1:])
    refs[-1][keep_ref.shape[0] :, :] = parts_ref[...]


def is_keeper():
    return lax.axis_index("tp") // 2 == lax.axis_index("ctx")


def choose_kernel(straight_ref, own_ref, level_ref, other_ref, out_ref, total_ref):
    keeper = is_keeper()

    @pl.when(keeper)
    def _():
        rows = straight_ref.shape[0] - STEP
        out_ref[:rows, :] = straight_ref[:rows, :]

    @pl.when(jnp.logical_not(keeper))
    def _():
        out_ref[: own_ref.shape[0], :] = own_ref[...]

    total = level_ref[...] + other_ref[...]
    total_ref[...] = total
    put_behind(out_ref, out_ref.shape[0] - STEP, total)


def finish_kernel(start, count, *refs):
    level_ref, norm_ref, direction_ref, keep_ref, core_ref, hop_ref, first_ref = refs[:7]
    second_ref = None if start else refs[7]
    rows = level_ref.shape[1]
    if start:
        out_hbm, out_near, sems = refs[-3:]
        level = level_ref[...]
        copies = []
    else:
        out_hbm, level_hbm, level_near, level_out, out_near, sems = refs[-6:]
        level = level_ref[...] + take_behind(second_ref, second_ref.shape[0] - STEP, rows)
        level = level / norm_ref[0:1, 0:1]
        level_near[...] = level
        level_out[...] = level
        copies = [pltpu.make_async_copy(level_out, level_hbm, sems.at[2])]
        copies[0].start()
    direction = direction_ref[...]
    keeper = is_keeper()
    column = jnp.transpose(jnp.broadcast_to(level, (LANES, rows)))

    def put(row, *pieces):
        here = slice(row, row + STEP)
        total = pieces[0][here, :].astype(jnp.float32)
        for piece in pieces[1:]:
            total = total + piece[here, :].astype(jnp.float32)
        total = total - column[start + row : start + row + STEP, 0:1] * direction
        out_near[here, :] = total.astype(jnp.bfloat16)

    for i in range(2):
        begin, end = i * count // 2, (i + 1) * count // 2

        @pl.when(keeper)
        def _():
            for row in range(begin, end, STEP):
                put(row, keep_ref, core_ref, hop_ref)

        @pl.when(jnp.logical_not(keeper))
        def _():
            for row in range(begin, end, STEP):
                put(row, *((first_ref,) if start else (first_ref, second_ref)))

        here, there = pl.ds(begin, end - begin), pl.ds(start + begin, end - begin)
        copies.append(pltpu.make_async_copy(out_near.at[here], out_hbm.at[there], sems.at[i]))
        copies[-1].start()
    for copy in copies:
        copy.wait()


def run_finish(start, rows, operands, before=()):
    count, width = operands[3].shape
    one_row = jax.ShapeDtypeStruct((1, rows), jnp.float32)
    out_shape, out_specs = [pltpu.HBM((rows, width), jnp.bfloat16)], [AWAY]
    scratch_shapes = [pltpu.VMEM((count, width), jnp.bfloat16), pltpu.SemaphoreType.DMA((3,))]
    if not before:
        out_shape += [pltpu.HBM(one_row.shape, one_row.dtype), one_row]
        out_specs += [AWAY, WHOLE]
        scratch_shapes = [pltpu.VMEM(one_row.shape, one_row.dtype)] + scratch_shapes
    return pl.pallas_call(
        functools.partial(finish_kernel, start, count),
        out_shape=out_shape,
        in_specs=[WHOLE] * len(operands) + [AWAY] * len(before),
        out_specs=out_specs,
        scratch_shapes=scratch_shapes,
        input_output_aliases={len(operands): 0} if before else {},
        compiler_params=params(),
        cost_estimate=cost(10**6),
        name="finish",
    )(*operands, *[far(x) for x in before])


def plane_plan(q, k, v, short_taps, decay_rate, residue, out_weight, direction):
    rows, width = q.shape
    cut = rows // 2
    blocks = width // LANES
    axes = ("ctx", "tp")
    across = [(4 * c + p, 4 * (1 - c) + p) for c in range(2) for p in range(4)]
    sibling = [(4 * c + p, 4 * c + (p ^ 1)) for c in range(2) for p in range(4)]
    pair = [(4 * c + p, 4 * c + (p ^ 2)) for c in range(2) for p in range(4)]

    ended, signal, decay, taps, edge, rate, residue, q = run_front(q, k, v, short_taps, decay_rate.T, residue.T)
    carry = lax.ppermute(ended, axes, across)
    local, query, gain, weight, direction = run_local(
        q, signal, decay, taps, gains_of(rate, residue), out_weight, direction.reshape(1, -1)
    )
    first, state = run_correct(0, cut, decay, gain, local, query, blocks, carry, taps, edge)
    second, _ = run_correct(cut, rows - cut, decay, gain, local, query, blocks, state)
    far_first = lax.ppermute(first, axes, across)
    far_second = lax.ppermute(second, axes, across)

    def exchange(arrays, pairs):
        return [lax.ppermute(array, axes, pairs) for array in arrays]

    weight = after(weight, first)
    parts, norm, direction = run_inner(direction, weight)
    sends0, keep0 = run_project(weight, first, 0, cut, 1)
    sends1, keep1 = run_project(weight, second, 0, rows - cut, 1)
    (core0,) = exchange(sends0, sibling)
    (hop0,) = exchange(run_merge((keep0,), (core0,), 1), pair)

    sends, far_keep = run_project(weight, far_first, 0, cut, 2, parts, *sends0, *sends1)
    (sums0,) = call(
        merge_parts_kernel, "merge", [rows_of(cut + STEP, far_keep)], far_keep, parts, *exchange(sends, sibling)
    )
    (straight,) = exchange([sums0], across)

    sends, far_keep = run_project(weight, after(far_second, sums0, hop0), 0, rows - cut, 2)
    sums1 = run_merge((far_keep,), exchange(sends, sibling), 1)
    moved = exchange(sums1, pair)
    (core1,) = exchange(sends1, sibling)
    (own1,) = run_merge((keep1,), (core1,), 1)

    one_row = jax.ShapeDtypeStruct((1, rows), jnp.float32)
    (level,) = call(level_kernel, "level", [one_row], parts, straight, first, second)
    payload = rows_of(max(cut, rows - cut) + STEP, far_keep)
    turned, level = call(
        choose_kernel,
        "choose",
        [payload, one_row],
        straight,
        own1,
        level,
        *exchange([level], sibling),
    )
    (turned,) = exchange([turned], pair)
    (merged,) = exchange(run_merge(sums1, moved, 1), across)
    shared = (norm, direction)
    before, level, near = run_finish(0, rows, (level, *shared, keep0, core0, hop0, straight, turned))
    (ablated,) = run_finish(cut, rows, (near, *shared, keep1, core1, turned, merged), (before,))
    return ablated, level.reshape(rows)


def gather_plan(q, k, v, short_taps, decay_rate, residue, out_weight, direction):
    rows, width = q.shape
    blocks = width // LANES
    modes = decay_rate.shape[1]
    tp = lax.axis_index("tp")
    ctx_size = lax.axis_size("ctx")
    next_one = [(i, i + 1) for i in range(ctx_size - 1)]
    ended, signal, decay, taps, edge, rate, residue, q = run_front(q, k, v, short_taps, decay_rate.T, residue.T)
    halo = lax.ppermute(ended[modes * blocks :], "ctx", next_one)
    local, query, gain = run_local(q, signal, decay, taps, gains_of(rate, residue))
    k2, k1, v2, v1 = [halo[i * blocks : (i + 1) * blocks] for i in range(4)]
    tap = taps.reshape(9, blocks, LANES)
    key0, key1, value0, value1 = edge.reshape(4, blocks, LANES)
    extra0 = (key0 + tap[4] * k1 + tap[5] * k2) * (value0 + tap[7] * v1 + tap[8] * v2) - key0 * value0
    extra1 = (key1 + tap[5] * k1) * (value1 + tap[8] * v1) - key1 * value1
    wide_rate = decay_rate.T.reshape(modes, blocks, LANES)
    state = (
        ended[: modes * blocks].reshape(modes, blocks, LANES)
        + jnp.exp(-wide_rate * (rows - 1)) * extra0
        + jnp.exp(-wide_rate * (rows - 2)) * extra1
    )
    reach = 1
    while reach < ctx_size:
        earlier = lax.ppermute(state, "ctx", [(i, i + reach) for i in range(ctx_size - reach)])
        state = state + jnp.exp(-wide_rate * (rows * reach)) * earlier
        reach *= 2
    start = lax.ppermute(state, "ctx", next_one).reshape(modes * blocks, LANES)
    carry = jnp.concatenate([start, halo], axis=0)
    gated, _ = run_correct(0, rows, decay, gain, local, query, blocks, carry, taps, edge)
    partial_terms = lax.dot_general(
        gated,
        lax.all_gather(out_weight, "ctx", axis=1, tiled=True),
        (((1,), (0,)), ((), ())),
        preferred_element_type=jnp.float32,
    )
    summed = lax.psum_scatter(
        partial_terms.astype(jnp.bfloat16), "tp", scatter_dimension=1, tiled=True
    ).astype(jnp.float32)
    width_here = summed.shape[1]
    direction_here = lax.dynamic_slice_in_dim(direction, tp * width_here, width_here, 0)
    norm_total = jnp.sum(direction * direction) + EPSILON
    local_inner = jnp.dot(summed, direction_here, precision=HIGHEST)
    feature_level = lax.psum(local_inner, "tp") / norm_total
    ablated = (summed - feature_level[:, None] * direction_here[None, :]).astype(jnp.bfloat16)
    return ablated, feature_level


def solution(mesh):
    placed = (
        P(("dp", "ctx"), "tp"),
        P(("dp", "ctx"), "tp"),
        P(("dp", "ctx"), "tp"),
        P(None, None, "tp"),
        P("tp", None),
        P("tp", None),
        P("tp", "ctx"),
        P(),
    )
    plane = mesh.shape["ctx"] == 2 and mesh.shape["tp"] == 4
    return jax.shard_map(
        plane_plan if plane else gather_plan,
        mesh=mesh,
        in_specs=placed,
        out_specs=(P(("dp", "ctx"), "tp"), P(("dp", "ctx"))),
        check_vma=False,
    )
```

```python
import functools

import jax
import jax.numpy as jnp
from jax import lax
from jax.experimental import pallas as pl
from jax.experimental.pallas import tpu as pltpu
from jax.sharding import PartitionSpec as P

EPSILON = 1e-06
HIGHEST = lax.Precision.HIGHEST
LANES = 128
GROUP = 8
STEP = 16
WHOLE = pl.BlockSpec(memory_space=pltpu.VMEM)
AWAY = pl.BlockSpec(memory_space=pltpu.HBM)


def params(mebibytes=20):
    return pltpu.CompilerParams(vmem_limit_bytes=mebibytes * 1024 * 1024)


def cost(flops):
    return pl.CostEstimate(flops=flops, bytes_accessed=1024, transcendentals=0)


def spread(source, scratch, row, to):
    blocks = source.shape[1] // LANES
    for block in range(blocks):
        piece = source[pl.ds(row, STEP), block * LANES : (block + 1) * LANES].astype(jnp.float32)
        for half in range(STEP // GROUP):
            start = (half * blocks + block) * GROUP
            scratch[pl.ds(to + start, GROUP), :] = piece[half * GROUP : (half + 1) * GROUP]


def spread_rows(source, target):
    count, width = source.shape
    blocks = width // LANES
    for block in range(blocks):
        target[pl.ds(block, count, stride=blocks), :] = source[:, block * LANES : (block + 1) * LANES]


def place_of(index, blocks):
    return pl.ds((index // GROUP) * (blocks * GROUP) + index % GROUP, blocks, stride=GROUP)


def tile(ref, index, blocks):
    return ref[index * blocks : (index + 1) * blocks, :]


def moving_tile(index, blocks):
    return pl.ds(pl.multiple_of(index * blocks, blocks), blocks)


def front_kernel(*refs):
    k_hbm, v_hbm, q_hbm, taps_hbm, rate_hbm, residue_hbm = refs[:6]
    carry_ref, signal_ref, decay_ref, taps_ref, edge_ref, rate_ref, residue_ref, q_near = refs[6:14]
    k_near, v_near, taps_near, *wides, sems, late_sems = refs[-9:]
    wides = (wides[:2], wides[2:])
    rows, width = k_near.shape
    blocks = width // LANES
    modes = rate_ref.shape[0]
    pieces = sems.shape[0] // 2 - 1
    height = rows // pieces

    def part(i):
        here = pl.ds(i * height, height)
        return (
            pltpu.make_async_copy(k_hbm.at[here], k_near.at[here], sems.at[2 * i]),
            pltpu.make_async_copy(v_hbm.at[here], v_near.at[here], sems.at[2 * i + 1]),
        )

    rate_copy = pltpu.make_async_copy(rate_hbm, rate_ref, sems.at[2 * pieces])
    taps_copy = pltpu.make_async_copy(taps_hbm, taps_near, sems.at[2 * pieces + 1])
    late = [(residue_hbm, residue_ref), (q_hbm, q_near)]
    late = [pltpu.make_async_copy(source, target, late_sems.at[i]) for i, (source, target) in enumerate(late)]
    rate_copy.start()
    taps_copy.start()
    for i in range(pieces):
        for copy in part(i):
            copy.start()
    for copy in late:
        copy.start()
    rate_copy.wait()
    taps_copy.wait()
    spread_rows(jnp.exp(-rate_ref[...]), decay_ref)
    for i in range(3):
        for block in range(blocks):
            taps_ref[pl.ds(3 * i * blocks + block, 3, stride=blocks), :] = taps_near[
                i, :, block * LANES : (block + 1) * LANES
            ]
    zero = jnp.zeros((blocks, LANES), jnp.float32)
    key_taps = [tile(taps_ref, 3 + j, blocks) for j in range(3)]
    value_taps = [tile(taps_ref, 6 + j, blocks) for j in range(3)]
    decay = [tile(decay_ref, m, blocks) for m in range(modes)]

    def step(row, held):
        state, (k2, k1, v2, v1) = list(held[:modes]), held[modes:]
        for half, (k_wide, v_wide) in enumerate(wides):
            spread(k_near, k_wide, row + half * STEP, 0)
            spread(v_near, v_wide, row + half * STEP, 0)
        for half, (k_wide, v_wide) in enumerate(wides):
            for index in range(STEP):
                k0 = k_wide[place_of(index, blocks), :]
                v0 = v_wide[place_of(index, blocks), :]
                key = key_taps[0] * k0 + key_taps[1] * k1 + key_taps[2] * k2
                value = value_taps[0] * v0 + value_taps[1] * v1 + value_taps[2] * v2
                signal = key * value
                signal_ref[moving_tile(row + half * STEP + index, blocks), :] = signal
                state = [decay[m] * state[m] + signal for m in range(modes)]
                k2, k1, v2, v1 = k1, k0, v1, v0
        return tuple(state) + (k2, k1, v2, v1)

    held = (zero,) * (modes + 4)
    for i in range(pieces):
        for copy in part(i):
            copy.wait()
        if i == 0:
            spread(k_near, wides[0][0], 0, 0)
            spread(v_near, wides[0][1], 0, 0)
            for wide, taps, place in ((wides[0][0], key_taps, 0), (wides[0][1], value_taps, 2)):
                x0, x1 = wide[place_of(0, blocks), :], wide[place_of(1, blocks), :]
                edge_ref[place * blocks : (place + 1) * blocks, :] = taps[0] * x0
                edge_ref[(place + 1) * blocks : (place + 2) * blocks, :] = taps[0] * x1 + taps[1] * x0
        held = lax.fori_loop(
            0,
            height // (2 * STEP),
            lambda j, held, i=i: step(pl.multiple_of(i * height + j * 2 * STEP, 2 * STEP), held),
            held,
        )
    for m in range(modes + 4):
        carry_ref[m * blocks : (m + 1) * blocks, :] = held[m]
    for copy in late:
        copy.wait()
    k_wide = wides[0][0]
    spread(q_near, k_wide, rows - STEP, 0)
    for i in range(2):
        start = (modes + 4 + i) * blocks
        carry_ref[start : start + blocks, :] = k_wide[place_of(STEP - 2 + i, blocks), :]


def far(x):
    return pltpu.with_memory_space_constraint(x, pltpu.HBM)


def run_front(q, k, v, short_taps, rate, residue):
    rows, width = k.shape
    modes = rate.shape[0]
    blocks = width // LANES
    pieces = 4

    def wide(n):
        return jax.ShapeDtypeStruct((n * blocks, LANES), jnp.float32)

    def like(x):
        return jax.ShapeDtypeStruct(x.shape, x.dtype)

    out_shape = [wide(modes + 6), wide(rows), wide(modes), wide(9), wide(4), like(rate), like(residue), like(q)]
    return pl.pallas_call(
        front_kernel,
        out_shape=out_shape,
        in_specs=[AWAY] * 6,
        out_specs=[WHOLE] * len(out_shape),
        scratch_shapes=[
            pltpu.VMEM((rows, width), jnp.bfloat16),
            pltpu.VMEM((rows, width), jnp.bfloat16),
            pltpu.VMEM(short_taps.shape, jnp.float32),
            *[pltpu.VMEM((STEP * blocks, LANES), jnp.float32)] * 4,
            pltpu.SemaphoreType.DMA((2 * pieces + 2,)),
            pltpu.SemaphoreType.DMA((2,)),
        ],
        compiler_params=params(),
        cost_estimate=cost(10**8),
        name="front",
    )(*[far(x) for x in (k, v, q, short_taps, rate, residue)])


def local_kernel(q_near, signal_ref, decay_ref, taps_ref, gain_near, *refs):
    copies = []
    if len(refs) > 5:
        weight_hbm, direction_hbm, weight_ref, direction_ref, sems = refs[:2] + refs[5:7] + refs[-1:]
        refs = refs[2:5] + refs[7:-1]
        count = sems.shape[0] - 1
        copies.append(pltpu.make_async_copy(direction_hbm, direction_ref, sems.at[count]))
        copies[-1].start()
        depth = weight_ref.shape[0] // count
        for i in range(count):
            here = pl.ds(i * depth, depth)
            copies.append(pltpu.make_async_copy(weight_hbm.at[here], weight_ref.at[here], sems.at[i]))
            copies[-1].start()
    out_ref, query_ref, gain_ref, *wides = refs
    rows, width = q_near.shape
    blocks = width // LANES
    modes = gain_near.shape[0]
    spread_rows(gain_near[...], gain_ref)
    zero = jnp.zeros((blocks, LANES), jnp.float32)
    taps = [tile(taps_ref, j, blocks) for j in range(3)]
    decay = [tile(decay_ref, m, blocks) for m in range(modes)]
    gain = [tile(gain_ref, m, blocks) for m in range(modes)]

    def step(j, held):
        row = pl.multiple_of(j * 2 * STEP, 2 * STEP)
        state, (q2, q1) = list(held[:modes]), held[modes:]
        for half, q_wide in enumerate(wides):
            spread(q_near, q_wide, row + half * STEP, 0)
        for half, q_wide in enumerate(wides):
            for index in range(STEP):
                q0 = q_wide[place_of(index, blocks), :]
                here = moving_tile(row + half * STEP + index, blocks)
                signal = signal_ref[here, :]
                query_ref[here, :] = taps[0] * q0 + taps[1] * q1 + taps[2] * q2
                state = [decay[m] * state[m] + signal for m in range(modes)]
                sums = [gain[m] * state[m] for m in range(modes)]
                while len(sums) > 1:
                    sums = [sums[i] + sums[i + 1] for i in range(0, len(sums), 2)]
                out_ref[here, :] = sums[0]
                q2, q1 = q1, q0
        return tuple(state) + (q2, q1)

    lax.fori_loop(0, rows // (2 * STEP), step, (zero,) * (modes + 2))
    for copy in copies:
        copy.wait()


def run_local(q, signal, decay, taps, gain, *weight):
    rows, width = q.shape
    blocks = width // LANES
    wide = jax.ShapeDtypeStruct((rows * blocks, LANES), jnp.float32)
    out_shape = [wide, wide, jax.ShapeDtypeStruct(decay.shape, jnp.float32)]
    scratch_shapes = [pltpu.VMEM((STEP * blocks, LANES), jnp.float32)] * 2
    if weight:
        out_shape += [jax.ShapeDtypeStruct(x.shape, x.dtype) for x in weight]
        scratch_shapes.append(pltpu.SemaphoreType.DMA((5,)))
        weight = tuple(far(x) for x in weight)
    return pl.pallas_call(
        local_kernel,
        out_shape=out_shape,
        in_specs=[WHOLE] * 5 + [AWAY] * len(weight),
        out_specs=[WHOLE] * len(out_shape),
        scratch_shapes=scratch_shapes,
        compiler_params=params(),
        cost_estimate=cost(10**6),
        name="local_filter",
    )(q, signal, decay, taps, gain, *weight)


def correct_kernel(blocks, start, decay_ref, gain_ref, local_ref, query_ref, *refs):
    wide, outs = refs[-1], refs[1 if start else 3 : -1]
    out_ref = outs[0]
    rows = out_ref.shape[0]
    modes = decay_ref.shape[0] // blocks
    decay = [tile(decay_ref, m, blocks) for m in range(modes)]
    extra = query_extra = ()
    if start:
        state = tuple(tile(refs[0], m, blocks) for m in range(modes))
    else:
        carry_ref, taps_ref, edge_ref = refs[:3]
        carried = jnp.where(lax.axis_index("ctx") > 0, 1.0, 0.0)
        k2, k1, v2, v1, q2, q1 = [carried * tile(carry_ref, modes + i, blocks) for i in range(6)]
        tap = [tile(taps_ref, i, blocks) for i in range(9)]
        key0, key1, value0, value1 = [tile(edge_ref, i, blocks) for i in range(4)]
        extra = (
            (key0 + tap[4] * k1 + tap[5] * k2) * (value0 + tap[7] * v1 + tap[8] * v2) - key0 * value0,
            (key1 + tap[5] * k1) * (value1 + tap[8] * v1) - key1 * value1,
        )
        query_extra = (tap[1] * q1 + tap[2] * q2, tap[2] * q1)
        state = tuple(tile(gain_ref, m, blocks) * (carried * tile(carry_ref, m, blocks)) for m in range(modes))

    def step(row, state, first):
        state = list(state)
        for index in range(STEP):
            here = moving_tile(start + row + index, blocks)
            state = [decay[m] * state[m] for m in range(modes)]
            query = query_ref[here, :]
            if first and index < 2:
                state = [state[m] + tile(gain_ref, m, blocks) * extra[index] for m in range(modes)]
                query = query + query_extra[index]
            sums = state
            while len(sums) > 1:
                sums = [sums[i] + sums[i + 1] for i in range(0, len(sums), 2)]
            wide[place_of(index, blocks), :] = query * (local_ref[here, :] + sums[0])
        for block in range(blocks):
            halves = [
                wide[(half * blocks + block) * GROUP : (half * blocks + block + 1) * GROUP, :]
                for half in range(STEP // GROUP)
            ]
            out_ref[pl.ds(row, STEP), block * LANES : (block + 1) * LANES] = jnp.concatenate(
                halves, axis=0
            ).astype(jnp.bfloat16)
        return tuple(state)

    begin = 0
    if start == 0:
        state = step(0, state, True)
        begin = 1
    state = lax.fori_loop(
        begin, rows // STEP, lambda j, state: step(pl.multiple_of(j * STEP, STEP), state, False), state
    )
    for state_out_ref in outs[1:]:
        for m in range(modes):
            state_out_ref[m * blocks : (m + 1) * blocks, :] = state[m]


def run_correct(start, rows, decay, gain, local, query, blocks, *before):
    more = start + rows < local.shape[0] // blocks
    return pl.pallas_call(
        functools.partial(correct_kernel, blocks, start),
        out_shape=[jax.ShapeDtypeStruct((rows, blocks * LANES), jnp.bfloat16)]
        + [jax.ShapeDtypeStruct(decay.shape, jnp.float32)] * more,
        in_specs=[WHOLE] * (4 + len(before)),
        out_specs=[WHOLE] * (1 + more),
        scratch_shapes=[pltpu.VMEM((STEP * blocks, LANES), jnp.float32)],
        compiler_params=params(),
        cost_estimate=cost(10**8),
        name="carried_filter",
    )(decay, gain, local, query, *before)


def gains_of(rate, residue):
    return residue * jnp.sqrt(-jnp.expm1(-2.0 * rate)) * rate.shape[0] ** (-0.5)


def split_three(x):
    high = x.astype(jnp.bfloat16)
    rest = x - high.astype(jnp.float32)
    middle = rest.astype(jnp.bfloat16)
    low = (rest - middle.astype(jnp.float32)).astype(jnp.bfloat16)
    return high, middle, low


def in_parts(row):
    return jnp.concatenate(list(split_three(row)) + [jnp.zeros((13, row.shape[1]), jnp.bfloat16)], axis=0)


def dot_parts(parts, matrix):
    out = lax.dot_general(parts, matrix, (((1,), (1,)), ((), ())), preferred_element_type=jnp.float32)
    return out[0:1] + out[1:2] + out[2:3]


def idle_kernel(*refs):
    pass


def after(array, *others):
    return pl.pallas_call(
        idle_kernel,
        out_shape=jax.ShapeDtypeStruct(array.shape, array.dtype),
        in_specs=[pl.BlockSpec(memory_space=pl.ANY)] * (1 + len(others)),
        out_specs=pl.BlockSpec(memory_space=pl.ANY),
        input_output_aliases={0: 0},
        compiler_params=params(),
        cost_estimate=cost(1),
        name="after",
    )(array, *others)


def rows_of(count, like, dtype=jnp.bfloat16):
    return jax.ShapeDtypeStruct((count, like.shape[1]), dtype)


def call(kernel, name, out_shape, *operands, tokens=()):
    def with_tokens(*refs):
        kernel(*refs[: len(operands)], *refs[len(operands) + len(tokens) :])

    return pl.pallas_call(
        with_tokens,
        out_shape=out_shape,
        in_specs=[WHOLE] * len(operands) + [pl.BlockSpec(memory_space=pl.ANY)] * len(tokens),
        out_specs=[WHOLE] * len(out_shape),
        compiler_params=params(),
        cost_estimate=cost(10**6),
        name=name,
    )(*operands, *tokens)


def inner_kernel(direction_ref, weight_ref, parts_ref, norm_ref, here_ref):
    everything = direction_ref[...]
    norm_ref[...] = jnp.broadcast_to(
        jnp.sum(everything * everything, axis=1, keepdims=True) + EPSILON, norm_ref.shape
    )
    size, width = weight_ref.shape[1], here_ref.shape[1]
    here_ref[...] = direction_ref[:, pl.ds(pl.multiple_of(lax.axis_index("tp") * width, LANES), width)]
    here = direction_ref[:, pl.ds(pl.multiple_of(lax.axis_index("ctx") * size, LANES), size)]
    parts_ref[...] = in_parts(dot_parts(in_parts(here), weight_ref[...]))


def run_inner(direction, weight):
    out_shape = [
        jax.ShapeDtypeStruct((STEP, weight.shape[0]), jnp.bfloat16),
        jax.ShapeDtypeStruct((1, LANES), jnp.float32),
        jax.ShapeDtypeStruct((1, weight.shape[1] // 2), jnp.float32),
    ]
    return call(inner_kernel, "inner", out_shape, direction, weight)


def project_kernel(begin, rows, away, weight_ref, piece_ref, *outs):
    cut = outs[0].shape[1]
    width = cut * len(outs)
    side = lax.axis_index("tp") % 2
    which = 1 - side if away else side
    for start in range(0, width, 256):
        columns = pl.ds(pl.multiple_of(which * width + start, 256), 256)
        out = jnp.dot(piece_ref[begin : begin + rows, :], weight_ref[:, columns], preferred_element_type=jnp.float32)
        ref, to = outs[start // cut], start % cut
        ref[:, to : to + 256] = out.astype(ref.dtype)


def run_project(weight, piece, begin, rows, count, *tokens):
    width = weight.shape[1] // 2
    sends = [jax.ShapeDtypeStruct((rows, width // count), jnp.bfloat16)] * count
    keep = [jax.ShapeDtypeStruct((rows, width), jnp.float32)]
    away, here = [functools.partial(project_kernel, begin, rows, x) for x in (True, False)]
    sends = call(away, "project", sends, weight, piece, tokens=tokens)
    return sends, call(here, "project", keep, weight, piece, tokens=tokens)[0]


def put_behind(ref, rows, row):
    here = slice(rows, rows + STEP)
    ref[here, :] = jnp.zeros((STEP, ref.shape[1]), jnp.bfloat16)
    ref[here, : row.shape[1]] = in_parts(row)


def take_behind(ref, rows, width):
    return jnp.sum(ref[rows : rows + STEP, :width].astype(jnp.float32), axis=0, keepdims=True)


def level_kernel(parts_ref, far_ref, *refs):
    *pieces, out_ref = refs
    far_parts = far_ref[far_ref.shape[0] - STEP :, :]
    start = 0
    for piece in pieces:
        end = start + piece.shape[0]
        out_ref[:, start:end] = dot_parts(parts_ref[...], piece[...]) + dot_parts(far_parts, piece[...])
        start = end


def add_shares(lefts, rights, outs):
    width = sum(ref.shape[1] for ref in lefts)
    rows = lefts[0].shape[0]
    step = min(ref.shape[1] for ref in (*lefts, *rights, *outs))

    def at(pieces, row, column):
        size = pieces[0].shape[1]
        return pieces[column // size].at[row : row + STEP, column % size : column % size + step]

    for row in range(0, rows, STEP):
        for column in range(0, width, step):
            left = at(lefts, row, column)[...].astype(jnp.float32)
            right = at(rights, row, column)[...].astype(jnp.float32)
            at(outs, row, column)[...] = (left + right).astype(jnp.bfloat16)


def merge_kernel(left, right, *refs):
    add_shares(refs[:left], refs[left : left + right], refs[left + right :])


def run_merge(lefts, rights, count):
    rows, width = lefts[0].shape[0], sum(x.shape[1] for x in lefts)
    kernel = functools.partial(merge_kernel, len(lefts), len(rights))
    out_shape = [jax.ShapeDtypeStruct((rows, width // count), jnp.bfloat16)] * count
    return call(kernel, "merge", out_shape, *lefts, *rights)


def merge_parts_kernel(keep_ref, parts_ref, *refs):
    add_shares((keep_ref,), refs[:-1], refs[-1:])
    refs[-1][keep_ref.shape[0] :, :] = parts_ref[...]


def is_keeper():
    return lax.axis_index("tp") // 2 == lax.axis_index("ctx")


def choose_kernel(straight_ref, own_ref, level_ref, other_ref, out_ref, total_ref):
    keeper = is_keeper()

    @pl.when(keeper)
    def _():
        rows = straight_ref.shape[0] - STEP
        out_ref[:rows, :] = straight_ref[:rows, :]

    @pl.when(jnp.logical_not(keeper))
    def _():
        out_ref[: own_ref.shape[0], :] = own_ref[...]

    total = level_ref[...] + other_ref[...]
    total_ref[...] = total
    put_behind(out_ref, out_ref.shape[0] - STEP, total)


def finish_kernel(start, count, *refs):
    level_ref, norm_ref, direction_ref, keep_ref, core_ref, hop_ref, first_ref = refs[:7]
    second_ref = None if start else refs[7]
    rows = level_ref.shape[1]
    if start:
        out_hbm, out_near, sems = refs[-3:]
        level = level_ref[...]
        copies = []
    else:
        out_hbm, level_hbm, level_near, level_out, out_near, sems = refs[-6:]
        level = level_ref[...] + take_behind(second_ref, second_ref.shape[0] - STEP, rows)
        level = level / norm_ref[0:1, 0:1]
        level_near[...] = level
        level_out[...] = level
        copies = [pltpu.make_async_copy(level_out, level_hbm, sems.at[2])]
        copies[0].start()
    direction = direction_ref[...]
    keeper = is_keeper()
    column = jnp.transpose(jnp.broadcast_to(level, (LANES, rows)))

    def put(row, *pieces):
        here = slice(row, row + STEP)
        total = pieces[0][here, :].astype(jnp.float32)
        for piece in pieces[1:]:
            total = total + piece[here, :].astype(jnp.float32)
        total = total - column[start + row : start + row + STEP, 0:1] * direction
        out_near[here, :] = total.astype(jnp.bfloat16)

    for i in range(2):
        begin, end = i * count // 2, (i + 1) * count // 2

        @pl.when(keeper)
        def _():
            for row in range(begin, end, STEP):
                put(row, keep_ref, core_ref, hop_ref)

        @pl.when(jnp.logical_not(keeper))
        def _():
            for row in range(begin, end, STEP):
                put(row, *((first_ref,) if start else (first_ref, second_ref)))

        here, there = pl.ds(begin, end - begin), pl.ds(start + begin, end - begin)
        copies.append(pltpu.make_async_copy(out_near.at[here], out_hbm.at[there], sems.at[i]))
        copies[-1].start()
    for copy in copies:
        copy.wait()


def run_finish(start, rows, operands, before=()):
    count, width = operands[3].shape
    one_row = jax.ShapeDtypeStruct((1, rows), jnp.float32)
    out_shape, out_specs = [pltpu.HBM((rows, width), jnp.bfloat16)], [AWAY]
    scratch_shapes = [pltpu.VMEM((count, width), jnp.bfloat16), pltpu.SemaphoreType.DMA((3,))]
    if not before:
        out_shape += [pltpu.HBM(one_row.shape, one_row.dtype), one_row]
        out_specs += [AWAY, WHOLE]
        scratch_shapes = [pltpu.VMEM(one_row.shape, one_row.dtype)] + scratch_shapes
    return pl.pallas_call(
        functools.partial(finish_kernel, start, count),
        out_shape=out_shape,
        in_specs=[WHOLE] * len(operands) + [AWAY] * len(before),
        out_specs=out_specs,
        scratch_shapes=scratch_shapes,
        input_output_aliases={len(operands): 0} if before else {},
        compiler_params=params(),
        cost_estimate=cost(10**6),
        name="finish",
    )(*operands, *[far(x) for x in before])


def plane_plan(q, k, v, short_taps, decay_rate, residue, out_weight, direction):
    rows, width = q.shape
    cut = rows // 2
    blocks = width // LANES
    axes = ("ctx", "tp")
    across = [(4 * c + p, 4 * (1 - c) + p) for c in range(2) for p in range(4)]
    sibling = [(4 * c + p, 4 * c + (p ^ 1)) for c in range(2) for p in range(4)]
    pair = [(4 * c + p, 4 * c + (p ^ 2)) for c in range(2) for p in range(4)]

    ended, signal, decay, taps, edge, rate, residue, q = run_front(q, k, v, short_taps, decay_rate.T, residue.T)
    carry = lax.ppermute(ended, axes, across)
    local, query, gain, weight, direction = run_local(
        q, signal, decay, taps, gains_of(rate, residue), out_weight, direction.reshape(1, -1)
    )
    first, state = run_correct(0, cut, decay, gain, local, query, blocks, carry, taps, edge)
    (second,) = run_correct(cut, rows - cut, decay, gain, local, query, blocks, state)
    far_first = lax.ppermute(first, axes, across)
    far_second = lax.ppermute(second, axes, across)

    def exchange(arrays, pairs):
        return [lax.ppermute(array, axes, pairs) for array in arrays]

    weight = after(weight, first)
    parts, norm, direction = run_inner(direction, weight)
    sends0, keep0 = run_project(weight, first, 0, cut, 1)
    sends1, keep1 = run_project(weight, second, 0, rows - cut, 1)
    (core0,) = exchange(sends0, sibling)
    (hop0,) = exchange(run_merge((keep0,), (core0,), 1), pair)

    sends, far_keep = run_project(weight, far_first, 0, cut, 2, parts, *sends0, *sends1)
    (sums0,) = call(
        merge_parts_kernel, "merge", [rows_of(cut + STEP, far_keep)], far_keep, parts, *exchange(sends, sibling)
    )
    (straight,) = exchange([sums0], across)

    sends, far_keep = run_project(weight, after(far_second, sums0, hop0), 0, rows - cut, 2)
    sums1 = run_merge((far_keep,), exchange(sends, sibling), 2)
    moved = exchange(sums1, pair)
    (core1,) = exchange(sends1, sibling)
    (own1,) = run_merge((keep1,), (core1,), 1)

    one_row = jax.ShapeDtypeStruct((1, rows), jnp.float32)
    (level,) = call(level_kernel, "level", [one_row], parts, straight, first, second)
    payload = rows_of(max(cut, rows - cut) + STEP, far_keep)
    turned, level = call(
        choose_kernel,
        "choose",
        [payload, one_row],
        straight,
        own1,
        level,
        *exchange([level], sibling),
    )
    (turned,) = exchange([turned], pair)
    (merged,) = exchange(run_merge(sums1, moved, 1), across)
    shared = (norm, direction)
    before, level, near = run_finish(0, rows, (level, *shared, keep0, core0, hop0, straight, turned))
    (ablated,) = run_finish(cut, rows, (near, *shared, keep1, core1, turned, merged), (before,))
    return ablated, level.reshape(rows)


def gather_plan(q, k, v, short_taps, decay_rate, residue, out_weight, direction):
    rows, width = q.shape
    blocks = width // LANES
    modes = decay_rate.shape[1]
    tp = lax.axis_index("tp")
    ctx_size = lax.axis_size("ctx")
    next_one = [(i, i + 1) for i in range(ctx_size - 1)]
    ended, signal, decay, taps, edge, rate, residue, q = run_front(q, k, v, short_taps, decay_rate.T, residue.T)
    halo = lax.ppermute(ended[modes * blocks :], "ctx", next_one)
    local, query, gain = run_local(q, signal, decay, taps, gains_of(rate, residue))
    k2, k1, v2, v1 = [halo[i * blocks : (i + 1) * blocks] for i in range(4)]
    tap = taps.reshape(9, blocks, LANES)
    key0, key1, value0, value1 = edge.reshape(4, blocks, LANES)
    extra0 = (key0 + tap[4] * k1 + tap[5] * k2) * (value0 + tap[7] * v1 + tap[8] * v2) - key0 * value0
    extra1 = (key1 + tap[5] * k1) * (value1 + tap[8] * v1) - key1 * value1
    wide_rate = decay_rate.T.reshape(modes, blocks, LANES)
    state = (
        ended[: modes * blocks].reshape(modes, blocks, LANES)
        + jnp.exp(-wide_rate * (rows - 1)) * extra0
        + jnp.exp(-wide_rate * (rows - 2)) * extra1
    )
    reach = 1
    while reach < ctx_size:
        earlier = lax.ppermute(state, "ctx", [(i, i + reach) for i in range(ctx_size - reach)])
        state = state + jnp.exp(-wide_rate * (rows * reach)) * earlier
        reach *= 2
    start = lax.ppermute(state, "ctx", next_one).reshape(modes * blocks, LANES)
    carry = jnp.concatenate([start, halo], axis=0)
    (gated,) = run_correct(0, rows, decay, gain, local, query, blocks, carry, taps, edge)
    partial_terms = lax.dot_general(
        gated,
        lax.all_gather(out_weight, "ctx", axis=1, tiled=True),
        (((1,), (0,)), ((), ())),
        preferred_element_type=jnp.float32,
    )
    summed = lax.psum_scatter(
        partial_terms.astype(jnp.bfloat16), "tp", scatter_dimension=1, tiled=True
    ).astype(jnp.float32)
    width_here = summed.shape[1]
    direction_here = lax.dynamic_slice_in_dim(direction, tp * width_here, width_here, 0)
    norm_total = jnp.sum(direction * direction) + EPSILON
    local_inner = jnp.dot(summed, direction_here, precision=HIGHEST)
    feature_level = lax.psum(local_inner, "tp") / norm_total
    ablated = (summed - feature_level[:, None] * direction_here[None, :]).astype(jnp.bfloat16)
    return ablated, feature_level


def solution(mesh):
    placed = (
        P(("dp", "ctx"), "tp"),
        P(("dp", "ctx"), "tp"),
        P(("dp", "ctx"), "tp"),
        P(None, None, "tp"),
        P("tp", None),
        P("tp", None),
        P("tp", "ctx"),
        P(),
    )
    plane = mesh.shape["ctx"] == 2 and mesh.shape["tp"] == 4
    return jax.shard_map(
        plane_plan if plane else gather_plan,
        mesh=mesh,
        in_specs=placed,
        out_specs=(P(("dp", "ctx"), "tp"), P(("dp", "ctx"))),
        check_vma=False,
    )
```

```python
import functools

import jax
import jax.numpy as jnp
from jax import lax
from jax.experimental import pallas as pl
from jax.experimental.pallas import tpu as pltpu
from jax.sharding import PartitionSpec as P

EPSILON = 1e-06
HIGHEST = lax.Precision.HIGHEST
LANES = 128
GROUP = 8
STEP = 16
WHOLE = pl.BlockSpec(memory_space=pltpu.VMEM)
AWAY = pl.BlockSpec(memory_space=pltpu.HBM)


def params(mebibytes=20):
    return pltpu.CompilerParams(vmem_limit_bytes=mebibytes * 1024 * 1024)


def cost(flops):
    return pl.CostEstimate(flops=flops, bytes_accessed=1024, transcendentals=0)


def spread(source, scratch, row, to):
    blocks = source.shape[1] // LANES
    for block in range(blocks):
        piece = source[pl.ds(row, STEP), block * LANES : (block + 1) * LANES].astype(jnp.float32)
        for half in range(STEP // GROUP):
            start = (half * blocks + block) * GROUP
            scratch[pl.ds(to + start, GROUP), :] = piece[half * GROUP : (half + 1) * GROUP]


def spread_rows(source, target):
    count, width = source.shape
    blocks = width // LANES
    for block in range(blocks):
        target[pl.ds(block, count, stride=blocks), :] = source[:, block * LANES : (block + 1) * LANES]


def place_of(index, blocks):
    return pl.ds((index // GROUP) * (blocks * GROUP) + index % GROUP, blocks, stride=GROUP)


def tile(ref, index, blocks):
    return ref[index * blocks : (index + 1) * blocks, :]


def moving_tile(index, blocks):
    return pl.ds(pl.multiple_of(index * blocks, blocks), blocks)


def front_kernel(*refs):
    k_hbm, v_hbm, q_hbm, taps_hbm, rate_hbm, residue_hbm = refs[:6]
    carry_ref, signal_ref, decay_ref, taps_ref, edge_ref, rate_ref, residue_ref, q_near = refs[6:14]
    k_near, v_near, taps_near, *wides, sems, late_sems = refs[-9:]
    wides = (wides[:2], wides[2:])
    rows, width = k_near.shape
    blocks = width // LANES
    modes = rate_ref.shape[0]
    pieces = sems.shape[0] // 2 - 1
    height = rows // pieces

    def part(i):
        here = pl.ds(i * height, height)
        return (
            pltpu.make_async_copy(k_hbm.at[here], k_near.at[here], sems.at[2 * i]),
            pltpu.make_async_copy(v_hbm.at[here], v_near.at[here], sems.at[2 * i + 1]),
        )

    rate_copy = pltpu.make_async_copy(rate_hbm, rate_ref, sems.at[2 * pieces])
    taps_copy = pltpu.make_async_copy(taps_hbm, taps_near, sems.at[2 * pieces + 1])
    late = [(residue_hbm, residue_ref), (q_hbm, q_near)]
    late = [pltpu.make_async_copy(source, target, late_sems.at[i]) for i, (source, target) in enumerate(late)]
    rate_copy.start()
    taps_copy.start()
    for i in range(pieces):
        for copy in part(i):
            copy.start()
    for copy in late:
        copy.start()
    rate_copy.wait()
    taps_copy.wait()
    spread_rows(jnp.exp(-rate_ref[...]), decay_ref)
    for i in range(3):
        for block in range(blocks):
            taps_ref[pl.ds(3 * i * blocks + block, 3, stride=blocks), :] = taps_near[
                i, :, block * LANES : (block + 1) * LANES
            ]
    zero = jnp.zeros((blocks, LANES), jnp.float32)
    key_taps = [tile(taps_ref, 3 + j, blocks) for j in range(3)]
    value_taps = [tile(taps_ref, 6 + j, blocks) for j in range(3)]
    decay = [tile(decay_ref, m, blocks) for m in range(modes)]

    def step(row, held):
        state, (k2, k1, v2, v1) = list(held[:modes]), held[modes:]
        for half, (k_wide, v_wide) in enumerate(wides):
            spread(k_near, k_wide, row + half * STEP, 0)
            spread(v_near, v_wide, row + half * STEP, 0)
        for half, (k_wide, v_wide) in enumerate(wides):
            for index in range(STEP):
                k0 = k_wide[place_of(index, blocks), :]
                v0 = v_wide[place_of(index, blocks), :]
                key = key_taps[0] * k0 + key_taps[1] * k1 + key_taps[2] * k2
                value = value_taps[0] * v0 + value_taps[1] * v1 + value_taps[2] * v2
                signal = key * value
                signal_ref[moving_tile(row + half * STEP + index, blocks), :] = signal
                state = [decay[m] * state[m] + signal for m in range(modes)]
                k2, k1, v2, v1 = k1, k0, v1, v0
        return tuple(state) + (k2, k1, v2, v1)

    held = (zero,) * (modes + 4)
    for i in range(pieces):
        for copy in part(i):
            copy.wait()
        if i == 0:
            spread(k_near, wides[0][0], 0, 0)
            spread(v_near, wides[0][1], 0, 0)
            for wide, taps, place in ((wides[0][0], key_taps, 0), (wides[0][1], value_taps, 2)):
                x0, x1 = wide[place_of(0, blocks), :], wide[place_of(1, blocks), :]
                edge_ref[place * blocks : (place + 1) * blocks, :] = taps[0] * x0
                edge_ref[(place + 1) * blocks : (place + 2) * blocks, :] = taps[0] * x1 + taps[1] * x0
        held = lax.fori_loop(
            0,
            height // (2 * STEP),
            lambda j, held, i=i: step(pl.multiple_of(i * height + j * 2 * STEP, 2 * STEP), held),
            held,
        )
    for m in range(modes + 4):
        carry_ref[m * blocks : (m + 1) * blocks, :] = held[m]
    for copy in late:
        copy.wait()
    k_wide = wides[0][0]
    spread(q_near, k_wide, rows - STEP, 0)
    for i in range(2):
        start = (modes + 4 + i) * blocks
        carry_ref[start : start + blocks, :] = k_wide[place_of(STEP - 2 + i, blocks), :]


def far(x):
    return pltpu.with_memory_space_constraint(x, pltpu.HBM)


def run_front(q, k, v, short_taps, rate, residue):
    rows, width = k.shape
    modes = rate.shape[0]
    blocks = width // LANES
    pieces = 4

    def wide(n):
        return jax.ShapeDtypeStruct((n * blocks, LANES), jnp.float32)

    def like(x):
        return jax.ShapeDtypeStruct(x.shape, x.dtype)

    out_shape = [wide(modes + 6), wide(rows), wide(modes), wide(9), wide(4), like(rate), like(residue), like(q)]
    return pl.pallas_call(
        front_kernel,
        out_shape=out_shape,
        in_specs=[AWAY] * 6,
        out_specs=[WHOLE] * len(out_shape),
        scratch_shapes=[
            pltpu.VMEM((rows, width), jnp.bfloat16),
            pltpu.VMEM((rows, width), jnp.bfloat16),
            pltpu.VMEM(short_taps.shape, jnp.float32),
            *[pltpu.VMEM((STEP * blocks, LANES), jnp.float32)] * 4,
            pltpu.SemaphoreType.DMA((2 * pieces + 2,)),
            pltpu.SemaphoreType.DMA((2,)),
        ],
        compiler_params=params(),
        cost_estimate=cost(10**8),
        name="front",
    )(*[far(x) for x in (k, v, q, short_taps, rate, residue)])


def local_kernel(q_near, signal_ref, decay_ref, taps_ref, gain_near, *refs):
    copies = []
    if len(refs) > 5:
        weight_hbm, direction_hbm, weight_ref, direction_ref, sems = refs[:2] + refs[5:7] + refs[-1:]
        refs = refs[2:5] + refs[7:-1]
        count = sems.shape[0] - 1
        copies.append(pltpu.make_async_copy(direction_hbm, direction_ref, sems.at[count]))
        copies[-1].start()
        depth = weight_ref.shape[0] // count
        for i in range(count):
            here = pl.ds(i * depth, depth)
            copies.append(pltpu.make_async_copy(weight_hbm.at[here], weight_ref.at[here], sems.at[i]))
            copies[-1].start()
    out_ref, query_ref, gain_ref, *wides = refs
    rows, width = q_near.shape
    blocks = width // LANES
    modes = gain_near.shape[0]
    spread_rows(gain_near[...], gain_ref)
    zero = jnp.zeros((blocks, LANES), jnp.float32)
    taps = [tile(taps_ref, j, blocks) for j in range(3)]
    decay = [tile(decay_ref, m, blocks) for m in range(modes)]
    gain = [tile(gain_ref, m, blocks) for m in range(modes)]

    def step(j, held):
        row = pl.multiple_of(j * 2 * STEP, 2 * STEP)
        state, (q2, q1) = list(held[:modes]), held[modes:]
        for half, q_wide in enumerate(wides):
            spread(q_near, q_wide, row + half * STEP, 0)
        for half, q_wide in enumerate(wides):
            for index in range(STEP):
                q0 = q_wide[place_of(index, blocks), :]
                here = moving_tile(row + half * STEP + index, blocks)
                signal = signal_ref[here, :]
                query_ref[here, :] = taps[0] * q0 + taps[1] * q1 + taps[2] * q2
                state = [decay[m] * state[m] + signal for m in range(modes)]
                sums = [gain[m] * state[m] for m in range(modes)]
                while len(sums) > 1:
                    sums = [sums[i] + sums[i + 1] for i in range(0, len(sums), 2)]
                out_ref[here, :] = sums[0]
                q2, q1 = q1, q0
        return tuple(state) + (q2, q1)

    lax.fori_loop(0, rows // (2 * STEP), step, (zero,) * (modes + 2))
    for copy in copies:
        copy.wait()


def run_local(q, signal, decay, taps, gain, *weight):
    rows, width = q.shape
    blocks = width // LANES
    wide = jax.ShapeDtypeStruct((rows * blocks, LANES), jnp.float32)
    out_shape = [wide, wide, jax.ShapeDtypeStruct(decay.shape, jnp.float32)]
    scratch_shapes = [pltpu.VMEM((STEP * blocks, LANES), jnp.float32)] * 2
    if weight:
        out_shape += [jax.ShapeDtypeStruct(x.shape, x.dtype) for x in weight]
        scratch_shapes.append(pltpu.SemaphoreType.DMA((5,)))
        weight = tuple(far(x) for x in weight)
    return pl.pallas_call(
        local_kernel,
        out_shape=out_shape,
        in_specs=[WHOLE] * 5 + [AWAY] * len(weight),
        out_specs=[WHOLE] * len(out_shape),
        scratch_shapes=scratch_shapes,
        compiler_params=params(),
        cost_estimate=cost(10**6),
        name="local_filter",
    )(q, signal, decay, taps, gain, *weight)


def correct_kernel(blocks, start, decay_ref, gain_ref, local_ref, query_ref, *refs):
    wide, outs = refs[-1], refs[1 if start else 3 : -1]
    out_ref = outs[0]
    rows = out_ref.shape[0]
    modes = decay_ref.shape[0] // blocks
    decay = [tile(decay_ref, m, blocks) for m in range(modes)]
    extra = query_extra = ()
    if start:
        state = tuple(tile(refs[0], m, blocks) for m in range(modes))
    else:
        carry_ref, taps_ref, edge_ref = refs[:3]
        carried = jnp.where(lax.axis_index("ctx") > 0, 1.0, 0.0)
        k2, k1, v2, v1, q2, q1 = [carried * tile(carry_ref, modes + i, blocks) for i in range(6)]
        tap = [tile(taps_ref, i, blocks) for i in range(9)]
        key0, key1, value0, value1 = [tile(edge_ref, i, blocks) for i in range(4)]
        extra = (
            (key0 + tap[4] * k1 + tap[5] * k2) * (value0 + tap[7] * v1 + tap[8] * v2) - key0 * value0,
            (key1 + tap[5] * k1) * (value1 + tap[8] * v1) - key1 * value1,
        )
        query_extra = (tap[1] * q1 + tap[2] * q2, tap[2] * q1)
        state = tuple(tile(gain_ref, m, blocks) * (carried * tile(carry_ref, m, blocks)) for m in range(modes))

    def step(row, state, first):
        state = list(state)
        for index in range(STEP):
            here = moving_tile(start + row + index, blocks)
            state = [decay[m] * state[m] for m in range(modes)]
            query = query_ref[here, :]
            if first and index < 2:
                state = [state[m] + tile(gain_ref, m, blocks) * extra[index] for m in range(modes)]
                query = query + query_extra[index]
            sums = state
            while len(sums) > 1:
                sums = [sums[i] + sums[i + 1] for i in range(0, len(sums), 2)]
            wide[place_of(index, blocks), :] = query * (local_ref[here, :] + sums[0])
        for block in range(blocks):
            halves = [
                wide[(half * blocks + block) * GROUP : (half * blocks + block + 1) * GROUP, :]
                for half in range(STEP // GROUP)
            ]
            out_ref[pl.ds(row, STEP), block * LANES : (block + 1) * LANES] = jnp.concatenate(
                halves, axis=0
            ).astype(jnp.bfloat16)
        return tuple(state)

    begin = 0
    if start == 0:
        state = step(0, state, True)
        begin = 1
    state = lax.fori_loop(
        begin, rows // STEP, lambda j, state: step(pl.multiple_of(j * STEP, STEP), state, False), state
    )
    for state_out_ref in outs[1:]:
        for m in range(modes):
            state_out_ref[m * blocks : (m + 1) * blocks, :] = state[m]


def run_correct(start, rows, decay, gain, local, query, blocks, *before):
    more = start + rows < local.shape[0] // blocks
    return pl.pallas_call(
        functools.partial(correct_kernel, blocks, start),
        out_shape=[jax.ShapeDtypeStruct((rows, blocks * LANES), jnp.bfloat16)]
        + [jax.ShapeDtypeStruct(decay.shape, jnp.float32)] * more,
        in_specs=[WHOLE] * (4 + len(before)),
        out_specs=[WHOLE] * (1 + more),
        scratch_shapes=[pltpu.VMEM((STEP * blocks, LANES), jnp.float32)],
        compiler_params=params(),
        cost_estimate=cost(10**8),
        name="carried_filter",
    )(decay, gain, local, query, *before)


def gains_of(rate, residue):
    return residue * jnp.sqrt(-jnp.expm1(-2.0 * rate)) * rate.shape[0] ** (-0.5)


def split_three(x):
    high = x.astype(jnp.bfloat16)
    rest = x - high.astype(jnp.float32)
    middle = rest.astype(jnp.bfloat16)
    low = (rest - middle.astype(jnp.float32)).astype(jnp.bfloat16)
    return high, middle, low


def in_parts(row):
    return jnp.concatenate(list(split_three(row)) + [jnp.zeros((13, row.shape[1]), jnp.bfloat16)], axis=0)


def dot_parts(parts, matrix):
    out = lax.dot_general(parts, matrix, (((1,), (1,)), ((), ())), preferred_element_type=jnp.float32)
    return out[0:1] + out[1:2] + out[2:3]


def idle_kernel(*refs):
    pass


def after(array, *others):
    return pl.pallas_call(
        idle_kernel,
        out_shape=jax.ShapeDtypeStruct(array.shape, array.dtype),
        in_specs=[pl.BlockSpec(memory_space=pl.ANY)] * (1 + len(others)),
        out_specs=pl.BlockSpec(memory_space=pl.ANY),
        input_output_aliases={0: 0},
        compiler_params=params(),
        cost_estimate=cost(1),
        name="after",
    )(array, *others)


def rows_of(count, like, dtype=jnp.bfloat16):
    return jax.ShapeDtypeStruct((count, like.shape[1]), dtype)


def call(kernel, name, out_shape, *operands, tokens=()):
    def with_tokens(*refs):
        kernel(*refs[: len(operands)], *refs[len(operands) + len(tokens) :])

    return pl.pallas_call(
        with_tokens,
        out_shape=out_shape,
        in_specs=[WHOLE] * len(operands) + [pl.BlockSpec(memory_space=pl.ANY)] * len(tokens),
        out_specs=[WHOLE] * len(out_shape),
        compiler_params=params(),
        cost_estimate=cost(10**6),
        name=name,
    )(*operands, *tokens)


def inner_kernel(direction_ref, weight_ref, parts_ref, norm_ref, here_ref):
    everything = direction_ref[...]
    norm_ref[...] = jnp.broadcast_to(
        jnp.sum(everything * everything, axis=1, keepdims=True) + EPSILON, norm_ref.shape
    )
    size, width = weight_ref.shape[1], here_ref.shape[1]
    here_ref[...] = direction_ref[:, pl.ds(pl.multiple_of(lax.axis_index("tp") * width, LANES), width)]
    here = direction_ref[:, pl.ds(pl.multiple_of(lax.axis_index("ctx") * size, LANES), size)]
    parts_ref[...] = in_parts(dot_parts(in_parts(here), weight_ref[...]))


def run_inner(direction, weight):
    out_shape = [
        jax.ShapeDtypeStruct((STEP, weight.shape[0]), jnp.bfloat16),
        jax.ShapeDtypeStruct((1, LANES), jnp.float32),
        jax.ShapeDtypeStruct((1, weight.shape[1] // 2), jnp.float32),
    ]
    return call(inner_kernel, "inner", out_shape, direction, weight)


def project_kernel(begin, rows, away, weight_ref, piece_ref, *outs):
    cut = outs[0].shape[1]
    width = cut * len(outs)
    side = lax.axis_index("tp") % 2
    which = 1 - side if away else side
    for start in range(0, width, 512):
        columns = pl.ds(pl.multiple_of(which * width + start, 512), 512)
        out = jnp.dot(piece_ref[begin : begin + rows, :], weight_ref[:, columns], preferred_element_type=jnp.float32)
        ref, to = outs[start // cut], start % cut
        ref[:, to : to + 512] = out.astype(ref.dtype)


def run_project(weight, piece, begin, rows, count, *tokens):
    width = weight.shape[1] // 2
    sends = [jax.ShapeDtypeStruct((rows, width // count), jnp.bfloat16)] * count
    keep = [jax.ShapeDtypeStruct((rows, width), jnp.float32)]
    away, here = [functools.partial(project_kernel, begin, rows, x) for x in (True, False)]
    sends = call(away, "project", sends, weight, piece, tokens=tokens)
    return sends, call(here, "project", keep, weight, piece, tokens=tokens)[0]


def put_behind(ref, rows, row):
    here = slice(rows, rows + STEP)
    ref[here, :] = jnp.zeros((STEP, ref.shape[1]), jnp.bfloat16)
    ref[here, : row.shape[1]] = in_parts(row)


def take_behind(ref, rows, width):
    return jnp.sum(ref[rows : rows + STEP, :width].astype(jnp.float32), axis=0, keepdims=True)


def level_kernel(parts_ref, far_ref, *refs):
    *pieces, out_ref = refs
    far_parts = far_ref[far_ref.shape[0] - STEP :, :]
    start = 0
    for piece in pieces:
        end = start + piece.shape[0]
        out_ref[:, start:end] = dot_parts(parts_ref[...], piece[...]) + dot_parts(far_parts, piece[...])
        start = end


def add_shares(lefts, rights, outs):
    width = sum(ref.shape[1] for ref in lefts)
    rows = lefts[0].shape[0]
    step = min(ref.shape[1] for ref in (*lefts, *rights, *outs))

    def at(pieces, row, column):
        size = pieces[0].shape[1]
        return pieces[column // size].at[row : row + STEP, column % size : column % size + step]

    for row in range(0, rows, STEP):
        for column in range(0, width, step):
            left = at(lefts, row, column)[...].astype(jnp.float32)
            right = at(rights, row, column)[...].astype(jnp.float32)
            at(outs, row, column)[...] = (left + right).astype(jnp.bfloat16)


def merge_kernel(left, right, *refs):
    add_shares(refs[:left], refs[left : left + right], refs[left + right :])


def run_merge(lefts, rights, count):
    rows, width = lefts[0].shape[0], sum(x.shape[1] for x in lefts)
    kernel = functools.partial(merge_kernel, len(lefts), len(rights))
    out_shape = [jax.ShapeDtypeStruct((rows, width // count), jnp.bfloat16)] * count
    return call(kernel, "merge", out_shape, *lefts, *rights)


def merge_parts_kernel(keep_ref, parts_ref, *refs):
    add_shares((keep_ref,), refs[:-1], refs[-1:])
    refs[-1][keep_ref.shape[0] :, :] = parts_ref[...]


def is_keeper():
    return lax.axis_index("tp") // 2 == lax.axis_index("ctx")


def choose_kernel(straight_ref, own_ref, level_ref, other_ref, out_ref, total_ref):
    keeper = is_keeper()

    @pl.when(keeper)
    def _():
        rows = straight_ref.shape[0] - STEP
        out_ref[:rows, :] = straight_ref[:rows, :]

    @pl.when(jnp.logical_not(keeper))
    def _():
        out_ref[: own_ref.shape[0], :] = own_ref[...]

    total = level_ref[...] + other_ref[...]
    total_ref[...] = total
    put_behind(out_ref, out_ref.shape[0] - STEP, total)


def finish_kernel(start, count, *refs):
    level_ref, norm_ref, direction_ref, keep_ref, core_ref, hop_ref, first_ref = refs[:7]
    second_ref = None if start else refs[7]
    rows = level_ref.shape[1]
    if start:
        out_hbm, out_near, sems = refs[-3:]
        level = level_ref[...]
        copies = []
    else:
        out_hbm, level_hbm, level_near, level_out, out_near, sems = refs[-6:]
        level = level_ref[...] + take_behind(second_ref, second_ref.shape[0] - STEP, rows)
        level = level / norm_ref[0:1, 0:1]
        level_near[...] = level
        level_out[...] = level
        copies = [pltpu.make_async_copy(level_out, level_hbm, sems.at[2])]
        copies[0].start()
    direction = direction_ref[...]
    keeper = is_keeper()
    column = jnp.transpose(jnp.broadcast_to(level, (LANES, rows)))

    def put(row, *pieces):
        here = slice(row, row + STEP)
        total = pieces[0][here, :].astype(jnp.float32)
        for piece in pieces[1:]:
            total = total + piece[here, :].astype(jnp.float32)
        total = total - column[start + row : start + row + STEP, 0:1] * direction
        out_near[here, :] = total.astype(jnp.bfloat16)

    for i in range(2):
        begin, end = i * count // 2, (i + 1) * count // 2

        @pl.when(keeper)
        def _():
            for row in range(begin, end, STEP):
                put(row, keep_ref, core_ref, hop_ref)

        @pl.when(jnp.logical_not(keeper))
        def _():
            for row in range(begin, end, STEP):
                put(row, *((first_ref,) if start else (first_ref, second_ref)))

        here, there = pl.ds(begin, end - begin), pl.ds(start + begin, end - begin)
        copies.append(pltpu.make_async_copy(out_near.at[here], out_hbm.at[there], sems.at[i]))
        copies[-1].start()
    for copy in copies:
        copy.wait()


def run_finish(start, rows, operands, before=()):
    count, width = operands[3].shape
    one_row = jax.ShapeDtypeStruct((1, rows), jnp.float32)
    out_shape, out_specs = [pltpu.HBM((rows, width), jnp.bfloat16)], [AWAY]
    scratch_shapes = [pltpu.VMEM((count, width), jnp.bfloat16), pltpu.SemaphoreType.DMA((3,))]
    if not before:
        out_shape += [pltpu.HBM(one_row.shape, one_row.dtype), one_row]
        out_specs += [AWAY, WHOLE]
        scratch_shapes = [pltpu.VMEM(one_row.shape, one_row.dtype)] + scratch_shapes
    return pl.pallas_call(
        functools.partial(finish_kernel, start, count),
        out_shape=out_shape,
        in_specs=[WHOLE] * len(operands) + [AWAY] * len(before),
        out_specs=out_specs,
        scratch_shapes=scratch_shapes,
        input_output_aliases={len(operands): 0} if before else {},
        compiler_params=params(),
        cost_estimate=cost(10**6),
        name="finish",
    )(*operands, *[far(x) for x in before])


def plane_plan(q, k, v, short_taps, decay_rate, residue, out_weight, direction):
    rows, width = q.shape
    cut = rows // 2
    blocks = width // LANES
    axes = ("ctx", "tp")
    across = [(4 * c + p, 4 * (1 - c) + p) for c in range(2) for p in range(4)]
    sibling = [(4 * c + p, 4 * c + (p ^ 1)) for c in range(2) for p in range(4)]
    pair = [(4 * c + p, 4 * c + (p ^ 2)) for c in range(2) for p in range(4)]

    ended, signal, decay, taps, edge, rate, residue, q = run_front(q, k, v, short_taps, decay_rate.T, residue.T)
    carry = lax.ppermute(ended, axes, across)
    local, query, gain, weight, direction = run_local(
        q, signal, decay, taps, gains_of(rate, residue), out_weight, direction.reshape(1, -1)
    )
    first, state = run_correct(0, cut, decay, gain, local, query, blocks, carry, taps, edge)
    (second,) = run_correct(cut, rows - cut, decay, gain, local, query, blocks, state)
    far_first = lax.ppermute(first, axes, across)
    far_second = lax.ppermute(second, axes, across)

    def exchange(arrays, pairs):
        return [lax.ppermute(array, axes, pairs) for array in arrays]

    weight = after(weight, first)
    parts, norm, direction = run_inner(direction, weight)
    sends0, keep0 = run_project(weight, first, 0, cut, 1)
    sends1, keep1 = run_project(weight, second, 0, rows - cut, 1)
    (core0,) = exchange(sends0, sibling)
    (hop0,) = exchange(run_merge((keep0,), (core0,), 1), pair)

    sends, far_keep = run_project(weight, far_first, 0, cut, 2, parts, *sends0, *sends1)
    (sums0,) = call(
        merge_parts_kernel, "merge", [rows_of(cut + STEP, far_keep)], far_keep, parts, *exchange(sends, sibling)
    )
    (straight,) = exchange([sums0], across)

    sends, far_keep = run_project(weight, after(far_second, sums0, hop0), 0, rows - cut, 2)
    sums1 = run_merge((far_keep,), exchange(sends, sibling), 2)
    moved = exchange(sums1, pair)
    (core1,) = exchange(sends1, sibling)
    (own1,) = run_merge((keep1,), (core1,), 1)

    one_row = jax.ShapeDtypeStruct((1, rows), jnp.float32)
    (level,) = call(level_kernel, "level", [one_row], parts, straight, first, second)
    payload = rows_of(max(cut, rows - cut) + STEP, far_keep)
    turned, level = call(
        choose_kernel,
        "choose",
        [payload, one_row],
        straight,
        own1,
        level,
        *exchange([level], sibling),
    )
    (turned,) = exchange([turned], pair)
    (merged,) = exchange(run_merge(sums1, moved, 1), across)
    shared = (norm, direction)
    before, level, near = run_finish(0, rows, (level, *shared, keep0, core0, hop0, straight, turned))
    (ablated,) = run_finish(cut, rows, (near, *shared, keep1, core1, turned, merged), (before,))
    return ablated, level.reshape(rows)


def gather_plan(q, k, v, short_taps, decay_rate, residue, out_weight, direction):
    rows, width = q.shape
    blocks = width // LANES
    modes = decay_rate.shape[1]
    tp = lax.axis_index("tp")
    ctx_size = lax.axis_size("ctx")
    next_one = [(i, i + 1) for i in range(ctx_size - 1)]
    ended, signal, decay, taps, edge, rate, residue, q = run_front(q, k, v, short_taps, decay_rate.T, residue.T)
    halo = lax.ppermute(ended[modes * blocks :], "ctx", next_one)
    local, query, gain = run_local(q, signal, decay, taps, gains_of(rate, residue))
    k2, k1, v2, v1 = [halo[i * blocks : (i + 1) * blocks] for i in range(4)]
    tap = taps.reshape(9, blocks, LANES)
    key0, key1, value0, value1 = edge.reshape(4, blocks, LANES)
    extra0 = (key0 + tap[4] * k1 + tap[5] * k2) * (value0 + tap[7] * v1 + tap[8] * v2) - key0 * value0
    extra1 = (key1 + tap[5] * k1) * (value1 + tap[8] * v1) - key1 * value1
    wide_rate = decay_rate.T.reshape(modes, blocks, LANES)
    state = (
        ended[: modes * blocks].reshape(modes, blocks, LANES)
        + jnp.exp(-wide_rate * (rows - 1)) * extra0
        + jnp.exp(-wide_rate * (rows - 2)) * extra1
    )
    reach = 1
    while reach < ctx_size:
        earlier = lax.ppermute(state, "ctx", [(i, i + reach) for i in range(ctx_size - reach)])
        state = state + jnp.exp(-wide_rate * (rows * reach)) * earlier
        reach *= 2
    start = lax.ppermute(state, "ctx", next_one).reshape(modes * blocks, LANES)
    carry = jnp.concatenate([start, halo], axis=0)
    (gated,) = run_correct(0, rows, decay, gain, local, query, blocks, carry, taps, edge)
    partial_terms = lax.dot_general(
        gated,
        lax.all_gather(out_weight, "ctx", axis=1, tiled=True),
        (((1,), (0,)), ((), ())),
        preferred_element_type=jnp.float32,
    )
    summed = lax.psum_scatter(
        partial_terms.astype(jnp.bfloat16), "tp", scatter_dimension=1, tiled=True
    ).astype(jnp.float32)
    width_here = summed.shape[1]
    direction_here = lax.dynamic_slice_in_dim(direction, tp * width_here, width_here, 0)
    norm_total = jnp.sum(direction * direction) + EPSILON
    local_inner = jnp.dot(summed, direction_here, precision=HIGHEST)
    feature_level = lax.psum(local_inner, "tp") / norm_total
    ablated = (summed - feature_level[:, None] * direction_here[None, :]).astype(jnp.bfloat16)
    return ablated, feature_level


def solution(mesh):
    placed = (
        P(("dp", "ctx"), "tp"),
        P(("dp", "ctx"), "tp"),
        P(("dp", "ctx"), "tp"),
        P(None, None, "tp"),
        P("tp", None),
        P("tp", None),
        P("tp", "ctx"),
        P(),
    )
    plane = mesh.shape["ctx"] == 2 and mesh.shape["tp"] == 4
    return jax.shard_map(
        plane_plan if plane else gather_plan,
        mesh=mesh,
        in_specs=placed,
        out_specs=(P(("dp", "ctx"), "tp"), P(("dp", "ctx"))),
        check_vma=False,
    )
```
